32 devices in a mesh: slide: 4 (over y, x), blk: 8 (over z, core).
Axes of the slice: x: 2, y: 2, z: 4, core: 2. Of those that a mesh axis runs over, the one named last changes fastest.
Arguments:
- counts: int32 [4, 1024, 13500], P('slide', 'blk'), may hold values from 0 to 7, as said below
- library: int32 [4, 1024], P('slide', 'blk'), may hold values from 2000 to 39999
- coords: int32 [4, 1024, 2], P('slide', 'blk'), may hold values from 0 to 1023
- noise: float32 [4, 1024, 512], P('slide', 'blk'), may hold values from -5 to 5
- decoded_cot: bfloat16 [4, 1024, 13500], P('slide', 'blk'), may hold values from -6 to 6
- prior_cot: float32 [4, 1024], P('slide', 'blk'), may hold values from -6 to 6
- embed_t: bfloat16 [1024, 13500], P('blk'), may hold values from -0.0546875 to 0.0546875
- w_qkv: bfloat16 [1024, 3072], P('blk'), may hold values from -0.1875 to 0.1875
- w_attn_out: bfloat16 [1024, 1024], P('blk'), may hold values from -0.625 to 0.625
- w_up: bfloat16 [1024, 4096], P('blk'), may hold values from -0.1875 to 0.1875
- up_bias: bfloat16 [4096], P('blk'), may hold values from -3 to 3
- w_down: bfloat16 [4096, 1024], P('blk'), may hold values from -0.09375 to 0.09375
- w_latent: bfloat16 [1024, 1024], P('blk'), may hold values from -0.046875 to 0.046875
- w_decode: bfloat16 [512, 13500], P('blk'), may hold values from -0.25 to 0.25
- comp_means: bfloat16 [512, 16], P('blk'), may hold values from -3 to 3
- norm_params: bfloat16 [1024, 4], P('blk'), as said below
Outputs:
- decoded: bfloat16 [4, 1024, 13500], P('slide', 'blk')
- prior: float32 [4, 1024], P('slide', 'blk')
- expr_grad: float32 [4, 1024, 13500], P('slide', 'blk')
- embed_grad: float32 [1024, 13500], P('blk')
- qkv_grad: float32 [1024, 3072], P('blk')
- attn_out_grad: float32 [1024, 1024], P('blk')
- up_grad: float32 [1024, 4096], P('blk')
- up_bias_grad: float32 [4096], P('blk')
- down_grad: float32 [4096, 1024], P('blk')
- latent_grad: float32 [1024, 1024], P('blk')
- decode_grad: float32 [512, 13500], P('blk')
- means_grad: float32 [512, 16], P('blk')
- norm_grad: float32 [1024, 4], P('blk')
The draws below stay inside these ranges and needn't reach their ends.
Inputs may be any that keep to these rules, and one draw needn't show every extreme that they name: Most counts are zero; the others are 1 to 7. `norm_params`: columns 0 and 2 are gains near 1; columns 1 and 3 are shifts of order a fifth, of either sign.
All inputs are finite; a program needn't handle non-finite values.
Results may differ from the reference program's by a relative error of at most 0.02.
Values may be sent and summed in bfloat16 or wider, within the bound.
No kernel may reach another device: no remote copies, remote signals or barrier semaphores. Data moves between devices by JAX's collectives and lax.ppermute only.
A program may use at most 384 MiB of HBM per device.

```python
import math
import jax
import jax.numpy as jnp
from jax import lax

D = 1024
HEADS = 16
HEAD_DIM = 64
FF = 4096
LAT = 512
K = 16
G = 13500
CELLS = 1024
SLIDES = 4


def draw_counts(key, part):
    key = jax.random.fold_in(key, 5)
    first_key, second_key = jax.random.split(key)
    values = jax.random.randint(first_key, (SLIDES, CELLS, G), 1, 8, jnp.int32)
    present = jax.random.randint(second_key, (SLIDES, CELLS, G), 0, 4, jnp.int32)
    return jnp.where(present == 0, values, 0).astype(jnp.int32)


def draw_norm_params(key, part):
    key = jax.random.fold_in(key, 11)
    first_key, second_key = jax.random.split(key)
    gains = 1.0 + 0.3 * jax.random.uniform(first_key, (D, 4), jnp.float32, -1.0, 1.0)
    shifts = 0.2 * jax.random.normal(second_key, (D, 4), jnp.float32)
    column = jnp.arange(4) % 2
    return jnp.where(column[None, :] == 0, gains, shifts).astype(jnp.bfloat16)


def set_ends(array, own_key, least, top_value):
    longest = array.shape.index(max(array.shape))
    spots = []
    for shift in (0, 1):
        where = [jax.random.randint(jax.random.fold_in(own_key, axis), (), 0, length) for axis, length in enumerate(array.shape)]
        where[longest] = (where[longest] + shift) % array.shape[longest]
        spots.append(tuple(where))
    return array.at[spots[0]].set(least).at[spots[1]].set(top_value)


def block_levels(stream_key, extent, cuts, low, high):
    def one(position, shards_of):
        steps = jax.random.uniform(jax.random.fold_in(jax.random.fold_in(stream_key, 6), position), (shards_of,), jnp.float32, low / len(cuts), high / len(cuts))
        return jnp.repeat(jnp.exp(steps), extent[position] // shards_of).reshape((-1,) + (1,) * (len(extent) - position - 1))

    factor_of = one(*cuts[0])
    for cut in cuts[1:]:
        factor_of = factor_of * one(*cut)
    return factor_of


def normal_values(rng, shape, spread, bound, cuts=(), kind=jnp.bfloat16):
    factor_of = block_levels(rng, shape, cuts, -0.22, 0.18) if cuts else 1.0
    array = jax.random.normal(rng, shape, jnp.float32) * spread * factor_of
    return jnp.minimum(jnp.maximum(array, -bound), bound).astype(kind)


def setup_inputs(seed: int = 0) -> dict:
    seeds = jax.random.split(jax.random.key(seed), 17)
    return {
        "counts": draw_counts(jax.random.fold_in(seeds[16], 71), 0),
        "library": set_ends(jax.random.randint(seeds[1], (SLIDES, CELLS), 2000, 40000), jax.random.fold_in(seeds[1], 1), 2000, 39999).astype(jnp.int32),
        "coords": set_ends(jax.random.randint(seeds[2], (SLIDES, CELLS, 2), 0, 1024), jax.random.fold_in(seeds[2], 1), 0, 1023).astype(jnp.int32),
        "noise": normal_values(seeds[3], (SLIDES, CELLS, LAT), 1.0, 5.0, ((0, 4), (1, 8)), jnp.float32),
        "decoded_cot": normal_values(seeds[4], (SLIDES, CELLS, G), 1.0, 6.0, ((0, 4), (1, 8))),
        "prior_cot": normal_values(seeds[5], (SLIDES, CELLS), 1.0, 6.0, ((0, 4), (1, 8)), jnp.float32),
        "embed_t": normal_values(seeds[6], (D, G), G ** -0.5, 0.0546875, ((0, 8),)),
        "w_qkv": normal_values(seeds[7], (D, 3 * D), D ** -0.5, 0.1875, ((0, 8),)),
        "w_attn_out": normal_values(seeds[8], (D, D), (0.6 * CELLS ** 0.25 * D ** -0.5), 0.625, ((0, 8),)),
        "w_up": normal_values(seeds[9], (D, FF), D ** -0.5, 0.1875, ((0, 8),)),
        "up_bias": normal_values(seeds[10], (FF,), 0.5, 3.0, ((0, 8),)),
        "w_down": normal_values(seeds[11], (FF, D), FF ** -0.5, 0.09375, ((0, 8),)),
        "w_latent": normal_values(seeds[12], (D, 2 * LAT), (16 * D) ** -0.5, 0.046875, ((0, 8),)),
        "w_decode": normal_values(seeds[13], (LAT, G), LAT ** -0.5, 0.25, ((0, 8),)),
        "comp_means": normal_values(seeds[14], (LAT, K), 0.5, 3.0, ((0, 8),)),
        "norm_params": draw_norm_params(jax.random.fold_in(seeds[16], 71), 0),
    }


@jax.custom_vjp
def low(v):
    return lax.optimization_barrier(v.astype(jnp.bfloat16)).astype(jnp.float32)

@jax.custom_vjp
def low_back(v):
    return v

def low_keep(v):
    return (low(v), None)

def low_pass(kept, grad):
    return (grad,)

def back_keep(v):
    return (v, None)

def back_low(kept, grad):
    return (low(grad),)
low.defvjp(low_keep, low_pass)
low_back.defvjp(back_keep, back_low)
eps_norm = 1e-05

def multiply(former, latter):
    return jnp.dot(former, latter, precision=lax.Precision.HIGHEST, preferred_element_type=jnp.float32)

def layer_norm(tensor, norm_gain, norm_shift):
    center = tensor - lax.optimization_barrier(jnp.mean(tensor, axis=-1, keepdims=True))
    inverse = lax.rsqrt(lax.optimization_barrier(jnp.mean(center * center, axis=-1, keepdims=True)) + eps_norm)
    return center * inverse * norm_gain + norm_shift

def spatial_code(coords, model_width):
    quarter = model_width // 4
    frequency = jnp.exp(-math.log(10000.0) * jnp.arange(quarter, dtype=jnp.float32) / quarter)
    first_axis = coords[..., 0:1].astype(jnp.float32) * frequency
    second_axis = coords[..., 1:2].astype(jnp.float32) * frequency
    return jnp.concatenate([jnp.sin(first_axis), jnp.cos(first_axis), jnp.sin(second_axis), jnp.cos(second_axis)], axis=-1)

def mixture_term(latent, centres):
    scores = (multiply(latent, centres) - 0.5 * lax.optimization_barrier(jnp.sum(centres * centres, axis=0))) * latent.shape[-1] ** (-0.5)
    return -jax.nn.logsumexp(scores, axis=-1)

def attend(queries, key_rows, value_rows):
    cell_count = queries.shape[0]
    row_block = math.gcd(cell_count, 512)
    scaling = HEAD_DIM ** (-0.5)

    def per_block(query_block):
        scores = low_back(jnp.einsum('qhd,khd->hqk', query_block, key_rows, precision=lax.Precision.HIGHEST) * scaling)
        weights_block = low(jax.nn.softmax(scores, axis=-1))
        return jnp.einsum('hqk,khd->qhd', weights_block, value_rows, precision=lax.Precision.HIGHEST)
    blocked = queries.reshape(cell_count // row_block, row_block, HEADS, HEAD_DIM)
    return lax.map(jax.checkpoint(per_block), blocked).reshape(cell_count, HEADS * HEAD_DIM)

def slide_forward(params, expression, spatial, noise_rows):
    embedding, weight_qkv, weight_out, weight_up, bias_up, weight_down, weight_latent, weight_decode, centres, norm_table = params
    cell_count = expression.shape[0]
    h_zero = low_back(multiply(low(expression), embedding.T) + spatial)
    normed_one = layer_norm(h_zero, norm_table[:, 0], norm_table[:, 1])
    projected = low(low_back(multiply(low(normed_one), weight_qkv)))
    queries = projected[:, :D].reshape(cell_count, HEADS, HEAD_DIM)
    key_rows = projected[:, D:2 * D].reshape(cell_count, HEADS, HEAD_DIM)
    value_rows = projected[:, 2 * D:].reshape(cell_count, HEADS, HEAD_DIM)
    attended = low(low_back(attend(queries, key_rows, value_rows)))
    h_one = h_zero + low_back(multiply(attended, weight_out))
    normed_two = layer_norm(h_one, norm_table[:, 2], norm_table[:, 3])
    hidden_pre = low_back(multiply(low(normed_two), weight_up) + bias_up)
    hidden_low = low(jax.nn.gelu(hidden_pre))
    h_two = h_one + low_back(multiply(hidden_low, weight_down))
    latent_pre = low_back(multiply(low(h_two), weight_latent))
    latent = latent_pre[:, :LAT] + jnp.exp(0.5 * latent_pre[:, LAT:]) * noise_rows
    decoded = multiply(low(latent), weight_decode)
    prior = mixture_term(latent, centres)
    return (decoded, prior)

def reference(counts, library, coords, noise, decoded_cot, prior_cot, embed_t, w_qkv, w_attn_out, w_up, up_bias, w_down, w_latent, w_decode, comp_means, norm_params):
    params = (embed_t.astype(jnp.float32), w_qkv.astype(jnp.float32), w_attn_out.astype(jnp.float32), w_up.astype(jnp.float32), up_bias.astype(jnp.float32), w_down.astype(jnp.float32), w_latent.astype(jnp.float32), w_decode.astype(jnp.float32), comp_means.astype(jnp.float32), norm_params.astype(jnp.float32))

    def per_slide(totals, pieces):
        count_rows, library_rows, coord_rows, noise_rows, decoded_rows, prior_rows = pieces
        expression = jnp.log1p(count_rows.astype(jnp.float32) * 10000.0 / library_rows.astype(jnp.float32)[:, None])
        spatial = spatial_code(coord_rows, D)

        def forward(weights, inputs):
            return slide_forward(weights, inputs, spatial, noise_rows)
        (decoded, prior), pullback = jax.vjp(forward, params, expression)
        weight_grads, expr_grad = pullback((decoded_rows.astype(jnp.float32), prior_rows))
        totals = jax.tree.map(lambda former, latter: former + latter, totals, weight_grads)
        return (totals, (decoded.astype(jnp.bfloat16), prior, expr_grad))
    starting = jax.tree.map(jnp.zeros_like, params)
    weight_grads, outputs = lax.scan(per_slide, starting, (counts, library, coords, noise, decoded_cot, prior_cot))
    decoded, prior, expr_grad = outputs
    return (decoded, prior, expr_grad, weight_grads[0], weight_grads[1], weight_grads[2], weight_grads[3], weight_grads[4], weight_grads[5], weight_grads[6], weight_grads[7], weight_grads[8], weight_grads[9])
```

```python
import math

import jax
import jax.numpy as jnp
from jax import lax
from jax.sharding import PartitionSpec as P

HEADS = 16
HEAD_DIM = 64


eps_norm = 1e-05


def contract_rows(former, latter):
    return lax.dot_general(
        former, latter, (((0,), (0,)), ((), ())), preferred_element_type=jnp.float32
    )


def contract_cols(former, latter):
    return lax.dot_general(
        former, latter, (((1,), (1,)), ((), ())), preferred_element_type=jnp.float32
    )


def layer_norm(tensor, norm_gain, norm_shift):
    center = tensor - jnp.mean(tensor, axis=-1, keepdims=True)
    inverse = lax.rsqrt(jnp.mean(center * center, axis=-1, keepdims=True) + eps_norm)
    return center * inverse * norm_gain + norm_shift


def spatial_code(coords, model_width):
    quarter = model_width // 4
    frequency = jnp.exp(-math.log(10000.0) * jnp.arange(quarter, dtype=jnp.float32) / quarter)
    first_axis = coords[..., 0:1].astype(jnp.float32) * frequency
    second_axis = coords[..., 1:2].astype(jnp.float32) * frequency
    return jnp.concatenate(
        [jnp.sin(first_axis), jnp.cos(first_axis), jnp.sin(second_axis), jnp.cos(second_axis)],
        axis=-1,
    )


def mixture_term(latent, centres):
    scores = (
        jnp.dot(
            latent, centres, precision=lax.Precision.HIGHEST, preferred_element_type=jnp.float32
        )
        - 0.5 * jnp.sum(centres * centres, axis=0)
    ) * latent.shape[-1] ** (-0.5)
    return -jax.nn.logsumexp(scores, axis=-1)


def split_single(rows_in, head_count):
    arrived_rows = rows_in.shape[0]
    block_rows = 512
    return rows_in.reshape(
        (arrived_rows // block_rows, block_rows, head_count, rows_in.shape[1] // head_count)
    )


def split_blocks(key_rows, value_rows, head_count):
    return (split_single(key_rows, head_count), split_single(value_rows, head_count))


def local(
    counts,
    library,
    coords,
    noise,
    decoded_cot,
    prior_cot,
    embed_t,
    w_qkv,
    w_attn_out,
    w_up,
    up_bias,
    w_down,
    w_latent,
    w_decode,
    comp_means,
    norm_params,
):
    gathered = (
        lax.all_gather(embed_t, "blk", axis=0, tiled=True),
        lax.all_gather(w_qkv, "blk", axis=0, tiled=True),
        lax.all_gather(w_attn_out, "blk", axis=0, tiled=True),
        lax.all_gather(w_up, "blk", axis=0, tiled=True),
        lax.all_gather(up_bias, "blk", axis=0, tiled=True),
        lax.all_gather(w_down, "blk", axis=0, tiled=True),
        lax.all_gather(w_latent, "blk", axis=0, tiled=True),
        lax.all_gather(w_decode, "blk", axis=0, tiled=True),
        lax.all_gather(comp_means, "blk", axis=0, tiled=True),
        lax.all_gather(norm_params, "blk", axis=0, tiled=True),
    )
    (
        embedding,
        weight_qkv,
        weight_out,
        weight_up,
        bias_up,
        weight_down,
        weight_latent,
        weight_decode,
        centres,
        norm_table,
    ) = gathered
    head_count = HEADS
    head_width = HEAD_DIM
    scaling = head_width ** (-0.5)
    model_width = embedding.shape[0]
    latent_width = weight_decode.shape[0]
    blk_count = lax.axis_size("blk")
    expression = jnp.log1p(
        counts[0].astype(jnp.float32) * 10000.0 / library[0].astype(jnp.float32)[:, None]
    )
    expression_low = expression.astype(jnp.bfloat16)
    local_cells = expression.shape[0]
    norm_float = norm_table.astype(jnp.float32)
    h_zero = contract_cols(expression_low, embedding) + spatial_code(coords[0], model_width)
    normed_one, norm_one_back = jax.vjp(layer_norm, h_zero, norm_float[:, 0], norm_float[:, 1])
    normed_one_low = normed_one.astype(jnp.bfloat16)
    projected = jnp.dot(normed_one_low, weight_qkv, preferred_element_type=jnp.float32).astype(
        jnp.bfloat16
    )
    queries = projected[:, :model_width].reshape(local_cells, head_count, head_width)
    key_rows = projected[:, model_width : 2 * model_width]
    value_rows = projected[:, 2 * model_width :]
    stat_start = (
        jnp.full((head_count, local_cells), -1e30, jnp.float32),
        jnp.zeros((head_count, local_cells), jnp.float32),
    )
    key_blocks = split_single(lax.all_gather(key_rows, "blk", axis=0, tiled=True), head_count)

    def per_block(status, key_block):
        running_max, running_sum = status
        scores = (
            jnp.einsum("thd,khd->htk", queries, key_block, preferred_element_type=jnp.float32)
            * scaling
        )
        new_max = jnp.maximum(running_max, jnp.max(scores, axis=-1))
        running_sum = running_sum * jnp.exp(running_max - new_max) + jnp.sum(
            jnp.exp(scores - new_max[..., None]), axis=-1
        )
        return ((new_max, running_sum), None)

    result, unused = lax.scan(per_block, stat_start, key_blocks)
    running_max, running_sum = result
    log_total = running_max + jnp.log(running_sum)
    arrived = (
        lax.all_gather(key_rows, "blk", axis=0, tiled=True),
        lax.all_gather(value_rows, "blk", axis=0, tiled=True),
    )
    key_blocks, value_blocks = split_blocks(arrived[0], arrived[1], head_count)

    def per_block(weighted, block_pair):
        scores = (
            jnp.einsum("thd,khd->htk", queries, block_pair[0], preferred_element_type=jnp.float32)
            * scaling
        )
        probs_low = jnp.exp(scores - log_total[..., None]).astype(jnp.bfloat16)
        weighted = weighted + jnp.einsum(
            "htk,khd->htd", probs_low, block_pair[1], preferred_element_type=jnp.float32
        )
        return (weighted, None)

    result, unused = lax.scan(
        per_block,
        jnp.zeros((head_count, local_cells, head_width), jnp.float32),
        (key_blocks, value_blocks),
    )
    attended_cells = jnp.transpose(result, (1, 0, 2))
    attended_low = attended_cells.reshape(local_cells, model_width).astype(jnp.bfloat16)
    h_one = h_zero + jnp.dot(attended_low, weight_out, preferred_element_type=jnp.float32)
    normed_two, norm_two_back = jax.vjp(layer_norm, h_one, norm_float[:, 2], norm_float[:, 3])
    normed_two_low = normed_two.astype(jnp.bfloat16)
    hidden_pre = jnp.dot(
        normed_two_low, weight_up, preferred_element_type=jnp.float32
    ) + bias_up.astype(jnp.float32)
    hidden_act, gelu_back = jax.vjp(jax.nn.gelu, hidden_pre)
    hidden_low = hidden_act.astype(jnp.bfloat16)
    h_two = h_one + jnp.dot(hidden_low, weight_down, preferred_element_type=jnp.float32)
    h_two_low = h_two.astype(jnp.bfloat16)
    latent_pre = jnp.dot(h_two_low, weight_latent, preferred_element_type=jnp.float32)
    spread = jnp.exp(0.5 * latent_pre[:, latent_width:])
    latent = latent_pre[:, :latent_width] + spread * noise[0]
    latent_low = latent.astype(jnp.bfloat16)
    decoded = jnp.dot(latent_low, weight_decode, preferred_element_type=jnp.float32).astype(
        jnp.bfloat16
    )
    prior, prior_back = jax.vjp(mixture_term, latent, centres.astype(jnp.float32))
    out_grad = decoded_cot[0]
    latent_from_decode = contract_cols(out_grad, weight_decode)
    latent_from_prior, centre_grad = prior_back(prior_cot[0])
    latent_total = latent_from_decode + latent_from_prior
    pre_grad = jnp.concatenate(
        [latent_total, latent_total * noise[0] * spread * 0.5], axis=-1
    ).astype(jnp.bfloat16)
    latent_weight_grad = contract_rows(h_two_low, pre_grad)
    h_two_grad = contract_cols(pre_grad, weight_latent)
    down_input = h_two_grad.astype(jnp.bfloat16)
    down_grad = contract_rows(hidden_low, down_input)
    hidden_grad = contract_cols(down_input, weight_down)
    pre_hidden_grad = gelu_back(hidden_grad)[0].astype(jnp.bfloat16)
    up_bias_grad = jnp.sum(pre_hidden_grad.astype(jnp.float32), axis=0)
    up_grad = contract_rows(normed_two_low, pre_hidden_grad)
    normed_two_grad = contract_cols(pre_hidden_grad, weight_up)
    h_one_part, gain_two_grad, shift_two_grad = norm_two_back(normed_two_grad)
    h_one_grad = h_two_grad + h_one_part
    out_input = h_one_grad.astype(jnp.bfloat16)
    attn_out_grad = contract_rows(attended_low, out_input)
    attended_grad = contract_cols(out_input, weight_out).astype(jnp.bfloat16)
    out_heads = attended_grad.reshape(local_cells, head_count, head_width)
    row_delta = jnp.sum(out_heads.astype(jnp.float32) * attended_cells, axis=-1).T
    query_zero = jnp.zeros((head_count, local_cells, head_width), jnp.float32)
    start_back = (query_zero, jnp.zeros((local_cells * blk_count, 2 * model_width), jnp.float32))
    arrived = (
        lax.all_gather(key_rows, "blk", axis=0, tiled=True),
        lax.all_gather(value_rows, "blk", axis=0, tiled=True),
    )
    key_blocks, value_blocks = split_blocks(arrived[0], arrived[1], head_count)
    arrived_rows = arrived[0].shape[0]

    def per_block(query_sum, block_pair):
        scores = (
            jnp.einsum("thd,khd->htk", queries, block_pair[0], preferred_element_type=jnp.float32)
            * scaling
        )
        probs = jnp.exp(scores - log_total[..., None])
        prob_grad = jnp.einsum(
            "thd,khd->htk", out_heads, block_pair[1], preferred_element_type=jnp.float32
        )
        score_grad = (probs * (prob_grad - row_delta[..., None])).astype(jnp.bfloat16)
        query_sum = query_sum + jnp.einsum(
            "htk,khd->htd", score_grad, block_pair[0], preferred_element_type=jnp.float32
        )
        key_part = (
            jnp.einsum("htk,thd->khd", score_grad, queries, preferred_element_type=jnp.float32)
            * scaling
        )
        value_part = jnp.einsum(
            "htk,thd->khd",
            probs.astype(jnp.bfloat16),
            out_heads,
            preferred_element_type=jnp.float32,
        )
        block_rows = key_part.shape[0]
        return (
            query_sum,
            jnp.concatenate(
                [key_part.reshape(block_rows, -1), value_part.reshape(block_rows, -1)], axis=-1
            ),
        )

    query_total, stacked = lax.scan(per_block, start_back[0], (key_blocks, value_blocks))
    stacked = stacked.reshape(arrived_rows, stacked.shape[-1])
    carried_back = (query_total, stacked)
    query_total = carried_back[0]
    own_pairs = lax.psum_scatter(
        carried_back[1].astype(jnp.bfloat16), "blk", scatter_dimension=0, tiled=True
    ).astype(jnp.float32)
    query_rows = jnp.transpose(query_total * scaling, (1, 0, 2)).reshape(local_cells, model_width)
    projected_grad = jnp.concatenate([query_rows, own_pairs], axis=-1).astype(jnp.bfloat16)
    qkv_grad = contract_rows(normed_one_low, projected_grad)
    normed_one_grad = contract_cols(projected_grad, weight_qkv)
    h_zero_part, gain_one_grad, shift_one_grad = norm_one_back(normed_one_grad)
    h_zero_low = (h_one_grad + h_zero_part).astype(jnp.bfloat16)
    expr_grad = jnp.dot(h_zero_low, embedding, preferred_element_type=jnp.float32)
    norm_grad = jnp.stack([gain_one_grad, shift_one_grad, gain_two_grad, shift_two_grad], axis=0).T
    centre_grad = centre_grad.T.T
    embed_slot = contract_rows(h_zero_low, expression_low)
    decode_slot = contract_rows(latent_low, out_grad)
    block_parts = (
        lax.psum_scatter(
            embed_slot.astype(jnp.bfloat16), "blk", scatter_dimension=0, tiled=True
        ).astype(jnp.float32),
        lax.psum_scatter(
            qkv_grad.astype(jnp.bfloat16), "blk", scatter_dimension=0, tiled=True
        ).astype(jnp.float32),
        lax.psum_scatter(
            attn_out_grad.astype(jnp.bfloat16), "blk", scatter_dimension=0, tiled=True
        ).astype(jnp.float32),
        lax.psum_scatter(
            up_grad.astype(jnp.bfloat16), "blk", scatter_dimension=0, tiled=True
        ).astype(jnp.float32),
        lax.psum_scatter(
            up_bias_grad.astype(jnp.bfloat16), "blk", scatter_dimension=0, tiled=True
        ).astype(jnp.float32),
        lax.psum_scatter(
            down_grad.astype(jnp.bfloat16), "blk", scatter_dimension=0, tiled=True
        ).astype(jnp.float32),
        lax.psum_scatter(
            latent_weight_grad.astype(jnp.bfloat16), "blk", scatter_dimension=0, tiled=True
        ).astype(jnp.float32),
        lax.psum_scatter(
            decode_slot.astype(jnp.bfloat16), "blk", scatter_dimension=0, tiled=True
        ).astype(jnp.float32),
        lax.psum_scatter(
            centre_grad.astype(jnp.bfloat16), "blk", scatter_dimension=0, tiled=True
        ).astype(jnp.float32),
        lax.psum_scatter(
            norm_grad.astype(jnp.bfloat16), "blk", scatter_dimension=0, tiled=True
        ).astype(jnp.float32),
    )
    summed = (
        lax.psum(block_parts[0].astype(jnp.bfloat16), "slide").astype(jnp.float32),
        lax.psum(block_parts[1].astype(jnp.bfloat16), "slide").astype(jnp.float32),
        lax.psum(block_parts[2].astype(jnp.bfloat16), "slide").astype(jnp.float32),
        lax.psum(block_parts[3].astype(jnp.bfloat16), "slide").astype(jnp.float32),
        lax.psum(block_parts[4].astype(jnp.bfloat16), "slide").astype(jnp.float32),
        lax.psum(block_parts[5].astype(jnp.bfloat16), "slide").astype(jnp.float32),
        lax.psum(block_parts[6].astype(jnp.bfloat16), "slide").astype(jnp.float32),
        lax.psum(block_parts[7].astype(jnp.bfloat16), "slide").astype(jnp.float32),
        lax.psum(block_parts[8].astype(jnp.bfloat16), "slide").astype(jnp.float32),
        lax.psum(block_parts[9].astype(jnp.bfloat16), "slide").astype(jnp.float32),
    )
    embed_out = summed[0]
    decode_out = summed[7]
    return (
        decoded[None],
        prior[None],
        expr_grad[None],
        embed_out,
        summed[1],
        summed[2],
        summed[3],
        summed[4],
        summed[5],
        summed[6],
        decode_out,
        summed[8],
        summed[9],
    )


def peers(offset, count):
    return [(place, place ^ offset) for place in range(count)]


def swap(pieces):
    count = len(pieces)
    return [pieces[0]] + [
        lax.ppermute(pieces[k], "slide", peers(k, count)) for k in range(1, count)
    ]


def share(rows, count):
    return swap([rows] * count)


def in_order(pieces, me, axis):
    stacked = jnp.stack(pieces)
    return jnp.concatenate(
        [
            lax.dynamic_index_in_dim(stacked, jnp.bitwise_xor(me, k), 0, keepdims=False)
            for k in range(len(pieces))
        ],
        axis=axis,
    )


def collect(partials):
    arrived = swap([partials[0]] + [piece.astype(jnp.bfloat16) for piece in partials[1:]])
    total = arrived[0]
    for piece in arrived[1:]:
        total = total + piece.astype(jnp.float32)
    return total


def gather_blk(piece, axis=0):
    return lax.all_gather(piece, "blk", axis=axis, tiled=True)


def scatter_blk(piece):
    return lax.psum_scatter(
        piece.astype(jnp.bfloat16), "blk", scatter_dimension=0, tiled=True
    )


def split_rows(rows, count):
    height = rows.shape[0] // count
    return [rows[k * height : (k + 1) * height] for k in range(count)]


def split_model(
    counts,
    library,
    coords,
    noise,
    decoded_cot,
    prior_cot,
    embed_t,
    w_qkv,
    w_attn_out,
    w_up,
    up_bias,
    w_down,
    w_latent,
    w_decode,
    comp_means,
    norm_params,
):
    slides = lax.axis_size("slide")
    blocks = lax.axis_size("blk")
    me = lax.axis_index("slide")
    genes = embed_t.shape[1]
    cells = counts.shape[1]
    model_width = w_attn_out.shape[1]
    own_rows = w_qkv.shape[0]
    latent_width = w_decode.shape[0] * blocks
    mixture_count = comp_means.shape[1]
    quarter = -(-genes // (slides * 128)) * 128
    padded = quarter * slides
    head_part = model_width // slides
    pair = model_width // blocks
    pairs = head_part // pair
    ff_part = up_bias.shape[0] // slides
    scaling = HEAD_DIM ** (-0.5)

    def gene_part(rows, place):
        return lax.dynamic_slice_in_dim(rows, place * quarter, quarter, 1)

    def pad_genes(rows):
        return jnp.pad(rows, ((0, 0), (0, padded - genes)))

    def place_of(k):
        return jnp.bitwise_xor(me, k)

    embedding = gather_blk(gene_part(pad_genes(embed_t), me))
    qkv_part = lax.dynamic_index_in_dim(
        w_qkv.reshape(own_rows, 3, slides, pairs, pair), me, 2, keepdims=False
    )
    qkv_part = jnp.transpose(qkv_part, (0, 2, 1, 3)).reshape(own_rows, pairs * 3 * pair)
    bias_part = lax.dynamic_slice_in_dim(up_bias, me * ff_part, ff_part, 0)
    mean_cols = comp_means.size // own_rows
    small = jnp.concatenate(
        [norm_params, comp_means.reshape(own_rows, mean_cols), bias_part.reshape(own_rows, -1)],
        axis=1,
    )
    small_cols = small.shape[1]
    small = jnp.pad(small, ((0, 0), (0, 128 - small_cols)))
    first = gather_blk(jnp.concatenate([qkv_part, small], axis=1))
    weight_qkv = first[:, : pairs * 3 * pair].reshape(model_width, pairs, 3 * pair)
    small_all = first[:, pairs * 3 * pair :]
    norm_float = small_all[:, :4].astype(jnp.float32)
    centres = small_all[:, 4 : 4 + mean_cols].reshape(latent_width, mixture_count)
    bias_up = small_all[:, 4 + mean_cols : small_cols].reshape(-1).astype(jnp.float32)
    weight_out = gather_blk(w_attn_out)
    up_part = lax.dynamic_index_in_dim(
        w_up.reshape(own_rows, blocks, slides, ff_part), me, 2, keepdims=False
    ).reshape(own_rows, blocks * ff_part)
    weight_up = gather_blk(up_part)
    weight_down = gather_blk(lax.dynamic_slice_in_dim(w_down, me * ff_part, ff_part, 0))
    weight_latent = gather_blk(w_latent)
    weight_decode = gather_blk(gene_part(pad_genes(w_decode), me))

    expression = jnp.log1p(
        counts[0].astype(jnp.float32) * 10000.0 / library[0].astype(jnp.float32)[:, None]
    )
    expression_low = pad_genes(expression.astype(jnp.bfloat16))
    expr_parts = swap([gene_part(expression_low, place_of(k)) for k in range(slides)])
    h_zero = collect([contract_cols(part, embedding) for part in expr_parts])
    h_zero = h_zero + spatial_code(coords[0], model_width)
    normed_one, norm_one_back = jax.vjp(layer_norm, h_zero, norm_float[:, 0], norm_float[:, 1])
    normed_one_all = jnp.concatenate(share(normed_one.astype(jnp.bfloat16), slides), axis=0)
    projected = jnp.einsum(
        "ck,kpf->pcf", normed_one_all, weight_qkv, preferred_element_type=jnp.float32
    ).astype(jnp.bfloat16)

    def to_heads(rows):
        return lax.all_to_all(
            rows.reshape(blocks, cells, rows.shape[-1]), "blk", 0, 0, tiled=True
        ).reshape(blocks * cells, rows.shape[-1])

    head_rows = to_heads(projected)
    per_pair = pair // HEAD_DIM

    def heads_of(rows):
        return jnp.transpose(rows.reshape(blocks * cells, per_pair, HEAD_DIM), (1, 0, 2))

    queries = heads_of(head_rows[:, :pair])
    key_rows = heads_of(head_rows[:, pair : 2 * pair])
    value_rows = heads_of(head_rows[:, 2 * pair :])
    scores = (
        jnp.einsum("htd,hkd->htk", queries, key_rows, preferred_element_type=jnp.float32)
        * scaling
    )
    probs = jax.nn.softmax(scores, axis=-1)
    probs_low = probs.astype(jnp.bfloat16)
    head_out = jnp.einsum(
        "htk,hkd->thd", probs_low, value_rows, preferred_element_type=jnp.float32
    ).astype(jnp.bfloat16)
    own_heads = to_heads(head_out.reshape(blocks * cells, pair)).reshape(
        pairs, slides, cells, pair
    )
    attended_parts = swap(
        [
            jnp.transpose(own_heads[:, k], (1, 0, 2)).reshape(cells, head_part)
            for k in range(slides)
        ]
    )
    attended_low = in_order(attended_parts, me, 1)
    h_one = h_zero + jnp.dot(attended_low, weight_out, preferred_element_type=jnp.float32)
    normed_two, norm_two_back = jax.vjp(layer_norm, h_one, norm_float[:, 2], norm_float[:, 3])
    normed_two_all = jnp.concatenate(share(normed_two.astype(jnp.bfloat16), slides), axis=0)
    hidden_pre = (
        jnp.dot(normed_two_all, weight_up, preferred_element_type=jnp.float32) + bias_up
    )
    hidden_act, gelu_back = jax.vjp(jax.nn.gelu, hidden_pre)
    hidden_low = hidden_act.astype(jnp.bfloat16)
    h_two = h_one + collect(
        split_rows(jnp.dot(hidden_low, weight_down, preferred_element_type=jnp.float32), slides)
    )
    h_two_low = h_two.astype(jnp.bfloat16)
    latent_pre = jnp.dot(h_two_low, weight_latent, preferred_element_type=jnp.float32)
    spread = jnp.exp(0.5 * latent_pre[:, latent_width:])
    latent = latent_pre[:, :latent_width] + spread * noise[0]
    prior, prior_back = jax.vjp(mixture_term, latent, centres.astype(jnp.float32))

    cot_all = pad_genes(decoded_cot[0])
    cot_parts = swap([gene_part(cot_all, place_of(k)) for k in range(slides)])
    latent_from_decode = collect([contract_cols(part, weight_decode) for part in cot_parts])
    latent_from_prior, centre_grad = prior_back(prior_cot[0])
    latent_total = latent_from_decode + latent_from_prior
    pre_grad = jnp.concatenate(
        [latent_total, latent_total * noise[0] * spread * 0.5], axis=-1
    ).astype(jnp.bfloat16)
    pre_grad_all = jnp.concatenate(share(pre_grad, slides), axis=0)
    h_two_grad_all = contract_cols(pre_grad_all, weight_latent)
    down_input = h_two_grad_all.astype(jnp.bfloat16)
    hidden_grad = contract_cols(down_input, weight_down)
    pre_hidden_grad = gelu_back(hidden_grad)[0].astype(jnp.bfloat16)
    normed_two_grad = collect(split_rows(contract_cols(pre_hidden_grad, weight_up), slides))
    h_one_part, gain_two_grad, shift_two_grad = norm_two_back(normed_two_grad)
    h_one_grad = h_two_grad_all[:cells] + h_one_part
    out_input = h_one_grad.astype(jnp.bfloat16)
    attended_grad = contract_cols(out_input, weight_out).astype(jnp.bfloat16)

    def column_part(rows, width, place):
        return lax.dynamic_slice_in_dim(rows, place * width, width, 1)

    grad_parts = swap([column_part(attended_grad, head_part, place_of(k)) for k in range(slides)])
    grad_pairs = jnp.stack([part.reshape(cells, pairs, pair) for part in grad_parts])
    grad_pairs = jnp.transpose(grad_pairs, (2, 0, 1, 3))
    out_heads = heads_of(to_heads(grad_pairs))
    prob_grad = jnp.einsum(
        "htd,hkd->htk", out_heads, value_rows, preferred_element_type=jnp.float32
    )
    row_delta = jnp.sum(probs * prob_grad, axis=-1, keepdims=True)
    score_grad = (probs * (prob_grad - row_delta)).astype(jnp.bfloat16)
    query_grad = (
        jnp.einsum("htk,hkd->thd", score_grad, key_rows, preferred_element_type=jnp.float32)
        * scaling
    )
    key_grad = (
        jnp.einsum("htk,htd->khd", score_grad, queries, preferred_element_type=jnp.float32)
        * scaling
    )
    value_grad = jnp.einsum(
        "htk,htd->khd", probs_low, out_heads, preferred_element_type=jnp.float32
    )
    head_grads = jnp.concatenate(
        [
            part.reshape(blocks * cells, pair).astype(jnp.bfloat16)
            for part in (query_grad, key_grad, value_grad)
        ],
        axis=1,
    )
    projected_grad = to_heads(head_grads).reshape(pairs, slides * cells, 3 * pair)
    normed_one_grad = collect(
        split_rows(
            jnp.einsum(
                "pcf,kpf->ck", projected_grad, weight_qkv, preferred_element_type=jnp.float32
            ),
            slides,
        )
    )
    h_zero_part, gain_one_grad, shift_one_grad = norm_one_back(normed_one_grad)
    h_zero_low = (h_one_grad + h_zero_part).astype(jnp.bfloat16)
    h_zero_parts = share(h_zero_low, slides)
    expr_grad_parts = swap(
        [
            jnp.dot(part, embedding, preferred_element_type=jnp.float32).astype(jnp.bfloat16)
            for part in h_zero_parts
        ]
    )
    expr_grad = in_order(expr_grad_parts, me, 1)[:, :genes].astype(jnp.float32)

    latent_all = jnp.concatenate(share(latent.astype(jnp.bfloat16), slides), axis=0)
    decoded_rows = jnp.dot(latent_all, weight_decode, preferred_element_type=jnp.float32)
    decoded = in_order(swap(split_rows(decoded_rows.astype(jnp.bfloat16), slides)), me, 1)
    decoded = decoded[:, :genes]

    def whole(piece, axis):
        return in_order(share(piece, slides), me, axis)

    cot_stack = jnp.concatenate(cot_parts, axis=0)
    decode_grad = whole(scatter_blk(contract_rows(latent_all, cot_stack)), 1)[:, :genes]
    h_two_all = jnp.concatenate(share(h_two_low, slides), axis=0)
    latent_part = model_width // slides
    latent_grad = whole(
        scatter_blk(contract_rows(h_two_all, column_part(pre_grad_all, latent_part, me))), 1
    )
    down_grad = whole(scatter_blk(contract_rows(hidden_low, down_input)), 0)
    up_grad = scatter_blk(contract_rows(normed_two_all, pre_hidden_grad))
    up_grad = whole(up_grad.reshape(own_rows, blocks, 1, ff_part), 2)
    attended_all = jnp.concatenate(share(attended_low, slides), axis=0)
    out_parts = swap([column_part(out_input, head_part, place_of(k)) for k in range(slides)])
    attn_out_grad = whole(
        scatter_blk(contract_rows(attended_all, jnp.concatenate(out_parts, axis=0))), 1
    )
    qkv_grad = jnp.einsum(
        "ck,pcf->kpf", normed_one_all, projected_grad, preferred_element_type=jnp.float32
    ).reshape(model_width, pairs * 3 * pair)
    up_bias_grad = jnp.sum(pre_hidden_grad.astype(jnp.float32), axis=0)
    small_grad = jnp.concatenate(
        [
            jnp.stack([gain_one_grad, shift_one_grad, gain_two_grad, shift_two_grad], axis=1),
            centre_grad.reshape(model_width, mean_cols),
            up_bias_grad.reshape(model_width, -1),
        ],
        axis=1,
    )
    small_grad = jnp.pad(small_grad, ((0, 0), (0, 128 - small_cols)))
    first_grad = scatter_blk(jnp.concatenate([qkv_grad, small_grad], axis=1))
    first_parts = share(first_grad, slides)
    qkv_grad = in_order(
        [
            jnp.transpose(
                part[:, : pairs * 3 * pair].reshape(own_rows, pairs, 3, 1, pair), (0, 2, 3, 1, 4)
            )
            for part in first_parts
        ],
        me,
        2,
    ).reshape(own_rows, 3 * model_width)
    small_parts = [part[:, pairs * 3 * pair :] for part in first_parts]
    summed = sum(part.astype(jnp.float32) for part in small_parts)
    up_bias_out = in_order(
        [part[:, 4 + mean_cols : small_cols].reshape(-1) for part in small_parts], me, 0
    )
    embed_grad = whole(
        scatter_blk(contract_rows(jnp.concatenate(h_zero_parts, axis=0), jnp.concatenate(expr_parts, axis=0))),
        1,
    )[:, :genes]

    def wide(piece):
        return piece.astype(jnp.float32)

    return (
        decoded[None],
        prior[None],
        expr_grad[None],
        wide(embed_grad),
        wide(qkv_grad),
        wide(attn_out_grad),
        wide(up_grad.reshape(own_rows, -1)),
        wide(up_bias_out),
        wide(down_grad),
        wide(latent_grad),
        wide(decode_grad),
        summed[:, 4 : 4 + mean_cols].reshape(comp_means.shape),
        summed[:, :4],
    )


def fits(mesh):
    slides, blocks = mesh.shape["slide"], mesh.shape["blk"]
    return slides & (slides - 1) == 0 and HEADS % slides == 0 and HEADS % blocks == 0


def solution(mesh):
    placed = (
        P("slide", "blk", None),
        P("slide", "blk"),
        P("slide", "blk", None),
        P("slide", "blk", None),
        P("slide", "blk", None),
        P("slide", "blk"),
        P("blk", None),
        P("blk", None),
        P("blk", None),
        P("blk", None),
        P("blk"),
        P("blk", None),
        P("blk", None),
        P("blk", None),
        P("blk", None),
        P("blk", None),
    )
    return jax.shard_map(
        split_model if fits(mesh) else local,
        mesh=mesh,
        in_specs=placed,
        out_specs=(
            P("slide", "blk", None),
            P("slide", "blk"),
            P("slide", "blk", None),
            P("blk", None),
            P("blk", None),
            P("blk", None),
            P("blk", None),
            P("blk"),
            P("blk", None),
            P("blk", None),
            P("blk", None),
            P("blk", None),
            P("blk", None),
        ),
        check_vma=False,
    )
```

```python
import functools
import math

import jax
import jax.numpy as jnp
from jax import lax
from jax.experimental import pallas as pl
from jax.experimental.pallas import tpu as pltpu
from jax.sharding import PartitionSpec as P

HEADS = 16
HEAD_DIM = 64


eps_norm = 1e-05


def contract_rows(former, latter):
    return lax.dot_general(
        former, latter, (((0,), (0,)), ((), ())), preferred_element_type=jnp.float32
    )


def contract_cols(former, latter):
    return lax.dot_general(
        former, latter, (((1,), (1,)), ((), ())), preferred_element_type=jnp.float32
    )


def layer_norm(tensor, norm_gain, norm_shift):
    center = tensor - jnp.mean(tensor, axis=-1, keepdims=True)
    inverse = lax.rsqrt(jnp.mean(center * center, axis=-1, keepdims=True) + eps_norm)
    return center * inverse * norm_gain + norm_shift


def spatial_code(coords, model_width):
    quarter = model_width // 4
    frequency = jnp.exp(-math.log(10000.0) * jnp.arange(quarter, dtype=jnp.float32) / quarter)
    first_axis = coords[..., 0:1].astype(jnp.float32) * frequency
    second_axis = coords[..., 1:2].astype(jnp.float32) * frequency
    return jnp.concatenate(
        [jnp.sin(first_axis), jnp.cos(first_axis), jnp.sin(second_axis), jnp.cos(second_axis)],
        axis=-1,
    )


def mixture_term(latent, centres):
    scores = (
        jnp.dot(
            latent, centres, precision=lax.Precision.HIGHEST, preferred_element_type=jnp.float32
        )
        - 0.5 * jnp.sum(centres * centres, axis=0)
    ) * latent.shape[-1] ** (-0.5)
    return -jax.nn.logsumexp(scores, axis=-1)


def split_single(rows_in, head_count):
    arrived_rows = rows_in.shape[0]
    block_rows = 512
    return rows_in.reshape(
        (arrived_rows // block_rows, block_rows, head_count, rows_in.shape[1] // head_count)
    )


def split_blocks(key_rows, value_rows, head_count):
    return (split_single(key_rows, head_count), split_single(value_rows, head_count))


def local(
    counts,
    library,
    coords,
    noise,
    decoded_cot,
    prior_cot,
    embed_t,
    w_qkv,
    w_attn_out,
    w_up,
    up_bias,
    w_down,
    w_latent,
    w_decode,
    comp_means,
    norm_params,
):
    gathered = (
        lax.all_gather(embed_t, "blk", axis=0, tiled=True),
        lax.all_gather(w_qkv, "blk", axis=0, tiled=True),
        lax.all_gather(w_attn_out, "blk", axis=0, tiled=True),
        lax.all_gather(w_up, "blk", axis=0, tiled=True),
        lax.all_gather(up_bias, "blk", axis=0, tiled=True),
        lax.all_gather(w_down, "blk", axis=0, tiled=True),
        lax.all_gather(w_latent, "blk", axis=0, tiled=True),
        lax.all_gather(w_decode, "blk", axis=0, tiled=True),
        lax.all_gather(comp_means, "blk", axis=0, tiled=True),
        lax.all_gather(norm_params, "blk", axis=0, tiled=True),
    )
    (
        embedding,
        weight_qkv,
        weight_out,
        weight_up,
        bias_up,
        weight_down,
        weight_latent,
        weight_decode,
        centres,
        norm_table,
    ) = gathered
    head_count = HEADS
    head_width = HEAD_DIM
    scaling = head_width ** (-0.5)
    model_width = embedding.shape[0]
    latent_width = weight_decode.shape[0]
    blk_count = lax.axis_size("blk")
    expression = jnp.log1p(
        counts[0].astype(jnp.float32) * 10000.0 / library[0].astype(jnp.float32)[:, None]
    )
    expression_low = expression.astype(jnp.bfloat16)
    local_cells = expression.shape[0]
    norm_float = norm_table.astype(jnp.float32)
    h_zero = contract_cols(expression_low, embedding) + spatial_code(coords[0], model_width)
    normed_one, norm_one_back = jax.vjp(layer_norm, h_zero, norm_float[:, 0], norm_float[:, 1])
    normed_one_low = normed_one.astype(jnp.bfloat16)
    projected = jnp.dot(normed_one_low, weight_qkv, preferred_element_type=jnp.float32).astype(
        jnp.bfloat16
    )
    queries = projected[:, :model_width].reshape(local_cells, head_count, head_width)
    key_rows = projected[:, model_width : 2 * model_width]
    value_rows = projected[:, 2 * model_width :]
    stat_start = (
        jnp.full((head_count, local_cells), -1e30, jnp.float32),
        jnp.zeros((head_count, local_cells), jnp.float32),
    )
    key_blocks = split_single(lax.all_gather(key_rows, "blk", axis=0, tiled=True), head_count)

    def per_block(status, key_block):
        running_max, running_sum = status
        scores = (
            jnp.einsum("thd,khd->htk", queries, key_block, preferred_element_type=jnp.float32)
            * scaling
        )
        new_max = jnp.maximum(running_max, jnp.max(scores, axis=-1))
        running_sum = running_sum * jnp.exp(running_max - new_max) + jnp.sum(
            jnp.exp(scores - new_max[..., None]), axis=-1
        )
        return ((new_max, running_sum), None)

    result, unused = lax.scan(per_block, stat_start, key_blocks)
    running_max, running_sum = result
    log_total = running_max + jnp.log(running_sum)
    arrived = (
        lax.all_gather(key_rows, "blk", axis=0, tiled=True),
        lax.all_gather(value_rows, "blk", axis=0, tiled=True),
    )
    key_blocks, value_blocks = split_blocks(arrived[0], arrived[1], head_count)

    def per_block(weighted, block_pair):
        scores = (
            jnp.einsum("thd,khd->htk", queries, block_pair[0], preferred_element_type=jnp.float32)
            * scaling
        )
        probs_low = jnp.exp(scores - log_total[..., None]).astype(jnp.bfloat16)
        weighted = weighted + jnp.einsum(
            "htk,khd->htd", probs_low, block_pair[1], preferred_element_type=jnp.float32
        )
        return (weighted, None)

    result, unused = lax.scan(
        per_block,
        jnp.zeros((head_count, local_cells, head_width), jnp.float32),
        (key_blocks, value_blocks),
    )
    attended_cells = jnp.transpose(result, (1, 0, 2))
    attended_low = attended_cells.reshape(local_cells, model_width).astype(jnp.bfloat16)
    h_one = h_zero + jnp.dot(attended_low, weight_out, preferred_element_type=jnp.float32)
    normed_two, norm_two_back = jax.vjp(layer_norm, h_one, norm_float[:, 2], norm_float[:, 3])
    normed_two_low = normed_two.astype(jnp.bfloat16)
    hidden_pre = jnp.dot(
        normed_two_low, weight_up, preferred_element_type=jnp.float32
    ) + bias_up.astype(jnp.float32)
    hidden_act, gelu_back = jax.vjp(jax.nn.gelu, hidden_pre)
    hidden_low = hidden_act.astype(jnp.bfloat16)
    h_two = h_one + jnp.dot(hidden_low, weight_down, preferred_element_type=jnp.float32)
    h_two_low = h_two.astype(jnp.bfloat16)
    latent_pre = jnp.dot(h_two_low, weight_latent, preferred_element_type=jnp.float32)
    spread = jnp.exp(0.5 * latent_pre[:, latent_width:])
    latent = latent_pre[:, :latent_width] + spread * noise[0]
    latent_low = latent.astype(jnp.bfloat16)
    decoded = jnp.dot(latent_low, weight_decode, preferred_element_type=jnp.float32).astype(
        jnp.bfloat16
    )
    prior, prior_back = jax.vjp(mixture_term, latent, centres.astype(jnp.float32))
    out_grad = decoded_cot[0]
    latent_from_decode = contract_cols(out_grad, weight_decode)
    latent_from_prior, centre_grad = prior_back(prior_cot[0])
    latent_total = latent_from_decode + latent_from_prior
    pre_grad = jnp.concatenate(
        [latent_total, latent_total * noise[0] * spread * 0.5], axis=-1
    ).astype(jnp.bfloat16)
    latent_weight_grad = contract_rows(h_two_low, pre_grad)
    h_two_grad = contract_cols(pre_grad, weight_latent)
    down_input = h_two_grad.astype(jnp.bfloat16)
    down_grad = contract_rows(hidden_low, down_input)
    hidden_grad = contract_cols(down_input, weight_down)
    pre_hidden_grad = gelu_back(hidden_grad)[0].astype(jnp.bfloat16)
    up_bias_grad = jnp.sum(pre_hidden_grad.astype(jnp.float32), axis=0)
    up_grad = contract_rows(normed_two_low, pre_hidden_grad)
    normed_two_grad = contract_cols(pre_hidden_grad, weight_up)
    h_one_part, gain_two_grad, shift_two_grad = norm_two_back(normed_two_grad)
    h_one_grad = h_two_grad + h_one_part
    out_input = h_one_grad.astype(jnp.bfloat16)
    attn_out_grad = contract_rows(attended_low, out_input)
    attended_grad = contract_cols(out_input, weight_out).astype(jnp.bfloat16)
    out_heads = attended_grad.reshape(local_cells, head_count, head_width)
    row_delta = jnp.sum(out_heads.astype(jnp.float32) * attended_cells, axis=-1).T
    query_zero = jnp.zeros((head_count, local_cells, head_width), jnp.float32)
    start_back = (query_zero, jnp.zeros((local_cells * blk_count, 2 * model_width), jnp.float32))
    arrived = (
        lax.all_gather(key_rows, "blk", axis=0, tiled=True),
        lax.all_gather(value_rows, "blk", axis=0, tiled=True),
    )
    key_blocks, value_blocks = split_blocks(arrived[0], arrived[1], head_count)
    arrived_rows = arrived[0].shape[0]

    def per_block(query_sum, block_pair):
        scores = (
            jnp.einsum("thd,khd->htk", queries, block_pair[0], preferred_element_type=jnp.float32)
            * scaling
        )
        probs = jnp.exp(scores - log_total[..., None])
        prob_grad = jnp.einsum(
            "thd,khd->htk", out_heads, block_pair[1], preferred_element_type=jnp.float32
        )
        score_grad = (probs * (prob_grad - row_delta[..., None])).astype(jnp.bfloat16)
        query_sum = query_sum + jnp.einsum(
            "htk,khd->htd", score_grad, block_pair[0], preferred_element_type=jnp.float32
        )
        key_part = (
            jnp.einsum("htk,thd->khd", score_grad, queries, preferred_element_type=jnp.float32)
            * scaling
        )
        value_part = jnp.einsum(
            "htk,thd->khd",
            probs.astype(jnp.bfloat16),
            out_heads,
            preferred_element_type=jnp.float32,
        )
        block_rows = key_part.shape[0]
        return (
            query_sum,
            jnp.concatenate(
                [key_part.reshape(block_rows, -1), value_part.reshape(block_rows, -1)], axis=-1
            ),
        )

    query_total, stacked = lax.scan(per_block, start_back[0], (key_blocks, value_blocks))
    stacked = stacked.reshape(arrived_rows, stacked.shape[-1])
    carried_back = (query_total, stacked)
    query_total = carried_back[0]
    own_pairs = lax.psum_scatter(
        carried_back[1].astype(jnp.bfloat16), "blk", scatter_dimension=0, tiled=True
    ).astype(jnp.float32)
    query_rows = jnp.transpose(query_total * scaling, (1, 0, 2)).reshape(local_cells, model_width)
    projected_grad = jnp.concatenate([query_rows, own_pairs], axis=-1).astype(jnp.bfloat16)
    qkv_grad = contract_rows(normed_one_low, projected_grad)
    normed_one_grad = contract_cols(projected_grad, weight_qkv)
    h_zero_part, gain_one_grad, shift_one_grad = norm_one_back(normed_one_grad)
    h_zero_low = (h_one_grad + h_zero_part).astype(jnp.bfloat16)
    expr_grad = jnp.dot(h_zero_low, embedding, preferred_element_type=jnp.float32)
    norm_grad = jnp.stack([gain_one_grad, shift_one_grad, gain_two_grad, shift_two_grad], axis=0).T
    centre_grad = centre_grad.T.T
    embed_slot = contract_rows(h_zero_low, expression_low)
    decode_slot = contract_rows(latent_low, out_grad)
    block_parts = (
        lax.psum_scatter(
            embed_slot.astype(jnp.bfloat16), "blk", scatter_dimension=0, tiled=True
        ).astype(jnp.float32),
        lax.psum_scatter(
            qkv_grad.astype(jnp.bfloat16), "blk", scatter_dimension=0, tiled=True
        ).astype(jnp.float32),
        lax.psum_scatter(
            attn_out_grad.astype(jnp.bfloat16), "blk", scatter_dimension=0, tiled=True
        ).astype(jnp.float32),
        lax.psum_scatter(
            up_grad.astype(jnp.bfloat16), "blk", scatter_dimension=0, tiled=True
        ).astype(jnp.float32),
        lax.psum_scatter(
            up_bias_grad.astype(jnp.bfloat16), "blk", scatter_dimension=0, tiled=True
        ).astype(jnp.float32),
        lax.psum_scatter(
            down_grad.astype(jnp.bfloat16), "blk", scatter_dimension=0, tiled=True
        ).astype(jnp.float32),
        lax.psum_scatter(
            latent_weight_grad.astype(jnp.bfloat16), "blk", scatter_dimension=0, tiled=True
        ).astype(jnp.float32),
        lax.psum_scatter(
            decode_slot.astype(jnp.bfloat16), "blk", scatter_dimension=0, tiled=True
        ).astype(jnp.float32),
        lax.psum_scatter(
            centre_grad.astype(jnp.bfloat16), "blk", scatter_dimension=0, tiled=True
        ).astype(jnp.float32),
        lax.psum_scatter(
            norm_grad.astype(jnp.bfloat16), "blk", scatter_dimension=0, tiled=True
        ).astype(jnp.float32),
    )
    summed = (
        lax.psum(block_parts[0].astype(jnp.bfloat16), "slide").astype(jnp.float32),
        lax.psum(block_parts[1].astype(jnp.bfloat16), "slide").astype(jnp.float32),
        lax.psum(block_parts[2].astype(jnp.bfloat16), "slide").astype(jnp.float32),
        lax.psum(block_parts[3].astype(jnp.bfloat16), "slide").astype(jnp.float32),
        lax.psum(block_parts[4].astype(jnp.bfloat16), "slide").astype(jnp.float32),
        lax.psum(block_parts[5].astype(jnp.bfloat16), "slide").astype(jnp.float32),
        lax.psum(block_parts[6].astype(jnp.bfloat16), "slide").astype(jnp.float32),
        lax.psum(block_parts[7].astype(jnp.bfloat16), "slide").astype(jnp.float32),
        lax.psum(block_parts[8].astype(jnp.bfloat16), "slide").astype(jnp.float32),
        lax.psum(block_parts[9].astype(jnp.bfloat16), "slide").astype(jnp.float32),
    )
    embed_out = summed[0]
    decode_out = summed[7]
    return (
        decoded[None],
        prior[None],
        expr_grad[None],
        embed_out,
        summed[1],
        summed[2],
        summed[3],
        summed[4],
        summed[5],
        summed[6],
        decode_out,
        summed[8],
        summed[9],
    )


def peers(offset, count):
    return [(place, place ^ offset) for place in range(count)]


def swap(pieces):
    count = len(pieces)
    return [pieces[0]] + [
        lax.ppermute(pieces[k], "slide", peers(k, count)) for k in range(1, count)
    ]


def share(rows, count):
    return swap([rows] * count)


def after(value, *earlier):
    return lax.optimization_barrier((value,) + earlier)[0]


def in_order(pieces, me, axis):
    stacked = jnp.stack(pieces)
    return jnp.concatenate(
        [
            lax.dynamic_index_in_dim(stacked, jnp.bitwise_xor(me, k), 0, keepdims=False)
            for k in range(len(pieces))
        ],
        axis=axis,
    )


def collect(partials):
    arrived = swap([partials[0]] + [piece.astype(jnp.bfloat16) for piece in partials[1:]])
    total = arrived[0]
    for piece in arrived[1:]:
        total = total + piece.astype(jnp.float32)
    return total


def gather_blk(piece, axis=0):
    return lax.all_gather(piece, "blk", axis=axis, tiled=True)


def scatter_blk(piece, axis=0):
    return lax.psum_scatter(piece, "blk", scatter_dimension=axis, tiled=True)


def split_rows(rows, count):
    height = rows.shape[0] // count
    return [rows[k * height : (k + 1) * height] for k in range(count)]


ROWS = 432
TALL = 1728
WIDE = 3456
CHUNKS = 2
SMALL = 16
COST = pl.CostEstimate(flops=0, bytes_accessed=0, transcendentals=0)


def expression_kernel(count, quarter, genes, me_ref, library_ref, counts_ref, *rest):
    outs, buffers, sems = rest[:count], rest[count], rest[count + 1]
    me = me_ref[0]
    tail = genes - (count - 1) * quarter
    library = library_ref[...].astype(jnp.float32)

    def copy(k, rows):
        start = pl.multiple_of(jnp.bitwise_xor(me, k) * quarter, 8)
        return pltpu.make_async_copy(
            counts_ref.at[pl.ds(start, rows), 0, :],
            buffers.at[k, pl.ds(0, rows), :],
            sems.at[k],
        )

    def each(k, act):
        last = jnp.bitwise_xor(me, k) == count - 1

        @pl.when(last)
        def _():
            act(copy(k, tail))

        @pl.when(jnp.logical_not(last))
        def _():
            act(copy(k, quarter))

    order = list(range(1, count)) + [0]
    for k in order:
        each(k, lambda one: one.start())
    for k in order:
        each(k, lambda one: one.wait())
        have = genes - jnp.bitwise_xor(me, k) * quarter

        @pl.loop(0, quarter // ROWS)
        def _(step):
            start = pl.multiple_of(step * ROWS, ROWS)
            values = buffers[k, pl.ds(start, ROWS), :].astype(jnp.float32)
            values = jnp.log1p(values * 10000.0 / library)
            row = start + lax.broadcasted_iota(jnp.int32, values.shape, 0)
            outs[k][pl.ds(start, ROWS), :] = jnp.where(row < have, values, 0.0).astype(jnp.bfloat16)


def expression_parts(counts, library, me, count, quarter):
    genes = counts.shape[2]
    cells = counts.shape[1]
    part = jax.ShapeDtypeStruct((quarter, cells), jnp.bfloat16)
    return pl.pallas_call(
        functools.partial(expression_kernel, count, quarter, genes),
        out_shape=[part] * count,
        in_specs=[
            pl.BlockSpec(memory_space=pltpu.SMEM),
            pl.BlockSpec(memory_space=pltpu.VMEM),
            pl.BlockSpec(memory_space=pltpu.HBM),
        ],
        out_specs=[pl.BlockSpec(memory_space=pltpu.VMEM)] * count,
        scratch_shapes=[
            pltpu.VMEM((count, quarter, cells), jnp.int32),
            pltpu.SemaphoreType.DMA((count,)),
        ],
        compiler_params=pltpu.CompilerParams(vmem_limit_bytes=40 * 2**20),
        cost_estimate=COST,
        name="expression",
    )(me.reshape(1), library, jnp.transpose(counts, (2, 0, 1)))


def spread_kernel(count, quarter, genes, me_ref, *rest):
    pieces, out, held, wide, sems_in, sems_out = rest[:count], *rest[count:]
    me = me_ref[0]
    tail = genes - (count - 1) * quarter

    def arrive(k):
        return pltpu.make_async_copy(pieces[k], held.at[k], sems_in.at[k])

    def leave(k):
        rows = tail if k == count - 1 else quarter
        return pltpu.make_async_copy(
            wide.at[k, pl.ds(0, rows), :], out.at[pl.ds(k * quarter, rows), 0, :], sems_out.at[k]
        )

    for k in range(count):
        arrive(k).start()
    for k in range(count):
        arrive(k).wait()
    for k in range(count):
        source = jnp.bitwise_xor(me, k)

        @pl.loop(0, quarter // ROWS)
        def _(step):
            rows = pl.ds(pl.multiple_of(step * ROWS, ROWS), ROWS)
            wide[k, rows, :] = held[source, rows, :].astype(jnp.float32)

        leave(k).start()
    for k in range(count):
        leave(k).wait()


def spread_parts(pieces, me, genes):
    count = len(pieces)
    quarter, cells = pieces[0].shape
    out = pl.pallas_call(
        functools.partial(spread_kernel, count, quarter, genes),
        out_shape=jax.ShapeDtypeStruct((genes, 1, cells), jnp.float32),
        in_specs=[pl.BlockSpec(memory_space=pltpu.SMEM)]
        + [pl.BlockSpec(memory_space=pl.ANY)] * count,
        out_specs=pl.BlockSpec(memory_space=pltpu.HBM),
        scratch_shapes=[
            pltpu.VMEM((count, quarter, cells), jnp.bfloat16),
            pltpu.VMEM((count, quarter, cells), jnp.float32),
            pltpu.SemaphoreType.DMA((count,)),
            pltpu.SemaphoreType.DMA((count,)),
        ],
        compiler_params=pltpu.CompilerParams(vmem_limit_bytes=40 * 2**20),
        cost_estimate=COST,
        name="spread",
    )(me.reshape(1), *pieces)
    return jnp.transpose(out, (1, 2, 0))


def join_kernel(count, me_ref, *rest):
    pieces, out, held, sems = rest[:count], *rest[count:]
    slot = pl.program_id(0)

    def arrive(k):
        rows = pl.ds(0, held.shape[1])
        return pltpu.make_async_copy(pieces[k].at[rows, :], held.at[k], sems.at[k])

    @pl.when(slot == 0)
    def _():
        for k in range(count):
            arrive(k).start()
        for k in range(count):
            arrive(k).wait()

    source = jnp.bitwise_xor(me_ref[0], slot)

    @pl.loop(0, out.shape[0] // ROWS)
    def _(step):
        rows = pl.ds(pl.multiple_of(step * ROWS, ROWS), ROWS)
        out[rows, :] = held[source, rows, :].astype(out.dtype)


def join_parts(pieces, me, quarter, genes, dtype):
    count = len(pieces)
    cells = pieces[0].shape[1]
    return pl.pallas_call(
        functools.partial(join_kernel, count),
        grid=(count,),
        out_shape=jax.ShapeDtypeStruct((genes, cells), dtype),
        in_specs=[pl.BlockSpec(memory_space=pltpu.SMEM)]
        + [pl.BlockSpec(memory_space=pl.ANY)] * count,
        out_specs=pl.BlockSpec((quarter, cells), lambda slot: (slot, 0)),
        scratch_shapes=[
            pltpu.VMEM((count, quarter, cells), jnp.bfloat16),
            pltpu.SemaphoreType.DMA((count,)),
        ],
        compiler_params=pltpu.CompilerParams(vmem_limit_bytes=40 * 2**20),
        cost_estimate=COST,
        name="join",
    )(me.reshape(1), *pieces)


def turn_kernel(count, *refs):
    out = refs[-1]
    for k in range(count):
        height = refs[k].shape[1]
        out[k * height : (k + 1) * height, :] = jnp.transpose(refs[k][...])


def turn_parts(parts):
    count = len(parts)
    quarter, cells = parts[0].shape
    return pl.pallas_call(
        functools.partial(turn_kernel, count),
        grid=(quarter // WIDE,),
        out_shape=jax.ShapeDtypeStruct((count * cells, quarter), jnp.bfloat16),
        in_specs=[pl.BlockSpec((WIDE, cells), lambda step: (step, 0))] * count,
        out_specs=pl.BlockSpec((count * cells, WIDE), lambda step: (0, step)),
        compiler_params=pltpu.CompilerParams(vmem_limit_bytes=40 * 2**20),
        cost_estimate=COST,
        name="turn_parts",
    )(*parts)


def scores_kernel(rows, table, *refs):
    outs, total = refs[:-1], refs[-1]
    step = pl.program_id(0)
    product = jnp.dot(rows[...], table[...], preferred_element_type=jnp.float32)

    @pl.when(step == 0)
    def _():
        total[...] = product

    @pl.when(step > 0)
    def _():
        total[...] += product

    @pl.when(step == pl.num_programs(0) - 1)
    def _():
        height = outs[0].shape[0]
        for k in range(len(outs)):
            outs[k][...] = total[k * height : (k + 1) * height, :].astype(outs[k].dtype)


def embed_cells(rows, table, count):
    height, quarter = rows.shape
    width = table.shape[1]
    return pl.pallas_call(
        scores_kernel,
        grid=(quarter // WIDE,),
        out_shape=[
            jax.ShapeDtypeStruct((height // count, width), jnp.float32 if k == 0 else jnp.bfloat16)
            for k in range(count)
        ],
        in_specs=[
            pl.BlockSpec((height, WIDE), lambda step: (0, step)),
            pl.BlockSpec((WIDE, width), lambda step: (step, 0)),
        ],
        out_specs=[pl.BlockSpec((height // count, width), lambda step: (0, 0))] * count,
        scratch_shapes=[pltpu.VMEM((height, width), jnp.float32)],
        compiler_params=pltpu.CompilerParams(vmem_limit_bytes=58 * 2**20),
        cost_estimate=COST,
        name="embed_cells",
    )(rows, table)


def latents_kernel(count, table, *refs):
    cots, outs, total = refs[:count], refs[count:-1], refs[-1]
    step = pl.program_id(0)
    product = jnp.dot(
        table[...],
        jnp.concatenate([one[...] for one in cots], axis=1),
        preferred_element_type=jnp.float32,
    )

    @pl.when(step == 0)
    def _():
        total[...] = product

    @pl.when(step > 0)
    def _():
        total[...] += product

    @pl.when(step == pl.num_programs(0) - 1)
    def _():
        cells = outs[0].shape[0]
        for k in range(count):
            outs[k][...] = jnp.transpose(total[:, k * cells : (k + 1) * cells]).astype(
                outs[k].dtype
            )


def cots_to_latents(cots, table):
    count = len(cots)
    width, quarter = table.shape
    cells = cots[0].shape[1]
    return pl.pallas_call(
        functools.partial(latents_kernel, count),
        grid=(quarter // WIDE,),
        out_shape=[
            jax.ShapeDtypeStruct((cells, width), jnp.float32 if k == 0 else jnp.bfloat16)
            for k in range(count)
        ],
        in_specs=[pl.BlockSpec((width, WIDE), lambda step: (0, step))]
        + [pl.BlockSpec((WIDE, cells), lambda step: (step, 0))] * count,
        out_specs=[pl.BlockSpec((cells, width), lambda step: (0, 0))] * count,
        scratch_shapes=[pltpu.VMEM((width, count * cells), jnp.float32)],
        compiler_params=pltpu.CompilerParams(vmem_limit_bytes=40 * 2**20),
        cost_estimate=COST,
        name="cots_to_latents",
    )(table, *cots)


def decode_kernel(count, table, *refs):
    rows, outs = refs[:count], refs[count:]
    cells = rows[0].shape[0]
    product = jnp.dot(
        jnp.concatenate([one[...] for one in rows], axis=0),
        table[...],
        preferred_element_type=jnp.float32,
    ).astype(jnp.bfloat16)
    for k in range(count):
        outs[k][...] = jnp.transpose(product[k * cells : (k + 1) * cells, :])


def decode_genes(latents, table):
    count = len(latents)
    width, quarter = table.shape
    cells = latents[0].shape[0]
    return pl.pallas_call(
        functools.partial(decode_kernel, count),
        grid=(quarter // WIDE,),
        out_shape=[jax.ShapeDtypeStruct((quarter, cells), jnp.bfloat16)] * count,
        in_specs=[pl.BlockSpec((width, WIDE), lambda step: (0, step))]
        + [pl.BlockSpec((cells, width), lambda step: (0, 0))] * count,
        out_specs=[pl.BlockSpec((WIDE, cells), lambda step: (step, 0))] * count,
        compiler_params=pltpu.CompilerParams(vmem_limit_bytes=40 * 2**20),
        cost_estimate=COST,
        name="decode_genes",
    )(table, *latents)


def genes_kernel(count, table, *refs):
    rows, outs, stacked = refs[:count], refs[count : 2 * count], refs[-1]
    cells = rows[0].shape[0]

    @pl.when(pl.program_id(0) == 0)
    def _():
        for k in range(count):
            stacked[:, k * cells : (k + 1) * cells] = jnp.transpose(rows[k][...])

    product = jnp.dot(table[...], stacked[...], preferred_element_type=jnp.float32)
    for k in range(count):
        outs[k][...] = product[:, k * cells : (k + 1) * cells].astype(outs[k].dtype)


def cells_to_genes(table, rows, quarter):
    count = len(rows)
    cells, width = rows[0].shape
    return pl.pallas_call(
        functools.partial(genes_kernel, count),
        grid=(quarter // TALL,),
        out_shape=[jax.ShapeDtypeStruct((quarter, cells), jnp.bfloat16)] * count,
        in_specs=[pl.BlockSpec((TALL, width), lambda step: (step, 0))]
        + [pl.BlockSpec((cells, width), lambda step: (0, 0))] * count,
        out_specs=[pl.BlockSpec((TALL, cells), lambda step: (step, 0))] * count,
        scratch_shapes=[pltpu.VMEM((width, count * cells), jnp.bfloat16)],
        compiler_params=pltpu.CompilerParams(vmem_limit_bytes=58 * 2**20),
        cost_estimate=COST,
        name="cells_to_genes",
    )(table, *rows)


def embed_kernel(count, *refs):
    parts, rows = refs[:count], refs[count : 2 * count]
    small, out, stacked, results, sems = refs[2 * count :]
    steps = parts[0].shape[0] // ROWS
    height = rows[0].shape[0]
    blocks, _, block = out.shape
    for k in range(count):
        stacked[k * height : (k + 1) * height, :] = rows[k][...]

    def leave(slot, step):
        start = pl.multiple_of(step * ROWS, ROWS)
        return pltpu.make_async_copy(
            results.at[slot], out.at[:, pl.ds(start, ROWS), :], sems.at[slot]
        )

    last = pltpu.make_async_copy(
        small, out.at[:, pl.ds(steps * ROWS, small.shape[1]), :], sems.at[2]
    )
    last.start()

    @pl.loop(0, steps)
    def _(step):
        slot = lax.rem(step, 2)

        @pl.when(step >= 2)
        def _():
            leave(slot, step - 2).wait()

        here = pl.ds(pl.multiple_of(step * ROWS, ROWS), ROWS)
        product = jnp.dot(
            jnp.concatenate([part[here, :] for part in parts], axis=1),
            stacked[...],
            preferred_element_type=jnp.float32,
        ).astype(results.dtype)
        for k in range(blocks):
            results[slot, k] = product[:, k * block : (k + 1) * block]
        leave(slot, step).start()

    for step in range(max(steps - 2, 0), steps):
        leave(step % 2, step).wait()
    last.wait()


def embed_products(parts, rows, small):
    count = len(parts)
    quarter, cells = parts[0].shape
    width = rows[0].shape[1]
    blocks, extra, block = small.shape
    return pl.pallas_call(
        functools.partial(embed_kernel, count),
        out_shape=jax.ShapeDtypeStruct((blocks, quarter + extra, block), jnp.bfloat16),
        in_specs=[pl.BlockSpec(memory_space=pltpu.VMEM)] * (2 * count + 1),
        out_specs=pl.BlockSpec(memory_space=pltpu.HBM),
        scratch_shapes=[
            pltpu.VMEM((count * cells, width), jnp.bfloat16),
            pltpu.VMEM((2, blocks, ROWS, block), jnp.bfloat16),
            pltpu.SemaphoreType.DMA((3,)),
        ],
        compiler_params=pltpu.CompilerParams(vmem_limit_bytes=40 * 2**20),
        cost_estimate=COST,
        name="embed_products",
    )(*parts, *rows, small)


def products_kernel(count, *refs):
    out = refs[-1]
    spot = 0
    for k in range(count):
        rows = jnp.transpose(refs[2 * k][...])
        columns = refs[2 * k + 1]
        width = columns.shape[1]
        for start in range(0, width, 256):
            out[:, spot + start : spot + start + 256] = jnp.dot(
                rows, columns[:, start : start + 256], preferred_element_type=jnp.float32
            ).astype(out.dtype)
        spot += width


def row_products(pairs):
    operands = [one for pair in pairs for one in pair]
    height = pairs[0][0].shape[1]
    width = sum(b.shape[1] for _, b in pairs)
    return pl.pallas_call(
        functools.partial(products_kernel, len(pairs)),
        out_shape=jax.ShapeDtypeStruct((height, width), jnp.bfloat16),
        in_specs=[pl.BlockSpec(memory_space=pltpu.VMEM)] * len(operands),
        out_specs=pl.BlockSpec(memory_space=pltpu.VMEM),
        compiler_params=pltpu.CompilerParams(vmem_limit_bytes=48 * 2**20),
        cost_estimate=COST,
        name="row_products",
    )(*operands)


def decoder_kernel(count, *refs):
    rows, cots, out, turned = refs[:count], refs[count : 2 * count], refs[-2], refs[-1]
    cells = rows[0].shape[0]

    @pl.when(pl.program_id(0) == 0)
    def _():
        for k in range(count):
            turned[:, k * cells : (k + 1) * cells] = jnp.transpose(rows[k][...])

    out[...] = lax.dot_general(
        turned[...],
        jnp.concatenate([one[...] for one in cots], axis=1),
        (((1,), (1,)), ((), ())),
        preferred_element_type=jnp.float32,
    ).astype(out.dtype)


def decoder_products(latents, cots):
    count = len(latents)
    cells, width = latents[0].shape
    quarter = cots[0].shape[0]
    step_rows = math.gcd(quarter, 1152)
    return pl.pallas_call(
        functools.partial(decoder_kernel, count),
        grid=(quarter // step_rows,),
        out_shape=jax.ShapeDtypeStruct((width, quarter), jnp.bfloat16),
        in_specs=[pl.BlockSpec((cells, width), lambda step: (0, 0))] * count
        + [pl.BlockSpec((step_rows, cells), lambda step: (step, 0))] * count,
        out_specs=pl.BlockSpec((width, step_rows), lambda step: (0, step)),
        scratch_shapes=[pltpu.VMEM((width, count * cells), jnp.bfloat16)],
        compiler_params=pltpu.CompilerParams(vmem_limit_bytes=40 * 2**20),
        cost_estimate=COST,
        name="decoder_products",
    )(*latents, *cots)


def head_probs(keys, queries, scaling):
    scores = (
        lax.dot_general(keys, queries, (((1,), (1,)), ((), ())), preferred_element_type=jnp.float32)
        * scaling
    )
    scores = jnp.exp(scores - jnp.max(scores, axis=0, keepdims=True))
    return scores * (1.0 / jnp.sum(scores, axis=0, keepdims=True))


def attend_kernel(heads, width, rows_ref, out, turned):
    step = pl.program_id(0)
    height = out.shape[0]
    group = heads * width

    @pl.when(step == 0)
    def _():
        turned[...] = jnp.transpose(rows_ref[:, 2 * group : 3 * group])

    block = rows_ref[pl.ds(pl.multiple_of(step * height, height), height), :group]
    results = []
    for h in range(heads):
        probs = head_probs(
            rows_ref[:, group + h * width : group + (h + 1) * width],
            block[:, h * width : (h + 1) * width],
            width ** (-0.5),
        ).astype(jnp.bfloat16)
        results.append(
            jnp.dot(turned[h * width : (h + 1) * width, :], probs, preferred_element_type=jnp.float32)
        )
    out[...] = jnp.transpose(jnp.concatenate(results, axis=0)).astype(out.dtype)


def attend(rows, heads):
    cells, total = rows.shape
    group = total // 3
    height = math.gcd(cells, 256)
    return pl.pallas_call(
        functools.partial(attend_kernel, heads, group // heads),
        grid=(cells // height,),
        out_shape=jax.ShapeDtypeStruct((cells, group), jnp.bfloat16),
        in_specs=[pl.BlockSpec((cells, total), lambda step: (0, 0))],
        out_specs=pl.BlockSpec((height, group), lambda step: (step, 0)),
        scratch_shapes=[pltpu.VMEM((group, cells), jnp.bfloat16)],
        compiler_params=pltpu.CompilerParams(vmem_limit_bytes=40 * 2**20),
        cost_estimate=COST,
        name="attend",
    )(rows)


def attend_back_kernel(heads, width, rows_ref, cot_ref, out, turned, key_sum, value_sum):
    step = pl.program_id(0)
    group = heads * width
    height = rows_ref.shape[0] // pl.num_programs(0)
    scaling = width ** (-0.5)

    @pl.when(step == 0)
    def _():
        turned[...] = jnp.transpose(rows_ref[:, group : 2 * group])
        key_sum[...] = jnp.zeros_like(key_sum)
        value_sum[...] = jnp.zeros_like(value_sum)

    here = pl.ds(pl.multiple_of(step * height, height), height)
    block = rows_ref[here, :group]
    cots = cot_ref[here, :]
    results = []
    for h in range(heads):
        columns = slice(h * width, (h + 1) * width)
        queries = block[:, columns]
        cot = cots[:, columns]
        probs = head_probs(
            rows_ref[:, group + h * width : group + (h + 1) * width], queries, scaling
        )
        prob_grad = lax.dot_general(
            rows_ref[:, 2 * group + h * width : 2 * group + (h + 1) * width],
            cot,
            (((1,), (1,)), ((), ())),
            preferred_element_type=jnp.float32,
        )
        delta = jnp.sum(probs * prob_grad, axis=0, keepdims=True)
        score_grad = (probs * (prob_grad - delta)).astype(jnp.bfloat16)
        results.append(
            jnp.dot(turned[columns, :], score_grad, preferred_element_type=jnp.float32) * scaling
        )
        key_sum[:, columns] += jnp.dot(score_grad, queries, preferred_element_type=jnp.float32)
        value_sum[:, columns] += jnp.dot(
            probs.astype(jnp.bfloat16), cot, preferred_element_type=jnp.float32
        )
    out[here, :group] = jnp.transpose(jnp.concatenate(results, axis=0)).astype(out.dtype)

    @pl.when(step == pl.num_programs(0) - 1)
    def _():
        out[:, group : 2 * group] = (key_sum[...] * scaling).astype(out.dtype)
        out[:, 2 * group :] = value_sum[...].astype(out.dtype)


def attend_back(rows, cot, heads):
    cells, total = rows.shape
    group = total // 3
    height = math.gcd(cells, 256)
    return pl.pallas_call(
        functools.partial(attend_back_kernel, heads, group // heads),
        grid=(cells // height,),
        out_shape=jax.ShapeDtypeStruct((cells, total), jnp.bfloat16),
        in_specs=[
            pl.BlockSpec((cells, total), lambda step: (0, 0)),
            pl.BlockSpec((cells, group), lambda step: (0, 0)),
        ],
        out_specs=pl.BlockSpec((cells, total), lambda step: (0, 0)),
        scratch_shapes=[
            pltpu.VMEM((group, cells), jnp.bfloat16),
            pltpu.VMEM((cells, group), jnp.float32),
            pltpu.VMEM((cells, group), jnp.float32),
        ],
        compiler_params=pltpu.CompilerParams(vmem_limit_bytes=40 * 2**20),
        cost_estimate=COST,
        name="attend_back",
    )(rows, cot)


def split_model(
    counts,
    library,
    coords,
    noise,
    decoded_cot,
    prior_cot,
    embed_t,
    w_qkv,
    w_attn_out,
    w_up,
    up_bias,
    w_down,
    w_latent,
    w_decode,
    comp_means,
    norm_params,
):
    slides = lax.axis_size("slide")
    blocks = lax.axis_size("blk")
    me = lax.axis_index("slide")
    genes = embed_t.shape[1]
    cells = counts.shape[1]
    model_width = w_attn_out.shape[1]
    own_rows = w_qkv.shape[0]
    latent_width = w_decode.shape[0] * blocks
    mixture_count = comp_means.shape[1]
    quarter = -(-genes // (slides * ROWS)) * ROWS
    padded = quarter * slides
    head_part = model_width // slides
    pair = model_width // blocks
    pairs = head_part // pair
    ff_part = up_bias.shape[0] // slides
    latent_part = model_width // slides

    def place_of(k):
        return jnp.bitwise_xor(me, k)

    def column_part(rows, width, place):
        return lax.dynamic_slice_in_dim(rows, place * width, width, 1)

    def whole(piece, axis):
        return in_order(share(piece, slides), me, axis)

    def wide(piece):
        return piece.astype(jnp.float32)

    embed_part = lax.dynamic_slice_in_dim(
        jnp.pad(embed_t.T, ((0, padded - genes), (0, 0))), me * quarter, quarter, 0
    )
    bias_part = lax.dynamic_slice_in_dim(up_bias, me * ff_part, ff_part, 0)
    mean_cols = comp_means.size // own_rows
    small = jnp.concatenate(
        [norm_params, comp_means.reshape(own_rows, mean_cols), bias_part.reshape(own_rows, -1)],
        axis=1,
    ).T
    small_rows = small.shape[0]
    small = jnp.pad(small, ((0, SMALL - small_rows), (0, 0)))
    qkv_width = pairs * 3 * pair
    qkv_part = [
        lax.dynamic_slice_in_dim(w_qkv, k * model_width + me * head_part, head_part, 1)
        for k in range(3)
    ]
    qkv_part = jnp.concatenate(
        [part[:, j * pair : (j + 1) * pair] for j in range(pairs) for part in qkv_part], axis=1
    ).T
    embedding = gather_blk(jnp.concatenate([embed_part, small, qkv_part], axis=0), 1)
    small_all = embedding[quarter : quarter + SMALL]
    weight_qkv = embedding[quarter + SMALL :].reshape(pairs, 3 * pair, model_width)
    norm_float = small_all[:4].astype(jnp.float32)
    centres = small_all[4 : 4 + mean_cols].T.reshape(latent_width, mixture_count)
    bias_up = small_all[4 + mean_cols : small_rows].T.reshape(-1).astype(jnp.float32)
    expr_parts = swap(expression_parts(counts, library, me, slides, quarter))

    cot_all = jnp.pad(decoded_cot[0].T, ((0, padded - genes), (0, 0)))
    cot_first = [
        lax.dynamic_slice_in_dim(cot_all, place_of(k) * quarter, quarter, 0)
        for k in range(slides)
    ]
    cot_parts = swap([after(piece, *expr_parts[1:]) for piece in cot_first])
    up_part = jnp.concatenate(
        [
            lax.dynamic_slice_in_dim(w_up, (k * slides + me) * ff_part, ff_part, 1)
            for k in range(blocks)
        ],
        axis=1,
    )
    down_part = lax.dynamic_slice_in_dim(w_down, me * ff_part, ff_part, 0)
    expr_rows = turn_parts(expr_parts)
    middle = gather_blk(
        after(
            jnp.concatenate([w_attn_out, up_part, down_part, w_latent], axis=1),
            embedding,
            expr_rows,
            *cot_parts[1:],
        )
    )
    weight_out, weight_up, weight_down, weight_latent = jnp.split(middle, 4, axis=1)
    decode_part = lax.dynamic_slice_in_dim(
        jnp.pad(w_decode, ((0, 0), (0, padded - genes))), me * quarter, quarter, 1
    )

    h_zero = collect(embed_cells(expr_rows, embedding, slides))
    h_zero = h_zero + spatial_code(coords[0], model_width)
    normed_one, norm_one_back = jax.vjp(layer_norm, h_zero, norm_float[0], norm_float[1])
    normed_one_all = jnp.concatenate(share(normed_one.astype(jnp.bfloat16), slides), axis=0)
    projected = jnp.einsum(
        "ck,pfk->pcf", normed_one_all, weight_qkv, preferred_element_type=jnp.float32
    ).astype(jnp.bfloat16)

    def to_heads(rows):
        return lax.all_to_all(
            rows.reshape(blocks, cells, rows.shape[-1]), "blk", 0, 0, tiled=True
        ).reshape(blocks * cells, rows.shape[-1])

    head_rows = to_heads(projected)
    per_pair = pair // HEAD_DIM
    own_heads = to_heads(attend(head_rows, per_pair)).reshape(pairs, slides, cells, pair)
    weight_decode = gather_blk(after(decode_part, middle, own_heads))
    attended_parts = swap(
        [
            jnp.concatenate([own_heads[j, k] for j in range(pairs)], axis=1)
            for k in range(slides)
        ]
    )
    attended_low = in_order(attended_parts, me, 1)
    h_one = h_zero + jnp.dot(attended_low, weight_out, preferred_element_type=jnp.float32)
    normed_two, norm_two_back = jax.vjp(layer_norm, h_one, norm_float[2], norm_float[3])
    normed_two_low = normed_two.astype(jnp.bfloat16)
    normed_two_all = jnp.concatenate(share(normed_two_low, slides), axis=0)
    hidden_pre = (
        jnp.dot(normed_two_all, weight_up, preferred_element_type=jnp.float32) + bias_up
    )
    hidden_act, gelu_back = jax.vjp(jax.nn.gelu, hidden_pre)
    hidden_low = hidden_act.astype(jnp.bfloat16)
    h_two = h_one + collect(
        split_rows(jnp.dot(hidden_low, weight_down, preferred_element_type=jnp.float32), slides)
    )
    h_two_low = h_two.astype(jnp.bfloat16)
    latent_pre = jnp.dot(h_two_low, weight_latent, preferred_element_type=jnp.float32)
    spread = jnp.exp(0.5 * latent_pre[:, latent_width:])
    latent = latent_pre[:, :latent_width] + spread * noise[0]
    prior, prior_back = jax.vjp(mixture_term, latent, centres.astype(jnp.float32))

    latent_from_decode = collect(cots_to_latents(cot_parts, weight_decode))
    latent_from_prior, centre_grad = prior_back(prior_cot[0])
    latent_total = latent_from_decode + latent_from_prior
    pre_grad = jnp.concatenate(
        [latent_total, latent_total * noise[0] * spread * 0.5], axis=-1
    ).astype(jnp.bfloat16)
    latent_parts = share(latent.astype(jnp.bfloat16), slides)
    pre_grad_all = jnp.concatenate(share(after(pre_grad, *latent_parts[1:]), slides), axis=0)
    decode_local = decoder_products(latent_parts, cot_parts)
    pre_grad_all = after(pre_grad_all, decode_local)
    decode_own = scatter_blk(decode_local)
    h_two_grad_all = contract_cols(pre_grad_all, weight_latent)
    down_input = h_two_grad_all.astype(jnp.bfloat16)
    hidden_grad = contract_cols(down_input, weight_down)
    pre_hidden_grad = gelu_back(hidden_grad)[0].astype(jnp.bfloat16)
    h_two_all = jnp.concatenate(share(after(h_two_low, pre_grad_all), slides), axis=0)
    normed_two_parts = split_rows(contract_cols(pre_hidden_grad, weight_up), slides)
    normed_two_grad = collect(normed_two_parts)
    middle_local = row_products(
        [
            (hidden_low, after(down_input, normed_two_parts[-1])),
            (normed_two_all, pre_hidden_grad),
            (h_two_all, column_part(pre_grad_all, latent_part, me)),
        ]
    )
    normed_two_grad = after(normed_two_grad, middle_local)
    middle_grad = scatter_blk(after(middle_local, decode_own))
    h_one_part, gain_two_grad, shift_two_grad = norm_two_back(normed_two_grad)
    h_one_grad = h_two_grad_all[:cells] + h_one_part
    out_input = h_one_grad.astype(jnp.bfloat16)
    attended_grad = contract_cols(out_input, weight_out).astype(jnp.bfloat16)

    grad_parts = swap([column_part(attended_grad, head_part, place_of(k)) for k in range(slides)])
    grad_pairs = jnp.stack(
        [part[:, j * pair : (j + 1) * pair] for j in range(pairs) for part in grad_parts]
    )
    out_heads = to_heads(grad_pairs)

    decoded_rows = decode_genes(
        [after(rows, *grad_parts[1:]) for rows in latent_parts], weight_decode
    )
    out_heads = after(out_heads, *decoded_rows)
    decoded_parts = swap(decoded_rows)
    attended_all = jnp.concatenate(share(after(attended_low, *grad_parts[1:]), slides), axis=0)
    head_grads = attend_back(head_rows, out_heads, per_pair)
    out_parts = swap(
        [
            after(column_part(out_input, head_part, place_of(k)), *grad_parts[1:])
            for k in range(slides)
        ]
    )
    decode_shares = share(after(decode_own, *grad_parts[1:]), slides)
    projected_grad = to_heads(head_grads).reshape(pairs, slides * cells, 3 * pair)
    projected_grad = after(projected_grad, attended_all, *out_parts[1:], *decoded_parts[1:])
    normed_one_grad = collect(
        split_rows(
            jnp.einsum(
                "pcf,pfk->ck", projected_grad, weight_qkv, preferred_element_type=jnp.float32
            ),
            slides,
        )
    )
    last_local = row_products(
        [
            (normed_one_all, jnp.concatenate(list(projected_grad), axis=1)),
            (attended_all, jnp.concatenate(out_parts, axis=0)),
        ]
    )
    normed_one_grad = after(normed_one_grad, last_local, *decode_shares[1:])
    last_grad = scatter_blk(after(last_local, middle_grad))
    h_zero_part, gain_one_grad, shift_one_grad = norm_one_back(normed_one_grad)
    h_zero_low = (h_one_grad + h_zero_part).astype(jnp.bfloat16)
    h_zero_parts = share(h_zero_low, slides)

    up_bias_grad = jnp.sum(pre_hidden_grad.astype(jnp.float32), axis=0)
    small_grad = jnp.concatenate(
        [
            jnp.stack([gain_one_grad, shift_one_grad, gain_two_grad, shift_two_grad], axis=0),
            centre_grad.reshape(model_width, mean_cols).T,
            up_bias_grad.reshape(model_width, -1).T,
        ],
        axis=0,
    )
    small_grad = jnp.pad(small_grad, ((0, SMALL - small_rows), (0, 0))).astype(jnp.bfloat16)
    small_grad = jnp.transpose(small_grad.reshape(SMALL, blocks, own_rows), (1, 0, 2))
    embed_local = embed_products(expr_parts, h_zero_parts, small_grad)
    gene_rows = cells_to_genes(
        embedding, [after(part, embed_local) for part in h_zero_parts], quarter
    )
    embed_own = scatter_blk(after(embed_local, last_grad))[0]
    middle_parts = share(after(middle_grad, embed_local), slides)
    gene_parts = swap(gene_rows)
    last_parts = share(after(last_grad, embed_local), slides)
    expr_grad = spread_parts(gene_parts, me, genes)
    decoded = join_parts(
        [after(part, *gene_rows[1:]) for part in decoded_parts], me, quarter, genes, jnp.bfloat16
    ).T
    middle_parts = [after(part, *gene_rows[1:]) for part in middle_parts]
    up_end = model_width + blocks * ff_part
    down_grad = in_order([part[:, :model_width] for part in middle_parts], me, 0)
    up_grad = in_order(
        [
            part[:, model_width:up_end].reshape(own_rows, blocks, 1, ff_part)
            for part in middle_parts
        ],
        me,
        2,
    )
    latent_grad = in_order([part[:, up_end:] for part in middle_parts], me, 1)
    decode_grad = in_order([after(part, *gene_rows[1:]) for part in decode_shares], me, 1)
    decode_grad = decode_grad[:, :genes]
    qkv_grad = in_order(
        [
            jnp.transpose(
                part[:, :qkv_width].reshape(own_rows, pairs, 3, 1, pair), (0, 2, 3, 1, 4)
            )
            for part in last_parts
        ],
        me,
        2,
    ).reshape(own_rows, 3 * model_width)
    attn_out_grad = in_order([part[:, qkv_width:] for part in last_parts], me, 1)

    outs = [
        wide(one)
        for one in (
            decode_grad,
            qkv_grad,
            attn_out_grad,
            up_grad.reshape(own_rows, -1),
            down_grad,
            latent_grad,
        )
    ]
    embed_shares = share(after(embed_own, expr_grad, *outs), slides)
    embed_grad = join_parts(embed_shares, me, quarter, genes, jnp.float32).T
    small_parts = [part[quarter : quarter + small_rows].T for part in embed_shares]
    summed = sum(part.astype(jnp.float32) for part in small_parts)
    up_bias_out = in_order([part[:, 4 + mean_cols :].reshape(-1) for part in small_parts], me, 0)


    return (
        decoded[None],
        prior[None],
        expr_grad,
        embed_grad,
        outs[1],
        outs[2],
        outs[3],
        wide(up_bias_out),
        outs[4],
        outs[5],
        outs[0],
        summed[:, 4 : 4 + mean_cols].reshape(comp_means.shape),
        summed[:, :4],
    )


def fits(mesh):
    slides, blocks = mesh.shape["slide"], mesh.shape["blk"]
    return slides & (slides - 1) == 0 and HEADS % slides == 0 and HEADS % blocks == 0


def solution(mesh):
    placed = (
        P("slide", "blk", None),
        P("slide", "blk"),
        P("slide", "blk", None),
        P("slide", "blk", None),
        P("slide", "blk", None),
        P("slide", "blk"),
        P("blk", None),
        P("blk", None),
        P("blk", None),
        P("blk", None),
        P("blk"),
        P("blk", None),
        P("blk", None),
        P("blk", None),
        P("blk", None),
        P("blk", None),
    )
    return jax.shard_map(
        split_model if fits(mesh) else local,
        mesh=mesh,
        in_specs=placed,
        out_specs=(
            P("slide", "blk", None),
            P("slide", "blk"),
            P("slide", "blk", None),
            P("blk", None),
            P("blk", None),
            P("blk", None),
            P("blk", None),
            P("blk"),
            P("blk", None),
            P("blk", None),
            P("blk", None),
            P("blk", None),
            P("blk", None),
        ),
        check_vma=False,
    )
```

```python
import functools
import math

import jax
import jax.numpy as jnp
from jax import lax
from jax.experimental import pallas as pl
from jax.experimental.pallas import tpu as pltpu
from jax.sharding import PartitionSpec as P

HEADS = 16
HEAD_DIM = 64


eps_norm = 1e-05


def contract_rows(former, latter):
    return lax.dot_general(
        former, latter, (((0,), (0,)), ((), ())), preferred_element_type=jnp.float32
    )


def contract_cols(former, latter):
    return lax.dot_general(
        former, latter, (((1,), (1,)), ((), ())), preferred_element_type=jnp.float32
    )


def layer_norm(tensor, norm_gain, norm_shift):
    center = tensor - jnp.mean(tensor, axis=-1, keepdims=True)
    inverse = lax.rsqrt(jnp.mean(center * center, axis=-1, keepdims=True) + eps_norm)
    return center * inverse * norm_gain + norm_shift


def spatial_code(coords, model_width):
    quarter = model_width // 4
    frequency = jnp.exp(-math.log(10000.0) * jnp.arange(quarter, dtype=jnp.float32) / quarter)
    first_axis = coords[..., 0:1].astype(jnp.float32) * frequency
    second_axis = coords[..., 1:2].astype(jnp.float32) * frequency
    return jnp.concatenate(
        [jnp.sin(first_axis), jnp.cos(first_axis), jnp.sin(second_axis), jnp.cos(second_axis)],
        axis=-1,
    )


def mixture_term(latent, centres):
    scores = (
        jnp.dot(
            latent, centres, precision=lax.Precision.HIGHEST, preferred_element_type=jnp.float32
        )
        - 0.5 * jnp.sum(centres * centres, axis=0)
    ) * latent.shape[-1] ** (-0.5)
    return -jax.nn.logsumexp(scores, axis=-1)


def split_single(rows_in, head_count):
    arrived_rows = rows_in.shape[0]
    block_rows = 512
    return rows_in.reshape(
        (arrived_rows // block_rows, block_rows, head_count, rows_in.shape[1] // head_count)
    )


def split_blocks(key_rows, value_rows, head_count):
    return (split_single(key_rows, head_count), split_single(value_rows, head_count))


def local(
    counts,
    library,
    coords,
    noise,
    decoded_cot,
    prior_cot,
    embed_t,
    w_qkv,
    w_attn_out,
    w_up,
    up_bias,
    w_down,
    w_latent,
    w_decode,
    comp_means,
    norm_params,
):
    gathered = (
        lax.all_gather(embed_t, "blk", axis=0, tiled=True),
        lax.all_gather(w_qkv, "blk", axis=0, tiled=True),
        lax.all_gather(w_attn_out, "blk", axis=0, tiled=True),
        lax.all_gather(w_up, "blk", axis=0, tiled=True),
        lax.all_gather(up_bias, "blk", axis=0, tiled=True),
        lax.all_gather(w_down, "blk", axis=0, tiled=True),
        lax.all_gather(w_latent, "blk", axis=0, tiled=True),
        lax.all_gather(w_decode, "blk", axis=0, tiled=True),
        lax.all_gather(comp_means, "blk", axis=0, tiled=True),
        lax.all_gather(norm_params, "blk", axis=0, tiled=True),
    )
    (
        embedding,
        weight_qkv,
        weight_out,
        weight_up,
        bias_up,
        weight_down,
        weight_latent,
        weight_decode,
        centres,
        norm_table,
    ) = gathered
    head_count = HEADS
    head_width = HEAD_DIM
    scaling = head_width ** (-0.5)
    model_width = embedding.shape[0]
    latent_width = weight_decode.shape[0]
    blk_count = lax.axis_size("blk")
    expression = jnp.log1p(
        counts[0].astype(jnp.float32) * 10000.0 / library[0].astype(jnp.float32)[:, None]
    )
    expression_low = expression.astype(jnp.bfloat16)
    local_cells = expression.shape[0]
    norm_float = norm_table.astype(jnp.float32)
    h_zero = contract_cols(expression_low, embedding) + spatial_code(coords[0], model_width)
    normed_one, norm_one_back = jax.vjp(layer_norm, h_zero, norm_float[:, 0], norm_float[:, 1])
    normed_one_low = normed_one.astype(jnp.bfloat16)
    projected = jnp.dot(normed_one_low, weight_qkv, preferred_element_type=jnp.float32).astype(
        jnp.bfloat16
    )
    queries = projected[:, :model_width].reshape(local_cells, head_count, head_width)
    key_rows = projected[:, model_width : 2 * model_width]
    value_rows = projected[:, 2 * model_width :]
    stat_start = (
        jnp.full((head_count, local_cells), -1e30, jnp.float32),
        jnp.zeros((head_count, local_cells), jnp.float32),
    )
    key_blocks = split_single(lax.all_gather(key_rows, "blk", axis=0, tiled=True), head_count)

    def per_block(status, key_block):
        running_max, running_sum = status
        scores = (
            jnp.einsum("thd,khd->htk", queries, key_block, preferred_element_type=jnp.float32)
            * scaling
        )
        new_max = jnp.maximum(running_max, jnp.max(scores, axis=-1))
        running_sum = running_sum * jnp.exp(running_max - new_max) + jnp.sum(
            jnp.exp(scores - new_max[..., None]), axis=-1
        )
        return ((new_max, running_sum), None)

    result, unused = lax.scan(per_block, stat_start, key_blocks)
    running_max, running_sum = result
    log_total = running_max + jnp.log(running_sum)
    arrived = (
        lax.all_gather(key_rows, "blk", axis=0, tiled=True),
        lax.all_gather(value_rows, "blk", axis=0, tiled=True),
    )
    key_blocks, value_blocks = split_blocks(arrived[0], arrived[1], head_count)

    def per_block(weighted, block_pair):
        scores = (
            jnp.einsum("thd,khd->htk", queries, block_pair[0], preferred_element_type=jnp.float32)
            * scaling
        )
        probs_low = jnp.exp(scores - log_total[..., None]).astype(jnp.bfloat16)
        weighted = weighted + jnp.einsum(
            "htk,khd->htd", probs_low, block_pair[1], preferred_element_type=jnp.float32
        )
        return (weighted, None)

    result, unused = lax.scan(
        per_block,
        jnp.zeros((head_count, local_cells, head_width), jnp.float32),
        (key_blocks, value_blocks),
    )
    attended_cells = jnp.transpose(result, (1, 0, 2))
    attended_low = attended_cells.reshape(local_cells, model_width).astype(jnp.bfloat16)
    h_one = h_zero + jnp.dot(attended_low, weight_out, preferred_element_type=jnp.float32)
    normed_two, norm_two_back = jax.vjp(layer_norm, h_one, norm_float[:, 2], norm_float[:, 3])
    normed_two_low = normed_two.astype(jnp.bfloat16)
    hidden_pre = jnp.dot(
        normed_two_low, weight_up, preferred_element_type=jnp.float32
    ) + bias_up.astype(jnp.float32)
    hidden_act, gelu_back = jax.vjp(jax.nn.gelu, hidden_pre)
    hidden_low = hidden_act.astype(jnp.bfloat16)
    h_two = h_one + jnp.dot(hidden_low, weight_down, preferred_element_type=jnp.float32)
    h_two_low = h_two.astype(jnp.bfloat16)
    latent_pre = jnp.dot(h_two_low, weight_latent, preferred_element_type=jnp.float32)
    spread = jnp.exp(0.5 * latent_pre[:, latent_width:])
    latent = latent_pre[:, :latent_width] + spread * noise[0]
    latent_low = latent.astype(jnp.bfloat16)
    decoded = jnp.dot(latent_low, weight_decode, preferred_element_type=jnp.float32).astype(
        jnp.bfloat16
    )
    prior, prior_back = jax.vjp(mixture_term, latent, centres.astype(jnp.float32))
    out_grad = decoded_cot[0]
    latent_from_decode = contract_cols(out_grad, weight_decode)
    latent_from_prior, centre_grad = prior_back(prior_cot[0])
    latent_total = latent_from_decode + latent_from_prior
    pre_grad = jnp.concatenate(
        [latent_total, latent_total * noise[0] * spread * 0.5], axis=-1
    ).astype(jnp.bfloat16)
    latent_weight_grad = contract_rows(h_two_low, pre_grad)
    h_two_grad = contract_cols(pre_grad, weight_latent)
    down_input = h_two_grad.astype(jnp.bfloat16)
    down_grad = contract_rows(hidden_low, down_input)
    hidden_grad = contract_cols(down_input, weight_down)
    pre_hidden_grad = gelu_back(hidden_grad)[0].astype(jnp.bfloat16)
    up_bias_grad = jnp.sum(pre_hidden_grad.astype(jnp.float32), axis=0)
    up_grad = contract_rows(normed_two_low, pre_hidden_grad)
    normed_two_grad = contract_cols(pre_hidden_grad, weight_up)
    h_one_part, gain_two_grad, shift_two_grad = norm_two_back(normed_two_grad)
    h_one_grad = h_two_grad + h_one_part
    out_input = h_one_grad.astype(jnp.bfloat16)
    attn_out_grad = contract_rows(attended_low, out_input)
    attended_grad = contract_cols(out_input, weight_out).astype(jnp.bfloat16)
    out_heads = attended_grad.reshape(local_cells, head_count, head_width)
    row_delta = jnp.sum(out_heads.astype(jnp.float32) * attended_cells, axis=-1).T
    query_zero = jnp.zeros((head_count, local_cells, head_width), jnp.float32)
    start_back = (query_zero, jnp.zeros((local_cells * blk_count, 2 * model_width), jnp.float32))
    arrived = (
        lax.all_gather(key_rows, "blk", axis=0, tiled=True),
        lax.all_gather(value_rows, "blk", axis=0, tiled=True),
    )
    key_blocks, value_blocks = split_blocks(arrived[0], arrived[1], head_count)
    arrived_rows = arrived[0].shape[0]

    def per_block(query_sum, block_pair):
        scores = (
            jnp.einsum("thd,khd->htk", queries, block_pair[0], preferred_element_type=jnp.float32)
            * scaling
        )
        probs = jnp.exp(scores - log_total[..., None])
        prob_grad = jnp.einsum(
            "thd,khd->htk", out_heads, block_pair[1], preferred_element_type=jnp.float32
        )
        score_grad = (probs * (prob_grad - row_delta[..., None])).astype(jnp.bfloat16)
        query_sum = query_sum + jnp.einsum(
            "htk,khd->htd", score_grad, block_pair[0], preferred_element_type=jnp.float32
        )
        key_part = (
            jnp.einsum("htk,thd->khd", score_grad, queries, preferred_element_type=jnp.float32)
            * scaling
        )
        value_part = jnp.einsum(
            "htk,thd->khd",
            probs.astype(jnp.bfloat16),
            out_heads,
            preferred_element_type=jnp.float32,
        )
        block_rows = key_part.shape[0]
        return (
            query_sum,
            jnp.concatenate(
                [key_part.reshape(block_rows, -1), value_part.reshape(block_rows, -1)], axis=-1
            ),
        )

    query_total, stacked = lax.scan(per_block, start_back[0], (key_blocks, value_blocks))
    stacked = stacked.reshape(arrived_rows, stacked.shape[-1])
    carried_back = (query_total, stacked)
    query_total = carried_back[0]
    own_pairs = lax.psum_scatter(
        carried_back[1].astype(jnp.bfloat16), "blk", scatter_dimension=0, tiled=True
    ).astype(jnp.float32)
    query_rows = jnp.transpose(query_total * scaling, (1, 0, 2)).reshape(local_cells, model_width)
    projected_grad = jnp.concatenate([query_rows, own_pairs], axis=-1).astype(jnp.bfloat16)
    qkv_grad = contract_rows(normed_one_low, projected_grad)
    normed_one_grad = contract_cols(projected_grad, weight_qkv)
    h_zero_part, gain_one_grad, shift_one_grad = norm_one_back(normed_one_grad)
    h_zero_low = (h_one_grad + h_zero_part).astype(jnp.bfloat16)
    expr_grad = jnp.dot(h_zero_low, embedding, preferred_element_type=jnp.float32)
    norm_grad = jnp.stack([gain_one_grad, shift_one_grad, gain_two_grad, shift_two_grad], axis=0).T
    centre_grad = centre_grad.T.T
    embed_slot = contract_rows(h_zero_low, expression_low)
    decode_slot = contract_rows(latent_low, out_grad)
    block_parts = (
        lax.psum_scatter(
            embed_slot.astype(jnp.bfloat16), "blk", scatter_dimension=0, tiled=True
        ).astype(jnp.float32),
        lax.psum_scatter(
            qkv_grad.astype(jnp.bfloat16), "blk", scatter_dimension=0, tiled=True
        ).astype(jnp.float32),
        lax.psum_scatter(
            attn_out_grad.astype(jnp.bfloat16), "blk", scatter_dimension=0, tiled=True
        ).astype(jnp.float32),
        lax.psum_scatter(
            up_grad.astype(jnp.bfloat16), "blk", scatter_dimension=0, tiled=True
        ).astype(jnp.float32),
        lax.psum_scatter(
            up_bias_grad.astype(jnp.bfloat16), "blk", scatter_dimension=0, tiled=True
        ).astype(jnp.float32),
        lax.psum_scatter(
            down_grad.astype(jnp.bfloat16), "blk", scatter_dimension=0, tiled=True
        ).astype(jnp.float32),
        lax.psum_scatter(
            latent_weight_grad.astype(jnp.bfloat16), "blk", scatter_dimension=0, tiled=True
        ).astype(jnp.float32),
        lax.psum_scatter(
            decode_slot.astype(jnp.bfloat16), "blk", scatter_dimension=0, tiled=True
        ).astype(jnp.float32),
        lax.psum_scatter(
            centre_grad.astype(jnp.bfloat16), "blk", scatter_dimension=0, tiled=True
        ).astype(jnp.float32),
        lax.psum_scatter(
            norm_grad.astype(jnp.bfloat16), "blk", scatter_dimension=0, tiled=True
        ).astype(jnp.float32),
    )
    summed = (
        lax.psum(block_parts[0].astype(jnp.bfloat16), "slide").astype(jnp.float32),
        lax.psum(block_parts[1].astype(jnp.bfloat16), "slide").astype(jnp.float32),
        lax.psum(block_parts[2].astype(jnp.bfloat16), "slide").astype(jnp.float32),
        lax.psum(block_parts[3].astype(jnp.bfloat16), "slide").astype(jnp.float32),
        lax.psum(block_parts[4].astype(jnp.bfloat16), "slide").astype(jnp.float32),
        lax.psum(block_parts[5].astype(jnp.bfloat16), "slide").astype(jnp.float32),
        lax.psum(block_parts[6].astype(jnp.bfloat16), "slide").astype(jnp.float32),
        lax.psum(block_parts[7].astype(jnp.bfloat16), "slide").astype(jnp.float32),
        lax.psum(block_parts[8].astype(jnp.bfloat16), "slide").astype(jnp.float32),
        lax.psum(block_parts[9].astype(jnp.bfloat16), "slide").astype(jnp.float32),
    )
    embed_out = summed[0]
    decode_out = summed[7]
    return (
        decoded[None],
        prior[None],
        expr_grad[None],
        embed_out,
        summed[1],
        summed[2],
        summed[3],
        summed[4],
        summed[5],
        summed[6],
        decode_out,
        summed[8],
        summed[9],
    )


def peers(offset, count):
    return [(place, place ^ offset) for place in range(count)]


def swap(pieces):
    count = len(pieces)
    return [pieces[0]] + [
        lax.ppermute(pieces[k], "slide", peers(k, count)) for k in range(1, count)
    ]


def share(rows, count):
    return swap([rows] * count)


def after(value, *earlier):
    return lax.optimization_barrier((value,) + earlier)[0]


def in_order(pieces, me, axis):
    stacked = jnp.stack(pieces)
    return jnp.concatenate(
        [
            lax.dynamic_index_in_dim(stacked, jnp.bitwise_xor(me, k), 0, keepdims=False)
            for k in range(len(pieces))
        ],
        axis=axis,
    )


def lowered(partials):
    return [partials[0]] + [piece.astype(jnp.bfloat16) for piece in partials[1:]]


def collect(partials):
    arrived = swap(partials)
    total = arrived[0]
    for piece in arrived[1:]:
        total = total + piece.astype(jnp.float32)
    return total


def gather_blk(piece, axis=0):
    return lax.all_gather(piece, "blk", axis=axis, tiled=True)


def scatter_blk(piece, axis=0):
    return lax.psum_scatter(piece, "blk", scatter_dimension=axis, tiled=True)


def split_rows(rows, count):
    height = rows.shape[0] // count
    return [rows[k * height : (k + 1) * height] for k in range(count)]


ROWS = 432
TALL = 1728
WIDE = 3456
CHUNKS = 2
SMALL = 16
COST = pl.CostEstimate(flops=0, bytes_accessed=0, transcendentals=0)


def expression_kernel(count, quarter, genes, me_ref, library_ref, counts_ref, *rest):
    outs, buffers, sems = rest[:count], rest[count], rest[count + 1]
    me = me_ref[0]
    tail = genes - (count - 1) * quarter
    library = library_ref[...].astype(jnp.float32)

    def copy(k, rows):
        start = pl.multiple_of(jnp.bitwise_xor(me, k) * quarter, 8)
        return pltpu.make_async_copy(
            counts_ref.at[pl.ds(start, rows), 0, :],
            buffers.at[k, pl.ds(0, rows), :],
            sems.at[k],
        )

    def each(k, act):
        last = jnp.bitwise_xor(me, k) == count - 1

        @pl.when(last)
        def _():
            act(copy(k, tail))

        @pl.when(jnp.logical_not(last))
        def _():
            act(copy(k, quarter))

    order = list(range(1, count)) + [0]
    for k in order:
        each(k, lambda one: one.start())
    for k in order:
        each(k, lambda one: one.wait())
        have = genes - jnp.bitwise_xor(me, k) * quarter

        @pl.loop(0, quarter // ROWS)
        def _(step):
            start = pl.multiple_of(step * ROWS, ROWS)
            values = buffers[k, pl.ds(start, ROWS), :].astype(jnp.float32)
            values = jnp.log1p(values * 10000.0 / library)
            row = start + lax.broadcasted_iota(jnp.int32, values.shape, 0)
            outs[k][pl.ds(start, ROWS), :] = jnp.where(row < have, values, 0.0).astype(jnp.bfloat16)


def expression_parts(counts, library, me, count, quarter):
    genes = counts.shape[2]
    cells = counts.shape[1]
    part = jax.ShapeDtypeStruct((quarter, cells), jnp.bfloat16)
    return pl.pallas_call(
        functools.partial(expression_kernel, count, quarter, genes),
        out_shape=[part] * count,
        in_specs=[
            pl.BlockSpec(memory_space=pltpu.SMEM),
            pl.BlockSpec(memory_space=pltpu.VMEM),
            pl.BlockSpec(memory_space=pltpu.HBM),
        ],
        out_specs=[pl.BlockSpec(memory_space=pltpu.VMEM)] * count,
        scratch_shapes=[
            pltpu.VMEM((count, quarter, cells), jnp.int32),
            pltpu.SemaphoreType.DMA((count,)),
        ],
        compiler_params=pltpu.CompilerParams(vmem_limit_bytes=40 * 2**20),
        cost_estimate=COST,
        name="expression",
    )(me.reshape(1), library, jnp.transpose(counts, (2, 0, 1)))


def spread_kernel(count, quarter, genes, me_ref, *rest):
    pieces, out, held, wide, sems_in, sems_out = rest[:count], *rest[count:]
    me = me_ref[0]
    tail = genes - (count - 1) * quarter

    def arrive(k):
        return pltpu.make_async_copy(pieces[k], held.at[k], sems_in.at[k])

    def leave(k):
        rows = tail if k == count - 1 else quarter
        return pltpu.make_async_copy(
            wide.at[k, pl.ds(0, rows), :], out.at[pl.ds(k * quarter, rows), 0, :], sems_out.at[k]
        )

    for k in range(count):
        arrive(k).start()
    for k in range(count):
        arrive(k).wait()
    for k in range(count):
        source = jnp.bitwise_xor(me, k)

        @pl.loop(0, quarter // ROWS)
        def _(step):
            rows = pl.ds(pl.multiple_of(step * ROWS, ROWS), ROWS)
            wide[k, rows, :] = held[source, rows, :].astype(jnp.float32)

        leave(k).start()
    for k in range(count):
        leave(k).wait()


def spread_parts(pieces, me, genes):
    count = len(pieces)
    quarter, cells = pieces[0].shape
    out = pl.pallas_call(
        functools.partial(spread_kernel, count, quarter, genes),
        out_shape=jax.ShapeDtypeStruct((genes, 1, cells), jnp.float32),
        in_specs=[pl.BlockSpec(memory_space=pltpu.SMEM)]
        + [pl.BlockSpec(memory_space=pl.ANY)] * count,
        out_specs=pl.BlockSpec(memory_space=pltpu.HBM),
        scratch_shapes=[
            pltpu.VMEM((count, quarter, cells), jnp.bfloat16),
            pltpu.VMEM((count, quarter, cells), jnp.float32),
            pltpu.SemaphoreType.DMA((count,)),
            pltpu.SemaphoreType.DMA((count,)),
        ],
        compiler_params=pltpu.CompilerParams(vmem_limit_bytes=40 * 2**20),
        cost_estimate=COST,
        name="spread",
    )(me.reshape(1), *pieces)
    return jnp.transpose(out, (1, 2, 0))


def join_kernel(count, me_ref, *rest):
    pieces, out, held, sems = rest[:count], *rest[count:]
    slot = pl.program_id(0)

    def arrive(k):
        rows = pl.ds(0, held.shape[1])
        return pltpu.make_async_copy(pieces[k].at[rows, :], held.at[k], sems.at[k])

    @pl.when(slot == 0)
    def _():
        for k in range(count):
            arrive(k).start()
        for k in range(count):
            arrive(k).wait()

    source = jnp.bitwise_xor(me_ref[0], slot)

    @pl.loop(0, out.shape[0] // ROWS)
    def _(step):
        rows = pl.ds(pl.multiple_of(step * ROWS, ROWS), ROWS)
        out[rows, :] = held[source, rows, :].astype(out.dtype)


def join_parts(pieces, me, quarter, genes, dtype):
    count = len(pieces)
    cells = pieces[0].shape[1]
    return pl.pallas_call(
        functools.partial(join_kernel, count),
        grid=(count,),
        out_shape=jax.ShapeDtypeStruct((genes, cells), dtype),
        in_specs=[pl.BlockSpec(memory_space=pltpu.SMEM)]
        + [pl.BlockSpec(memory_space=pl.ANY)] * count,
        out_specs=pl.BlockSpec((quarter, cells), lambda slot: (slot, 0)),
        scratch_shapes=[
            pltpu.VMEM((count, quarter, cells), jnp.bfloat16),
            pltpu.SemaphoreType.DMA((count,)),
        ],
        compiler_params=pltpu.CompilerParams(vmem_limit_bytes=40 * 2**20),
        cost_estimate=COST,
        name="join",
    )(me.reshape(1), *pieces)


def turn_kernel(count, *refs):
    out = refs[-1]
    for k in range(count):
        height = refs[k].shape[1]
        out[k * height : (k + 1) * height, :] = jnp.transpose(refs[k][...])


def turn_parts(parts):
    count = len(parts)
    quarter, cells = parts[0].shape
    return pl.pallas_call(
        functools.partial(turn_kernel, count),
        grid=(quarter // WIDE,),
        out_shape=jax.ShapeDtypeStruct((count * cells, quarter), jnp.bfloat16),
        in_specs=[pl.BlockSpec((WIDE, cells), lambda step: (step, 0))] * count,
        out_specs=pl.BlockSpec((count * cells, WIDE), lambda step: (0, step)),
        compiler_params=pltpu.CompilerParams(vmem_limit_bytes=40 * 2**20),
        cost_estimate=COST,
        name="turn_parts",
    )(*parts)


def finish_kernel(count, quarter, mean_cols, folds, me_ref, *refs):
    pieces = refs[:count]
    out, norm, means, bias, held, sems = refs[count:]
    slot = pl.program_id(0)

    def arrive(k):
        place = jnp.bitwise_xor(me_ref[0], k)
        return pltpu.make_async_copy(pieces[k], held.at[place], sems.at[k])

    @pl.when(slot == 0)
    def _():
        for k in range(count):
            arrive(k).start()
        for k in range(count):
            arrive(k).wait()
        small = [held[q, quarter:, :].astype(jnp.float32) for q in range(count)]
        total = sum(small[1:], small[0])
        norm[...] = total[:4, :]
        width = means.shape[1]
        for k in range(folds):
            means[k * mean_cols : (k + 1) * mean_cols, :] = total[
                4 : 4 + mean_cols, k * width : (k + 1) * width
            ]
        bias[...] = jnp.concatenate(
            [one[4 + mean_cols : 5 + mean_cols, :] for one in small], axis=0
        )

    out[...] = held[slot, :quarter, :].astype(out.dtype)


def finish(pieces, me, quarter, genes, mean_cols, folds):
    count = len(pieces)
    height, cells = pieces[0].shape
    return pl.pallas_call(
        functools.partial(finish_kernel, count, quarter, mean_cols, folds),
        grid=(count,),
        out_shape=[
            jax.ShapeDtypeStruct((genes, cells), jnp.float32),
            jax.ShapeDtypeStruct((4, cells), jnp.float32),
            jax.ShapeDtypeStruct((folds * mean_cols, cells // folds), jnp.float32),
            jax.ShapeDtypeStruct((count, cells), jnp.float32),
        ],
        in_specs=[pl.BlockSpec(memory_space=pltpu.SMEM)]
        + [pl.BlockSpec(memory_space=pl.ANY)] * count,
        out_specs=[
            pl.BlockSpec((quarter, cells), lambda slot: (slot, 0)),
            pl.BlockSpec((4, cells), lambda slot: (0, 0)),
            pl.BlockSpec((folds * mean_cols, cells // folds), lambda slot: (0, 0)),
            pl.BlockSpec((count, cells), lambda slot: (0, 0)),
        ],
        scratch_shapes=[
            pltpu.VMEM((count, height, cells), jnp.bfloat16),
            pltpu.SemaphoreType.DMA((count,)),
        ],
        compiler_params=pltpu.CompilerParams(vmem_limit_bytes=40 * 2**20),
        cost_estimate=COST,
        name="finish",
    )(me.reshape(1), *pieces)


def scores_kernel(rows, table, *refs):
    outs, total = refs[:-1], refs[-1]
    step = pl.program_id(0)
    product = jnp.dot(rows[...], table[...], preferred_element_type=jnp.float32)

    @pl.when(step == 0)
    def _():
        total[...] = product

    @pl.when(step > 0)
    def _():
        total[...] += product

    @pl.when(step == pl.num_programs(0) - 1)
    def _():
        height = outs[0].shape[0]
        for k in range(len(outs)):
            outs[k][...] = total[k * height : (k + 1) * height, :].astype(outs[k].dtype)


def embed_cells(rows, table, count):
    height, quarter = rows.shape
    width = table.shape[1]
    return pl.pallas_call(
        scores_kernel,
        grid=(quarter // WIDE,),
        out_shape=[
            jax.ShapeDtypeStruct((height // count, width), jnp.float32 if k == 0 else jnp.bfloat16)
            for k in range(count)
        ],
        in_specs=[
            pl.BlockSpec((height, WIDE), lambda step: (0, step)),
            pl.BlockSpec((WIDE, width), lambda step: (step, 0)),
        ],
        out_specs=[pl.BlockSpec((height // count, width), lambda step: (0, 0))] * count,
        scratch_shapes=[pltpu.VMEM((height, width), jnp.float32)],
        compiler_params=pltpu.CompilerParams(vmem_limit_bytes=58 * 2**20),
        cost_estimate=COST,
        name="embed_cells",
    )(rows, table)


def latents_kernel(count, table, *refs):
    cots, outs, total = refs[:count], refs[count:-1], refs[-1]
    step = pl.program_id(0)
    product = jnp.dot(
        table[...],
        jnp.concatenate([one[...] for one in cots], axis=1),
        preferred_element_type=jnp.float32,
    )

    @pl.when(step == 0)
    def _():
        total[...] = product

    @pl.when(step > 0)
    def _():
        total[...] += product

    @pl.when(step == pl.num_programs(0) - 1)
    def _():
        cells = outs[0].shape[0]
        for k in range(count):
            outs[k][...] = jnp.transpose(total[:, k * cells : (k + 1) * cells]).astype(
                outs[k].dtype
            )


def cots_to_latents(cots, table):
    count = len(cots)
    width, quarter = table.shape
    cells = cots[0].shape[1]
    return pl.pallas_call(
        functools.partial(latents_kernel, count),
        grid=(quarter // WIDE,),
        out_shape=[
            jax.ShapeDtypeStruct((cells, width), jnp.float32 if k == 0 else jnp.bfloat16)
            for k in range(count)
        ],
        in_specs=[pl.BlockSpec((width, WIDE), lambda step: (0, step))]
        + [pl.BlockSpec((WIDE, cells), lambda step: (step, 0))] * count,
        out_specs=[pl.BlockSpec((cells, width), lambda step: (0, 0))] * count,
        scratch_shapes=[pltpu.VMEM((width, count * cells), jnp.float32)],
        compiler_params=pltpu.CompilerParams(vmem_limit_bytes=40 * 2**20),
        cost_estimate=COST,
        name="cots_to_latents",
    )(table, *cots)


def gelu_slope(rows):
    scale = math.sqrt(2.0 / math.pi)
    squares = rows * rows
    bent = jnp.tanh(scale * (rows + 0.044715 * (squares * rows)))
    inner = scale * (1.0 + (3.0 * 0.044715) * squares)
    return 0.5 * (1.0 + bent) + 0.5 * rows * (1.0 - bent * bent) * inner


def feed_back_kernel(count, latent, down, up, pre, *refs):
    parts = refs[:count]
    own, down_input, pre_grad, bias, *outs = refs[count:]
    cells = own.shape[0]
    width = own.shape[1]
    h_grad = jnp.dot(
        jnp.concatenate([part[:, : latent.shape[0]] for part in parts], axis=0),
        latent[...],
        preferred_element_type=jnp.float32,
    )
    own[...] = h_grad[:cells, :]
    down_input[...] = h_grad.astype(jnp.bfloat16)
    step = 256
    for start in range(0, pre.shape[1], step):
        columns = slice(start, start + step)
        hidden_grad = lax.dot_general(
            down_input[...],
            down[columns, :],
            (((1,), (1,)), ((), ())),
            preferred_element_type=jnp.float32,
        )
        low = (hidden_grad * gelu_slope(pre[:, columns])).astype(jnp.bfloat16)
        pre_grad[:, columns] = low
        bias[:, columns] = jnp.sum(low.astype(jnp.float32), axis=0, keepdims=True)
    product = lax.dot_general(
        pre_grad[...], up[...], (((1,), (1,)), ((), ())), preferred_element_type=jnp.float32
    )
    for k in range(count):
        outs[k][...] = product[k * cells : (k + 1) * cells, :].astype(outs[k].dtype)


def feed_back(parts, latent, down, up, pre):
    count = len(parts)
    cells = parts[0].shape[0]
    width = latent.shape[1]
    units = pre.shape[1]

    def whole(array):
        return pl.BlockSpec(array.shape, lambda step: (0,) * len(array.shape))

    shapes = [
        jax.ShapeDtypeStruct((cells, width), jnp.float32),
        jax.ShapeDtypeStruct((count * cells, width), jnp.bfloat16),
        jax.ShapeDtypeStruct((count * cells, units), jnp.bfloat16),
        jax.ShapeDtypeStruct((1, units), jnp.float32),
    ] + [
        jax.ShapeDtypeStruct((cells, width), jnp.float32 if k == 0 else jnp.bfloat16)
        for k in range(count)
    ]
    operands = [latent, down, up, pre, *parts]
    return pl.pallas_call(
        functools.partial(feed_back_kernel, count),
        grid=(1,),
        out_shape=shapes,
        in_specs=[whole(one) for one in operands],
        out_specs=[whole(one) for one in shapes],
        compiler_params=pltpu.CompilerParams(vmem_limit_bytes=56 * 2**20),
        cost_estimate=COST,
        name="feed_back",
    )(*operands)


def decode_kernel(count, table, *refs):
    rows, outs = refs[:count], refs[count:]
    cells = rows[0].shape[0]
    product = jnp.dot(
        jnp.concatenate([one[...] for one in rows], axis=0),
        table[...],
        preferred_element_type=jnp.float32,
    ).astype(jnp.bfloat16)
    for k in range(count):
        outs[k][...] = jnp.transpose(product[k * cells : (k + 1) * cells, :])


def decode_genes(latents, table):
    count = len(latents)
    cells, width = latents[0].shape
    quarter = table.shape[1]
    return pl.pallas_call(
        functools.partial(decode_kernel, count),
        grid=(1,),
        out_shape=[jax.ShapeDtypeStruct((quarter, cells), jnp.bfloat16)] * count,
        in_specs=[pl.BlockSpec((width, quarter), lambda step: (0, 0))]
        + [pl.BlockSpec((cells, width), lambda step: (0, 0))] * count,
        out_specs=[pl.BlockSpec((quarter, cells), lambda step: (0, 0))] * count,
        compiler_params=pltpu.CompilerParams(vmem_limit_bytes=40 * 2**20),
        cost_estimate=COST,
        name="decode_genes",
    )(table, *latents)


def last_kernel(count, first, me_ref, normed, projected, both, *refs):
    pre_grads, cots, out = refs[:count], refs[count : 2 * count], refs[-1]
    cells = cots[0].shape[0]

    width = normed.shape[1]

    def by_offset(first):
        return jnp.concatenate(
            [
                both[
                    pl.ds(pl.multiple_of(jnp.bitwise_xor(me_ref[0], k) * cells, cells), cells),
                    first : first + width,
                ]
                for k in range(count)
            ],
            axis=0,
        )

    spot = 0
    for rows, columns in (
        (normed[...], [projected[k] for k in range(projected.shape[0])]),
        (by_offset(0), [jnp.concatenate([one[:, first:] for one in cots], axis=0)]),
        (by_offset(width), [jnp.concatenate([one[...] for one in pre_grads], axis=0)]),
    ):
        turned = jnp.transpose(rows)
        for one in columns:
            size = one.shape[1]
            out[:, spot : spot + size] = jnp.dot(
                turned, one, preferred_element_type=jnp.float32
            ).astype(out.dtype)
            spot += size


def last_products(normed, projected, pre_grads, both, cots, first, me):
    count = len(cots)
    height = normed.shape[1]
    width = projected.shape[0] * projected.shape[2] + 2 * pre_grads[0].shape[1]
    return pl.pallas_call(
        functools.partial(last_kernel, count, first),
        out_shape=jax.ShapeDtypeStruct((height, width), jnp.bfloat16),
        in_specs=[pl.BlockSpec(memory_space=pltpu.SMEM)]
        + [pl.BlockSpec(memory_space=pltpu.VMEM)] * (3 + 2 * count),
        out_specs=pl.BlockSpec(memory_space=pltpu.VMEM),
        compiler_params=pltpu.CompilerParams(vmem_limit_bytes=40 * 2**20),
        cost_estimate=COST,
        name="last_products",
    )(me.reshape(1), normed, projected, both, *pre_grads, *cots)


def pair_kernel(count, *refs):
    parts, out = refs[:count], refs[-1]
    width = out.shape[2]
    for j in range(out.shape[0] // count):
        for k in range(count):
            out[j * count + k] = parts[k][:, j * width : (j + 1) * width]


def pair_up(parts, pairs):
    count = len(parts)
    cells, width = parts[0].shape
    return pl.pallas_call(
        functools.partial(pair_kernel, count),
        out_shape=jax.ShapeDtypeStruct((pairs * count, cells, width // pairs), parts[0].dtype),
        in_specs=[pl.BlockSpec(memory_space=pltpu.VMEM)] * count,
        out_specs=pl.BlockSpec(memory_space=pltpu.VMEM),
        cost_estimate=COST,
        name="pair_up",
    )(*parts)


def assemble_kernel(count, sizes, me_ref, *refs):
    parts, decoder = refs[:count], refs[count : 2 * count]
    down, up, qkv, attn, latent, decode, held, halves, sems = refs[2 * count :]
    blocks, pairs, pair, quarter, half = sizes

    def arrive(k):
        place = jnp.bitwise_xor(me_ref[0], k)
        return (
            pltpu.make_async_copy(parts[k], held.at[place], sems.at[0, k]),
            pltpu.make_async_copy(decoder[k], halves.at[place], sems.at[1, k]),
        )

    for k in range(count):
        for one in arrive(k):
            one.start()
    for k in range(count):
        for one in arrive(k):
            one.wait()
    rows, width = attn.shape
    part = width // count
    ff = up.shape[1] // (count * blocks)
    latents, genes = decode.shape

    def piece(q, spot, size):
        return held[q, :, spot : spot + size].astype(jnp.float32)

    for q in range(count):
        down[q * rows : (q + 1) * rows, :] = piece(q, 0, width)
        spot = width
        for b in range(blocks):
            up[:, (b * count + q) * ff : (b * count + q + 1) * ff] = piece(q, spot, ff)
            spot += ff
        for j in range(pairs):
            for t in range(3):
                first = t * width + q * part + j * pair
                qkv[:, first : first + pair] = piece(q, spot, pair)
                spot += pair
        for out in (attn, latent):
            out[:, q * part : (q + 1) * part] = piece(q, spot, part)
            spot += part
        for side in range(2):
            first = q * quarter + side * half
            size = min(half, quarter - side * half, genes - first)
            if size > 0:
                decode[:, first : first + size] = halves[
                    q, side * latents : (side + 1) * latents, :size
                ].astype(jnp.float32)


def assemble(parts, decoder, me, genes, quarter, half, latents, blocks, pairs, pair):
    count = len(parts)
    rows = parts[0].shape[0]
    width = blocks * rows
    shapes = [
        (count * rows, width),
        (rows, count * width),
        (rows, 3 * width),
        (rows, width),
        (rows, width),
        (latents, genes),
    ]
    return pl.pallas_call(
        functools.partial(assemble_kernel, count, (blocks, pairs, pair, quarter, half)),
        out_shape=[jax.ShapeDtypeStruct(shape, jnp.float32) for shape in shapes],
        in_specs=[pl.BlockSpec(memory_space=pltpu.SMEM)]
        + [pl.BlockSpec(memory_space=pl.ANY)] * (2 * count),
        out_specs=[pl.BlockSpec(memory_space=pltpu.VMEM)] * len(shapes),
        scratch_shapes=[
            pltpu.VMEM((count,) + parts[0].shape, jnp.bfloat16),
            pltpu.VMEM((count,) + decoder[0].shape, jnp.bfloat16),
            pltpu.SemaphoreType.DMA((2, count)),
        ],
        compiler_params=pltpu.CompilerParams(vmem_limit_bytes=48 * 2**20),
        cost_estimate=COST,
        name="assemble",
    )(me.reshape(1), *parts, *decoder)


def genes_kernel(count, table, *refs):
    rows, outs, stacked = refs[:count], refs[count : 2 * count], refs[-1]
    cells = rows[0].shape[0]

    @pl.when(pl.program_id(0) == 0)
    def _():
        for k in range(count):
            stacked[:, k * cells : (k + 1) * cells] = jnp.transpose(rows[k][...])

    product = jnp.dot(table[...], stacked[...], preferred_element_type=jnp.float32)
    for k in range(count):
        outs[k][...] = product[:, k * cells : (k + 1) * cells].astype(outs[k].dtype)


def cells_to_genes(table, rows, quarter):
    count = len(rows)
    cells, width = rows[0].shape
    return pl.pallas_call(
        functools.partial(genes_kernel, count),
        grid=(quarter // TALL,),
        out_shape=[jax.ShapeDtypeStruct((quarter, cells), jnp.bfloat16)] * count,
        in_specs=[pl.BlockSpec((TALL, width), lambda step: (step, 0))]
        + [pl.BlockSpec((cells, width), lambda step: (0, 0))] * count,
        out_specs=[pl.BlockSpec((TALL, cells), lambda step: (step, 0))] * count,
        scratch_shapes=[pltpu.VMEM((width, count * cells), jnp.bfloat16)],
        compiler_params=pltpu.CompilerParams(vmem_limit_bytes=58 * 2**20),
        cost_estimate=COST,
        name="cells_to_genes",
    )(table, *rows)


def embed_kernel(count, *refs):
    parts, rows = refs[:count], refs[count : 2 * count]
    small, out, stacked, results, sems = refs[2 * count :]
    steps = parts[0].shape[0] // ROWS
    height = rows[0].shape[0]
    blocks, _, block = out.shape
    for k in range(count):
        stacked[k * height : (k + 1) * height, :] = rows[k][...]

    def leave(slot, step):
        start = pl.multiple_of(step * ROWS, ROWS)
        return pltpu.make_async_copy(
            results.at[slot], out.at[:, pl.ds(start, ROWS), :], sems.at[slot]
        )

    last = pltpu.make_async_copy(
        small, out.at[:, pl.ds(steps * ROWS, small.shape[1]), :], sems.at[2]
    )
    last.start()

    @pl.loop(0, steps)
    def _(step):
        slot = lax.rem(step, 2)

        @pl.when(step >= 2)
        def _():
            leave(slot, step - 2).wait()

        here = pl.ds(pl.multiple_of(step * ROWS, ROWS), ROWS)
        product = jnp.dot(
            jnp.concatenate([part[here, :] for part in parts], axis=1),
            stacked[...],
            preferred_element_type=jnp.float32,
        ).astype(results.dtype)
        for k in range(blocks):
            results[slot, k] = product[:, k * block : (k + 1) * block]
        leave(slot, step).start()

    for step in range(max(steps - 2, 0), steps):
        leave(step % 2, step).wait()
    last.wait()


def embed_products(parts, rows, small):
    count = len(parts)
    quarter, cells = parts[0].shape
    width = rows[0].shape[1]
    blocks, extra, block = small.shape
    return pl.pallas_call(
        functools.partial(embed_kernel, count),
        out_shape=jax.ShapeDtypeStruct((blocks, quarter + extra, block), jnp.bfloat16),
        in_specs=[pl.BlockSpec(memory_space=pltpu.VMEM)] * (2 * count + 1),
        out_specs=pl.BlockSpec(memory_space=pltpu.HBM),
        scratch_shapes=[
            pltpu.VMEM((count * cells, width), jnp.bfloat16),
            pltpu.VMEM((2, blocks, ROWS, block), jnp.bfloat16),
            pltpu.SemaphoreType.DMA((3,)),
        ],
        compiler_params=pltpu.CompilerParams(vmem_limit_bytes=58 * 2**20),
        cost_estimate=COST,
        name="embed_products",
    )(*parts, *rows, small)


def products_kernel(count, *refs):
    out = refs[-1]
    spot = 0
    for k in range(count):
        rows = jnp.transpose(refs[2 * k][...])
        columns = refs[2 * k + 1]
        width = columns.shape[1]
        for start in range(0, width, 256):
            out[:, spot + start : spot + start + 256] = jnp.dot(
                rows, columns[:, start : start + 256], preferred_element_type=jnp.float32
            ).astype(out.dtype)
        spot += width


def row_products(pairs):
    operands = [one for pair in pairs for one in pair]
    height = pairs[0][0].shape[1]
    width = sum(b.shape[1] for _, b in pairs)
    return pl.pallas_call(
        functools.partial(products_kernel, len(pairs)),
        out_shape=jax.ShapeDtypeStruct((height, width), jnp.bfloat16),
        in_specs=[pl.BlockSpec(memory_space=pltpu.VMEM)] * len(operands),
        out_specs=pl.BlockSpec(memory_space=pltpu.VMEM),
        compiler_params=pltpu.CompilerParams(vmem_limit_bytes=48 * 2**20),
        cost_estimate=COST,
        name="row_products",
    )(*operands)


def decoder_kernel(count, *refs):
    rows, cots, out, turned = refs[:count], refs[count : 2 * count], refs[-2], refs[-1]
    cells = rows[0].shape[0]

    @pl.when(pl.program_id(0) == 0)
    def _():
        for k in range(count):
            turned[:, k * cells : (k + 1) * cells] = jnp.transpose(rows[k][...])

    out[...] = lax.dot_general(
        turned[...],
        jnp.concatenate([one[...] for one in cots], axis=1),
        (((1,), (1,)), ((), ())),
        preferred_element_type=jnp.float32,
    ).astype(out.dtype)


def decoder_products(latents, cots):
    count = len(latents)
    cells, width = latents[0].shape
    quarter = cots[0].shape[0]
    step_rows = math.gcd(quarter, 1152)
    return pl.pallas_call(
        functools.partial(decoder_kernel, count),
        grid=(quarter // step_rows,),
        out_shape=jax.ShapeDtypeStruct((width, quarter), jnp.bfloat16),
        in_specs=[pl.BlockSpec((cells, width), lambda step: (0, 0))] * count
        + [pl.BlockSpec((step_rows, cells), lambda step: (step, 0))] * count,
        out_specs=pl.BlockSpec((width, step_rows), lambda step: (0, step)),
        scratch_shapes=[pltpu.VMEM((width, count * cells), jnp.bfloat16)],
        compiler_params=pltpu.CompilerParams(vmem_limit_bytes=40 * 2**20),
        cost_estimate=COST,
        name="decoder_products",
    )(*latents, *cots)


def head_probs(keys, queries, scaling):
    scores = (
        lax.dot_general(keys, queries, (((1,), (1,)), ((), ())), preferred_element_type=jnp.float32)
        * scaling
    )
    scores = jnp.exp(scores - jnp.max(scores, axis=0, keepdims=True))
    return scores * (1.0 / jnp.sum(scores, axis=0, keepdims=True))


def attend_kernel(heads, width, rows_ref, out, turned):
    step = pl.program_id(0)
    height = out.shape[0]
    group = heads * width

    @pl.when(step == 0)
    def _():
        turned[...] = jnp.transpose(rows_ref[:, 2 * group : 3 * group])

    block = rows_ref[pl.ds(pl.multiple_of(step * height, height), height), :group]
    results = []
    for h in range(heads):
        probs = head_probs(
            rows_ref[:, group + h * width : group + (h + 1) * width],
            block[:, h * width : (h + 1) * width],
            width ** (-0.5),
        ).astype(jnp.bfloat16)
        results.append(
            jnp.dot(turned[h * width : (h + 1) * width, :], probs, preferred_element_type=jnp.float32)
        )
    out[...] = jnp.transpose(jnp.concatenate(results, axis=0)).astype(out.dtype)


def attend(rows, heads):
    cells, total = rows.shape
    group = total // 3
    height = math.gcd(cells, 256)
    return pl.pallas_call(
        functools.partial(attend_kernel, heads, group // heads),
        grid=(cells // height,),
        out_shape=jax.ShapeDtypeStruct((cells, group), jnp.bfloat16),
        in_specs=[pl.BlockSpec((cells, total), lambda step: (0, 0))],
        out_specs=pl.BlockSpec((height, group), lambda step: (step, 0)),
        scratch_shapes=[pltpu.VMEM((group, cells), jnp.bfloat16)],
        compiler_params=pltpu.CompilerParams(vmem_limit_bytes=40 * 2**20),
        cost_estimate=COST,
        name="attend",
    )(rows)


def attend_back_kernel(heads, width, rows_ref, cot_ref, out, turned, key_sum, value_sum):
    step = pl.program_id(0)
    group = heads * width
    height = rows_ref.shape[0] // pl.num_programs(0)
    scaling = width ** (-0.5)

    @pl.when(step == 0)
    def _():
        turned[...] = jnp.transpose(rows_ref[:, group : 2 * group])
        key_sum[...] = jnp.zeros_like(key_sum)
        value_sum[...] = jnp.zeros_like(value_sum)

    here = pl.ds(pl.multiple_of(step * height, height), height)
    block = rows_ref[here, :group]
    cots = cot_ref[here, :]
    results = []
    for h in range(heads):
        columns = slice(h * width, (h + 1) * width)
        queries = block[:, columns]
        cot = cots[:, columns]
        probs = head_probs(
            rows_ref[:, group + h * width : group + (h + 1) * width], queries, scaling
        )
        prob_grad = lax.dot_general(
            rows_ref[:, 2 * group + h * width : 2 * group + (h + 1) * width],
            cot,
            (((1,), (1,)), ((), ())),
            preferred_element_type=jnp.float32,
        )
        delta = jnp.sum(probs * prob_grad, axis=0, keepdims=True)
        score_grad = (probs * (prob_grad - delta)).astype(jnp.bfloat16)
        results.append(
            jnp.dot(turned[columns, :], score_grad, preferred_element_type=jnp.float32) * scaling
        )
        key_sum[:, columns] += jnp.dot(score_grad, queries, preferred_element_type=jnp.float32)
        value_sum[:, columns] += jnp.dot(
            probs.astype(jnp.bfloat16), cot, preferred_element_type=jnp.float32
        )
    out[here, :group] = jnp.transpose(jnp.concatenate(results, axis=0)).astype(out.dtype)

    @pl.when(step == pl.num_programs(0) - 1)
    def _():
        out[:, group : 2 * group] = (key_sum[...] * scaling).astype(out.dtype)
        out[:, 2 * group :] = value_sum[...].astype(out.dtype)


def attend_back(rows, cot, heads):
    cells, total = rows.shape
    group = total // 3
    height = math.gcd(cells, 256)
    return pl.pallas_call(
        functools.partial(attend_back_kernel, heads, group // heads),
        grid=(cells // height,),
        out_shape=jax.ShapeDtypeStruct((cells, total), jnp.bfloat16),
        in_specs=[
            pl.BlockSpec((cells, total), lambda step: (0, 0)),
            pl.BlockSpec((cells, group), lambda step: (0, 0)),
        ],
        out_specs=pl.BlockSpec((cells, total), lambda step: (0, 0)),
        scratch_shapes=[
            pltpu.VMEM((group, cells), jnp.bfloat16),
            pltpu.VMEM((cells, group), jnp.float32),
            pltpu.VMEM((cells, group), jnp.float32),
        ],
        compiler_params=pltpu.CompilerParams(vmem_limit_bytes=40 * 2**20),
        cost_estimate=COST,
        name="attend_back",
    )(rows, cot)


def split_model(
    counts,
    library,
    coords,
    noise,
    decoded_cot,
    prior_cot,
    embed_t,
    w_qkv,
    w_attn_out,
    w_up,
    up_bias,
    w_down,
    w_latent,
    w_decode,
    comp_means,
    norm_params,
):
    slides = lax.axis_size("slide")
    blocks = lax.axis_size("blk")
    me = lax.axis_index("slide")
    genes = embed_t.shape[1]
    cells = counts.shape[1]
    model_width = w_attn_out.shape[1]
    own_rows = w_qkv.shape[0]
    latent_width = w_decode.shape[0] * blocks
    mixture_count = comp_means.shape[1]
    quarter = -(-genes // (slides * ROWS)) * ROWS
    padded = quarter * slides
    head_part = model_width // slides
    pair = model_width // blocks
    pairs = head_part // pair
    ff_part = up_bias.shape[0] // slides
    latent_part = model_width // slides

    def place_of(k):
        return jnp.bitwise_xor(me, k)

    def column_part(rows, width, place):
        return lax.dynamic_slice_in_dim(rows, place * width, width, 1)

    def whole(piece, axis):
        return in_order(share(piece, slides), me, axis)

    def wide(piece):
        return piece.astype(jnp.float32)

    embed_part = lax.dynamic_slice_in_dim(
        jnp.pad(embed_t.T, ((0, padded - genes), (0, 0))), me * quarter, quarter, 0
    )
    bias_part = lax.dynamic_slice_in_dim(up_bias, me * ff_part, ff_part, 0)
    mean_cols = comp_means.size // own_rows
    folds = mixture_count // mean_cols
    own_latents = w_decode.shape[0]
    small = jnp.concatenate(
        [
            norm_params.T,
            jnp.concatenate(
                [comp_means.T[k * mean_cols : (k + 1) * mean_cols] for k in range(folds)], axis=1
            ),
            bias_part.reshape(-1, own_rows),
        ],
        axis=0,
    )
    small_rows = small.shape[0]
    small = jnp.pad(small, ((0, SMALL - small_rows), (0, 0)))
    qkv_width = pairs * 3 * pair
    qkv_part = [
        lax.dynamic_slice_in_dim(w_qkv, k * model_width + me * head_part, head_part, 1)
        for k in range(3)
    ]
    qkv_part = jnp.concatenate(
        [part[:, j * pair : (j + 1) * pair] for j in range(pairs) for part in qkv_part], axis=1
    ).T
    out_latent = jnp.concatenate(
        [
            lax.dynamic_slice_in_dim(weight, me * head_part, head_part, 1)
            for weight in (w_attn_out, w_latent)
        ],
        axis=1,
    ).T
    embedding = gather_blk(
        jnp.concatenate([embed_part, small, qkv_part, out_latent], axis=0), 1
    )
    small_all = embedding[quarter : quarter + SMALL]
    qkv_end = quarter + SMALL + qkv_width
    weight_qkv = embedding[quarter + SMALL : qkv_end].reshape(pairs, 3 * pair, model_width)
    out_latent = embedding[qkv_end:]
    norm_float = small_all[:4].astype(jnp.float32)
    centres = small_all[4 : 4 + mean_cols].reshape(mean_cols, blocks, folds, own_latents)
    centres = jnp.transpose(centres, (1, 3, 2, 0)).reshape(latent_width, mixture_count)
    bias_up = small_all[4 + mean_cols].astype(jnp.float32)
    expr_parts = swap(expression_parts(counts, library, me, slides, quarter))

    cot_all = jnp.pad(decoded_cot[0].T, ((0, padded - genes), (0, 0)))
    cot_first = [
        lax.dynamic_slice_in_dim(cot_all, place_of(k) * quarter, quarter, 0)
        for k in range(slides)
    ]
    cot_parts = swap([after(piece, *expr_parts[1:]) for piece in cot_first])
    up_part = jnp.concatenate(
        [
            lax.dynamic_slice_in_dim(w_up, (k * slides + me) * ff_part, ff_part, 1)
            for k in range(blocks)
        ],
        axis=1,
    )
    down_part = lax.dynamic_slice_in_dim(w_down, me * ff_part, ff_part, 0)
    expr_rows = turn_parts(expr_parts)
    half = -(-quarter // 256) * 128
    decode_part = lax.dynamic_slice_in_dim(
        jnp.pad(w_decode, ((0, 0), (0, padded - genes))), me * quarter, quarter, 1
    )
    decode_part = jnp.concatenate(
        [decode_part[:, :half], jnp.pad(decode_part[:, half:], ((0, 0), (0, 2 * half - quarter)))],
        axis=0,
    )
    middle = gather_blk(
        after(
            jnp.concatenate([up_part, decode_part], axis=1),
            embedding,
            expr_rows,
            *cot_parts[1:],
        )
    )
    weight_up, halves = jnp.split(middle, [model_width], axis=1)
    halves = halves.reshape(blocks, 2, own_latents, half)
    weight_decode = jnp.concatenate(
        [
            halves[:, 0].reshape(latent_width, half),
            halves[:, 1].reshape(latent_width, half)[:, : quarter - half],
        ],
        axis=1,
    )

    h_zero = collect(embed_cells(expr_rows, embedding, slides))
    h_zero = h_zero + spatial_code(coords[0], model_width)
    normed_one, norm_one_back = jax.vjp(layer_norm, h_zero, norm_float[0], norm_float[1])
    normed_one_all = jnp.concatenate(share(normed_one.astype(jnp.bfloat16), slides), axis=0)
    projected = jnp.einsum(
        "ck,pfk->pcf", normed_one_all, weight_qkv, preferred_element_type=jnp.float32
    ).astype(jnp.bfloat16)

    def to_heads(rows):
        return lax.all_to_all(
            rows.reshape(blocks, cells, rows.shape[-1]), "blk", 0, 0, tiled=True
        ).reshape(blocks * cells, rows.shape[-1])

    out_shares = share(after(out_latent[:head_part], normed_one_all), slides)
    head_rows = after(to_heads(projected), *out_shares[1:])
    per_pair = pair // HEAD_DIM
    weight_down = gather_blk(after(down_part, middle, head_rows))
    latent_shares = share(after(out_latent[head_part:], head_rows), slides)
    weight_out = in_order(out_shares, me, 0)
    weight_latent = in_order(latent_shares, me, 0)
    own_heads = to_heads(attend(head_rows, per_pair)).reshape(pairs, slides, cells, pair)
    latent_cots = cots_to_latents(cot_parts, weight_decode)
    own_heads = after(own_heads, latent_cots[-1], *latent_shares[1:])
    attended_parts = swap(
        [
            jnp.concatenate([own_heads[j, k] for j in range(pairs)], axis=1)
            for k in range(slides)
        ]
    )
    attended_low = in_order(attended_parts, me, 1)
    h_one = h_zero + contract_cols(attended_low, weight_out)
    normed_two, norm_two_back = jax.vjp(layer_norm, h_one, norm_float[2], norm_float[3])
    normed_two_low = normed_two.astype(jnp.bfloat16)
    normed_two_all = jnp.concatenate(share(normed_two_low, slides), axis=0)
    hidden_pre = (
        jnp.dot(normed_two_all, weight_up, preferred_element_type=jnp.float32) + bias_up
    )
    hidden_low = jax.nn.gelu(hidden_pre).astype(jnp.bfloat16)
    h_two_sum = collect(
        lowered(
            split_rows(
                jnp.dot(hidden_low, weight_down, preferred_element_type=jnp.float32), slides
            )
        )
    )
    latent_from_decode = collect(latent_cots)
    h_two = h_one + after(h_two_sum, latent_from_decode)
    h_two_low = h_two.astype(jnp.bfloat16)
    both_rows = lax.all_gather(
        jnp.concatenate([attended_low, h_two_low], axis=1), "slide", axis=0, tiled=True
    )
    latent_pre = contract_cols(h_two_low, weight_latent)
    spread = jnp.exp(0.5 * latent_pre[:, latent_width:])
    latent = latent_pre[:, :latent_width] + spread * noise[0]
    prior, prior_back = jax.vjp(mixture_term, latent, centres.astype(jnp.float32))

    latent_from_prior, centre_grad = prior_back(prior_cot[0])
    latent_total = latent_from_decode + latent_from_prior
    pre_grad = jnp.concatenate(
        [latent_total, latent_total * noise[0] * spread * 0.5], axis=-1
    ).astype(jnp.bfloat16)
    both_parts = share(
        jnp.concatenate([pre_grad, latent.astype(jnp.bfloat16)], axis=1), slides
    )
    h_two_grad, down_input, pre_hidden_grad, up_bias_grad, *normed_two_parts = feed_back(
        both_parts, weight_latent, weight_down, weight_up, hidden_pre
    )
    normed_two_grad = collect(normed_two_parts)
    latent_parts = [part[:, model_width:] for part in both_parts]
    latent_parts = [after(part, normed_two_parts[-1]) for part in latent_parts]
    decode_local = decoder_products(latent_parts, cot_parts)
    decoded_rows = decode_genes(latent_parts, weight_decode)
    normed_two_grad = after(normed_two_grad, decode_local, decoded_rows[-1])
    decode_own = scatter_blk(after(decode_local, both_rows))
    h_one_part, gain_two_grad, shift_two_grad = norm_two_back(normed_two_grad)
    h_one_grad = h_two_grad + h_one_part
    out_input = h_one_grad.astype(jnp.bfloat16)
    attended_grad = jnp.dot(out_input, weight_out, preferred_element_type=jnp.float32).astype(jnp.bfloat16)
    grad_parts = swap([column_part(attended_grad, head_part, place_of(k)) for k in range(slides)])
    out_heads = to_heads(pair_up(grad_parts, pairs))

    middle_local = row_products(
        [
            (hidden_low, after(down_input, *grad_parts[1:])),
            (normed_two_all, pre_hidden_grad),
        ]
    )
    out_heads = after(out_heads, middle_local)
    decoded_parts = swap(
        [after(one, *grad_parts[1:]) for one in decoded_rows[:-1]]
        + [after(decoded_rows[-1], out_heads)]
    )
    out_heads = after(out_heads, *decoded_parts[1:-1])
    head_grads = attend_back(head_rows, out_heads, per_pair)
    middle_grad = scatter_blk(after(middle_local, decode_own, head_grads))
    decode_half = jnp.concatenate(
        [decode_own[:, :half], jnp.pad(decode_own[:, half:], ((0, 0), (0, 2 * half - quarter)))],
        axis=0,
    )
    more_parts = swap(
        [
            after(
                jnp.concatenate(
                    [decode_half, column_part(out_input, head_part, place_of(k))], axis=1
                ),
                head_grads,
            )
            for k in range(slides)
        ]
    )
    projected_grad = to_heads(head_grads).reshape(pairs, slides * cells, 3 * pair)
    projected_grad = after(projected_grad, decoded_parts[-1], *more_parts[1:])
    normed_one_parts = lowered(
        split_rows(
            jnp.einsum(
                "pcf,pfk->ck", projected_grad, weight_qkv, preferred_element_type=jnp.float32
            ),
            slides,
        )
    )
    normed_one_grad = collect(normed_one_parts)
    last_local = last_products(
        normed_one_all,
        after(projected_grad, normed_one_parts[-1]),
        [column_part(part, latent_part, me) for part in both_parts],
        both_rows,
        more_parts,
        half,
        me,
    )
    normed_one_grad = after(normed_one_grad, last_local)
    last_grad = scatter_blk(after(last_local, middle_grad))
    h_zero_part, gain_one_grad, shift_one_grad = norm_one_back(normed_one_grad)
    h_zero_low = (h_one_grad + h_zero_part).astype(jnp.bfloat16)
    h_zero_parts = share(h_zero_low, slides)

    small_grad = jnp.concatenate(
        [
            jnp.stack([gain_one_grad, shift_one_grad, gain_two_grad, shift_two_grad], axis=0),
            jnp.transpose(
                centre_grad.reshape(blocks, own_latents, folds, mean_cols), (3, 0, 2, 1)
            ).reshape(mean_cols, model_width),
            up_bias_grad,
        ],
        axis=0,
    )
    small_grad = jnp.pad(small_grad, ((0, SMALL - small_rows), (0, 0))).astype(jnp.bfloat16)
    small_grad = jnp.transpose(small_grad.reshape(SMALL, blocks, own_rows), (1, 0, 2))
    embed_local = embed_products(expr_parts, h_zero_parts, small_grad)
    gene_rows = cells_to_genes(
        embedding, [after(part, embed_local) for part in h_zero_parts], quarter
    )
    embed_own = scatter_blk(after(embed_local, last_grad))[0]
    gene_parts = swap(gene_rows)
    grad_shares = share(
        after(jnp.concatenate([middle_grad, last_grad], axis=1), embed_local), slides
    )
    embed_shares = share(after(embed_own, *gene_parts[1:], *grad_shares[1:]), slides)
    expr_grad = spread_parts(gene_parts, me, genes)
    decoded = join_parts(decoded_parts, me, quarter, genes, jnp.bfloat16).T
    down_grad, up_grad, qkv_grad, attn_out_grad, latent_grad, decode_grad = assemble(
        grad_shares, more_parts, me, genes, quarter, half, own_latents, blocks, pairs, pair
    )
    embed_grad, norm_grad, means_grad, up_bias_grad = finish(
        embed_shares, me, quarter, genes, mean_cols, folds
    )

    return (
        decoded[None],
        prior[None],
        expr_grad,
        embed_grad.T,
        qkv_grad,
        attn_out_grad,
        up_grad,
        up_bias_grad.reshape(-1),
        down_grad,
        latent_grad,
        decode_grad,
        means_grad.T,
        norm_grad.T,
    )


def fits(mesh):
    slides, blocks = mesh.shape["slide"], mesh.shape["blk"]
    return slides & (slides - 1) == 0 and HEADS % slides == 0 and HEADS % blocks == 0


def solution(mesh):
    placed = (
        P("slide", "blk", None),
        P("slide", "blk"),
        P("slide", "blk", None),
        P("slide", "blk", None),
        P("slide", "blk", None),
        P("slide", "blk"),
        P("blk", None),
        P("blk", None),
        P("blk", None),
        P("blk", None),
        P("blk"),
        P("blk", None),
        P("blk", None),
        P("blk", None),
        P("blk", None),
        P("blk", None),
    )
    return jax.shard_map(
        split_model if fits(mesh) else local,
        mesh=mesh,
        in_specs=placed,
        out_specs=(
            P("slide", "blk", None),
            P("slide", "blk"),
            P("slide", "blk", None),
            P("blk", None),
            P("blk", None),
            P("blk", None),
            P("blk", None),
            P("blk"),
            P("blk", None),
            P("blk", None),
            P("blk", None),
            P("blk", None),
            P("blk", None),
        ),
        check_vma=False,
    )
```

```python
import functools
import math

import jax
import jax.numpy as jnp
from jax import lax
from jax.experimental import pallas as pl
from jax.experimental.pallas import tpu as pltpu
from jax.sharding import PartitionSpec as P

HEADS = 16
HEAD_DIM = 64


eps_norm = 1e-05


def contract_rows(former, latter):
    return lax.dot_general(
        former, latter, (((0,), (0,)), ((), ())), preferred_element_type=jnp.float32
    )


def contract_cols(former, latter):
    return lax.dot_general(
        former, latter, (((1,), (1,)), ((), ())), preferred_element_type=jnp.float32
    )


def layer_norm(tensor, norm_gain, norm_shift):
    center = tensor - jnp.mean(tensor, axis=-1, keepdims=True)
    inverse = lax.rsqrt(jnp.mean(center * center, axis=-1, keepdims=True) + eps_norm)
    return center * inverse * norm_gain + norm_shift


def spatial_code(coords, model_width):
    quarter = model_width // 4
    frequency = jnp.exp(-math.log(10000.0) * jnp.arange(quarter, dtype=jnp.float32) / quarter)
    first_axis = coords[..., 0:1].astype(jnp.float32) * frequency
    second_axis = coords[..., 1:2].astype(jnp.float32) * frequency
    return jnp.concatenate(
        [jnp.sin(first_axis), jnp.cos(first_axis), jnp.sin(second_axis), jnp.cos(second_axis)],
        axis=-1,
    )


def mixture_term(latent, centres):
    scores = (
        jnp.dot(
            latent, centres, precision=lax.Precision.HIGHEST, preferred_element_type=jnp.float32
        )
        - 0.5 * jnp.sum(centres * centres, axis=0)
    ) * latent.shape[-1] ** (-0.5)
    return -jax.nn.logsumexp(scores, axis=-1)


def split_single(rows_in, head_count):
    arrived_rows = rows_in.shape[0]
    block_rows = 512
    return rows_in.reshape(
        (arrived_rows // block_rows, block_rows, head_count, rows_in.shape[1] // head_count)
    )


def split_blocks(key_rows, value_rows, head_count):
    return (split_single(key_rows, head_count), split_single(value_rows, head_count))


def local(
    counts,
    library,
    coords,
    noise,
    decoded_cot,
    prior_cot,
    embed_t,
    w_qkv,
    w_attn_out,
    w_up,
    up_bias,
    w_down,
    w_latent,
    w_decode,
    comp_means,
    norm_params,
):
    gathered = (
        lax.all_gather(embed_t, "blk", axis=0, tiled=True),
        lax.all_gather(w_qkv, "blk", axis=0, tiled=True),
        lax.all_gather(w_attn_out, "blk", axis=0, tiled=True),
        lax.all_gather(w_up, "blk", axis=0, tiled=True),
        lax.all_gather(up_bias, "blk", axis=0, tiled=True),
        lax.all_gather(w_down, "blk", axis=0, tiled=True),
        lax.all_gather(w_latent, "blk", axis=0, tiled=True),
        lax.all_gather(w_decode, "blk", axis=0, tiled=True),
        lax.all_gather(comp_means, "blk", axis=0, tiled=True),
        lax.all_gather(norm_params, "blk", axis=0, tiled=True),
    )
    (
        embedding,
        weight_qkv,
        weight_out,
        weight_up,
        bias_up,
        weight_down,
        weight_latent,
        weight_decode,
        centres,
        norm_table,
    ) = gathered
    head_count = HEADS
    head_width = HEAD_DIM
    scaling = head_width ** (-0.5)
    model_width = embedding.shape[0]
    latent_width = weight_decode.shape[0]
    blk_count = lax.axis_size("blk")
    expression = jnp.log1p(
        counts[0].astype(jnp.float32) * 10000.0 / library[0].astype(jnp.float32)[:, None]
    )
    expression_low = expression.astype(jnp.bfloat16)
    local_cells = expression.shape[0]
    norm_float = norm_table.astype(jnp.float32)
    h_zero = contract_cols(expression_low, embedding) + spatial_code(coords[0], model_width)
    normed_one, norm_one_back = jax.vjp(layer_norm, h_zero, norm_float[:, 0], norm_float[:, 1])
    normed_one_low = normed_one.astype(jnp.bfloat16)
    projected = jnp.dot(normed_one_low, weight_qkv, preferred_element_type=jnp.float32).astype(
        jnp.bfloat16
    )
    queries = projected[:, :model_width].reshape(local_cells, head_count, head_width)
    key_rows = projected[:, model_width : 2 * model_width]
    value_rows = projected[:, 2 * model_width :]
    stat_start = (
        jnp.full((head_count, local_cells), -1e30, jnp.float32),
        jnp.zeros((head_count, local_cells), jnp.float32),
    )
    key_blocks = split_single(lax.all_gather(key_rows, "blk", axis=0, tiled=True), head_count)

    def per_block(status, key_block):
        running_max, running_sum = status
        scores = (
            jnp.einsum("thd,khd->htk", queries, key_block, preferred_element_type=jnp.float32)
            * scaling
        )
        new_max = jnp.maximum(running_max, jnp.max(scores, axis=-1))
        running_sum = running_sum * jnp.exp(running_max - new_max) + jnp.sum(
            jnp.exp(scores - new_max[..., None]), axis=-1
        )
        return ((new_max, running_sum), None)

    result, unused = lax.scan(per_block, stat_start, key_blocks)
    running_max, running_sum = result
    log_total = running_max + jnp.log(running_sum)
    arrived = (
        lax.all_gather(key_rows, "blk", axis=0, tiled=True),
        lax.all_gather(value_rows, "blk", axis=0, tiled=True),
    )
    key_blocks, value_blocks = split_blocks(arrived[0], arrived[1], head_count)

    def per_block(weighted, block_pair):
        scores = (
            jnp.einsum("thd,khd->htk", queries, block_pair[0], preferred_element_type=jnp.float32)
            * scaling
        )
        probs_low = jnp.exp(scores - log_total[..., None]).astype(jnp.bfloat16)
        weighted = weighted + jnp.einsum(
            "htk,khd->htd", probs_low, block_pair[1], preferred_element_type=jnp.float32
        )
        return (weighted, None)

    result, unused = lax.scan(
        per_block,
        jnp.zeros((head_count, local_cells, head_width), jnp.float32),
        (key_blocks, value_blocks),
    )
    attended_cells = jnp.transpose(result, (1, 0, 2))
    attended_low = attended_cells.reshape(local_cells, model_width).astype(jnp.bfloat16)
    h_one = h_zero + jnp.dot(attended_low, weight_out, preferred_element_type=jnp.float32)
    normed_two, norm_two_back = jax.vjp(layer_norm, h_one, norm_float[:, 2], norm_float[:, 3])
    normed_two_low = normed_two.astype(jnp.bfloat16)
    hidden_pre = jnp.dot(
        normed_two_low, weight_up, preferred_element_type=jnp.float32
    ) + bias_up.astype(jnp.float32)
    hidden_act, gelu_back = jax.vjp(jax.nn.gelu, hidden_pre)
    hidden_low = hidden_act.astype(jnp.bfloat16)
    h_two = h_one + jnp.dot(hidden_low, weight_down, preferred_element_type=jnp.float32)
    h_two_low = h_two.astype(jnp.bfloat16)
    latent_pre = jnp.dot(h_two_low, weight_latent, preferred_element_type=jnp.float32)
    spread = jnp.exp(0.5 * latent_pre[:, latent_width:])
    latent = latent_pre[:, :latent_width] + spread * noise[0]
    latent_low = latent.astype(jnp.bfloat16)
    decoded = jnp.dot(latent_low, weight_decode, preferred_element_type=jnp.float32).astype(
        jnp.bfloat16
    )
    prior, prior_back = jax.vjp(mixture_term, latent, centres.astype(jnp.float32))
    out_grad = decoded_cot[0]
    latent_from_decode = contract_cols(out_grad, weight_decode)
    latent_from_prior, centre_grad = prior_back(prior_cot[0])
    latent_total = latent_from_decode + latent_from_prior
    pre_grad = jnp.concatenate(
        [latent_total, latent_total * noise[0] * spread * 0.5], axis=-1
    ).astype(jnp.bfloat16)
    latent_weight_grad = contract_rows(h_two_low, pre_grad)
    h_two_grad = contract_cols(pre_grad, weight_latent)
    down_input = h_two_grad.astype(jnp.bfloat16)
    down_grad = contract_rows(hidden_low, down_input)
    hidden_grad = contract_cols(down_input, weight_down)
    pre_hidden_grad = gelu_back(hidden_grad)[0].astype(jnp.bfloat16)
    up_bias_grad = jnp.sum(pre_hidden_grad.astype(jnp.float32), axis=0)
    up_grad = contract_rows(normed_two_low, pre_hidden_grad)
    normed_two_grad = contract_cols(pre_hidden_grad, weight_up)
    h_one_part, gain_two_grad, shift_two_grad = norm_two_back(normed_two_grad)
    h_one_grad = h_two_grad + h_one_part
    out_input = h_one_grad.astype(jnp.bfloat16)
    attn_out_grad = contract_rows(attended_low, out_input)
    attended_grad = contract_cols(out_input, weight_out).astype(jnp.bfloat16)
    out_heads = attended_grad.reshape(local_cells, head_count, head_width)
    row_delta = jnp.sum(out_heads.astype(jnp.float32) * attended_cells, axis=-1).T
    query_zero = jnp.zeros((head_count, local_cells, head_width), jnp.float32)
    start_back = (query_zero, jnp.zeros((local_cells * blk_count, 2 * model_width), jnp.float32))
    arrived = (
        lax.all_gather(key_rows, "blk", axis=0, tiled=True),
        lax.all_gather(value_rows, "blk", axis=0, tiled=True),
    )
    key_blocks, value_blocks = split_blocks(arrived[0], arrived[1], head_count)
    arrived_rows = arrived[0].shape[0]

    def per_block(query_sum, block_pair):
        scores = (
            jnp.einsum("thd,khd->htk", queries, block_pair[0], preferred_element_type=jnp.float32)
            * scaling
        )
        probs = jnp.exp(scores - log_total[..., None])
        prob_grad = jnp.einsum(
            "thd,khd->htk", out_heads, block_pair[1], preferred_element_type=jnp.float32
        )
        score_grad = (probs * (prob_grad - row_delta[..., None])).astype(jnp.bfloat16)
        query_sum = query_sum + jnp.einsum(
            "htk,khd->htd", score_grad, block_pair[0], preferred_element_type=jnp.float32
        )
        key_part = (
            jnp.einsum("htk,thd->khd", score_grad, queries, preferred_element_type=jnp.float32)
            * scaling
        )
        value_part = jnp.einsum(
            "htk,thd->khd",
            probs.astype(jnp.bfloat16),
            out_heads,
            preferred_element_type=jnp.float32,
        )
        block_rows = key_part.shape[0]
        return (
            query_sum,
            jnp.concatenate(
                [key_part.reshape(block_rows, -1), value_part.reshape(block_rows, -1)], axis=-1
            ),
        )

    query_total, stacked = lax.scan(per_block, start_back[0], (key_blocks, value_blocks))
    stacked = stacked.reshape(arrived_rows, stacked.shape[-1])
    carried_back = (query_total, stacked)
    query_total = carried_back[0]
    own_pairs = lax.psum_scatter(
        carried_back[1].astype(jnp.bfloat16), "blk", scatter_dimension=0, tiled=True
    ).astype(jnp.float32)
    query_rows = jnp.transpose(query_total * scaling, (1, 0, 2)).reshape(local_cells, model_width)
    projected_grad = jnp.concatenate([query_rows, own_pairs], axis=-1).astype(jnp.bfloat16)
    qkv_grad = contract_rows(normed_one_low, projected_grad)
    normed_one_grad = contract_cols(projected_grad, weight_qkv)
    h_zero_part, gain_one_grad, shift_one_grad = norm_one_back(normed_one_grad)
    h_zero_low = (h_one_grad + h_zero_part).astype(jnp.bfloat16)
    expr_grad = jnp.dot(h_zero_low, embedding, preferred_element_type=jnp.float32)
    norm_grad = jnp.stack([gain_one_grad, shift_one_grad, gain_two_grad, shift_two_grad], axis=0).T
    centre_grad = centre_grad.T.T
    embed_slot = contract_rows(h_zero_low, expression_low)
    decode_slot = contract_rows(latent_low, out_grad)
    block_parts = (
        lax.psum_scatter(
            embed_slot.astype(jnp.bfloat16), "blk", scatter_dimension=0, tiled=True
        ).astype(jnp.float32),
        lax.psum_scatter(
            qkv_grad.astype(jnp.bfloat16), "blk", scatter_dimension=0, tiled=True
        ).astype(jnp.float32),
        lax.psum_scatter(
            attn_out_grad.astype(jnp.bfloat16), "blk", scatter_dimension=0, tiled=True
        ).astype(jnp.float32),
        lax.psum_scatter(
            up_grad.astype(jnp.bfloat16), "blk", scatter_dimension=0, tiled=True
        ).astype(jnp.float32),
        lax.psum_scatter(
            up_bias_grad.astype(jnp.bfloat16), "blk", scatter_dimension=0, tiled=True
        ).astype(jnp.float32),
        lax.psum_scatter(
            down_grad.astype(jnp.bfloat16), "blk", scatter_dimension=0, tiled=True
        ).astype(jnp.float32),
        lax.psum_scatter(
            latent_weight_grad.astype(jnp.bfloat16), "blk", scatter_dimension=0, tiled=True
        ).astype(jnp.float32),
        lax.psum_scatter(
            decode_slot.astype(jnp.bfloat16), "blk", scatter_dimension=0, tiled=True
        ).astype(jnp.float32),
        lax.psum_scatter(
            centre_grad.astype(jnp.bfloat16), "blk", scatter_dimension=0, tiled=True
        ).astype(jnp.float32),
        lax.psum_scatter(
            norm_grad.astype(jnp.bfloat16), "blk", scatter_dimension=0, tiled=True
        ).astype(jnp.float32),
    )
    summed = (
        lax.psum(block_parts[0].astype(jnp.bfloat16), "slide").astype(jnp.float32),
        lax.psum(block_parts[1].astype(jnp.bfloat16), "slide").astype(jnp.float32),
        lax.psum(block_parts[2].astype(jnp.bfloat16), "slide").astype(jnp.float32),
        lax.psum(block_parts[3].astype(jnp.bfloat16), "slide").astype(jnp.float32),
        lax.psum(block_parts[4].astype(jnp.bfloat16), "slide").astype(jnp.float32),
        lax.psum(block_parts[5].astype(jnp.bfloat16), "slide").astype(jnp.float32),
        lax.psum(block_parts[6].astype(jnp.bfloat16), "slide").astype(jnp.float32),
        lax.psum(block_parts[7].astype(jnp.bfloat16), "slide").astype(jnp.float32),
        lax.psum(block_parts[8].astype(jnp.bfloat16), "slide").astype(jnp.float32),
        lax.psum(block_parts[9].astype(jnp.bfloat16), "slide").astype(jnp.float32),
    )
    embed_out = summed[0]
    decode_out = summed[7]
    return (
        decoded[None],
        prior[None],
        expr_grad[None],
        embed_out,
        summed[1],
        summed[2],
        summed[3],
        summed[4],
        summed[5],
        summed[6],
        decode_out,
        summed[8],
        summed[9],
    )


def peers(offset, count):
    return [(place, place ^ offset) for place in range(count)]


def swap(pieces):
    count = len(pieces)
    return [pieces[0]] + [
        lax.ppermute(pieces[k], "slide", peers(k, count)) for k in range(1, count)
    ]


def share(rows, count):
    return swap([rows] * count)


def after(value, *earlier):
    return lax.optimization_barrier((value,) + earlier)[0]


def in_order(pieces, me, axis):
    stacked = jnp.stack(pieces)
    return jnp.concatenate(
        [
            lax.dynamic_index_in_dim(stacked, jnp.bitwise_xor(me, k), 0, keepdims=False)
            for k in range(len(pieces))
        ],
        axis=axis,
    )


def exact_dot(former, latter, left, right):
    return lax.dot_general(
        former,
        latter,
        (((left,), (right,)), ((), ())),
        precision=lax.Precision.HIGHEST,
        preferred_element_type=jnp.float32,
    )


def lowered(partials):
    return [partials[0]] + [piece.astype(jnp.bfloat16) for piece in partials[1:]]


def collect(partials):
    arrived = swap(partials)
    total = arrived[0]
    for piece in arrived[1:]:
        total = total + piece.astype(jnp.float32)
    return total


def gather_blk(piece, axis=0):
    return lax.all_gather(piece, "blk", axis=axis, tiled=True)


def scatter_blk(piece, axis=0):
    return lax.psum_scatter(piece, "blk", scatter_dimension=axis, tiled=True)


def to_core(rows):
    count = lax.axis_size("blk")
    return lax.ppermute(rows, "blk", [(place, place ^ 1) for place in range(count)])


def to_chip(rows, offset):
    count = lax.axis_size("blk")
    return lax.ppermute(rows, "blk", [(place, place ^ (2 * offset)) for place in range(count)])


def split_rows(rows, count):
    height = rows.shape[0] // count
    return [rows[k * height : (k + 1) * height] for k in range(count)]


ROWS = 432
STEP = 864
TALL = 1728
WIDE = 3456
CHUNKS = 2
SMALL = 16
COST = pl.CostEstimate(flops=0, bytes_accessed=0, transcendentals=0)


def expression_kernel(count, quarter, genes, me_ref, library_ref, counts_ref, *rest):
    outs, buffers, sems = rest[:count], rest[count], rest[count + 1]
    me = me_ref[0]
    tail = genes - (count - 1) * quarter
    library = library_ref[...].astype(jnp.float32)

    def copy(k, rows):
        start = pl.multiple_of(jnp.bitwise_xor(me, k) * quarter, 8)
        return pltpu.make_async_copy(
            counts_ref.at[pl.ds(start, rows), 0, :],
            buffers.at[k, pl.ds(0, rows), :],
            sems.at[k],
        )

    def each(k, act):
        last = jnp.bitwise_xor(me, k) == count - 1

        @pl.when(last)
        def _():
            act(copy(k, tail))

        @pl.when(jnp.logical_not(last))
        def _():
            act(copy(k, quarter))

    order = list(range(1, count)) + [0]
    for k in order:
        each(k, lambda one: one.start())
    for k in order:
        each(k, lambda one: one.wait())
        have = genes - jnp.bitwise_xor(me, k) * quarter

        @pl.loop(0, quarter // ROWS)
        def _(step):
            start = pl.multiple_of(step * ROWS, ROWS)
            values = buffers[k, pl.ds(start, ROWS), :].astype(jnp.float32)
            values = jnp.log1p(values * 10000.0 / library)
            row = start + lax.broadcasted_iota(jnp.int32, values.shape, 0)
            outs[k][pl.ds(start, ROWS), :] = jnp.where(row < have, values, 0.0).astype(jnp.bfloat16)


def expression_parts(counts, library, me, count, quarter):
    genes = counts.shape[2]
    cells = counts.shape[1]
    part = jax.ShapeDtypeStruct((quarter, cells), jnp.bfloat16)
    return pl.pallas_call(
        functools.partial(expression_kernel, count, quarter, genes),
        out_shape=[part] * count,
        in_specs=[
            pl.BlockSpec(memory_space=pltpu.SMEM),
            pl.BlockSpec(memory_space=pltpu.VMEM),
            pl.BlockSpec(memory_space=pltpu.HBM),
        ],
        out_specs=[pl.BlockSpec(memory_space=pltpu.VMEM)] * count,
        scratch_shapes=[
            pltpu.VMEM((count, quarter, cells), jnp.int32),
            pltpu.SemaphoreType.DMA((count,)),
        ],
        compiler_params=pltpu.CompilerParams(vmem_limit_bytes=40 * 2**20),
        cost_estimate=COST,
        name="expression",
    )(me.reshape(1), library, jnp.transpose(counts, (2, 0, 1)))


def spread_kernel(count, quarter, genes, me_ref, *rest):
    pieces, out, held, wide, sems_in, sems_out = rest[:count], *rest[count:]
    me = me_ref[0]
    tail = genes - (count - 1) * quarter

    def arrive(k):
        return pltpu.make_async_copy(pieces[k], held.at[k], sems_in.at[k])

    def leave(k):
        rows = tail if k == count - 1 else quarter
        return pltpu.make_async_copy(
            wide.at[k, pl.ds(0, rows), :], out.at[pl.ds(k * quarter, rows), 0, :], sems_out.at[k]
        )

    for k in range(count):
        arrive(k).start()
    for k in range(count):
        arrive(k).wait()
    for k in range(count):
        source = jnp.bitwise_xor(me, k)

        @pl.loop(0, quarter // ROWS)
        def _(step):
            rows = pl.ds(pl.multiple_of(step * ROWS, ROWS), ROWS)
            wide[k, rows, :] = held[source, rows, :].astype(jnp.float32)

        leave(k).start()
    for k in range(count):
        leave(k).wait()


def spread_parts(pieces, me, genes):
    count = len(pieces)
    quarter, cells = pieces[0].shape
    out = pl.pallas_call(
        functools.partial(spread_kernel, count, quarter, genes),
        out_shape=jax.ShapeDtypeStruct((genes, 1, cells), jnp.float32),
        in_specs=[pl.BlockSpec(memory_space=pltpu.SMEM)]
        + [pl.BlockSpec(memory_space=pl.ANY)] * count,
        out_specs=pl.BlockSpec(memory_space=pltpu.HBM),
        scratch_shapes=[
            pltpu.VMEM((count, quarter, cells), jnp.bfloat16),
            pltpu.VMEM((count, quarter, cells), jnp.float32),
            pltpu.SemaphoreType.DMA((count,)),
            pltpu.SemaphoreType.DMA((count,)),
        ],
        compiler_params=pltpu.CompilerParams(vmem_limit_bytes=40 * 2**20),
        cost_estimate=COST,
        name="spread",
    )(me.reshape(1), *pieces)
    return jnp.transpose(out, (1, 2, 0))


def join_kernel(count, me_ref, *rest):
    pieces, out, held, sems = rest[:count], *rest[count:]
    slot = pl.program_id(0)

    def arrive(k):
        rows = pl.ds(0, held.shape[1])
        return pltpu.make_async_copy(pieces[k].at[rows, :], held.at[k], sems.at[k])

    @pl.when(slot == 0)
    def _():
        for k in range(count):
            arrive(k).start()
        for k in range(count):
            arrive(k).wait()

    source = jnp.bitwise_xor(me_ref[0], slot)

    @pl.loop(0, out.shape[0] // ROWS)
    def _(step):
        rows = pl.ds(pl.multiple_of(step * ROWS, ROWS), ROWS)
        out[rows, :] = held[source, rows, :].astype(out.dtype)


def join_parts(pieces, me, quarter, genes, dtype):
    count = len(pieces)
    cells = pieces[0].shape[1]
    return pl.pallas_call(
        functools.partial(join_kernel, count),
        grid=(count,),
        out_shape=jax.ShapeDtypeStruct((genes, cells), dtype),
        in_specs=[pl.BlockSpec(memory_space=pltpu.SMEM)]
        + [pl.BlockSpec(memory_space=pl.ANY)] * count,
        out_specs=pl.BlockSpec((quarter, cells), lambda slot: (slot, 0)),
        scratch_shapes=[
            pltpu.VMEM((count, quarter, cells), jnp.bfloat16),
            pltpu.SemaphoreType.DMA((count,)),
        ],
        compiler_params=pltpu.CompilerParams(vmem_limit_bytes=40 * 2**20),
        cost_estimate=COST,
        name="join",
    )(me.reshape(1), *pieces)


def turn_kernel(count, *refs):
    out = refs[-1]
    for k in range(count):
        height = refs[k].shape[1]
        out[k * height : (k + 1) * height, :] = jnp.transpose(refs[k][...])


def turn_parts(parts):
    count = len(parts)
    quarter, cells = parts[0].shape
    return pl.pallas_call(
        functools.partial(turn_kernel, count),
        grid=(quarter // WIDE,),
        out_shape=jax.ShapeDtypeStruct((count * cells, quarter), jnp.bfloat16),
        in_specs=[pl.BlockSpec((WIDE, cells), lambda step: (step, 0))] * count,
        out_specs=pl.BlockSpec((count * cells, WIDE), lambda step: (0, step)),
        compiler_params=pltpu.CompilerParams(vmem_limit_bytes=40 * 2**20),
        cost_estimate=COST,
        name="turn_parts",
    )(*parts)


def finish_kernel(count, quarter, mean_cols, folds, me_ref, *refs):
    pieces = refs[:count]
    out, norm, means, bias, held, sems = refs[count:]
    slot = pl.program_id(0)

    def arrive(k):
        place = jnp.bitwise_xor(me_ref[0], k)
        return pltpu.make_async_copy(pieces[k], held.at[place], sems.at[k])

    @pl.when(slot == 0)
    def _():
        for k in range(count):
            arrive(k).start()
        for k in range(count):
            arrive(k).wait()
        small = [held[q, quarter:, :].astype(jnp.float32) for q in range(count)]
        total = sum(small[1:], small[0])
        norm[...] = total[:4, :]
        width = means.shape[1]
        for k in range(folds):
            means[k * mean_cols : (k + 1) * mean_cols, :] = total[
                4 : 4 + mean_cols, k * width : (k + 1) * width
            ]
        bias[...] = jnp.concatenate(
            [one[4 + mean_cols : 5 + mean_cols, :] for one in small], axis=0
        )

    out[...] = held[slot, :quarter, :].astype(out.dtype)


def finish(pieces, me, quarter, genes, mean_cols, folds):
    count = len(pieces)
    height, cells = pieces[0].shape
    return pl.pallas_call(
        functools.partial(finish_kernel, count, quarter, mean_cols, folds),
        grid=(count,),
        out_shape=[
            jax.ShapeDtypeStruct((genes, cells), jnp.float32),
            jax.ShapeDtypeStruct((4, cells), jnp.float32),
            jax.ShapeDtypeStruct((folds * mean_cols, cells // folds), jnp.float32),
            jax.ShapeDtypeStruct((count, cells), jnp.float32),
        ],
        in_specs=[pl.BlockSpec(memory_space=pltpu.SMEM)]
        + [pl.BlockSpec(memory_space=pl.ANY)] * count,
        out_specs=[
            pl.BlockSpec((quarter, cells), lambda slot: (slot, 0)),
            pl.BlockSpec((4, cells), lambda slot: (0, 0)),
            pl.BlockSpec((folds * mean_cols, cells // folds), lambda slot: (0, 0)),
            pl.BlockSpec((count, cells), lambda slot: (0, 0)),
        ],
        scratch_shapes=[
            pltpu.VMEM((count, height, cells), jnp.bfloat16),
            pltpu.SemaphoreType.DMA((count,)),
        ],
        compiler_params=pltpu.CompilerParams(vmem_limit_bytes=40 * 2**20),
        cost_estimate=COST,
        name="finish",
    )(me.reshape(1), *pieces)


def scores_kernel(rows, table, *outs):
    product = jnp.dot(rows[...], table[...], preferred_element_type=jnp.float32)
    height = outs[0].shape[0]
    for k in range(len(outs)):
        outs[k][...] = product[k * height : (k + 1) * height, :].astype(outs[k].dtype)


def embed_cells(rows, table, count):
    height, quarter = rows.shape
    width = table.shape[1]
    block = math.gcd(width, 512)
    return pl.pallas_call(
        scores_kernel,
        grid=(width // block,),
        out_shape=[
            jax.ShapeDtypeStruct((height // count, width), jnp.float32 if k == 0 else jnp.bfloat16)
            for k in range(count)
        ],
        in_specs=[
            pl.BlockSpec((height, quarter), lambda step: (0, 0)),
            pl.BlockSpec((quarter, block), lambda step: (0, step)),
        ],
        out_specs=[pl.BlockSpec((height // count, block), lambda step: (0, step))] * count,
        compiler_params=pltpu.CompilerParams(vmem_limit_bytes=58 * 2**20),
        cost_estimate=COST,
        name="embed_cells",
    )(rows, table)


def latents_kernel(count, table, *refs):
    cots, outs, total = refs[:count], refs[count:-1], refs[-1]
    step = pl.program_id(0)
    product = jnp.dot(
        table[...],
        jnp.concatenate([one[...] for one in cots], axis=1),
        preferred_element_type=jnp.float32,
    )

    @pl.when(step == 0)
    def _():
        total[...] = product

    @pl.when(step > 0)
    def _():
        total[...] += product

    @pl.when(step == pl.num_programs(0) - 1)
    def _():
        cells = outs[0].shape[0]
        for k in range(count):
            outs[k][...] = jnp.transpose(total[:, k * cells : (k + 1) * cells]).astype(
                outs[k].dtype
            )


def cots_to_latents(cots, table):
    count = len(cots)
    width, quarter = table.shape
    cells = cots[0].shape[1]
    return pl.pallas_call(
        functools.partial(latents_kernel, count),
        grid=(quarter // WIDE,),
        out_shape=[
            jax.ShapeDtypeStruct((cells, width), jnp.float32 if k == 0 else jnp.bfloat16)
            for k in range(count)
        ],
        in_specs=[pl.BlockSpec((width, WIDE), lambda step: (0, step))]
        + [pl.BlockSpec((WIDE, cells), lambda step: (step, 0))] * count,
        out_specs=[pl.BlockSpec((cells, width), lambda step: (0, 0))] * count,
        scratch_shapes=[pltpu.VMEM((width, count * cells), jnp.float32)],
        compiler_params=pltpu.CompilerParams(vmem_limit_bytes=40 * 2**20),
        cost_estimate=COST,
        name="cots_to_latents",
    )(table, *cots)


def gelu_slope(rows):
    scale = math.sqrt(2.0 / math.pi)
    squares = rows * rows
    bent = jnp.tanh(scale * (rows + 0.044715 * (squares * rows)))
    inner = scale * (1.0 + (3.0 * 0.044715) * squares)
    return 0.5 * (1.0 + bent) + 0.5 * rows * (1.0 - bent * bent) * inner


def feed_back_kernel(count, latent, down, up, pre, *refs):
    parts = refs[:count]
    own, down_input, pre_grad, bias, *outs = refs[count:]
    cells = own.shape[0]
    width = own.shape[1]
    h_grad = jnp.dot(
        jnp.concatenate([part[:, : latent.shape[0]] for part in parts], axis=0),
        latent[...],
        preferred_element_type=jnp.float32,
    )
    own[...] = h_grad[:cells, :]
    down_input[...] = h_grad.astype(jnp.bfloat16)
    step = 256
    for start in range(0, pre.shape[1], step):
        columns = slice(start, start + step)
        hidden_grad = lax.dot_general(
            down_input[...],
            down[columns, :],
            (((1,), (1,)), ((), ())),
            preferred_element_type=jnp.float32,
        )
        low = (hidden_grad * gelu_slope(pre[:, columns])).astype(jnp.bfloat16)
        pre_grad[:, columns] = low
        bias[:, columns] = jnp.sum(low.astype(jnp.float32), axis=0, keepdims=True)
    product = lax.dot_general(
        pre_grad[...], up[...], (((1,), (1,)), ((), ())), preferred_element_type=jnp.float32
    )
    for k in range(count):
        outs[k][...] = product[k * cells : (k + 1) * cells, :].astype(outs[k].dtype)


def feed_back(parts, latent, down, up, pre):
    count = len(parts)
    cells = parts[0].shape[0]
    width = latent.shape[1]
    units = pre.shape[1]

    def whole(array):
        return pl.BlockSpec(array.shape, lambda step: (0,) * len(array.shape))

    shapes = [
        jax.ShapeDtypeStruct((cells, width), jnp.float32),
        jax.ShapeDtypeStruct((count * cells, width), jnp.bfloat16),
        jax.ShapeDtypeStruct((count * cells, units), jnp.bfloat16),
        jax.ShapeDtypeStruct((1, units), jnp.float32),
    ] + [
        jax.ShapeDtypeStruct((cells, width), jnp.float32 if k == 0 else jnp.bfloat16)
        for k in range(count)
    ]
    operands = [latent, down, up, pre, *parts]
    return pl.pallas_call(
        functools.partial(feed_back_kernel, count),
        grid=(1,),
        out_shape=shapes,
        in_specs=[whole(one) for one in operands],
        out_specs=[whole(one) for one in shapes],
        compiler_params=pltpu.CompilerParams(vmem_limit_bytes=56 * 2**20),
        cost_estimate=COST,
        name="feed_back",
    )(*operands)


def decode_kernel(count, table, *refs):
    rows, outs = refs[:count], refs[count:]
    cells = rows[0].shape[0]
    product = jnp.dot(
        jnp.concatenate([one[...] for one in rows], axis=0),
        table[...],
        preferred_element_type=jnp.float32,
    ).astype(jnp.bfloat16)
    for k in range(count):
        outs[k][...] = jnp.transpose(product[k * cells : (k + 1) * cells, :])


def decode_genes(latents, table):
    count = len(latents)
    cells = latents[0].shape[0]
    width, quarter = table.shape
    last = latents[0].shape[1] // width - 1
    return pl.pallas_call(
        functools.partial(decode_kernel, count),
        grid=(1,),
        out_shape=[jax.ShapeDtypeStruct((quarter, cells), jnp.bfloat16)] * count,
        in_specs=[pl.BlockSpec((width, quarter), lambda step: (0, 0))]
        + [pl.BlockSpec((cells, width), lambda step: (0, last))] * count,
        out_specs=[pl.BlockSpec((quarter, cells), lambda step: (0, 0))] * count,
        compiler_params=pltpu.CompilerParams(vmem_limit_bytes=40 * 2**20),
        cost_estimate=COST,
        name="decode_genes",
    )(table, *latents)


def chip_offsets(chips):
    order = [0]
    bit = chips // 2
    while bit:
        order = order + [one + bit for one in order]
        bit //= 2
    return order


def last_kernel(count, first, offsets, places, normed, projected, both, *refs):
    pre_grads, cots = refs[:count], refs[count : 2 * count]
    kept, sent, turned = refs[2 * count :]
    me, place = places[0], places[1]
    cells = cots[0].shape[0]
    width = normed.shape[1]
    block = kept.shape[0] // len(offsets)

    def by_offset(first):
        return jnp.concatenate(
            [
                both[
                    pl.ds(pl.multiple_of(jnp.bitwise_xor(me, k) * cells, cells), cells),
                    first : first + width,
                ]
                for k in range(count)
            ],
            axis=0,
        )

    spot = 0
    for group, (rows, columns) in enumerate(
        (
            (normed[...], [projected[k] for k in range(projected.shape[0])]),
            (by_offset(0), [jnp.concatenate([one[:, first:] for one in cots], axis=0)]),
            (by_offset(width), [jnp.concatenate([one[...] for one in pre_grads], axis=0)]),
        )
    ):
        turned[group] = jnp.transpose(rows)
        for one in columns:
            size = one.shape[1]
            for out, core in ((kept, place % 2), (sent, 1 - place % 2)):
                owners = [jnp.bitwise_xor(place // 2, k) * 2 + core for k in offsets]
                ordered = jnp.concatenate(
                    [
                        turned[group, pl.ds(pl.multiple_of(owner * block, block), block), :]
                        for owner in owners
                    ],
                    axis=0,
                )
                out[:, spot : spot + size] = jnp.dot(
                    ordered, one, preferred_element_type=jnp.float32
                ).astype(out.dtype)
            spot += size


def last_products(normed, projected, pre_grads, both, cots, first, me, place):
    count = len(cots)
    height = normed.shape[1]
    offsets = chip_offsets(lax.axis_size("blk") // 2)
    width = projected.shape[0] * projected.shape[2] + 2 * pre_grads[0].shape[1]
    return pl.pallas_call(
        functools.partial(last_kernel, count, first, offsets),
        out_shape=[
            jax.ShapeDtypeStruct((height // 2, width), jnp.float32),
            jax.ShapeDtypeStruct((height // 2, width), jnp.bfloat16),
        ],
        in_specs=[pl.BlockSpec(memory_space=pltpu.SMEM)]
        + [pl.BlockSpec(memory_space=pltpu.VMEM)] * (3 + 2 * count),
        out_specs=[pl.BlockSpec(memory_space=pltpu.VMEM)] * 2,
        scratch_shapes=[pltpu.VMEM((3, height, normed.shape[0]), jnp.bfloat16)],
        compiler_params=pltpu.CompilerParams(vmem_limit_bytes=40 * 2**20),
        cost_estimate=COST,
        name="last_products",
    )(jnp.stack([me, place]), normed, projected, both, *pre_grads, *cots)


def half_kernel(kept, other, stay, go):
    height = stay.shape[0]
    stay[...] = kept[:height, :] + other[:height, :].astype(jnp.float32)
    go[...] = (kept[height:, :] + other[height:, :].astype(jnp.float32)).astype(go.dtype)


def merge_half(kept, other):
    height, width = kept.shape
    return pl.pallas_call(
        half_kernel,
        out_shape=[
            jax.ShapeDtypeStruct((height // 2, width), jnp.float32),
            jax.ShapeDtypeStruct((height // 2, width), jnp.bfloat16),
        ],
        in_specs=[pl.BlockSpec(memory_space=pltpu.VMEM)] * 2,
        out_specs=[pl.BlockSpec(memory_space=pltpu.VMEM)] * 2,
        compiler_params=pltpu.CompilerParams(vmem_limit_bytes=40 * 2**20),
        cost_estimate=COST,
        name="merge_half",
    )(kept, other)


def pair_kernel(count, *refs):
    parts, out = refs[:count], refs[-1]
    width = out.shape[2]
    for j in range(out.shape[0] // count):
        for k in range(count):
            out[j * count + k] = parts[k][:, j * width : (j + 1) * width]


def pair_up(parts, pairs):
    count = len(parts)
    cells, width = parts[0].shape
    return pl.pallas_call(
        functools.partial(pair_kernel, count),
        out_shape=jax.ShapeDtypeStruct((pairs * count, cells, width // pairs), parts[0].dtype),
        in_specs=[pl.BlockSpec(memory_space=pltpu.VMEM)] * count,
        out_specs=pl.BlockSpec(memory_space=pltpu.VMEM),
        cost_estimate=COST,
        name="pair_up",
    )(*parts)


def assemble_kernel(count, sizes, me_ref, *refs):
    parts, decoder = refs[:count], refs[count : 2 * count]
    down, up, qkv, attn, latent, decode, held, halves, sems = refs[2 * count :]
    blocks, pairs, pair, quarter, half = sizes

    def arrive(k):
        place = jnp.bitwise_xor(me_ref[0], k)
        return (
            pltpu.make_async_copy(parts[k], held.at[place], sems.at[0, k]),
            pltpu.make_async_copy(decoder[k], halves.at[place], sems.at[1, k]),
        )

    for k in range(count):
        for one in arrive(k):
            one.start()
    for k in range(count):
        for one in arrive(k):
            one.wait()
    rows, width = attn.shape
    part = width // count
    ff = up.shape[1] // (count * blocks)
    latents, genes = decode.shape

    def piece(q, spot, size):
        return held[q, :, spot : spot + size].astype(jnp.float32)

    for q in range(count):
        down[q * rows : (q + 1) * rows, :] = piece(q, 0, width)
        spot = width
        for b in range(blocks):
            up[:, (b * count + q) * ff : (b * count + q + 1) * ff] = piece(q, spot, ff)
            spot += ff
        for j in range(pairs):
            for t in range(3):
                first = t * width + q * part + j * pair
                qkv[:, first : first + pair] = piece(q, spot, pair)
                spot += pair
        for out in (attn, latent):
            out[:, q * part : (q + 1) * part] = piece(q, spot, part)
            spot += part
        for side in range(2):
            first = q * quarter + side * half
            size = min(half, quarter - side * half, genes - first)
            if size > 0:
                decode[:, first : first + size] = halves[
                    q, side * latents : (side + 1) * latents, :size
                ].astype(jnp.float32)


def assemble(parts, decoder, me, genes, quarter, half, latents, blocks, pairs, pair):
    count = len(parts)
    rows = parts[0].shape[0]
    width = blocks * rows
    shapes = [
        (count * rows, width),
        (rows, count * width),
        (rows, 3 * width),
        (rows, width),
        (rows, width),
        (latents, genes),
    ]
    return pl.pallas_call(
        functools.partial(assemble_kernel, count, (blocks, pairs, pair, quarter, half)),
        out_shape=[jax.ShapeDtypeStruct(shape, jnp.float32) for shape in shapes],
        in_specs=[pl.BlockSpec(memory_space=pltpu.SMEM)]
        + [pl.BlockSpec(memory_space=pl.ANY)] * (2 * count),
        out_specs=[pl.BlockSpec(memory_space=pltpu.VMEM)] * len(shapes),
        scratch_shapes=[
            pltpu.VMEM((count,) + parts[0].shape, jnp.bfloat16),
            pltpu.VMEM((count,) + decoder[0].shape, jnp.bfloat16),
            pltpu.SemaphoreType.DMA((2, count)),
        ],
        compiler_params=pltpu.CompilerParams(vmem_limit_bytes=48 * 2**20),
        cost_estimate=COST,
        name="assemble",
    )(me.reshape(1), *parts, *decoder)


def genes_kernel(count, table, *refs):
    rows, outs, stacked = refs[:count], refs[count : 2 * count], refs[-1]
    cells = rows[0].shape[0]

    @pl.when(pl.program_id(0) == 0)
    def _():
        for k in range(count):
            stacked[:, k * cells : (k + 1) * cells] = jnp.transpose(rows[k][...])

    product = jnp.dot(table[...], stacked[...], preferred_element_type=jnp.float32)
    for k in range(count):
        outs[k][...] = product[:, k * cells : (k + 1) * cells].astype(outs[k].dtype)


def cells_to_genes(table, rows, quarter):
    count = len(rows)
    cells, width = rows[0].shape
    return pl.pallas_call(
        functools.partial(genes_kernel, count),
        grid=(quarter // TALL,),
        out_shape=[jax.ShapeDtypeStruct((quarter, cells), jnp.bfloat16)] * count,
        in_specs=[pl.BlockSpec((TALL, width), lambda step: (step, 0))]
        + [pl.BlockSpec((cells, width), lambda step: (0, 0))] * count,
        out_specs=[pl.BlockSpec((TALL, cells), lambda step: (step, 0))] * count,
        scratch_shapes=[pltpu.VMEM((width, count * cells), jnp.bfloat16)],
        compiler_params=pltpu.CompilerParams(vmem_limit_bytes=58 * 2**20),
        cost_estimate=COST,
        name="cells_to_genes",
    )(table, *rows)


def embed_kernel(count, *refs):
    parts, rows = refs[:count], refs[count : 2 * count]
    small, out, stacked, results, sems = refs[2 * count :]
    steps = parts[0].shape[0] // STEP
    height = rows[0].shape[0]
    blocks, _, block = out.shape
    for k in range(count):
        stacked[k * height : (k + 1) * height, :] = rows[k][...]

    def leave(slot, step):
        start = pl.multiple_of(step * STEP, STEP)
        return pltpu.make_async_copy(
            results.at[slot], out.at[:, pl.ds(start, STEP), :], sems.at[slot]
        )

    last = pltpu.make_async_copy(
        small, out.at[:, pl.ds(steps * STEP, small.shape[1]), :], sems.at[2]
    )
    last.start()

    @pl.loop(0, steps)
    def _(step):
        slot = lax.rem(step, 2)

        @pl.when(step >= 2)
        def _():
            leave(slot, step - 2).wait()

        here = pl.ds(pl.multiple_of(step * STEP, STEP), STEP)
        product = jnp.dot(
            jnp.concatenate([part[here, :] for part in parts], axis=1),
            stacked[...],
            preferred_element_type=jnp.float32,
        ).astype(results.dtype)
        for k in range(blocks):
            results[slot, k] = product[:, k * block : (k + 1) * block]
        leave(slot, step).start()

    for step in range(max(steps - 2, 0), steps):
        leave(step % 2, step).wait()
    last.wait()


def embed_products(parts, rows, small):
    count = len(parts)
    quarter, cells = parts[0].shape
    width = rows[0].shape[1]
    blocks, extra, block = small.shape
    return pl.pallas_call(
        functools.partial(embed_kernel, count),
        out_shape=jax.ShapeDtypeStruct((blocks, quarter + extra, block), jnp.bfloat16),
        in_specs=[pl.BlockSpec(memory_space=pltpu.VMEM)] * (2 * count + 1),
        out_specs=pl.BlockSpec(memory_space=pltpu.HBM),
        scratch_shapes=[
            pltpu.VMEM((count * cells, width), jnp.bfloat16),
            pltpu.VMEM((2, blocks, STEP, block), jnp.bfloat16),
            pltpu.SemaphoreType.DMA((3,)),
        ],
        compiler_params=pltpu.CompilerParams(vmem_limit_bytes=58 * 2**20),
        cost_estimate=COST,
        name="embed_products",
    )(*parts, *rows, small)


def products_kernel(count, *refs):
    out = refs[-1]
    spot = 0
    for k in range(count):
        rows = jnp.transpose(refs[2 * k][...])
        columns = refs[2 * k + 1]
        width = columns.shape[1]
        for start in range(0, width, 256):
            out[:, spot + start : spot + start + 256] = jnp.dot(
                rows, columns[:, start : start + 256], preferred_element_type=jnp.float32
            ).astype(out.dtype)
        spot += width


def row_products(pairs):
    operands = [one for pair in pairs for one in pair]
    height = pairs[0][0].shape[1]
    width = sum(b.shape[1] for _, b in pairs)
    return pl.pallas_call(
        functools.partial(products_kernel, len(pairs)),
        out_shape=jax.ShapeDtypeStruct((height, width), jnp.bfloat16),
        in_specs=[pl.BlockSpec(memory_space=pltpu.VMEM)] * len(operands),
        out_specs=pl.BlockSpec(memory_space=pltpu.VMEM),
        compiler_params=pltpu.CompilerParams(vmem_limit_bytes=48 * 2**20),
        cost_estimate=COST,
        name="row_products",
    )(*operands)


def decoder_kernel(count, *refs):
    rows, cots, out, turned = refs[:count], refs[count : 2 * count], refs[-2], refs[-1]
    cells = rows[0].shape[0]

    @pl.when(pl.program_id(0) == 0)
    def _():
        for k in range(count):
            turned[:, k * cells : (k + 1) * cells] = jnp.transpose(rows[k][...])

    out[...] = lax.dot_general(
        turned[...],
        jnp.concatenate([one[...] for one in cots], axis=1),
        (((1,), (1,)), ((), ())),
        preferred_element_type=jnp.float32,
    ).astype(out.dtype)


def decoder_products(latents, cots, width):
    count = len(latents)
    cells = latents[0].shape[0]
    last = latents[0].shape[1] // width - 1
    quarter = cots[0].shape[0]
    step_rows = math.gcd(quarter, 1152)
    return pl.pallas_call(
        functools.partial(decoder_kernel, count),
        grid=(quarter // step_rows,),
        out_shape=jax.ShapeDtypeStruct((width, quarter), jnp.bfloat16),
        in_specs=[pl.BlockSpec((cells, width), lambda step: (0, last))] * count
        + [pl.BlockSpec((step_rows, cells), lambda step: (step, 0))] * count,
        out_specs=pl.BlockSpec((width, step_rows), lambda step: (0, step)),
        scratch_shapes=[pltpu.VMEM((width, count * cells), jnp.bfloat16)],
        compiler_params=pltpu.CompilerParams(vmem_limit_bytes=40 * 2**20),
        cost_estimate=COST,
        name="decoder_products",
    )(*latents, *cots)


def head_probs(keys, queries, scaling):
    scores = (
        lax.dot_general(keys, queries, (((1,), (1,)), ((), ())), preferred_element_type=jnp.float32)
        * scaling
    )
    scores = jnp.exp(scores - jnp.max(scores, axis=0, keepdims=True))
    return scores * (1.0 / jnp.sum(scores, axis=0, keepdims=True))


def attend_kernel(heads, width, rows_ref, out, turned):
    step = pl.program_id(0)
    height = out.shape[0]
    group = heads * width

    @pl.when(step == 0)
    def _():
        turned[...] = jnp.transpose(rows_ref[:, 2 * group : 3 * group])

    block = rows_ref[pl.ds(pl.multiple_of(step * height, height), height), :group]
    results = []
    for h in range(heads):
        probs = head_probs(
            rows_ref[:, group + h * width : group + (h + 1) * width],
            block[:, h * width : (h + 1) * width],
            width ** (-0.5),
        ).astype(jnp.bfloat16)
        results.append(
            jnp.dot(turned[h * width : (h + 1) * width, :], probs, preferred_element_type=jnp.float32)
        )
    out[...] = jnp.transpose(jnp.concatenate(results, axis=0)).astype(out.dtype)


def attend(rows, heads):
    cells, total = rows.shape
    group = total // 3
    height = math.gcd(cells, 1024)
    return pl.pallas_call(
        functools.partial(attend_kernel, heads, group // heads),
        grid=(cells // height,),
        out_shape=jax.ShapeDtypeStruct((cells, group), jnp.bfloat16),
        in_specs=[pl.BlockSpec((cells, total), lambda step: (0, 0))],
        out_specs=pl.BlockSpec((height, group), lambda step: (step, 0)),
        scratch_shapes=[pltpu.VMEM((group, cells), jnp.bfloat16)],
        compiler_params=pltpu.CompilerParams(vmem_limit_bytes=40 * 2**20),
        cost_estimate=COST,
        name="attend",
    )(rows)


def attend_back_kernel(heads, width, rows_ref, cot_ref, out, turned, key_sum, value_sum):
    step = pl.program_id(0)
    group = heads * width
    height = rows_ref.shape[0] // pl.num_programs(0)
    scaling = width ** (-0.5)

    @pl.when(step == 0)
    def _():
        turned[...] = jnp.transpose(rows_ref[:, group : 2 * group])
        key_sum[...] = jnp.zeros_like(key_sum)
        value_sum[...] = jnp.zeros_like(value_sum)

    here = pl.ds(pl.multiple_of(step * height, height), height)
    block = rows_ref[here, :group]
    cots = cot_ref[here, :]
    results = []
    for h in range(heads):
        columns = slice(h * width, (h + 1) * width)
        queries = block[:, columns]
        cot = cots[:, columns]
        probs = head_probs(
            rows_ref[:, group + h * width : group + (h + 1) * width], queries, scaling
        )
        prob_grad = lax.dot_general(
            rows_ref[:, 2 * group + h * width : 2 * group + (h + 1) * width],
            cot,
            (((1,), (1,)), ((), ())),
            preferred_element_type=jnp.float32,
        )
        delta = jnp.sum(probs * prob_grad, axis=0, keepdims=True)
        score_grad = (probs * (prob_grad - delta)).astype(jnp.bfloat16)
        results.append(
            jnp.dot(turned[columns, :], score_grad, preferred_element_type=jnp.float32) * scaling
        )
        key_sum[:, columns] += jnp.dot(score_grad, queries, preferred_element_type=jnp.float32)
        value_sum[:, columns] += jnp.dot(
            probs.astype(jnp.bfloat16), cot, preferred_element_type=jnp.float32
        )
    out[here, :group] = jnp.transpose(jnp.concatenate(results, axis=0)).astype(out.dtype)

    @pl.when(step == pl.num_programs(0) - 1)
    def _():
        out[:, group : 2 * group] = (key_sum[...] * scaling).astype(out.dtype)
        out[:, 2 * group :] = value_sum[...].astype(out.dtype)


def attend_back(rows, cot, heads):
    cells, total = rows.shape
    group = total // 3
    height = math.gcd(cells, 1024)
    return pl.pallas_call(
        functools.partial(attend_back_kernel, heads, group // heads),
        grid=(cells // height,),
        out_shape=jax.ShapeDtypeStruct((cells, total), jnp.bfloat16),
        in_specs=[
            pl.BlockSpec((cells, total), lambda step: (0, 0)),
            pl.BlockSpec((cells, group), lambda step: (0, 0)),
        ],
        out_specs=pl.BlockSpec((cells, total), lambda step: (0, 0)),
        scratch_shapes=[
            pltpu.VMEM((group, cells), jnp.bfloat16),
            pltpu.VMEM((cells, group), jnp.float32),
            pltpu.VMEM((cells, group), jnp.float32),
        ],
        compiler_params=pltpu.CompilerParams(vmem_limit_bytes=40 * 2**20),
        cost_estimate=COST,
        name="attend_back",
    )(rows, cot)


def split_model(
    counts,
    library,
    coords,
    noise,
    decoded_cot,
    prior_cot,
    embed_t,
    w_qkv,
    w_attn_out,
    w_up,
    up_bias,
    w_down,
    w_latent,
    w_decode,
    comp_means,
    norm_params,
):
    slides = lax.axis_size("slide")
    blocks = lax.axis_size("blk")
    me = lax.axis_index("slide")
    genes = embed_t.shape[1]
    cells = counts.shape[1]
    model_width = w_attn_out.shape[1]
    own_rows = w_qkv.shape[0]
    latent_width = w_decode.shape[0] * blocks
    mixture_count = comp_means.shape[1]
    quarter = -(-genes // (slides * ROWS)) * ROWS
    padded = quarter * slides
    head_part = model_width // slides
    pair = model_width // blocks
    pairs = head_part // pair
    ff_part = up_bias.shape[0] // slides
    latent_part = model_width // slides

    def place_of(k):
        return jnp.bitwise_xor(me, k)

    def column_part(rows, width, place):
        return lax.dynamic_slice_in_dim(rows, place * width, width, 1)

    def whole(piece, axis):
        return in_order(share(piece, slides), me, axis)

    def wide(piece):
        return piece.astype(jnp.float32)

    embed_part = lax.dynamic_slice_in_dim(
        jnp.pad(embed_t.T, ((0, padded - genes), (0, 0))), me * quarter, quarter, 0
    )
    bias_part = lax.dynamic_slice_in_dim(up_bias, me * ff_part, ff_part, 0)
    mean_cols = comp_means.size // own_rows
    folds = mixture_count // mean_cols
    own_latents = w_decode.shape[0]
    small = jnp.concatenate(
        [
            norm_params.T,
            jnp.concatenate(
                [comp_means.T[k * mean_cols : (k + 1) * mean_cols] for k in range(folds)], axis=1
            ),
            bias_part.reshape(-1, own_rows),
        ],
        axis=0,
    )
    small_rows = small.shape[0]
    small = jnp.pad(small, ((0, SMALL - small_rows), (0, 0)))
    qkv_width = pairs * 3 * pair
    qkv_part = [
        lax.dynamic_slice_in_dim(w_qkv, k * model_width + me * head_part, head_part, 1)
        for k in range(3)
    ]
    qkv_part = jnp.concatenate(
        [part[:, j * pair : (j + 1) * pair] for j in range(pairs) for part in qkv_part], axis=1
    ).T
    out_latent = jnp.concatenate(
        [
            lax.dynamic_slice_in_dim(weight, me * head_part, head_part, 1)
            for weight in (w_attn_out, w_latent)
        ],
        axis=1,
    ).T
    embedding = gather_blk(
        jnp.concatenate([embed_part, small, qkv_part, out_latent], axis=0), 1
    )
    small_all = embedding[quarter : quarter + SMALL]
    qkv_end = quarter + SMALL + qkv_width
    weight_qkv = embedding[quarter + SMALL : qkv_end].reshape(pairs, 3 * pair, model_width)
    out_latent = embedding[qkv_end:]
    norm_float = small_all[:4].astype(jnp.float32)
    centres = small_all[4 : 4 + mean_cols].reshape(mean_cols, blocks, folds, own_latents)
    centres = jnp.transpose(centres, (1, 3, 2, 0)).reshape(latent_width, mixture_count)
    bias_up = small_all[4 + mean_cols].astype(jnp.float32)
    expr_parts = swap(expression_parts(counts, library, me, slides, quarter))

    cot_all = jnp.pad(decoded_cot[0].T, ((0, padded - genes), (0, 0)))
    cot_first = [
        lax.dynamic_slice_in_dim(cot_all, place_of(k) * quarter, quarter, 0)
        for k in range(slides)
    ]
    cot_parts = swap([after(piece, *expr_parts[1:]) for piece in cot_first])
    up_part = jnp.concatenate(
        [
            lax.dynamic_slice_in_dim(w_up, (k * slides + me) * ff_part, ff_part, 1)
            for k in range(blocks)
        ],
        axis=1,
    )
    down_part = lax.dynamic_slice_in_dim(w_down, me * ff_part, ff_part, 0)
    expr_rows = turn_parts(expr_parts)
    half = -(-quarter // 256) * 128
    decode_part = lax.dynamic_slice_in_dim(
        jnp.pad(w_decode, ((0, 0), (0, padded - genes))), me * quarter, quarter, 1
    )
    decode_part = jnp.concatenate(
        [decode_part[:, :half], jnp.pad(decode_part[:, half:], ((0, 0), (0, 2 * half - quarter)))],
        axis=0,
    )
    middle = gather_blk(
        after(
            jnp.concatenate([up_part, decode_part], axis=1),
            embedding,
            expr_rows,
            *cot_parts[1:],
        )
    )
    weight_up, halves = jnp.split(middle, [model_width], axis=1)
    halves = halves.reshape(blocks, 2, own_latents, half)
    weight_decode = jnp.concatenate(
        [
            halves[:, 0].reshape(latent_width, half),
            halves[:, 1].reshape(latent_width, half)[:, : quarter - half],
        ],
        axis=1,
    )

    h_zero = collect(embed_cells(expr_rows, embedding, slides))
    h_zero = h_zero + spatial_code(coords[0], model_width)
    normed_one, norm_one_back = jax.vjp(layer_norm, h_zero, norm_float[0], norm_float[1])
    normed_one_all = jnp.concatenate(share(normed_one.astype(jnp.bfloat16), slides), axis=0)
    projected = jnp.einsum(
        "ck,pfk->pcf", normed_one_all, weight_qkv, preferred_element_type=jnp.float32
    ).astype(jnp.bfloat16)

    def to_heads(rows):
        return lax.all_to_all(
            rows.reshape(blocks, cells, rows.shape[-1]), "blk", 0, 0, tiled=True
        ).reshape(blocks * cells, rows.shape[-1])

    out_shares = share(after(out_latent[:head_part], normed_one_all), slides)
    latent_cots = cots_to_latents(cot_parts, weight_decode)
    head_rows = after(to_heads(projected), latent_cots[-1], *out_shares[1:])
    per_pair = pair // HEAD_DIM
    weight_down = gather_blk(after(down_part, middle, head_rows))
    latent_shares = share(after(out_latent[head_part:], head_rows), slides)
    weight_out = in_order(out_shares, me, 0)
    weight_latent = in_order(latent_shares, me, 0)
    own_heads = to_heads(attend(head_rows, per_pair)).reshape(pairs, slides, cells, pair)
    own_heads = after(own_heads, *latent_shares[1:])
    attended_parts = swap(
        [
            jnp.concatenate([own_heads[j, k] for j in range(pairs)], axis=1)
            for k in range(slides)
        ]
    )
    attended_low = in_order(attended_parts, me, 1)
    h_one = h_zero + contract_cols(attended_low, weight_out)
    normed_two, norm_two_back = jax.vjp(layer_norm, h_one, norm_float[2], norm_float[3])
    normed_two_low = normed_two.astype(jnp.bfloat16)
    normed_two_all = jnp.concatenate(share(normed_two_low, slides), axis=0)
    centres_float = centres.astype(jnp.float32)
    half_norms = 0.5 * jnp.sum(centres_float * centres_float, axis=0)
    normed_two_all, half_norms, centres_float = lax.optimization_barrier(
        (after(normed_two_all, weight_latent), half_norms, centres_float)
    )
    hidden_pre = (
        jnp.dot(normed_two_all, weight_up, preferred_element_type=jnp.float32) + bias_up
    )
    hidden_low = jax.nn.gelu(hidden_pre).astype(jnp.bfloat16)
    h_two_sum = collect(
        lowered(
            split_rows(
                jnp.dot(hidden_low, weight_down, preferred_element_type=jnp.float32), slides
            )
        )
    )
    latent_from_decode = collect(latent_cots)
    h_two = h_one + after(h_two_sum, latent_from_decode)
    h_two_low = h_two.astype(jnp.bfloat16)
    both_rows = lax.all_gather(
        jnp.concatenate([attended_low, h_two_low], axis=1), "slide", axis=0, tiled=True
    )
    latent_pre = contract_cols(h_two_low, weight_latent)
    spread = jnp.exp(0.5 * latent_pre[:, latent_width:])
    latent = latent_pre[:, :latent_width] + spread * noise[0]
    mixing = latent_width ** (-0.5)
    mix = (exact_dot(latent, centres_float, 1, 0) - half_norms) * mixing
    mix_max = jnp.max(mix, axis=-1, keepdims=True)
    mix_exp = jnp.exp(mix - mix_max)
    mix_sum = jnp.sum(mix_exp, axis=-1, keepdims=True)
    prior = -(mix_max + jnp.log(mix_sum))[:, 0]
    shares = prior_cot[0][:, None] * (mix_exp / mix_sum)
    latent_from_prior = exact_dot(shares, centres_float, 1, 1) * -mixing
    centre_grad = (
        centres_float * jnp.sum(shares, axis=0) - exact_dot(latent, shares, 0, 0)
    ) * mixing

    latent_total = latent_from_decode + latent_from_prior
    pre_grad = jnp.concatenate(
        [latent_total, latent_total * noise[0] * spread * 0.5], axis=-1
    ).astype(jnp.bfloat16)
    both_parts = share(
        jnp.concatenate([pre_grad, latent.astype(jnp.bfloat16)], axis=1), slides
    )
    h_two_grad, down_input, pre_hidden_grad, up_bias_grad, *normed_two_parts = feed_back(
        both_parts, weight_latent, weight_down, weight_up, hidden_pre
    )
    normed_two_grad = collect(normed_two_parts)
    latent_parts = [after(part, normed_two_parts[-1]) for part in both_parts]
    decode_local = decoder_products(latent_parts, cot_parts, latent_width)
    decoded_rows = decode_genes(latent_parts, weight_decode)
    normed_two_grad = after(normed_two_grad, decode_local, decoded_rows[-1])
    decode_own = scatter_blk(after(decode_local, both_rows, normed_two_grad))
    h_one_part, gain_two_grad, shift_two_grad = norm_two_back(normed_two_grad)
    h_one_grad = h_two_grad + h_one_part
    out_input = h_one_grad.astype(jnp.bfloat16)
    attended_grad = jnp.dot(out_input, weight_out, preferred_element_type=jnp.float32).astype(jnp.bfloat16)
    grad_parts = swap([column_part(attended_grad, head_part, place_of(k)) for k in range(slides)])
    out_heads = to_heads(pair_up(grad_parts, pairs))

    middle_local = row_products(
        [
            (hidden_low, after(down_input, *grad_parts[1:])),
            (normed_two_all, pre_hidden_grad),
        ]
    )
    out_heads = after(out_heads, middle_local)
    decoded_parts = swap(
        [after(one, *grad_parts[1:]) for one in decoded_rows[:-1]]
        + [after(decoded_rows[-1], out_heads)]
    )
    out_heads = after(out_heads, *decoded_parts[1:-1])
    head_grads = attend_back(head_rows, out_heads, per_pair)
    middle_grad = scatter_blk(after(middle_local, decode_own, head_grads))
    decode_half = jnp.concatenate(
        [decode_own[:, :half], jnp.pad(decode_own[:, half:], ((0, 0), (0, 2 * half - quarter)))],
        axis=0,
    )
    more_parts = swap(
        [
            after(
                jnp.concatenate(
                    [decode_half, column_part(out_input, head_part, place_of(k))], axis=1
                ),
                head_grads,
            )
            for k in range(slides)
        ]
    )
    projected_grad = to_heads(head_grads).reshape(pairs, slides * cells, 3 * pair)
    projected_grad = after(projected_grad, decoded_parts[-1], *more_parts[1:])
    normed_one_parts = lowered(
        split_rows(
            jnp.einsum(
                "pcf,pfk->ck", projected_grad, weight_qkv, preferred_element_type=jnp.float32
            ),
            slides,
        )
    )
    normed_one_grad = collect(normed_one_parts)
    last_kept, last_sent = last_products(
        normed_one_all,
        after(projected_grad, normed_one_parts[-1]),
        [column_part(part, latent_part, me) for part in both_parts],
        both_rows,
        more_parts,
        half,
        me,
        lax.axis_index("blk"),
    )
    last_kept, last_sent = merge_half(last_kept, to_core(last_sent))
    normed_one_grad = after(normed_one_grad, last_sent)
    h_zero_part, gain_one_grad, shift_one_grad = norm_one_back(normed_one_grad)
    h_zero_low = (h_one_grad + h_zero_part).astype(jnp.bfloat16)
    h_zero_parts = share(h_zero_low, slides)
    bit = 1
    while last_kept.shape[0] > own_rows:
        last_kept, last_sent = merge_half(last_kept, to_chip(last_sent, bit))
        bit *= 2
    h_zero_parts = [after(h_zero_parts[0], last_sent)] + h_zero_parts[1:]
    last_grad = last_kept + to_chip(last_sent, bit).astype(jnp.float32)

    small_grad = jnp.concatenate(
        [
            jnp.stack([gain_one_grad, shift_one_grad, gain_two_grad, shift_two_grad], axis=0),
            jnp.transpose(
                centre_grad.reshape(blocks, own_latents, folds, mean_cols), (3, 0, 2, 1)
            ).reshape(mean_cols, model_width),
            up_bias_grad,
        ],
        axis=0,
    )
    small_grad = jnp.pad(small_grad, ((0, SMALL - small_rows), (0, 0))).astype(jnp.bfloat16)
    small_grad = jnp.transpose(small_grad.reshape(SMALL, blocks, own_rows), (1, 0, 2))
    embed_local = embed_products(expr_parts, h_zero_parts, small_grad)
    gene_rows = cells_to_genes(
        embedding, [after(part, embed_local) for part in h_zero_parts], quarter
    )
    embed_own = scatter_blk(after(embed_local, middle_grad))[0]
    gene_parts = swap(gene_rows)
    grad_shares = share(
        after(jnp.concatenate([middle_grad, last_grad.astype(jnp.bfloat16)], axis=1), embed_local), slides
    )
    embed_shares = share(after(embed_own, *gene_parts[1:], *grad_shares[1:]), slides)
    expr_grad = spread_parts(gene_parts, me, genes)
    decoded = join_parts(decoded_parts, me, quarter, genes, jnp.bfloat16).T
    down_grad, up_grad, qkv_grad, attn_out_grad, latent_grad, decode_grad = assemble(
        grad_shares, more_parts, me, genes, quarter, half, own_latents, blocks, pairs, pair
    )
    embed_grad, norm_grad, means_grad, up_bias_grad = finish(
        embed_shares, me, quarter, genes, mean_cols, folds
    )

    return (
        decoded[None],
        prior[None],
        expr_grad,
        embed_grad.T,
        qkv_grad,
        attn_out_grad,
        up_grad,
        up_bias_grad.reshape(-1),
        down_grad,
        latent_grad,
        decode_grad,
        means_grad.T,
        norm_grad.T,
    )


def fits(mesh):
    slides, blocks = mesh.shape["slide"], mesh.shape["blk"]
    return slides & (slides - 1) == 0 and HEADS % slides == 0 and HEADS % blocks == 0


def solution(mesh):
    placed = (
        P("slide", "blk", None),
        P("slide", "blk"),
        P("slide", "blk", None),
        P("slide", "blk", None),
        P("slide", "blk", None),
        P("slide", "blk"),
        P("blk", None),
        P("blk", None),
        P("blk", None),
        P("blk", None),
        P("blk"),
        P("blk", None),
        P("blk", None),
        P("blk", None),
        P("blk", None),
        P("blk", None),
    )
    return jax.shard_map(
        split_model if fits(mesh) else local,
        mesh=mesh,
        in_specs=placed,
        out_specs=(
            P("slide", "blk", None),
            P("slide", "blk"),
            P("slide", "blk", None),
            P("blk", None),
            P("blk", None),
            P("blk", None),
            P("blk", None),
            P("blk"),
            P("blk", None),
            P("blk", None),
            P("blk", None),
            P("blk", None),
            P("blk", None),
        ),
        check_vma=False,
    )
```

```python
import functools
import math

import jax
import jax.numpy as jnp
from jax import lax
from jax.experimental import pallas as pl
from jax.experimental.pallas import tpu as pltpu
from jax.sharding import PartitionSpec as P

HEADS = 16
HEAD_DIM = 64


eps_norm = 1e-05


def contract_rows(former, latter):
    return lax.dot_general(
        former, latter, (((0,), (0,)), ((), ())), preferred_element_type=jnp.float32
    )


def contract_cols(former, latter):
    return lax.dot_general(
        former, latter, (((1,), (1,)), ((), ())), preferred_element_type=jnp.float32
    )


def layer_norm(tensor, norm_gain, norm_shift):
    center = tensor - jnp.mean(tensor, axis=-1, keepdims=True)
    inverse = lax.rsqrt(jnp.mean(center * center, axis=-1, keepdims=True) + eps_norm)
    return center * inverse * norm_gain + norm_shift


def spatial_code(coords, model_width):
    quarter = model_width // 4
    frequency = jnp.exp(-math.log(10000.0) * jnp.arange(quarter, dtype=jnp.float32) / quarter)
    first_axis = coords[..., 0:1].astype(jnp.float32) * frequency
    second_axis = coords[..., 1:2].astype(jnp.float32) * frequency
    return jnp.concatenate(
        [jnp.sin(first_axis), jnp.cos(first_axis), jnp.sin(second_axis), jnp.cos(second_axis)],
        axis=-1,
    )


def mixture_term(latent, centres):
    scores = (
        jnp.dot(
            latent, centres, precision=lax.Precision.HIGHEST, preferred_element_type=jnp.float32
        )
        - 0.5 * jnp.sum(centres * centres, axis=0)
    ) * latent.shape[-1] ** (-0.5)
    return -jax.nn.logsumexp(scores, axis=-1)


def split_single(rows_in, head_count):
    arrived_rows = rows_in.shape[0]
    block_rows = 512
    return rows_in.reshape(
        (arrived_rows // block_rows, block_rows, head_count, rows_in.shape[1] // head_count)
    )


def split_blocks(key_rows, value_rows, head_count):
    return (split_single(key_rows, head_count), split_single(value_rows, head_count))


def local(
    counts,
    library,
    coords,
    noise,
    decoded_cot,
    prior_cot,
    embed_t,
    w_qkv,
    w_attn_out,
    w_up,
    up_bias,
    w_down,
    w_latent,
    w_decode,
    comp_means,
    norm_params,
):
    gathered = (
        lax.all_gather(embed_t, "blk", axis=0, tiled=True),
        lax.all_gather(w_qkv, "blk", axis=0, tiled=True),
        lax.all_gather(w_attn_out, "blk", axis=0, tiled=True),
        lax.all_gather(w_up, "blk", axis=0, tiled=True),
        lax.all_gather(up_bias, "blk", axis=0, tiled=True),
        lax.all_gather(w_down, "blk", axis=0, tiled=True),
        lax.all_gather(w_latent, "blk", axis=0, tiled=True),
        lax.all_gather(w_decode, "blk", axis=0, tiled=True),
        lax.all_gather(comp_means, "blk", axis=0, tiled=True),
        lax.all_gather(norm_params, "blk", axis=0, tiled=True),
    )
    (
        embedding,
        weight_qkv,
        weight_out,
        weight_up,
        bias_up,
        weight_down,
        weight_latent,
        weight_decode,
        centres,
        norm_table,
    ) = gathered
    head_count = HEADS
    head_width = HEAD_DIM
    scaling = head_width ** (-0.5)
    model_width = embedding.shape[0]
    latent_width = weight_decode.shape[0]
    blk_count = lax.axis_size("blk")
    expression = jnp.log1p(
        counts[0].astype(jnp.float32) * 10000.0 / library[0].astype(jnp.float32)[:, None]
    )
    expression_low = expression.astype(jnp.bfloat16)
    local_cells = expression.shape[0]
    norm_float = norm_table.astype(jnp.float32)
    h_zero = contract_cols(expression_low, embedding) + spatial_code(coords[0], model_width)
    normed_one, norm_one_back = jax.vjp(layer_norm, h_zero, norm_float[:, 0], norm_float[:, 1])
    normed_one_low = normed_one.astype(jnp.bfloat16)
    projected = jnp.dot(normed_one_low, weight_qkv, preferred_element_type=jnp.float32).astype(
        jnp.bfloat16
    )
    queries = projected[:, :model_width].reshape(local_cells, head_count, head_width)
    key_rows = projected[:, model_width : 2 * model_width]
    value_rows = projected[:, 2 * model_width :]
    stat_start = (
        jnp.full((head_count, local_cells), -1e30, jnp.float32),
        jnp.zeros((head_count, local_cells), jnp.float32),
    )
    key_blocks = split_single(lax.all_gather(key_rows, "blk", axis=0, tiled=True), head_count)

    def per_block(status, key_block):
        running_max, running_sum = status
        scores = (
            jnp.einsum("thd,khd->htk", queries, key_block, preferred_element_type=jnp.float32)
            * scaling
        )
        new_max = jnp.maximum(running_max, jnp.max(scores, axis=-1))
        running_sum = running_sum * jnp.exp(running_max - new_max) + jnp.sum(
            jnp.exp(scores - new_max[..., None]), axis=-1
        )
        return ((new_max, running_sum), None)

    result, unused = lax.scan(per_block, stat_start, key_blocks)
    running_max, running_sum = result
    log_total = running_max + jnp.log(running_sum)
    arrived = (
        lax.all_gather(key_rows, "blk", axis=0, tiled=True),
        lax.all_gather(value_rows, "blk", axis=0, tiled=True),
    )
    key_blocks, value_blocks = split_blocks(arrived[0], arrived[1], head_count)

    def per_block(weighted, block_pair):
        scores = (
            jnp.einsum("thd,khd->htk", queries, block_pair[0], preferred_element_type=jnp.float32)
            * scaling
        )
        probs_low = jnp.exp(scores - log_total[..., None]).astype(jnp.bfloat16)
        weighted = weighted + jnp.einsum(
            "htk,khd->htd", probs_low, block_pair[1], preferred_element_type=jnp.float32
        )
        return (weighted, None)

    result, unused = lax.scan(
        per_block,
        jnp.zeros((head_count, local_cells, head_width), jnp.float32),
        (key_blocks, value_blocks),
    )
    attended_cells = jnp.transpose(result, (1, 0, 2))
    attended_low = attended_cells.reshape(local_cells, model_width).astype(jnp.bfloat16)
    h_one = h_zero + jnp.dot(attended_low, weight_out, preferred_element_type=jnp.float32)
    normed_two, norm_two_back = jax.vjp(layer_norm, h_one, norm_float[:, 2], norm_float[:, 3])
    normed_two_low = normed_two.astype(jnp.bfloat16)
    hidden_pre = jnp.dot(
        normed_two_low, weight_up, preferred_element_type=jnp.float32
    ) + bias_up.astype(jnp.float32)
    hidden_act, gelu_back = jax.vjp(jax.nn.gelu, hidden_pre)
    hidden_low = hidden_act.astype(jnp.bfloat16)
    h_two = h_one + jnp.dot(hidden_low, weight_down, preferred_element_type=jnp.float32)
    h_two_low = h_two.astype(jnp.bfloat16)
    latent_pre = jnp.dot(h_two_low, weight_latent, preferred_element_type=jnp.float32)
    spread = jnp.exp(0.5 * latent_pre[:, latent_width:])
    latent = latent_pre[:, :latent_width] + spread * noise[0]
    latent_low = latent.astype(jnp.bfloat16)
    decoded = jnp.dot(latent_low, weight_decode, preferred_element_type=jnp.float32).astype(
        jnp.bfloat16
    )
    prior, prior_back = jax.vjp(mixture_term, latent, centres.astype(jnp.float32))
    out_grad = decoded_cot[0]
    latent_from_decode = contract_cols(out_grad, weight_decode)
    latent_from_prior, centre_grad = prior_back(prior_cot[0])
    latent_total = latent_from_decode + latent_from_prior
    pre_grad = jnp.concatenate(
        [latent_total, latent_total * noise[0] * spread * 0.5], axis=-1
    ).astype(jnp.bfloat16)
    latent_weight_grad = contract_rows(h_two_low, pre_grad)
    h_two_grad = contract_cols(pre_grad, weight_latent)
    down_input = h_two_grad.astype(jnp.bfloat16)
    down_grad = contract_rows(hidden_low, down_input)
    hidden_grad = contract_cols(down_input, weight_down)
    pre_hidden_grad = gelu_back(hidden_grad)[0].astype(jnp.bfloat16)
    up_bias_grad = jnp.sum(pre_hidden_grad.astype(jnp.float32), axis=0)
    up_grad = contract_rows(normed_two_low, pre_hidden_grad)
    normed_two_grad = contract_cols(pre_hidden_grad, weight_up)
    h_one_part, gain_two_grad, shift_two_grad = norm_two_back(normed_two_grad)
    h_one_grad = h_two_grad + h_one_part
    out_input = h_one_grad.astype(jnp.bfloat16)
    attn_out_grad = contract_rows(attended_low, out_input)
    attended_grad = contract_cols(out_input, weight_out).astype(jnp.bfloat16)
    out_heads = attended_grad.reshape(local_cells, head_count, head_width)
    row_delta = jnp.sum(out_heads.astype(jnp.float32) * attended_cells, axis=-1).T
    query_zero = jnp.zeros((head_count, local_cells, head_width), jnp.float32)
    start_back = (query_zero, jnp.zeros((local_cells * blk_count, 2 * model_width), jnp.float32))
    arrived = (
        lax.all_gather(key_rows, "blk", axis=0, tiled=True),
        lax.all_gather(value_rows, "blk", axis=0, tiled=True),
    )
    key_blocks, value_blocks = split_blocks(arrived[0], arrived[1], head_count)
    arrived_rows = arrived[0].shape[0]

    def per_block(query_sum, block_pair):
        scores = (
            jnp.einsum("thd,khd->htk", queries, block_pair[0], preferred_element_type=jnp.float32)
            * scaling
        )
        probs = jnp.exp(scores - log_total[..., None])
        prob_grad = jnp.einsum(
            "thd,khd->htk", out_heads, block_pair[1], preferred_element_type=jnp.float32
        )
        score_grad = (probs * (prob_grad - row_delta[..., None])).astype(jnp.bfloat16)
        query_sum = query_sum + jnp.einsum(
            "htk,khd->htd", score_grad, block_pair[0], preferred_element_type=jnp.float32
        )
        key_part = (
            jnp.einsum("htk,thd->khd", score_grad, queries, preferred_element_type=jnp.float32)
            * scaling
        )
        value_part = jnp.einsum(
            "htk,thd->khd",
            probs.astype(jnp.bfloat16),
            out_heads,
            preferred_element_type=jnp.float32,
        )
        block_rows = key_part.shape[0]
        return (
            query_sum,
            jnp.concatenate(
                [key_part.reshape(block_rows, -1), value_part.reshape(block_rows, -1)], axis=-1
            ),
        )

    query_total, stacked = lax.scan(per_block, start_back[0], (key_blocks, value_blocks))
    stacked = stacked.reshape(arrived_rows, stacked.shape[-1])
    carried_back = (query_total, stacked)
    query_total = carried_back[0]
    own_pairs = lax.psum_scatter(
        carried_back[1].astype(jnp.bfloat16), "blk", scatter_dimension=0, tiled=True
    ).astype(jnp.float32)
    query_rows = jnp.transpose(query_total * scaling, (1, 0, 2)).reshape(local_cells, model_width)
    projected_grad = jnp.concatenate([query_rows, own_pairs], axis=-1).astype(jnp.bfloat16)
    qkv_grad = contract_rows(normed_one_low, projected_grad)
    normed_one_grad = contract_cols(projected_grad, weight_qkv)
    h_zero_part, gain_one_grad, shift_one_grad = norm_one_back(normed_one_grad)
    h_zero_low = (h_one_grad + h_zero_part).astype(jnp.bfloat16)
    expr_grad = jnp.dot(h_zero_low, embedding, preferred_element_type=jnp.float32)
    norm_grad = jnp.stack([gain_one_grad, shift_one_grad, gain_two_grad, shift_two_grad], axis=0).T
    centre_grad = centre_grad.T.T
    embed_slot = contract_rows(h_zero_low, expression_low)
    decode_slot = contract_rows(latent_low, out_grad)
    block_parts = (
        lax.psum_scatter(
            embed_slot.astype(jnp.bfloat16), "blk", scatter_dimension=0, tiled=True
        ).astype(jnp.float32),
        lax.psum_scatter(
            qkv_grad.astype(jnp.bfloat16), "blk", scatter_dimension=0, tiled=True
        ).astype(jnp.float32),
        lax.psum_scatter(
            attn_out_grad.astype(jnp.bfloat16), "blk", scatter_dimension=0, tiled=True
        ).astype(jnp.float32),
        lax.psum_scatter(
            up_grad.astype(jnp.bfloat16), "blk", scatter_dimension=0, tiled=True
        ).astype(jnp.float32),
        lax.psum_scatter(
            up_bias_grad.astype(jnp.bfloat16), "blk", scatter_dimension=0, tiled=True
        ).astype(jnp.float32),
        lax.psum_scatter(
            down_grad.astype(jnp.bfloat16), "blk", scatter_dimension=0, tiled=True
        ).astype(jnp.float32),
        lax.psum_scatter(
            latent_weight_grad.astype(jnp.bfloat16), "blk", scatter_dimension=0, tiled=True
        ).astype(jnp.float32),
        lax.psum_scatter(
            decode_slot.astype(jnp.bfloat16), "blk", scatter_dimension=0, tiled=True
        ).astype(jnp.float32),
        lax.psum_scatter(
            centre_grad.astype(jnp.bfloat16), "blk", scatter_dimension=0, tiled=True
        ).astype(jnp.float32),
        lax.psum_scatter(
            norm_grad.astype(jnp.bfloat16), "blk", scatter_dimension=0, tiled=True
        ).astype(jnp.float32),
    )
    summed = (
        lax.psum(block_parts[0].astype(jnp.bfloat16), "slide").astype(jnp.float32),
        lax.psum(block_parts[1].astype(jnp.bfloat16), "slide").astype(jnp.float32),
        lax.psum(block_parts[2].astype(jnp.bfloat16), "slide").astype(jnp.float32),
        lax.psum(block_parts[3].astype(jnp.bfloat16), "slide").astype(jnp.float32),
        lax.psum(block_parts[4].astype(jnp.bfloat16), "slide").astype(jnp.float32),
        lax.psum(block_parts[5].astype(jnp.bfloat16), "slide").astype(jnp.float32),
        lax.psum(block_parts[6].astype(jnp.bfloat16), "slide").astype(jnp.float32),
        lax.psum(block_parts[7].astype(jnp.bfloat16), "slide").astype(jnp.float32),
        lax.psum(block_parts[8].astype(jnp.bfloat16), "slide").astype(jnp.float32),
        lax.psum(block_parts[9].astype(jnp.bfloat16), "slide").astype(jnp.float32),
    )
    embed_out = summed[0]
    decode_out = summed[7]
    return (
        decoded[None],
        prior[None],
        expr_grad[None],
        embed_out,
        summed[1],
        summed[2],
        summed[3],
        summed[4],
        summed[5],
        summed[6],
        decode_out,
        summed[8],
        summed[9],
    )


def peers(offset, count):
    return [(place, place ^ offset) for place in range(count)]


def swap(pieces):
    count = len(pieces)
    return [pieces[0]] + [
        lax.ppermute(pieces[k], "slide", peers(k, count)) for k in range(1, count)
    ]


def share_halves(rows):
    half = rows.shape[0] // 2
    upper, lower = rows[:half], rows[half:]
    upper_x = lax.ppermute(upper, "slide", peers(1, 4))
    lower_y = lax.ppermute(lower, "slide", peers(2, 4))
    uppers = lax.ppermute(jnp.concatenate([upper, upper_x], axis=0), "slide", peers(2, 4))
    lowers = lax.ppermute(jnp.concatenate([lower, lower_y], axis=0), "slide", peers(1, 4))
    return [rows, upper_x, lower_y, uppers, lowers]


def share(rows, count):
    return swap([rows] * count)


def after(value, *earlier):
    return lax.optimization_barrier((value,) + earlier)[0]


def in_order(pieces, me, axis):
    stacked = jnp.stack(pieces)
    return jnp.concatenate(
        [
            lax.dynamic_index_in_dim(stacked, jnp.bitwise_xor(me, k), 0, keepdims=False)
            for k in range(len(pieces))
        ],
        axis=axis,
    )


def exact_dot(former, latter, left, right):
    return lax.dot_general(
        former,
        latter,
        (((left,), (right,)), ((), ())),
        precision=lax.Precision.HIGHEST,
        preferred_element_type=jnp.float32,
    )


def lowered(partials):
    return [partials[0]] + [piece.astype(jnp.bfloat16) for piece in partials[1:]]


def collect(partials):
    arrived = swap(partials)
    total = arrived[0]
    for piece in arrived[1:]:
        total = total + piece.astype(jnp.float32)
    return total


def gather_blk(piece, axis=0):
    return lax.all_gather(piece, "blk", axis=axis, tiled=True)


def scatter_blk(piece, axis=0):
    return lax.psum_scatter(piece, "blk", scatter_dimension=axis, tiled=True)


def to_core(rows):
    count = lax.axis_size("blk")
    return lax.ppermute(rows, "blk", [(place, place ^ 1) for place in range(count)])


def to_chip(rows, offset):
    count = lax.axis_size("blk")
    return lax.ppermute(rows, "blk", [(place, place ^ (2 * offset)) for place in range(count)])


def split_rows(rows, count):
    height = rows.shape[0] // count
    return [rows[k * height : (k + 1) * height] for k in range(count)]


ROWS = 432
STEP = 864
TALL = 1728
WIDE = 3456
CHUNKS = 2
SMALL = 16
COST = pl.CostEstimate(flops=0, bytes_accessed=0, transcendentals=0)


def expression_kernel(count, quarter, genes, me_ref, library_ref, counts_ref, *rest):
    outs, buffers, sems = rest[:count], rest[count], rest[count + 1]
    me = me_ref[0]
    tail = genes - (count - 1) * quarter
    library = library_ref[...].astype(jnp.float32)

    def copy(k, rows):
        start = pl.multiple_of(jnp.bitwise_xor(me, k) * quarter, 8)
        return pltpu.make_async_copy(
            counts_ref.at[pl.ds(start, rows), 0, :],
            buffers.at[k, pl.ds(0, rows), :],
            sems.at[k],
        )

    def each(k, act):
        last = jnp.bitwise_xor(me, k) == count - 1

        @pl.when(last)
        def _():
            act(copy(k, tail))

        @pl.when(jnp.logical_not(last))
        def _():
            act(copy(k, quarter))

    order = list(range(1, count)) + [0]
    for k in order:
        each(k, lambda one: one.start())
    for k in order:
        each(k, lambda one: one.wait())
        have = genes - jnp.bitwise_xor(me, k) * quarter

        @pl.loop(0, quarter // ROWS)
        def _(step):
            start = pl.multiple_of(step * ROWS, ROWS)
            values = buffers[k, pl.ds(start, ROWS), :].astype(jnp.float32)
            values = jnp.log1p(values * 10000.0 / library)
            row = start + lax.broadcasted_iota(jnp.int32, values.shape, 0)
            outs[k][pl.ds(start, ROWS), :] = jnp.where(row < have, values, 0.0).astype(jnp.bfloat16)


def expression_parts(counts, library, me, count, quarter):
    genes = counts.shape[2]
    cells = counts.shape[1]
    part = jax.ShapeDtypeStruct((quarter, cells), jnp.bfloat16)
    return pl.pallas_call(
        functools.partial(expression_kernel, count, quarter, genes),
        out_shape=[part] * count,
        in_specs=[
            pl.BlockSpec(memory_space=pltpu.SMEM),
            pl.BlockSpec(memory_space=pltpu.VMEM),
            pl.BlockSpec(memory_space=pltpu.HBM),
        ],
        out_specs=[pl.BlockSpec(memory_space=pltpu.VMEM)] * count,
        scratch_shapes=[
            pltpu.VMEM((count, quarter, cells), jnp.int32),
            pltpu.SemaphoreType.DMA((count,)),
        ],
        compiler_params=pltpu.CompilerParams(vmem_limit_bytes=40 * 2**20),
        cost_estimate=COST,
        name="expression",
    )(me.reshape(1), library, jnp.transpose(counts, (2, 0, 1)))


def spread_kernel(count, quarter, genes, me_ref, *rest):
    pieces, out, held, wide, sems_in, sems_out = rest[:count], *rest[count:]
    me = me_ref[0]
    tail = genes - (count - 1) * quarter

    def arrive(k):
        return pltpu.make_async_copy(pieces[k], held.at[k], sems_in.at[k])

    def leave(k):
        rows = tail if k == count - 1 else quarter
        return pltpu.make_async_copy(
            wide.at[k, pl.ds(0, rows), :], out.at[pl.ds(k * quarter, rows), 0, :], sems_out.at[k]
        )

    for k in range(count):
        arrive(k).start()
    for k in range(count):
        arrive(k).wait()
    for k in range(count):
        source = jnp.bitwise_xor(me, k)

        @pl.loop(0, quarter // ROWS)
        def _(step):
            rows = pl.ds(pl.multiple_of(step * ROWS, ROWS), ROWS)
            wide[k, rows, :] = held[source, rows, :].astype(jnp.float32)

        leave(k).start()
    for k in range(count):
        leave(k).wait()


def spread_parts(pieces, me, genes):
    count = len(pieces)
    quarter, cells = pieces[0].shape
    out = pl.pallas_call(
        functools.partial(spread_kernel, count, quarter, genes),
        out_shape=jax.ShapeDtypeStruct((genes, 1, cells), jnp.float32),
        in_specs=[pl.BlockSpec(memory_space=pltpu.SMEM)]
        + [pl.BlockSpec(memory_space=pl.ANY)] * count,
        out_specs=pl.BlockSpec(memory_space=pltpu.HBM),
        scratch_shapes=[
            pltpu.VMEM((count, quarter, cells), jnp.bfloat16),
            pltpu.VMEM((count, quarter, cells), jnp.float32),
            pltpu.SemaphoreType.DMA((count,)),
            pltpu.SemaphoreType.DMA((count,)),
        ],
        compiler_params=pltpu.CompilerParams(vmem_limit_bytes=40 * 2**20),
        cost_estimate=COST,
        name="spread",
    )(me.reshape(1), *pieces)
    return jnp.transpose(out, (1, 2, 0))


def join_kernel(count, me_ref, *rest):
    pieces, out, held, sems = rest[:count], *rest[count:]
    slot = pl.program_id(0)

    def arrive(k):
        rows = pl.ds(0, held.shape[1])
        return pltpu.make_async_copy(pieces[k].at[rows, :], held.at[k], sems.at[k])

    @pl.when(slot == 0)
    def _():
        for k in range(count):
            arrive(k).start()
        for k in range(count):
            arrive(k).wait()

    source = jnp.bitwise_xor(me_ref[0], slot)

    @pl.loop(0, out.shape[0] // ROWS)
    def _(step):
        rows = pl.ds(pl.multiple_of(step * ROWS, ROWS), ROWS)
        out[rows, :] = held[source, rows, :].astype(out.dtype)


def join_parts(pieces, me, quarter, genes, dtype):
    count = len(pieces)
    cells = pieces[0].shape[1]
    return pl.pallas_call(
        functools.partial(join_kernel, count),
        grid=(count,),
        out_shape=jax.ShapeDtypeStruct((genes, cells), dtype),
        in_specs=[pl.BlockSpec(memory_space=pltpu.SMEM)]
        + [pl.BlockSpec(memory_space=pl.ANY)] * count,
        out_specs=pl.BlockSpec((quarter, cells), lambda slot: (slot, 0)),
        scratch_shapes=[
            pltpu.VMEM((count, quarter, cells), jnp.bfloat16),
            pltpu.SemaphoreType.DMA((count,)),
        ],
        compiler_params=pltpu.CompilerParams(vmem_limit_bytes=40 * 2**20),
        cost_estimate=COST,
        name="join",
    )(me.reshape(1), *pieces)


def order_kernel(count, me_ref, *refs):
    pieces, out, sems = refs[:count], refs[-2], refs[-1]
    height = pieces[0].shape[0]

    def move(k):
        first = pl.multiple_of(jnp.bitwise_xor(me_ref[0], k) * height, height)
        return pltpu.make_async_copy(pieces[k], out.at[pl.ds(first, height), :], sems.at[k])

    for k in range(count):
        move(k).start()
    for k in range(count):
        move(k).wait()


def order_rows(pieces, me):
    count = len(pieces)
    height, width = pieces[0].shape
    return pl.pallas_call(
        functools.partial(order_kernel, count),
        out_shape=jax.ShapeDtypeStruct((count * height, width), pieces[0].dtype),
        in_specs=[pl.BlockSpec(memory_space=pltpu.SMEM)]
        + [pl.BlockSpec(memory_space=pl.ANY)] * count,
        out_specs=pl.BlockSpec(memory_space=pltpu.VMEM),
        scratch_shapes=[pltpu.SemaphoreType.DMA((count,))],
        cost_estimate=COST,
        name="order_rows",
    )(me.reshape(1), *pieces)


def turn_kernel(count, *refs):
    out = refs[-1]
    for k in range(count):
        height = refs[k].shape[1]
        out[k * height : (k + 1) * height, :] = jnp.transpose(refs[k][...])


def turn_parts(parts):
    count = len(parts)
    quarter, cells = parts[0].shape
    return pl.pallas_call(
        functools.partial(turn_kernel, count),
        grid=(quarter // WIDE,),
        out_shape=jax.ShapeDtypeStruct((count * cells, quarter), jnp.bfloat16),
        in_specs=[pl.BlockSpec((WIDE, cells), lambda step: (step, 0))] * count,
        out_specs=pl.BlockSpec((count * cells, WIDE), lambda step: (0, step)),
        compiler_params=pltpu.CompilerParams(vmem_limit_bytes=40 * 2**20),
        cost_estimate=COST,
        name="turn_parts",
    )(*parts)


def finish_kernel(count, quarter, mean_cols, folds, me_ref, *refs):
    pieces = refs[:count]
    out, norm, means, bias, held, sems = refs[count:]
    slot = pl.program_id(0)

    def arrive(k):
        place = jnp.bitwise_xor(me_ref[0], k)
        return pltpu.make_async_copy(pieces[k], held.at[place], sems.at[k])

    @pl.when(slot == 0)
    def _():
        for k in range(count):
            arrive(k).start()
        for k in range(count):
            arrive(k).wait()
        small = [held[q, quarter:, :].astype(jnp.float32) for q in range(count)]
        total = sum(small[1:], small[0])
        norm[...] = total[:4, :]
        width = means.shape[1]
        for k in range(folds):
            means[k * mean_cols : (k + 1) * mean_cols, :] = total[
                4 : 4 + mean_cols, k * width : (k + 1) * width
            ]
        bias[...] = jnp.concatenate(
            [one[4 + mean_cols : 5 + mean_cols, :] for one in small], axis=0
        )

    out[...] = held[slot, :quarter, :].astype(out.dtype)


def finish(pieces, me, quarter, genes, mean_cols, folds):
    count = len(pieces)
    height, cells = pieces[0].shape
    return pl.pallas_call(
        functools.partial(finish_kernel, count, quarter, mean_cols, folds),
        grid=(count,),
        out_shape=[
            jax.ShapeDtypeStruct((genes, cells), jnp.float32),
            jax.ShapeDtypeStruct((4, cells), jnp.float32),
            jax.ShapeDtypeStruct((folds * mean_cols, cells // folds), jnp.float32),
            jax.ShapeDtypeStruct((count, cells), jnp.float32),
        ],
        in_specs=[pl.BlockSpec(memory_space=pltpu.SMEM)]
        + [pl.BlockSpec(memory_space=pl.ANY)] * count,
        out_specs=[
            pl.BlockSpec((quarter, cells), lambda slot: (slot, 0)),
            pl.BlockSpec((4, cells), lambda slot: (0, 0)),
            pl.BlockSpec((folds * mean_cols, cells // folds), lambda slot: (0, 0)),
            pl.BlockSpec((count, cells), lambda slot: (0, 0)),
        ],
        scratch_shapes=[
            pltpu.VMEM((count, height, cells), jnp.bfloat16),
            pltpu.SemaphoreType.DMA((count,)),
        ],
        compiler_params=pltpu.CompilerParams(vmem_limit_bytes=40 * 2**20),
        cost_estimate=COST,
        name="finish",
    )(me.reshape(1), *pieces)


def scores_kernel(rows, table, *outs):
    product = jnp.dot(rows[...], table[...], preferred_element_type=jnp.float32)
    height = outs[0].shape[0]
    for k in range(len(outs)):
        outs[k][...] = product[k * height : (k + 1) * height, :].astype(outs[k].dtype)


def embed_cells(rows, table, count):
    height, quarter = rows.shape
    width = table.shape[1]
    block = math.gcd(width, 512)
    return pl.pallas_call(
        scores_kernel,
        grid=(width // block,),
        out_shape=[
            jax.ShapeDtypeStruct((height // count, width), jnp.float32 if k == 0 else jnp.bfloat16)
            for k in range(count)
        ],
        in_specs=[
            pl.BlockSpec((height, quarter), lambda step: (0, 0)),
            pl.BlockSpec((quarter, block), lambda step: (0, step)),
        ],
        out_specs=[pl.BlockSpec((height // count, block), lambda step: (0, step))] * count,
        compiler_params=pltpu.CompilerParams(vmem_limit_bytes=58 * 2**20),
        cost_estimate=COST,
        name="embed_cells",
    )(rows, table)


def latents_kernel(count, table, *refs):
    cots, outs, total = refs[:count], refs[count:-1], refs[-1]
    step = pl.program_id(0)
    product = jnp.dot(
        table[...],
        jnp.concatenate([one[...] for one in cots], axis=1),
        preferred_element_type=jnp.float32,
    )

    @pl.when(step == 0)
    def _():
        total[...] = product

    @pl.when(step > 0)
    def _():
        total[...] += product

    @pl.when(step == pl.num_programs(0) - 1)
    def _():
        cells = outs[0].shape[0]
        for k in range(count):
            outs[k][...] = jnp.transpose(total[:, k * cells : (k + 1) * cells]).astype(
                outs[k].dtype
            )


def cots_to_latents(cots, table):
    count = len(cots)
    width, quarter = table.shape
    cells = cots[0].shape[1]
    return pl.pallas_call(
        functools.partial(latents_kernel, count),
        grid=(quarter // WIDE,),
        out_shape=[
            jax.ShapeDtypeStruct((cells, width), jnp.float32 if k == 0 else jnp.bfloat16)
            for k in range(count)
        ],
        in_specs=[pl.BlockSpec((width, WIDE), lambda step: (0, step))]
        + [pl.BlockSpec((WIDE, cells), lambda step: (step, 0))] * count,
        out_specs=[pl.BlockSpec((cells, width), lambda step: (0, 0))] * count,
        scratch_shapes=[pltpu.VMEM((width, count * cells), jnp.float32)],
        compiler_params=pltpu.CompilerParams(vmem_limit_bytes=40 * 2**20),
        cost_estimate=COST,
        name="cots_to_latents",
    )(table, *cots)


def gelu_slope(rows):
    scale = math.sqrt(2.0 / math.pi)
    squares = rows * rows
    bent = jnp.tanh(scale * (rows + 0.044715 * (squares * rows)))
    inner = scale * (1.0 + (3.0 * 0.044715) * squares)
    return 0.5 * (1.0 + bent) + 0.5 * rows * (1.0 - bent * bent) * inner


def feed_back_kernel(count, latent, down, up, pre, *refs):
    parts = refs[:count]
    own, down_input, pre_grad, bias, *outs = refs[count:]
    cells = own.shape[0]
    width = own.shape[1]
    h_grad = jnp.dot(
        jnp.concatenate([part[:, : latent.shape[0]] for part in parts], axis=0),
        latent[...],
        preferred_element_type=jnp.float32,
    )
    own[...] = h_grad[:cells, :]
    down_input[...] = h_grad.astype(jnp.bfloat16)
    step = 256
    for start in range(0, pre.shape[1], step):
        columns = slice(start, start + step)
        hidden_grad = lax.dot_general(
            down_input[...],
            down[columns, :],
            (((1,), (1,)), ((), ())),
            preferred_element_type=jnp.float32,
        )
        low = (hidden_grad * gelu_slope(pre[:, columns])).astype(jnp.bfloat16)
        pre_grad[:, columns] = low
        bias[:, columns] = jnp.sum(low.astype(jnp.float32), axis=0, keepdims=True)
    product = lax.dot_general(
        pre_grad[...], up[...], (((1,), (1,)), ((), ())), preferred_element_type=jnp.float32
    )
    for k in range(count):
        outs[k][...] = product[k * cells : (k + 1) * cells, :].astype(outs[k].dtype)


def feed_back(parts, latent, down, up, pre):
    count = len(parts)
    cells = parts[0].shape[0]
    width = latent.shape[1]
    units = pre.shape[1]

    def whole(array):
        return pl.BlockSpec(array.shape, lambda step: (0,) * len(array.shape))

    shapes = [
        jax.ShapeDtypeStruct((cells, width), jnp.float32),
        jax.ShapeDtypeStruct((count * cells, width), jnp.bfloat16),
        jax.ShapeDtypeStruct((count * cells, units), jnp.bfloat16),
        jax.ShapeDtypeStruct((1, units), jnp.float32),
    ] + [
        jax.ShapeDtypeStruct((cells, width), jnp.float32 if k == 0 else jnp.bfloat16)
        for k in range(count)
    ]
    operands = [latent, down, up, pre, *parts]
    return pl.pallas_call(
        functools.partial(feed_back_kernel, count),
        grid=(1,),
        out_shape=shapes,
        in_specs=[whole(one) for one in operands],
        out_specs=[whole(one) for one in shapes],
        compiler_params=pltpu.CompilerParams(vmem_limit_bytes=56 * 2**20),
        cost_estimate=COST,
        name="feed_back",
    )(*operands)


def decode_kernel(count, table, *refs):
    rows, outs = refs[:count], refs[count:]
    cells = rows[0].shape[0]
    product = jnp.dot(
        jnp.concatenate([one[...] for one in rows], axis=0),
        table[...],
        preferred_element_type=jnp.float32,
    ).astype(jnp.bfloat16)
    for k in range(count):
        outs[k][...] = jnp.transpose(product[k * cells : (k + 1) * cells, :])


def decode_genes(latents, table):
    count = len(latents)
    cells = latents[0].shape[0]
    width, quarter = table.shape
    last = latents[0].shape[1] // width - 1
    return pl.pallas_call(
        functools.partial(decode_kernel, count),
        grid=(1,),
        out_shape=[jax.ShapeDtypeStruct((quarter, cells), jnp.bfloat16)] * count,
        in_specs=[pl.BlockSpec((width, quarter), lambda step: (0, 0))]
        + [pl.BlockSpec((cells, width), lambda step: (0, last))] * count,
        out_specs=[pl.BlockSpec((quarter, cells), lambda step: (0, 0))] * count,
        compiler_params=pltpu.CompilerParams(vmem_limit_bytes=40 * 2**20),
        cost_estimate=COST,
        name="decode_genes",
    )(table, *latents)


def chip_offsets(chips):
    order = [0]
    bit = chips // 2
    while bit:
        order = order + [one + bit for one in order]
        bit //= 2
    return order


def last_kernel(count, first, offsets, places, normed, projected, both, *refs):
    pre_grads, cots = refs[:count], refs[count : 2 * count]
    kept, sent, turned = refs[2 * count :]
    me, place = places[0], places[1]
    cells = cots[0].shape[0]
    width = normed.shape[1]
    block = kept.shape[0] // len(offsets)

    def by_offset(first):
        return jnp.concatenate(
            [
                both[
                    pl.ds(pl.multiple_of(jnp.bitwise_xor(me, k) * cells, cells), cells),
                    first : first + width,
                ]
                for k in range(count)
            ],
            axis=0,
        )

    spot = 0
    for group, (rows, columns) in enumerate(
        (
            (normed[...], [projected[k] for k in range(projected.shape[0])]),
            (by_offset(0), [jnp.concatenate([one[:, first:] for one in cots], axis=0)]),
            (by_offset(width), [jnp.concatenate([one[...] for one in pre_grads], axis=0)]),
        )
    ):
        turned[group] = jnp.transpose(rows)
        for one in columns:
            size = one.shape[1]
            for out, core in ((kept, place % 2), (sent, 1 - place % 2)):
                owners = [jnp.bitwise_xor(place // 2, k) * 2 + core for k in offsets]
                ordered = jnp.concatenate(
                    [
                        turned[group, pl.ds(pl.multiple_of(owner * block, block), block), :]
                        for owner in owners
                    ],
                    axis=0,
                )
                out[:, spot : spot + size] = jnp.dot(
                    ordered, one, preferred_element_type=jnp.float32
                ).astype(out.dtype)
            spot += size


def last_products(normed, projected, pre_grads, both, cots, first, me, place):
    count = len(cots)
    height = normed.shape[1]
    offsets = chip_offsets(lax.axis_size("blk") // 2)
    width = projected.shape[0] * projected.shape[2] + 2 * pre_grads[0].shape[1]
    return pl.pallas_call(
        functools.partial(last_kernel, count, first, offsets),
        out_shape=[
            jax.ShapeDtypeStruct((height // 2, width), jnp.float32),
            jax.ShapeDtypeStruct((height // 2, width), jnp.bfloat16),
        ],
        in_specs=[pl.BlockSpec(memory_space=pltpu.SMEM)]
        + [pl.BlockSpec(memory_space=pltpu.VMEM)] * (3 + 2 * count),
        out_specs=[pl.BlockSpec(memory_space=pltpu.VMEM)] * 2,
        scratch_shapes=[pltpu.VMEM((3, height, normed.shape[0]), jnp.bfloat16)],
        compiler_params=pltpu.CompilerParams(vmem_limit_bytes=40 * 2**20),
        cost_estimate=COST,
        name="last_products",
    )(jnp.stack([me, place]), normed, projected, both, *pre_grads, *cots)


def half_kernel(kept, other, stay, go):
    height = stay.shape[0]
    stay[...] = kept[:height, :] + other[:height, :].astype(jnp.float32)
    go[...] = (kept[height:, :] + other[height:, :].astype(jnp.float32)).astype(go.dtype)


def merge_half(kept, other):
    height, width = kept.shape
    return pl.pallas_call(
        half_kernel,
        out_shape=[
            jax.ShapeDtypeStruct((height // 2, width), jnp.float32),
            jax.ShapeDtypeStruct((height // 2, width), jnp.bfloat16),
        ],
        in_specs=[pl.BlockSpec(memory_space=pltpu.VMEM)] * 2,
        out_specs=[pl.BlockSpec(memory_space=pltpu.VMEM)] * 2,
        compiler_params=pltpu.CompilerParams(vmem_limit_bytes=40 * 2**20),
        cost_estimate=COST,
        name="merge_half",
    )(kept, other)


def pair_kernel(count, *refs):
    parts, out = refs[:count], refs[-1]
    width = out.shape[2]
    for j in range(out.shape[0] // count):
        for k in range(count):
            out[j * count + k] = parts[k][:, j * width : (j + 1) * width]


def pair_up(parts, pairs):
    count = len(parts)
    cells, width = parts[0].shape
    return pl.pallas_call(
        functools.partial(pair_kernel, count),
        out_shape=jax.ShapeDtypeStruct((pairs * count, cells, width // pairs), parts[0].dtype),
        in_specs=[pl.BlockSpec(memory_space=pltpu.VMEM)] * count,
        out_specs=pl.BlockSpec(memory_space=pltpu.VMEM),
        cost_estimate=COST,
        name="pair_up",
    )(*parts)


def assemble_kernel(count, sizes, me_ref, *refs):
    early, parts = refs[:5], refs[5 : 5 + count]
    down, up, qkv, attn, latent, decode, middle, last, sems = refs[5 + count :]
    blocks, pairs, pair, quarter, half = sizes
    me = me_ref[0]
    rows, width = attn.shape
    cut = rows // 2
    upper, lower = pl.ds(0, cut), pl.ds(cut, cut)
    ours, upper_x, lower_y, uppers, lowers = early
    moves = [
        (ours, middle.at[me]),
        (upper_x, middle.at[jnp.bitwise_xor(me, 1), upper, :]),
        (lower_y, middle.at[jnp.bitwise_xor(me, 2), lower, :]),
        (uppers.at[upper, :], middle.at[jnp.bitwise_xor(me, 2), upper, :]),
        (uppers.at[lower, :], middle.at[jnp.bitwise_xor(me, 3), upper, :]),
        (lowers.at[upper, :], middle.at[jnp.bitwise_xor(me, 1), lower, :]),
        (lowers.at[lower, :], middle.at[jnp.bitwise_xor(me, 3), lower, :]),
    ] + [(parts[k], last.at[jnp.bitwise_xor(me, k)]) for k in range(count)]
    copies = [
        pltpu.make_async_copy(source, target, sems.at[k])
        for k, (source, target) in enumerate(moves)
    ]
    for one in copies:
        one.start()
    for one in copies:
        one.wait()
    part = width // count
    ff = up.shape[1] // (count * blocks)
    latents, genes = decode.shape

    def piece(array, q, spot, size):
        return array[q, :, spot : spot + size].astype(jnp.float32)

    for q in range(count):
        down[q * rows : (q + 1) * rows, :] = piece(middle, q, 0, width)
        spot = width
        for b in range(blocks):
            up[:, (b * count + q) * ff : (b * count + q + 1) * ff] = piece(middle, q, spot, ff)
            spot += ff
        for side in range(2):
            first = q * quarter + side * half
            size = min(half, quarter - side * half, genes - first)
            if size > 0:
                decode[:, first : first + size] = middle[
                    q, side * latents : (side + 1) * latents, spot : spot + size
                ].astype(jnp.float32)
        spot = 0
        for j in range(pairs):
            for t in range(3):
                first = t * width + q * part + j * pair
                qkv[:, first : first + pair] = piece(last, q, spot, pair)
                spot += pair
        for out in (attn, latent):
            out[:, q * part : (q + 1) * part] = piece(last, q, spot, part)
            spot += part


def assemble(early, last, me, genes, quarter, half, latents, blocks, pairs, pair):
    count = len(last)
    rows = last[0].shape[0]
    width = blocks * rows
    shapes = [
        (count * rows, width),
        (rows, count * width),
        (rows, 3 * width),
        (rows, width),
        (rows, width),
        (latents, genes),
    ]
    return pl.pallas_call(
        functools.partial(assemble_kernel, count, (blocks, pairs, pair, quarter, half)),
        out_shape=[jax.ShapeDtypeStruct(shape, jnp.float32) for shape in shapes],
        in_specs=[pl.BlockSpec(memory_space=pltpu.SMEM)]
        + [pl.BlockSpec(memory_space=pl.ANY)] * (5 + count),
        out_specs=[pl.BlockSpec(memory_space=pltpu.VMEM)] * len(shapes),
        scratch_shapes=[
            pltpu.VMEM((count,) + early[0].shape, jnp.bfloat16),
            pltpu.VMEM((count,) + last[0].shape, jnp.bfloat16),
            pltpu.SemaphoreType.DMA((7 + count,)),
        ],
        compiler_params=pltpu.CompilerParams(vmem_limit_bytes=48 * 2**20),
        cost_estimate=COST,
        name="assemble",
    )(me.reshape(1), *early, *last)


def genes_kernel(count, table, *refs):
    rows, outs, stacked = refs[:count], refs[count : 2 * count], refs[-1]
    cells = rows[0].shape[0]

    @pl.when(pl.program_id(0) == 0)
    def _():
        for k in range(count):
            stacked[:, k * cells : (k + 1) * cells] = jnp.transpose(rows[k][...])

    product = jnp.dot(table[...], stacked[...], preferred_element_type=jnp.float32)
    for k in range(count):
        outs[k][...] = product[:, k * cells : (k + 1) * cells].astype(outs[k].dtype)


def cells_to_genes(table, rows, quarter):
    count = len(rows)
    cells, width = rows[0].shape
    return pl.pallas_call(
        functools.partial(genes_kernel, count),
        grid=(quarter // TALL,),
        out_shape=[jax.ShapeDtypeStruct((quarter, cells), jnp.bfloat16)] * count,
        in_specs=[pl.BlockSpec((TALL, width), lambda step: (step, 0))]
        + [pl.BlockSpec((cells, width), lambda step: (0, 0))] * count,
        out_specs=[pl.BlockSpec((TALL, cells), lambda step: (step, 0))] * count,
        scratch_shapes=[pltpu.VMEM((width, count * cells), jnp.bfloat16)],
        compiler_params=pltpu.CompilerParams(vmem_limit_bytes=58 * 2**20),
        cost_estimate=COST,
        name="cells_to_genes",
    )(table, *rows)


def embed_kernel(count, *refs):
    parts, rows = refs[:count], refs[count : 2 * count]
    small, out, stacked, results, sems = refs[2 * count :]
    steps = parts[0].shape[0] // STEP
    height = rows[0].shape[0]
    blocks, _, block = out.shape
    for k in range(count):
        stacked[k * height : (k + 1) * height, :] = rows[k][...]

    def leave(slot, step):
        start = pl.multiple_of(step * STEP, STEP)
        return pltpu.make_async_copy(
            results.at[slot], out.at[:, pl.ds(start, STEP), :], sems.at[slot]
        )

    last = pltpu.make_async_copy(
        small, out.at[:, pl.ds(steps * STEP, small.shape[1]), :], sems.at[2]
    )
    last.start()

    @pl.loop(0, steps)
    def _(step):
        slot = lax.rem(step, 2)

        @pl.when(step >= 2)
        def _():
            leave(slot, step - 2).wait()

        here = pl.ds(pl.multiple_of(step * STEP, STEP), STEP)
        product = jnp.dot(
            jnp.concatenate([part[here, :] for part in parts], axis=1),
            stacked[...],
            preferred_element_type=jnp.float32,
        ).astype(results.dtype)
        for k in range(blocks):
            results[slot, k] = product[:, k * block : (k + 1) * block]
        leave(slot, step).start()

    for step in range(max(steps - 2, 0), steps):
        leave(step % 2, step).wait()
    last.wait()


def embed_products(parts, rows, small):
    count = len(parts)
    quarter, cells = parts[0].shape
    width = rows[0].shape[1]
    blocks, extra, block = small.shape
    return pl.pallas_call(
        functools.partial(embed_kernel, count),
        out_shape=jax.ShapeDtypeStruct((blocks, quarter + extra, block), jnp.bfloat16),
        in_specs=[pl.BlockSpec(memory_space=pltpu.VMEM)] * (2 * count + 1),
        out_specs=pl.BlockSpec(memory_space=pltpu.HBM),
        scratch_shapes=[
            pltpu.VMEM((count * cells, width), jnp.bfloat16),
            pltpu.VMEM((2, blocks, STEP, block), jnp.bfloat16),
            pltpu.SemaphoreType.DMA((3,)),
        ],
        compiler_params=pltpu.CompilerParams(vmem_limit_bytes=58 * 2**20),
        cost_estimate=COST,
        name="embed_products",
    )(*parts, *rows, small)


def products_kernel(count, *refs):
    out = refs[-1]
    spot = 0
    for k in range(count):
        rows = jnp.transpose(refs[2 * k][...])
        columns = refs[2 * k + 1]
        width = columns.shape[1]
        for start in range(0, width, 256):
            out[:, spot + start : spot + start + 256] = jnp.dot(
                rows, columns[:, start : start + 256], preferred_element_type=jnp.float32
            ).astype(out.dtype)
        spot += width


def row_products(pairs):
    operands = [one for pair in pairs for one in pair]
    height = pairs[0][0].shape[1]
    width = sum(b.shape[1] for _, b in pairs)
    return pl.pallas_call(
        functools.partial(products_kernel, len(pairs)),
        out_shape=jax.ShapeDtypeStruct((height, width), jnp.bfloat16),
        in_specs=[pl.BlockSpec(memory_space=pltpu.VMEM)] * len(operands),
        out_specs=pl.BlockSpec(memory_space=pltpu.VMEM),
        compiler_params=pltpu.CompilerParams(vmem_limit_bytes=48 * 2**20),
        cost_estimate=COST,
        name="row_products",
    )(*operands)


def decoder_kernel(count, *refs):
    rows, cots, out, turned = refs[:count], refs[count : 2 * count], refs[-2], refs[-1]
    cells = rows[0].shape[0]

    @pl.when(pl.program_id(0) == 0)
    def _():
        for k in range(count):
            turned[:, k * cells : (k + 1) * cells] = jnp.transpose(rows[k][...])

    out[...] = lax.dot_general(
        turned[...],
        jnp.concatenate([one[...] for one in cots], axis=1),
        (((1,), (1,)), ((), ())),
        preferred_element_type=jnp.float32,
    ).astype(out.dtype)


def decoder_products(latents, cots, width):
    count = len(latents)
    cells = latents[0].shape[0]
    last = latents[0].shape[1] // width - 1
    quarter = cots[0].shape[0]
    step_rows = math.gcd(quarter, 1152)
    return pl.pallas_call(
        functools.partial(decoder_kernel, count),
        grid=(quarter // step_rows,),
        out_shape=jax.ShapeDtypeStruct((width, quarter), jnp.bfloat16),
        in_specs=[pl.BlockSpec((cells, width), lambda step: (0, last))] * count
        + [pl.BlockSpec((step_rows, cells), lambda step: (step, 0))] * count,
        out_specs=pl.BlockSpec((width, step_rows), lambda step: (0, step)),
        scratch_shapes=[pltpu.VMEM((width, count * cells), jnp.bfloat16)],
        compiler_params=pltpu.CompilerParams(vmem_limit_bytes=40 * 2**20),
        cost_estimate=COST,
        name="decoder_products",
    )(*latents, *cots)


def head_probs(keys, queries, scaling):
    scores = (
        lax.dot_general(keys, queries, (((1,), (1,)), ((), ())), preferred_element_type=jnp.float32)
        * scaling
    )
    scores = jnp.exp(scores - jnp.max(scores, axis=0, keepdims=True))
    return scores * (1.0 / jnp.sum(scores, axis=0, keepdims=True))


def attend_kernel(heads, width, rows_ref, out, turned):
    step = pl.program_id(0)
    height = out.shape[0]
    group = heads * width

    @pl.when(step == 0)
    def _():
        turned[...] = jnp.transpose(rows_ref[:, 2 * group : 3 * group])

    block = rows_ref[pl.ds(pl.multiple_of(step * height, height), height), :group]
    results = []
    for h in range(heads):
        probs = head_probs(
            rows_ref[:, group + h * width : group + (h + 1) * width],
            block[:, h * width : (h + 1) * width],
            width ** (-0.5),
        ).astype(jnp.bfloat16)
        results.append(
            jnp.dot(turned[h * width : (h + 1) * width, :], probs, preferred_element_type=jnp.float32)
        )
    out[...] = jnp.transpose(jnp.concatenate(results, axis=0)).astype(out.dtype)


def attend(rows, heads):
    cells, total = rows.shape
    group = total // 3
    height = math.gcd(cells, 1024)
    return pl.pallas_call(
        functools.partial(attend_kernel, heads, group // heads),
        grid=(cells // height,),
        out_shape=jax.ShapeDtypeStruct((cells, group), jnp.bfloat16),
        in_specs=[pl.BlockSpec((cells, total), lambda step: (0, 0))],
        out_specs=pl.BlockSpec((height, group), lambda step: (step, 0)),
        scratch_shapes=[pltpu.VMEM((group, cells), jnp.bfloat16)],
        compiler_params=pltpu.CompilerParams(vmem_limit_bytes=40 * 2**20),
        cost_estimate=COST,
        name="attend",
    )(rows)


def attend_back_kernel(heads, width, rows_ref, cot_ref, out, turned, key_sum, value_sum):
    step = pl.program_id(0)
    group = heads * width
    height = rows_ref.shape[0] // pl.num_programs(0)
    scaling = width ** (-0.5)

    @pl.when(step == 0)
    def _():
        turned[...] = jnp.transpose(rows_ref[:, group : 2 * group])
        key_sum[...] = jnp.zeros_like(key_sum)
        value_sum[...] = jnp.zeros_like(value_sum)

    here = pl.ds(pl.multiple_of(step * height, height), height)
    block = rows_ref[here, :group]
    cots = cot_ref[here, :]
    results = []
    for h in range(heads):
        columns = slice(h * width, (h + 1) * width)
        queries = block[:, columns]
        cot = cots[:, columns]
        probs = head_probs(
            rows_ref[:, group + h * width : group + (h + 1) * width], queries, scaling
        )
        prob_grad = lax.dot_general(
            rows_ref[:, 2 * group + h * width : 2 * group + (h + 1) * width],
            cot,
            (((1,), (1,)), ((), ())),
            preferred_element_type=jnp.float32,
        )
        delta = jnp.sum(probs * prob_grad, axis=0, keepdims=True)
        score_grad = (probs * (prob_grad - delta)).astype(jnp.bfloat16)
        results.append(
            jnp.dot(turned[columns, :], score_grad, preferred_element_type=jnp.float32) * scaling
        )
        key_sum[:, columns] += jnp.dot(score_grad, queries, preferred_element_type=jnp.float32)
        value_sum[:, columns] += jnp.dot(
            probs.astype(jnp.bfloat16), cot, preferred_element_type=jnp.float32
        )
    out[here, :group] = jnp.transpose(jnp.concatenate(results, axis=0)).astype(out.dtype)

    @pl.when(step == pl.num_programs(0) - 1)
    def _():
        out[:, group : 2 * group] = (key_sum[...] * scaling).astype(out.dtype)
        out[:, 2 * group :] = value_sum[...].astype(out.dtype)


def attend_back(rows, cot, heads):
    cells, total = rows.shape
    group = total // 3
    height = math.gcd(cells, 1024)
    return pl.pallas_call(
        functools.partial(attend_back_kernel, heads, group // heads),
        grid=(cells // height,),
        out_shape=jax.ShapeDtypeStruct((cells, total), jnp.bfloat16),
        in_specs=[
            pl.BlockSpec((cells, total), lambda step: (0, 0)),
            pl.BlockSpec((cells, group), lambda step: (0, 0)),
        ],
        out_specs=pl.BlockSpec((cells, total), lambda step: (0, 0)),
        scratch_shapes=[
            pltpu.VMEM((group, cells), jnp.bfloat16),
            pltpu.VMEM((cells, group), jnp.float32),
            pltpu.VMEM((cells, group), jnp.float32),
        ],
        compiler_params=pltpu.CompilerParams(vmem_limit_bytes=40 * 2**20),
        cost_estimate=COST,
        name="attend_back",
    )(rows, cot)


def split_model(
    counts,
    library,
    coords,
    noise,
    decoded_cot,
    prior_cot,
    embed_t,
    w_qkv,
    w_attn_out,
    w_up,
    up_bias,
    w_down,
    w_latent,
    w_decode,
    comp_means,
    norm_params,
):
    slides = lax.axis_size("slide")
    blocks = lax.axis_size("blk")
    me = lax.axis_index("slide")
    genes = embed_t.shape[1]
    cells = counts.shape[1]
    model_width = w_attn_out.shape[1]
    own_rows = w_qkv.shape[0]
    latent_width = w_decode.shape[0] * blocks
    mixture_count = comp_means.shape[1]
    quarter = -(-genes // (slides * ROWS)) * ROWS
    padded = quarter * slides
    head_part = model_width // slides
    pair = model_width // blocks
    pairs = head_part // pair
    ff_part = up_bias.shape[0] // slides
    latent_part = model_width // slides

    def place_of(k):
        return jnp.bitwise_xor(me, k)

    def column_part(rows, width, place):
        return lax.dynamic_slice_in_dim(rows, place * width, width, 1)

    def whole(piece, axis):
        return in_order(share(piece, slides), me, axis)

    def wide(piece):
        return piece.astype(jnp.float32)

    embed_part = lax.dynamic_slice_in_dim(
        jnp.pad(embed_t.T, ((0, padded - genes), (0, 0))), me * quarter, quarter, 0
    )
    bias_part = lax.dynamic_slice_in_dim(up_bias, me * ff_part, ff_part, 0)
    mean_cols = comp_means.size // own_rows
    folds = mixture_count // mean_cols
    own_latents = w_decode.shape[0]
    small = jnp.concatenate(
        [
            norm_params.T,
            jnp.concatenate(
                [comp_means.T[k * mean_cols : (k + 1) * mean_cols] for k in range(folds)], axis=1
            ),
            bias_part.reshape(-1, own_rows),
        ],
        axis=0,
    )
    small_rows = small.shape[0]
    small = jnp.pad(small, ((0, SMALL - small_rows), (0, 0)))
    qkv_width = pairs * 3 * pair
    qkv_part = [
        lax.dynamic_slice_in_dim(w_qkv, k * model_width + me * head_part, head_part, 1)
        for k in range(3)
    ]
    qkv_part = jnp.concatenate(
        [part[:, j * pair : (j + 1) * pair] for j in range(pairs) for part in qkv_part], axis=1
    ).T
    out_latent = jnp.concatenate(
        [
            lax.dynamic_slice_in_dim(weight, me * head_part, head_part, 1)
            for weight in (w_attn_out, w_latent)
        ],
        axis=1,
    ).T
    embedding = gather_blk(
        jnp.concatenate([embed_part, small, qkv_part, out_latent], axis=0), 1
    )
    small_all = embedding[quarter : quarter + SMALL]
    qkv_end = quarter + SMALL + qkv_width
    weight_qkv = embedding[quarter + SMALL : qkv_end].reshape(pairs, 3 * pair, model_width)
    out_latent = embedding[qkv_end:]
    norm_float = small_all[:4].astype(jnp.float32)
    centres = small_all[4 : 4 + mean_cols].reshape(mean_cols, blocks, folds, own_latents)
    centres = jnp.transpose(centres, (1, 3, 2, 0)).reshape(latent_width, mixture_count)
    bias_up = small_all[4 + mean_cols].astype(jnp.float32)
    expr_parts = swap(expression_parts(counts, library, me, slides, quarter))

    cot_all = jnp.pad(decoded_cot[0].T, ((0, padded - genes), (0, 0)))
    cot_first = [
        lax.dynamic_slice_in_dim(cot_all, place_of(k) * quarter, quarter, 0)
        for k in range(slides)
    ]
    cot_parts = swap([after(piece, *expr_parts[1:]) for piece in cot_first])
    up_part = jnp.concatenate(
        [
            lax.dynamic_slice_in_dim(w_up, (k * slides + me) * ff_part, ff_part, 1)
            for k in range(blocks)
        ],
        axis=1,
    )
    down_part = lax.dynamic_slice_in_dim(w_down, me * ff_part, ff_part, 0)
    expr_rows = turn_parts(expr_parts)
    half = -(-quarter // 256) * 128
    decode_part = lax.dynamic_slice_in_dim(
        jnp.pad(w_decode, ((0, 0), (0, padded - genes))), me * quarter, quarter, 1
    )
    decode_part = jnp.concatenate(
        [decode_part[:, :half], jnp.pad(decode_part[:, half:], ((0, 0), (0, 2 * half - quarter)))],
        axis=0,
    )
    middle = gather_blk(
        after(
            jnp.concatenate([up_part, decode_part], axis=1),
            embedding,
            expr_rows,
            *cot_parts[1:],
        )
    )
    weight_up, halves = jnp.split(middle, [model_width], axis=1)
    halves = halves.reshape(blocks, 2, own_latents, half)
    weight_decode = jnp.concatenate(
        [
            halves[:, 0].reshape(latent_width, half),
            halves[:, 1].reshape(latent_width, half)[:, : quarter - half],
        ],
        axis=1,
    )

    h_zero = collect(embed_cells(expr_rows, embedding, slides))
    h_zero = h_zero + spatial_code(coords[0], model_width)
    normed_one, norm_one_back = jax.vjp(layer_norm, h_zero, norm_float[0], norm_float[1])
    normed_one_all = jnp.concatenate(share(normed_one.astype(jnp.bfloat16), slides), axis=0)
    projected = jnp.einsum(
        "ck,pfk->pcf", normed_one_all, weight_qkv, preferred_element_type=jnp.float32
    ).astype(jnp.bfloat16)

    def to_heads(rows):
        return lax.all_to_all(
            rows.reshape(blocks, cells, rows.shape[-1]), "blk", 0, 0, tiled=True
        ).reshape(blocks * cells, rows.shape[-1])

    out_shares = share(after(out_latent[:head_part], normed_one_all), slides)
    latent_cots = cots_to_latents(cot_parts, weight_decode)
    centres_float = centres.astype(jnp.float32)
    half_norms = 0.5 * jnp.sum(centres_float * centres_float, axis=0)
    head_rows, half_norms, centres_float = lax.optimization_barrier(
        (after(to_heads(projected), latent_cots[-1], *out_shares[1:]), half_norms, centres_float)
    )
    per_pair = pair // HEAD_DIM
    weight_down = gather_blk(after(down_part, middle, head_rows))
    latent_shares = share(after(out_latent[head_part:], head_rows), slides)
    weight_out = order_rows(out_shares, me)
    weight_latent = order_rows(latent_shares, me)
    own_heads = to_heads(attend(head_rows, per_pair)).reshape(pairs, slides, cells, pair)
    own_heads = after(own_heads, *latent_shares[1:])
    attended_parts = swap(
        [
            jnp.concatenate([own_heads[j, k] for j in range(pairs)], axis=1)
            for k in range(slides)
        ]
    )
    attended_low = in_order(attended_parts, me, 1)
    h_one = h_zero + contract_cols(attended_low, weight_out)
    normed_two, norm_two_back = jax.vjp(layer_norm, h_one, norm_float[2], norm_float[3])
    normed_two_low = normed_two.astype(jnp.bfloat16)
    normed_two_all = jnp.concatenate(share(normed_two_low, slides), axis=0)
    normed_two_all = after(normed_two_all, weight_latent)
    hidden_pre = (
        jnp.dot(normed_two_all, weight_up, preferred_element_type=jnp.float32) + bias_up
    )
    hidden_low = jax.nn.gelu(hidden_pre).astype(jnp.bfloat16)
    h_two_sum = collect(
        lowered(
            split_rows(
                jnp.dot(hidden_low, weight_down, preferred_element_type=jnp.float32), slides
            )
        )
    )
    latent_from_decode = collect(latent_cots)
    h_two = h_one + after(h_two_sum, latent_from_decode)
    h_two_low = h_two.astype(jnp.bfloat16)
    both_rows = lax.all_gather(
        jnp.concatenate([attended_low, h_two_low], axis=1), "slide", axis=0, tiled=True
    )
    latent_pre = contract_cols(h_two_low, weight_latent)
    spread = jnp.exp(0.5 * latent_pre[:, latent_width:])
    latent = latent_pre[:, :latent_width] + spread * noise[0]
    mixing = latent_width ** (-0.5)
    mix = (exact_dot(latent, centres_float, 1, 0) - half_norms) * mixing
    mix_max = jnp.max(mix, axis=-1, keepdims=True)
    mix_exp = jnp.exp(mix - mix_max)
    mix_sum = jnp.sum(mix_exp, axis=-1, keepdims=True)
    prior = -(mix_max + jnp.log(mix_sum))[:, 0]
    shares = prior_cot[0][:, None] * (mix_exp / mix_sum)
    latent_from_prior = exact_dot(shares, centres_float, 1, 1) * -mixing
    centre_grad = (
        centres_float * jnp.sum(shares, axis=0) - exact_dot(latent, shares, 0, 0)
    ) * mixing

    latent_total = latent_from_decode + latent_from_prior
    pre_grad = jnp.concatenate(
        [latent_total, latent_total * noise[0] * spread * 0.5], axis=-1
    ).astype(jnp.bfloat16)
    both_parts = share(
        jnp.concatenate([pre_grad, latent.astype(jnp.bfloat16)], axis=1), slides
    )
    h_two_grad, down_input, pre_hidden_grad, up_bias_grad, *normed_two_parts = feed_back(
        both_parts, weight_latent, weight_down, weight_up, hidden_pre
    )
    normed_two_grad = collect(normed_two_parts)
    latent_parts = [after(part, normed_two_parts[-1]) for part in both_parts]
    decode_local = decoder_products(latent_parts, cot_parts, latent_width)
    decoded_rows = decode_genes(latent_parts, weight_decode)
    normed_two_grad = after(normed_two_grad, decode_local, decoded_rows[-1])
    decode_own = scatter_blk(after(decode_local, both_rows, normed_two_grad))
    h_one_part, gain_two_grad, shift_two_grad = norm_two_back(normed_two_grad)
    h_one_grad = h_two_grad + h_one_part
    out_input = h_one_grad.astype(jnp.bfloat16)
    attended_grad = jnp.dot(out_input, weight_out, preferred_element_type=jnp.float32).astype(jnp.bfloat16)
    grad_parts = swap([column_part(attended_grad, head_part, place_of(k)) for k in range(slides)])
    out_heads = to_heads(pair_up(grad_parts, pairs))

    middle_local = row_products(
        [
            (hidden_low, after(down_input, *grad_parts[1:])),
            (normed_two_all, pre_hidden_grad),
        ]
    )
    out_heads = after(out_heads, middle_local)
    decoded_parts = swap(
        [after(one, *grad_parts[1:]) for one in decoded_rows[:-1]]
        + [after(decoded_rows[-1], out_heads)]
    )
    out_heads = after(out_heads, *decoded_parts[1:-1])
    head_grads = attend_back(head_rows, out_heads, per_pair)
    middle_grad = scatter_blk(after(middle_local, decode_own, head_grads))
    cot_cols = swap(
        [
            after(column_part(out_input, head_part, place_of(k)), head_grads)
            for k in range(slides)
        ]
    )
    projected_grad = to_heads(head_grads).reshape(pairs, slides * cells, 3 * pair)
    projected_grad = after(projected_grad, decoded_parts[-1], *cot_cols[1:])
    normed_one_parts = lowered(
        split_rows(
            jnp.einsum(
                "pcf,pfk->ck", projected_grad, weight_qkv, preferred_element_type=jnp.float32
            ),
            slides,
        )
    )
    normed_one_grad = collect(normed_one_parts)
    last_kept, last_sent = last_products(
        normed_one_all,
        after(projected_grad, normed_one_parts[-1]),
        [column_part(part, latent_part, me) for part in both_parts],
        both_rows,
        cot_cols,
        0,
        me,
        lax.axis_index("blk"),
    )
    last_kept, last_sent = merge_half(last_kept, to_core(last_sent))
    normed_one_grad = after(normed_one_grad, last_sent)
    h_zero_part, gain_one_grad, shift_one_grad = norm_one_back(normed_one_grad)
    h_zero_low = (h_one_grad + h_zero_part).astype(jnp.bfloat16)
    h_zero_parts = share(h_zero_low, slides)
    bit = 1
    while last_kept.shape[0] > own_rows:
        last_kept, last_sent = merge_half(last_kept, to_chip(last_sent, bit))
        bit *= 2
    h_zero_parts = [after(h_zero_parts[0], last_sent)] + h_zero_parts[1:]
    last_other = to_chip(last_sent, bit)

    small_grad = jnp.concatenate(
        [
            jnp.stack([gain_one_grad, shift_one_grad, gain_two_grad, shift_two_grad], axis=0),
            jnp.transpose(
                centre_grad.reshape(blocks, own_latents, folds, mean_cols), (3, 0, 2, 1)
            ).reshape(mean_cols, model_width),
            up_bias_grad,
        ],
        axis=0,
    )
    small_grad = jnp.pad(small_grad, ((0, SMALL - small_rows), (0, 0))).astype(jnp.bfloat16)
    small_grad = jnp.transpose(small_grad.reshape(SMALL, blocks, own_rows), (1, 0, 2))
    embed_local = embed_products(expr_parts, h_zero_parts, small_grad)
    gene_rows = cells_to_genes(
        embedding, [after(part, embed_local) for part in h_zero_parts], quarter
    )
    embed_own = scatter_blk(after(embed_local, middle_grad))[0]
    decode_half = jnp.concatenate(
        [decode_own[:, :half], jnp.pad(decode_own[:, half:], ((0, 0), (0, 2 * half - quarter)))],
        axis=0,
    )
    early = after(jnp.concatenate([middle_grad, decode_half], axis=1), *h_zero_parts[1:])
    early_parts = share_halves(early)
    gene_parts = swap([after(part, *early_parts[1:3]) for part in gene_rows])
    last_low = (last_kept + after(last_other, *gene_parts[1:3]).astype(jnp.float32)).astype(
        jnp.bfloat16
    )
    last_shares = share(last_low, slides)
    embed_shares = share(
        after(embed_own, *gene_parts[1:], *last_shares[1:], *early_parts[1:]), slides
    )
    expr_grad = spread_parts(gene_parts, me, genes)
    decoded = join_parts(decoded_parts, me, quarter, genes, jnp.bfloat16).T
    down_grad, up_grad, qkv_grad, attn_out_grad, latent_grad, decode_grad = assemble(
        early_parts, last_shares, me, genes, quarter, half, own_latents, blocks, pairs, pair
    )
    embed_grad, norm_grad, means_grad, up_bias_grad = finish(
        embed_shares, me, quarter, genes, mean_cols, folds
    )

    return (
        decoded[None],
        prior[None],
        expr_grad,
        embed_grad.T,
        qkv_grad,
        attn_out_grad,
        up_grad,
        up_bias_grad.reshape(-1),
        down_grad,
        latent_grad,
        decode_grad,
        means_grad.T,
        norm_grad.T,
    )


def fits(mesh):
    slides, blocks = mesh.shape["slide"], mesh.shape["blk"]
    return slides & (slides - 1) == 0 and HEADS % slides == 0 and HEADS % blocks == 0


def solution(mesh):
    placed = (
        P("slide", "blk", None),
        P("slide", "blk"),
        P("slide", "blk", None),
        P("slide", "blk", None),
        P("slide", "blk", None),
        P("slide", "blk"),
        P("blk", None),
        P("blk", None),
        P("blk", None),
        P("blk", None),
        P("blk"),
        P("blk", None),
        P("blk", None),
        P("blk", None),
        P("blk", None),
        P("blk", None),
    )
    return jax.shard_map(
        split_model if fits(mesh) else local,
        mesh=mesh,
        in_specs=placed,
        out_specs=(
            P("slide", "blk", None),
            P("slide", "blk"),
            P("slide", "blk", None),
            P("blk", None),
            P("blk", None),
            P("blk", None),
            P("blk", None),
            P("blk"),
            P("blk", None),
            P("blk", None),
            P("blk", None),
            P("blk", None),
            P("blk", None),
        ),
        check_vma=False,
    )
```

```python
import functools
import math

import jax
import jax.numpy as jnp
from jax import lax
from jax.experimental import pallas as pl
from jax.experimental.pallas import tpu as pltpu
from jax.sharding import PartitionSpec as P

HEADS = 16
HEAD_DIM = 64


eps_norm = 1e-05


def contract_rows(former, latter):
    return lax.dot_general(
        former, latter, (((0,), (0,)), ((), ())), preferred_element_type=jnp.float32
    )


def contract_cols(former, latter):
    return lax.dot_general(
        former, latter, (((1,), (1,)), ((), ())), preferred_element_type=jnp.float32
    )


def layer_norm(tensor, norm_gain, norm_shift):
    center = tensor - jnp.mean(tensor, axis=-1, keepdims=True)
    inverse = lax.rsqrt(jnp.mean(center * center, axis=-1, keepdims=True) + eps_norm)
    return center * inverse * norm_gain + norm_shift


def spatial_code(coords, model_width):
    quarter = model_width // 4
    frequency = jnp.exp(-math.log(10000.0) * jnp.arange(quarter, dtype=jnp.float32) / quarter)
    first_axis = coords[..., 0:1].astype(jnp.float32) * frequency
    second_axis = coords[..., 1:2].astype(jnp.float32) * frequency
    return jnp.concatenate(
        [jnp.sin(first_axis), jnp.cos(first_axis), jnp.sin(second_axis), jnp.cos(second_axis)],
        axis=-1,
    )


def mixture_term(latent, centres):
    scores = (
        jnp.dot(
            latent, centres, precision=lax.Precision.HIGHEST, preferred_element_type=jnp.float32
        )
        - 0.5 * jnp.sum(centres * centres, axis=0)
    ) * latent.shape[-1] ** (-0.5)
    return -jax.nn.logsumexp(scores, axis=-1)


def split_single(rows_in, head_count):
    arrived_rows = rows_in.shape[0]
    block_rows = 512
    return rows_in.reshape(
        (arrived_rows // block_rows, block_rows, head_count, rows_in.shape[1] // head_count)
    )


def split_blocks(key_rows, value_rows, head_count):
    return (split_single(key_rows, head_count), split_single(value_rows, head_count))


def local(
    counts,
    library,
    coords,
    noise,
    decoded_cot,
    prior_cot,
    embed_t,
    w_qkv,
    w_attn_out,
    w_up,
    up_bias,
    w_down,
    w_latent,
    w_decode,
    comp_means,
    norm_params,
):
    gathered = (
        lax.all_gather(embed_t, "blk", axis=0, tiled=True),
        lax.all_gather(w_qkv, "blk", axis=0, tiled=True),
        lax.all_gather(w_attn_out, "blk", axis=0, tiled=True),
        lax.all_gather(w_up, "blk", axis=0, tiled=True),
        lax.all_gather(up_bias, "blk", axis=0, tiled=True),
        lax.all_gather(w_down, "blk", axis=0, tiled=True),
        lax.all_gather(w_latent, "blk", axis=0, tiled=True),
        lax.all_gather(w_decode, "blk", axis=0, tiled=True),
        lax.all_gather(comp_means, "blk", axis=0, tiled=True),
        lax.all_gather(norm_params, "blk", axis=0, tiled=True),
    )
    (
        embedding,
        weight_qkv,
        weight_out,
        weight_up,
        bias_up,
        weight_down,
        weight_latent,
        weight_decode,
        centres,
        norm_table,
    ) = gathered
    head_count = HEADS
    head_width = HEAD_DIM
    scaling = head_width ** (-0.5)
    model_width = embedding.shape[0]
    latent_width = weight_decode.shape[0]
    blk_count = lax.axis_size("blk")
    expression = jnp.log1p(
        counts[0].astype(jnp.float32) * 10000.0 / library[0].astype(jnp.float32)[:, None]
    )
    expression_low = expression.astype(jnp.bfloat16)
    local_cells = expression.shape[0]
    norm_float = norm_table.astype(jnp.float32)
    h_zero = contract_cols(expression_low, embedding) + spatial_code(coords[0], model_width)
    normed_one, norm_one_back = jax.vjp(layer_norm, h_zero, norm_float[:, 0], norm_float[:, 1])
    normed_one_low = normed_one.astype(jnp.bfloat16)
    projected = jnp.dot(normed_one_low, weight_qkv, preferred_element_type=jnp.float32).astype(
        jnp.bfloat16
    )
    queries = projected[:, :model_width].reshape(local_cells, head_count, head_width)
    key_rows = projected[:, model_width : 2 * model_width]
    value_rows = projected[:, 2 * model_width :]
    stat_start = (
        jnp.full((head_count, local_cells), -1e30, jnp.float32),
        jnp.zeros((head_count, local_cells), jnp.float32),
    )
    key_blocks = split_single(lax.all_gather(key_rows, "blk", axis=0, tiled=True), head_count)

    def per_block(status, key_block):
        running_max, running_sum = status
        scores = (
            jnp.einsum("thd,khd->htk", queries, key_block, preferred_element_type=jnp.float32)
            * scaling
        )
        new_max = jnp.maximum(running_max, jnp.max(scores, axis=-1))
        running_sum = running_sum * jnp.exp(running_max - new_max) + jnp.sum(
            jnp.exp(scores - new_max[..., None]), axis=-1
        )
        return ((new_max, running_sum), None)

    result, unused = lax.scan(per_block, stat_start, key_blocks)
    running_max, running_sum = result
    log_total = running_max + jnp.log(running_sum)
    arrived = (
        lax.all_gather(key_rows, "blk", axis=0, tiled=True),
        lax.all_gather(value_rows, "blk", axis=0, tiled=True),
    )
    key_blocks, value_blocks = split_blocks(arrived[0], arrived[1], head_count)

    def per_block(weighted, block_pair):
        scores = (
            jnp.einsum("thd,khd->htk", queries, block_pair[0], preferred_element_type=jnp.float32)
            * scaling
        )
        probs_low = jnp.exp(scores - log_total[..., None]).astype(jnp.bfloat16)
        weighted = weighted + jnp.einsum(
            "htk,khd->htd", probs_low, block_pair[1], preferred_element_type=jnp.float32
        )
        return (weighted, None)

    result, unused = lax.scan(
        per_block,
        jnp.zeros((head_count, local_cells, head_width), jnp.float32),
        (key_blocks, value_blocks),
    )
    attended_cells = jnp.transpose(result, (1, 0, 2))
    attended_low = attended_cells.reshape(local_cells, model_width).astype(jnp.bfloat16)
    h_one = h_zero + jnp.dot(attended_low, weight_out, preferred_element_type=jnp.float32)
    normed_two, norm_two_back = jax.vjp(layer_norm, h_one, norm_float[:, 2], norm_float[:, 3])
    normed_two_low = normed_two.astype(jnp.bfloat16)
    hidden_pre = jnp.dot(
        normed_two_low, weight_up, preferred_element_type=jnp.float32
    ) + bias_up.astype(jnp.float32)
    hidden_act, gelu_back = jax.vjp(jax.nn.gelu, hidden_pre)
    hidden_low = hidden_act.astype(jnp.bfloat16)
    h_two = h_one + jnp.dot(hidden_low, weight_down, preferred_element_type=jnp.float32)
    h_two_low = h_two.astype(jnp.bfloat16)
    latent_pre = jnp.dot(h_two_low, weight_latent, preferred_element_type=jnp.float32)
    spread = jnp.exp(0.5 * latent_pre[:, latent_width:])
    latent = latent_pre[:, :latent_width] + spread * noise[0]
    latent_low = latent.astype(jnp.bfloat16)
    decoded = jnp.dot(latent_low, weight_decode, preferred_element_type=jnp.float32).astype(
        jnp.bfloat16
    )
    prior, prior_back = jax.vjp(mixture_term, latent, centres.astype(jnp.float32))
    out_grad = decoded_cot[0]
    latent_from_decode = contract_cols(out_grad, weight_decode)
    latent_from_prior, centre_grad = prior_back(prior_cot[0])
    latent_total = latent_from_decode + latent_from_prior
    pre_grad = jnp.concatenate(
        [latent_total, latent_total * noise[0] * spread * 0.5], axis=-1
    ).astype(jnp.bfloat16)
    latent_weight_grad = contract_rows(h_two_low, pre_grad)
    h_two_grad = contract_cols(pre_grad, weight_latent)
    down_input = h_two_grad.astype(jnp.bfloat16)
    down_grad = contract_rows(hidden_low, down_input)
    hidden_grad = contract_cols(down_input, weight_down)
    pre_hidden_grad = gelu_back(hidden_grad)[0].astype(jnp.bfloat16)
    up_bias_grad = jnp.sum(pre_hidden_grad.astype(jnp.float32), axis=0)
    up_grad = contract_rows(normed_two_low, pre_hidden_grad)
    normed_two_grad = contract_cols(pre_hidden_grad, weight_up)
    h_one_part, gain_two_grad, shift_two_grad = norm_two_back(normed_two_grad)
    h_one_grad = h_two_grad + h_one_part
    out_input = h_one_grad.astype(jnp.bfloat16)
    attn_out_grad = contract_rows(attended_low, out_input)
    attended_grad = contract_cols(out_input, weight_out).astype(jnp.bfloat16)
    out_heads = attended_grad.reshape(local_cells, head_count, head_width)
    row_delta = jnp.sum(out_heads.astype(jnp.float32) * attended_cells, axis=-1).T
    query_zero = jnp.zeros((head_count, local_cells, head_width), jnp.float32)
    start_back = (query_zero, jnp.zeros((local_cells * blk_count, 2 * model_width), jnp.float32))
    arrived = (
        lax.all_gather(key_rows, "blk", axis=0, tiled=True),
        lax.all_gather(value_rows, "blk", axis=0, tiled=True),
    )
    key_blocks, value_blocks = split_blocks(arrived[0], arrived[1], head_count)
    arrived_rows = arrived[0].shape[0]

    def per_block(query_sum, block_pair):
        scores = (
            jnp.einsum("thd,khd->htk", queries, block_pair[0], preferred_element_type=jnp.float32)
            * scaling
        )
        probs = jnp.exp(scores - log_total[..., None])
        prob_grad = jnp.einsum(
            "thd,khd->htk", out_heads, block_pair[1], preferred_element_type=jnp.float32
        )
        score_grad = (probs * (prob_grad - row_delta[..., None])).astype(jnp.bfloat16)
        query_sum = query_sum + jnp.einsum(
            "htk,khd->htd", score_grad, block_pair[0], preferred_element_type=jnp.float32
        )
        key_part = (
            jnp.einsum("htk,thd->khd", score_grad, queries, preferred_element_type=jnp.float32)
            * scaling
        )
        value_part = jnp.einsum(
            "htk,thd->khd",
            probs.astype(jnp.bfloat16),
            out_heads,
            preferred_element_type=jnp.float32,
        )
        block_rows = key_part.shape[0]
        return (
            query_sum,
            jnp.concatenate(
                [key_part.reshape(block_rows, -1), value_part.reshape(block_rows, -1)], axis=-1
            ),
        )

    query_total, stacked = lax.scan(per_block, start_back[0], (key_blocks, value_blocks))
    stacked = stacked.reshape(arrived_rows, stacked.shape[-1])
    carried_back = (query_total, stacked)
    query_total = carried_back[0]
    own_pairs = lax.psum_scatter(
        carried_back[1].astype(jnp.bfloat16), "blk", scatter_dimension=0, tiled=True
    ).astype(jnp.float32)
    query_rows = jnp.transpose(query_total * scaling, (1, 0, 2)).reshape(local_cells, model_width)
    projected_grad = jnp.concatenate([query_rows, own_pairs], axis=-1).astype(jnp.bfloat16)
    qkv_grad = contract_rows(normed_one_low, projected_grad)
    normed_one_grad = contract_cols(projected_grad, weight_qkv)
    h_zero_part, gain_one_grad, shift_one_grad = norm_one_back(normed_one_grad)
    h_zero_low = (h_one_grad + h_zero_part).astype(jnp.bfloat16)
    expr_grad = jnp.dot(h_zero_low, embedding, preferred_element_type=jnp.float32)
    norm_grad = jnp.stack([gain_one_grad, shift_one_grad, gain_two_grad, shift_two_grad], axis=0).T
    centre_grad = centre_grad.T.T
    embed_slot = contract_rows(h_zero_low, expression_low)
    decode_slot = contract_rows(latent_low, out_grad)
    block_parts = (
        lax.psum_scatter(
            embed_slot.astype(jnp.bfloat16), "blk", scatter_dimension=0, tiled=True
        ).astype(jnp.float32),
        lax.psum_scatter(
            qkv_grad.astype(jnp.bfloat16), "blk", scatter_dimension=0, tiled=True
        ).astype(jnp.float32),
        lax.psum_scatter(
            attn_out_grad.astype(jnp.bfloat16), "blk", scatter_dimension=0, tiled=True
        ).astype(jnp.float32),
        lax.psum_scatter(
            up_grad.astype(jnp.bfloat16), "blk", scatter_dimension=0, tiled=True
        ).astype(jnp.float32),
        lax.psum_scatter(
            up_bias_grad.astype(jnp.bfloat16), "blk", scatter_dimension=0, tiled=True
        ).astype(jnp.float32),
        lax.psum_scatter(
            down_grad.astype(jnp.bfloat16), "blk", scatter_dimension=0, tiled=True
        ).astype(jnp.float32),
        lax.psum_scatter(
            latent_weight_grad.astype(jnp.bfloat16), "blk", scatter_dimension=0, tiled=True
        ).astype(jnp.float32),
        lax.psum_scatter(
            decode_slot.astype(jnp.bfloat16), "blk", scatter_dimension=0, tiled=True
        ).astype(jnp.float32),
        lax.psum_scatter(
            centre_grad.astype(jnp.bfloat16), "blk", scatter_dimension=0, tiled=True
        ).astype(jnp.float32),
        lax.psum_scatter(
            norm_grad.astype(jnp.bfloat16), "blk", scatter_dimension=0, tiled=True
        ).astype(jnp.float32),
    )
    summed = (
        lax.psum(block_parts[0].astype(jnp.bfloat16), "slide").astype(jnp.float32),
        lax.psum(block_parts[1].astype(jnp.bfloat16), "slide").astype(jnp.float32),
        lax.psum(block_parts[2].astype(jnp.bfloat16), "slide").astype(jnp.float32),
        lax.psum(block_parts[3].astype(jnp.bfloat16), "slide").astype(jnp.float32),
        lax.psum(block_parts[4].astype(jnp.bfloat16), "slide").astype(jnp.float32),
        lax.psum(block_parts[5].astype(jnp.bfloat16), "slide").astype(jnp.float32),
        lax.psum(block_parts[6].astype(jnp.bfloat16), "slide").astype(jnp.float32),
        lax.psum(block_parts[7].astype(jnp.bfloat16), "slide").astype(jnp.float32),
        lax.psum(block_parts[8].astype(jnp.bfloat16), "slide").astype(jnp.float32),
        lax.psum(block_parts[9].astype(jnp.bfloat16), "slide").astype(jnp.float32),
    )
    embed_out = summed[0]
    decode_out = summed[7]
    return (
        decoded[None],
        prior[None],
        expr_grad[None],
        embed_out,
        summed[1],
        summed[2],
        summed[3],
        summed[4],
        summed[5],
        summed[6],
        decode_out,
        summed[8],
        summed[9],
    )


def peers(offset, count):
    return [(place, place ^ offset) for place in range(count)]


def swap(pieces):
    count = len(pieces)
    return [pieces[0]] + [
        lax.ppermute(pieces[k], "slide", peers(k, count)) for k in range(1, count)
    ]


def share_halves(rows):
    half = rows.shape[0] // 2
    upper, lower = rows[:half], rows[half:]
    upper_x = lax.ppermute(upper, "slide", peers(1, 4))
    lower_y = lax.ppermute(lower, "slide", peers(2, 4))
    uppers = lax.ppermute(jnp.concatenate([upper, upper_x], axis=0), "slide", peers(2, 4))
    lowers = lax.ppermute(jnp.concatenate([lower, lower_y], axis=0), "slide", peers(1, 4))
    return [rows, upper_x, lower_y, uppers, lowers]


def share(rows, count):
    return swap([rows] * count)


def after(value, *earlier):
    return lax.optimization_barrier((value,) + earlier)[0]


def in_order(pieces, me, axis):
    stacked = jnp.stack(pieces)
    return jnp.concatenate(
        [
            lax.dynamic_index_in_dim(stacked, jnp.bitwise_xor(me, k), 0, keepdims=False)
            for k in range(len(pieces))
        ],
        axis=axis,
    )


def exact_dot(former, latter, left, right):
    return lax.dot_general(
        former,
        latter,
        (((left,), (right,)), ((), ())),
        precision=lax.Precision.HIGHEST,
        preferred_element_type=jnp.float32,
    )


def lowered(partials):
    return [partials[0]] + [piece.astype(jnp.bfloat16) for piece in partials[1:]]


def collect(partials):
    arrived = swap(partials)
    total = arrived[0]
    for piece in arrived[1:]:
        total = total + piece.astype(jnp.float32)
    return total


def gather_blk(piece, axis=0):
    return lax.all_gather(piece, "blk", axis=axis, tiled=True)


def scatter_blk(piece, axis=0):
    return lax.psum_scatter(piece, "blk", scatter_dimension=axis, tiled=True)


def to_core(rows):
    count = lax.axis_size("blk")
    return lax.ppermute(rows, "blk", [(place, place ^ 1) for place in range(count)])


def to_chip(rows, offset):
    count = lax.axis_size("blk")
    return lax.ppermute(rows, "blk", [(place, place ^ (2 * offset)) for place in range(count)])


def split_rows(rows, count):
    height = rows.shape[0] // count
    return [rows[k * height : (k + 1) * height] for k in range(count)]


ROWS = 432
STEP = 864
TALL = 1728
WIDE = 3456
CHUNKS = 2
SMALL = 16
COST = pl.CostEstimate(flops=0, bytes_accessed=0, transcendentals=0)


def expression_kernel(count, quarter, genes, me_ref, library_ref, counts_ref, *rest):
    outs, buffers, sems = rest[:count], rest[count], rest[count + 1]
    me = me_ref[0]
    tail = genes - (count - 1) * quarter
    library = library_ref[...].astype(jnp.float32)

    def copy(k, rows):
        start = pl.multiple_of(jnp.bitwise_xor(me, k) * quarter, 8)
        return pltpu.make_async_copy(
            counts_ref.at[pl.ds(start, rows), 0, :],
            buffers.at[k, pl.ds(0, rows), :],
            sems.at[k],
        )

    def each(k, act):
        last = jnp.bitwise_xor(me, k) == count - 1

        @pl.when(last)
        def _():
            act(copy(k, tail))

        @pl.when(jnp.logical_not(last))
        def _():
            act(copy(k, quarter))

    order = list(range(1, count)) + [0]
    for k in order:
        each(k, lambda one: one.start())
    for k in order:
        each(k, lambda one: one.wait())
        have = genes - jnp.bitwise_xor(me, k) * quarter

        @pl.loop(0, quarter // ROWS)
        def _(step):
            start = pl.multiple_of(step * ROWS, ROWS)
            values = buffers[k, pl.ds(start, ROWS), :].astype(jnp.float32)
            values = jnp.log1p(values * 10000.0 / library)
            row = start + lax.broadcasted_iota(jnp.int32, values.shape, 0)
            outs[k][pl.ds(start, ROWS), :] = jnp.where(row < have, values, 0.0).astype(jnp.bfloat16)


def expression_parts(counts, library, me, count, quarter):
    genes = counts.shape[2]
    cells = counts.shape[1]
    part = jax.ShapeDtypeStruct((quarter, cells), jnp.bfloat16)
    return pl.pallas_call(
        functools.partial(expression_kernel, count, quarter, genes),
        out_shape=[part] * count,
        in_specs=[
            pl.BlockSpec(memory_space=pltpu.SMEM),
            pl.BlockSpec(memory_space=pltpu.VMEM),
            pl.BlockSpec(memory_space=pltpu.HBM),
        ],
        out_specs=[pl.BlockSpec(memory_space=pltpu.VMEM)] * count,
        scratch_shapes=[
            pltpu.VMEM((count, quarter, cells), jnp.int32),
            pltpu.SemaphoreType.DMA((count,)),
        ],
        compiler_params=pltpu.CompilerParams(vmem_limit_bytes=40 * 2**20),
        cost_estimate=COST,
        name="expression",
    )(me.reshape(1), library, jnp.transpose(counts, (2, 0, 1)))


def spread_kernel(count, quarter, genes, me_ref, *rest):
    pieces, out, held, wide, sems_in, sems_out = rest[:count], *rest[count:]
    me = me_ref[0]
    tail = genes - (count - 1) * quarter

    def arrive(k):
        return pltpu.make_async_copy(pieces[k], held.at[k], sems_in.at[k])

    def leave(k):
        rows = tail if k == count - 1 else quarter
        return pltpu.make_async_copy(
            wide.at[k, pl.ds(0, rows), :], out.at[pl.ds(k * quarter, rows), 0, :], sems_out.at[k]
        )

    for k in range(count):
        arrive(k).start()
    for k in range(count):
        arrive(k).wait()
    for k in range(count):
        source = jnp.bitwise_xor(me, k)

        @pl.loop(0, quarter // ROWS)
        def _(step):
            rows = pl.ds(pl.multiple_of(step * ROWS, ROWS), ROWS)
            wide[k, rows, :] = held[source, rows, :].astype(jnp.float32)

        leave(k).start()
    for k in range(count):
        leave(k).wait()


def spread_parts(pieces, me, genes):
    count = len(pieces)
    quarter, cells = pieces[0].shape
    out = pl.pallas_call(
        functools.partial(spread_kernel, count, quarter, genes),
        out_shape=jax.ShapeDtypeStruct((genes, 1, cells), jnp.float32),
        in_specs=[pl.BlockSpec(memory_space=pltpu.SMEM)]
        + [pl.BlockSpec(memory_space=pl.ANY)] * count,
        out_specs=pl.BlockSpec(memory_space=pltpu.HBM),
        scratch_shapes=[
            pltpu.VMEM((count, quarter, cells), jnp.bfloat16),
            pltpu.VMEM((count, quarter, cells), jnp.float32),
            pltpu.SemaphoreType.DMA((count,)),
            pltpu.SemaphoreType.DMA((count,)),
        ],
        compiler_params=pltpu.CompilerParams(vmem_limit_bytes=40 * 2**20),
        cost_estimate=COST,
        name="spread",
    )(me.reshape(1), *pieces)
    return jnp.transpose(out, (1, 2, 0))


def join_kernel(count, me_ref, *rest):
    pieces, out, held, sems = rest[:count], *rest[count:]
    slot = pl.program_id(0)

    def arrive(k):
        rows = pl.ds(0, held.shape[1])
        return pltpu.make_async_copy(pieces[k].at[rows, :], held.at[k], sems.at[k])

    @pl.when(slot == 0)
    def _():
        for k in range(count):
            arrive(k).start()
        for k in range(count):
            arrive(k).wait()

    source = jnp.bitwise_xor(me_ref[0], slot)

    @pl.loop(0, out.shape[0] // ROWS)
    def _(step):
        rows = pl.ds(pl.multiple_of(step * ROWS, ROWS), ROWS)
        out[rows, :] = held[source, rows, :].astype(out.dtype)


def join_parts(pieces, me, quarter, genes, dtype):
    count = len(pieces)
    cells = pieces[0].shape[1]
    return pl.pallas_call(
        functools.partial(join_kernel, count),
        grid=(count,),
        out_shape=jax.ShapeDtypeStruct((genes, cells), dtype),
        in_specs=[pl.BlockSpec(memory_space=pltpu.SMEM)]
        + [pl.BlockSpec(memory_space=pl.ANY)] * count,
        out_specs=pl.BlockSpec((quarter, cells), lambda slot: (slot, 0)),
        scratch_shapes=[
            pltpu.VMEM((count, quarter, cells), jnp.bfloat16),
            pltpu.SemaphoreType.DMA((count,)),
        ],
        compiler_params=pltpu.CompilerParams(vmem_limit_bytes=40 * 2**20),
        cost_estimate=COST,
        name="join",
    )(me.reshape(1), *pieces)


def order_kernel(count, me_ref, *refs):
    pieces, out, sems = refs[:count], refs[-2], refs[-1]
    height = pieces[0].shape[0]

    def move(k):
        first = pl.multiple_of(jnp.bitwise_xor(me_ref[0], k) * height, height)
        return pltpu.make_async_copy(pieces[k], out.at[pl.ds(first, height), :], sems.at[k])

    for k in range(count):
        move(k).start()
    for k in range(count):
        move(k).wait()


def order_rows(pieces, me):
    count = len(pieces)
    height, width = pieces[0].shape
    return pl.pallas_call(
        functools.partial(order_kernel, count),
        out_shape=jax.ShapeDtypeStruct((count * height, width), pieces[0].dtype),
        in_specs=[pl.BlockSpec(memory_space=pltpu.SMEM)]
        + [pl.BlockSpec(memory_space=pl.ANY)] * count,
        out_specs=pl.BlockSpec(memory_space=pltpu.VMEM),
        scratch_shapes=[pltpu.SemaphoreType.DMA((count,))],
        cost_estimate=COST,
        name="order_rows",
    )(me.reshape(1), *pieces)


def turn_kernel(count, *refs):
    out = refs[-1]
    for k in range(count):
        height = refs[k].shape[1]
        out[k * height : (k + 1) * height, :] = jnp.transpose(refs[k][...])


def turn_parts(parts):
    count = len(parts)
    quarter, cells = parts[0].shape
    return pl.pallas_call(
        functools.partial(turn_kernel, count),
        grid=(quarter // WIDE,),
        out_shape=jax.ShapeDtypeStruct((count * cells, quarter), jnp.bfloat16),
        in_specs=[pl.BlockSpec((WIDE, cells), lambda step: (step, 0))] * count,
        out_specs=pl.BlockSpec((count * cells, WIDE), lambda step: (0, step)),
        compiler_params=pltpu.CompilerParams(vmem_limit_bytes=40 * 2**20),
        cost_estimate=COST,
        name="turn_parts",
    )(*parts)


def finish_kernel(count, quarter, mean_cols, folds, me_ref, *refs):
    pieces = refs[:count]
    out, norm, means, bias, held, sems = refs[count:]
    slot = pl.program_id(0)

    def arrive(k):
        place = jnp.bitwise_xor(me_ref[0], k)
        return pltpu.make_async_copy(pieces[k], held.at[place], sems.at[k])

    @pl.when(slot == 0)
    def _():
        for k in range(count):
            arrive(k).start()
        for k in range(count):
            arrive(k).wait()
        small = [held[q, quarter:, :].astype(jnp.float32) for q in range(count)]
        total = sum(small[1:], small[0])
        norm[...] = total[:4, :]
        width = means.shape[1]
        for k in range(folds):
            means[k * mean_cols : (k + 1) * mean_cols, :] = total[
                4 : 4 + mean_cols, k * width : (k + 1) * width
            ]
        bias[...] = jnp.concatenate(
            [one[4 + mean_cols : 5 + mean_cols, :] for one in small], axis=0
        )

    out[...] = held[slot, :quarter, :].astype(out.dtype)


def finish(pieces, me, quarter, genes, mean_cols, folds):
    count = len(pieces)
    height, cells = pieces[0].shape
    return pl.pallas_call(
        functools.partial(finish_kernel, count, quarter, mean_cols, folds),
        grid=(count,),
        out_shape=[
            jax.ShapeDtypeStruct((genes, cells), jnp.float32),
            jax.ShapeDtypeStruct((4, cells), jnp.float32),
            jax.ShapeDtypeStruct((folds * mean_cols, cells // folds), jnp.float32),
            jax.ShapeDtypeStruct((count, cells), jnp.float32),
        ],
        in_specs=[pl.BlockSpec(memory_space=pltpu.SMEM)]
        + [pl.BlockSpec(memory_space=pl.ANY)] * count,
        out_specs=[
            pl.BlockSpec((quarter, cells), lambda slot: (slot, 0)),
            pl.BlockSpec((4, cells), lambda slot: (0, 0)),
            pl.BlockSpec((folds * mean_cols, cells // folds), lambda slot: (0, 0)),
            pl.BlockSpec((count, cells), lambda slot: (0, 0)),
        ],
        scratch_shapes=[
            pltpu.VMEM((count, height, cells), jnp.bfloat16),
            pltpu.SemaphoreType.DMA((count,)),
        ],
        compiler_params=pltpu.CompilerParams(vmem_limit_bytes=40 * 2**20),
        cost_estimate=COST,
        name="finish",
    )(me.reshape(1), *pieces)


def scores_kernel(rows, table, *outs):
    product = jnp.dot(rows[...], table[...], preferred_element_type=jnp.float32)
    height = outs[0].shape[0]
    for k in range(len(outs)):
        outs[k][...] = product[k * height : (k + 1) * height, :].astype(outs[k].dtype)


def embed_cells(rows, table, count):
    height, quarter = rows.shape
    width = table.shape[1]
    block = math.gcd(width, 512)
    return pl.pallas_call(
        scores_kernel,
        grid=(width // block,),
        out_shape=[
            jax.ShapeDtypeStruct((height // count, width), jnp.float32 if k == 0 else jnp.bfloat16)
            for k in range(count)
        ],
        in_specs=[
            pl.BlockSpec((height, quarter), lambda step: (0, 0)),
            pl.BlockSpec((quarter, block), lambda step: (0, step)),
        ],
        out_specs=[pl.BlockSpec((height // count, block), lambda step: (0, step))] * count,
        compiler_params=pltpu.CompilerParams(vmem_limit_bytes=58 * 2**20),
        cost_estimate=COST,
        name="embed_cells",
    )(rows, table)


def latents_kernel(count, table, *refs):
    cots, outs, total = refs[:count], refs[count:-1], refs[-1]
    step = pl.program_id(0)
    product = jnp.dot(
        table[...],
        jnp.concatenate([one[...] for one in cots], axis=1),
        preferred_element_type=jnp.float32,
    )

    @pl.when(step == 0)
    def _():
        total[...] = product

    @pl.when(step > 0)
    def _():
        total[...] += product

    @pl.when(step == pl.num_programs(0) - 1)
    def _():
        cells = outs[0].shape[0]
        for k in range(count):
            outs[k][...] = jnp.transpose(total[:, k * cells : (k + 1) * cells]).astype(
                outs[k].dtype
            )


def cots_to_latents(cots, table):
    count = len(cots)
    width, quarter = table.shape
    cells = cots[0].shape[1]
    return pl.pallas_call(
        functools.partial(latents_kernel, count),
        grid=(quarter // WIDE,),
        out_shape=[
            jax.ShapeDtypeStruct((cells, width), jnp.float32 if k == 0 else jnp.bfloat16)
            for k in range(count)
        ],
        in_specs=[pl.BlockSpec((width, WIDE), lambda step: (0, step))]
        + [pl.BlockSpec((WIDE, cells), lambda step: (step, 0))] * count,
        out_specs=[pl.BlockSpec((cells, width), lambda step: (0, 0))] * count,
        scratch_shapes=[pltpu.VMEM((width, count * cells), jnp.float32)],
        compiler_params=pltpu.CompilerParams(vmem_limit_bytes=40 * 2**20),
        cost_estimate=COST,
        name="cots_to_latents",
    )(table, *cots)


def gelu_slope(rows):
    scale = math.sqrt(2.0 / math.pi)
    squares = rows * rows
    bent = jnp.tanh(scale * (rows + 0.044715 * (squares * rows)))
    inner = scale * (1.0 + (3.0 * 0.044715) * squares)
    return 0.5 * (1.0 + bent) + 0.5 * rows * (1.0 - bent * bent) * inner


UNITS = 256


def feed_forward_kernel(count, up, bias, down, *refs):
    parts, stacked, total = refs[:count], refs[-2], refs[-1]
    pre, hidden, *outs = refs[count:-2]
    cells = parts[0].shape[0]
    step = pl.program_id(0)

    @pl.when(step == 0)
    def _():
        for k in range(count):
            stacked[k * cells : (k + 1) * cells, :] = parts[k][...]

    rows = jnp.dot(stacked[...], up[...], preferred_element_type=jnp.float32) + bias[...]
    pre[...] = rows
    bent = jnp.tanh(math.sqrt(2.0 / math.pi) * (rows + 0.044715 * (rows * rows * rows)))
    low = (rows * (0.5 * (1.0 + bent))).astype(jnp.bfloat16)
    hidden[...] = low
    product = jnp.dot(low, down[...], preferred_element_type=jnp.float32)

    @pl.when(step == 0)
    def _():
        total[...] = product

    @pl.when(step > 0)
    def _():
        total[...] += product

    @pl.when(step == pl.num_programs(0) - 1)
    def _():
        for k in range(count):
            outs[k][...] = total[k * cells : (k + 1) * cells, :].astype(outs[k].dtype)


def feed_forward(parts, up, bias, down):
    count = len(parts)
    cells, width = parts[0].shape
    units = down.shape[0]
    rows = count * cells
    return pl.pallas_call(
        functools.partial(feed_forward_kernel, count),
        grid=(units // UNITS,),
        out_shape=[
            jax.ShapeDtypeStruct((rows, units), jnp.float32),
            jax.ShapeDtypeStruct((rows, units), jnp.bfloat16),
        ]
        + [
            jax.ShapeDtypeStruct((cells, width), jnp.float32 if k == 0 else jnp.bfloat16)
            for k in range(count)
        ],
        in_specs=[
            pl.BlockSpec((width, UNITS), lambda step: (0, step)),
            pl.BlockSpec((1, UNITS), lambda step: (0, step)),
            pl.BlockSpec((UNITS, width), lambda step: (step, 0)),
        ]
        + [pl.BlockSpec((cells, width), lambda step: (0, 0))] * count,
        out_specs=[pl.BlockSpec((rows, UNITS), lambda step: (0, step))] * 2
        + [pl.BlockSpec((cells, width), lambda step: (0, 0))] * count,
        scratch_shapes=[
            pltpu.VMEM((rows, width), jnp.bfloat16),
            pltpu.VMEM((rows, width), jnp.float32),
        ],
        compiler_params=pltpu.CompilerParams(vmem_limit_bytes=48 * 2**20),
        cost_estimate=COST,
        name="feed_forward",
    )(up, bias, down, *parts)


def feed_back_kernel(count, latent, down, up, pre, *refs):
    parts = refs[:count]
    own, down_input, pre_grad, bias, *outs = refs[count:]
    cells = own.shape[0]
    width = own.shape[1]
    h_grad = jnp.dot(
        jnp.concatenate([part[:, : latent.shape[0]] for part in parts], axis=0),
        latent[...],
        preferred_element_type=jnp.float32,
    )
    own[...] = h_grad[:cells, :]
    down_input[...] = h_grad.astype(jnp.bfloat16)
    step = 256
    for start in range(0, pre.shape[1], step):
        columns = slice(start, start + step)
        hidden_grad = lax.dot_general(
            down_input[...],
            down[columns, :],
            (((1,), (1,)), ((), ())),
            preferred_element_type=jnp.float32,
        )
        low = (hidden_grad * gelu_slope(pre[:, columns])).astype(jnp.bfloat16)
        pre_grad[:, columns] = low
        bias[:, columns] = jnp.sum(low.astype(jnp.float32), axis=0, keepdims=True)
    product = lax.dot_general(
        pre_grad[...], up[...], (((1,), (1,)), ((), ())), preferred_element_type=jnp.float32
    )
    for k in range(count):
        outs[k][...] = product[k * cells : (k + 1) * cells, :].astype(outs[k].dtype)


def feed_back(parts, latent, down, up, pre):
    count = len(parts)
    cells = parts[0].shape[0]
    width = latent.shape[1]
    units = pre.shape[1]

    def whole(array):
        return pl.BlockSpec(array.shape, lambda step: (0,) * len(array.shape))

    shapes = [
        jax.ShapeDtypeStruct((cells, width), jnp.float32),
        jax.ShapeDtypeStruct((count * cells, width), jnp.bfloat16),
        jax.ShapeDtypeStruct((count * cells, units), jnp.bfloat16),
        jax.ShapeDtypeStruct((1, units), jnp.float32),
    ] + [
        jax.ShapeDtypeStruct((cells, width), jnp.float32 if k == 0 else jnp.bfloat16)
        for k in range(count)
    ]
    operands = [latent, down, up, pre, *parts]
    return pl.pallas_call(
        functools.partial(feed_back_kernel, count),
        grid=(1,),
        out_shape=shapes,
        in_specs=[whole(one) for one in operands[:2]]
        + [pl.BlockSpec((width, units), lambda step: (0, 0))]
        + [whole(one) for one in operands[3:]],
        out_specs=[whole(one) for one in shapes],
        compiler_params=pltpu.CompilerParams(vmem_limit_bytes=56 * 2**20),
        cost_estimate=COST,
        name="feed_back",
    )(*operands)


def decode_kernel(count, table, *refs):
    rows, outs = refs[:count], refs[count:]
    cells = rows[0].shape[0]
    product = jnp.dot(
        jnp.concatenate([one[...] for one in rows], axis=0),
        table[...],
        preferred_element_type=jnp.float32,
    ).astype(jnp.bfloat16)
    for k in range(count):
        outs[k][...] = jnp.transpose(product[k * cells : (k + 1) * cells, :])


def decode_genes(latents, table):
    count = len(latents)
    cells = latents[0].shape[0]
    width, quarter = table.shape
    last = latents[0].shape[1] // width - 1
    return pl.pallas_call(
        functools.partial(decode_kernel, count),
        grid=(1,),
        out_shape=[jax.ShapeDtypeStruct((quarter, cells), jnp.bfloat16)] * count,
        in_specs=[pl.BlockSpec((width, quarter), lambda step: (0, 0))]
        + [pl.BlockSpec((cells, width), lambda step: (0, last))] * count,
        out_specs=[pl.BlockSpec((quarter, cells), lambda step: (0, 0))] * count,
        compiler_params=pltpu.CompilerParams(vmem_limit_bytes=40 * 2**20),
        cost_estimate=COST,
        name="decode_genes",
    )(table, *latents)


def chip_offsets(chips):
    order = [0]
    bit = chips // 2
    while bit:
        order = order + [one + bit for one in order]
        bit //= 2
    return order


def last_kernel(count, first, offsets, places, normed, projected, both, *refs):
    pre_grads, cots = refs[:count], refs[count : 2 * count]
    kept, sent, turned = refs[2 * count :]
    me, place = places[0], places[1]
    cells = cots[0].shape[0]
    width = normed.shape[1]
    block = kept.shape[0] // len(offsets)

    def by_offset(first):
        return jnp.concatenate(
            [
                both[
                    pl.ds(pl.multiple_of(jnp.bitwise_xor(me, k) * cells, cells), cells),
                    first : first + width,
                ]
                for k in range(count)
            ],
            axis=0,
        )

    spot = 0
    for group, (rows, columns) in enumerate(
        (
            (normed[...], [projected[k] for k in range(projected.shape[0])]),
            (by_offset(0), [jnp.concatenate([one[:, first:] for one in cots], axis=0)]),
            (by_offset(width), [jnp.concatenate([one[...] for one in pre_grads], axis=0)]),
        )
    ):
        turned[group] = jnp.transpose(rows)
        for one in columns:
            size = one.shape[1]
            for out, core in ((kept, place % 2), (sent, 1 - place % 2)):
                owners = [jnp.bitwise_xor(place // 2, k) * 2 + core for k in offsets]
                ordered = jnp.concatenate(
                    [
                        turned[group, pl.ds(pl.multiple_of(owner * block, block), block), :]
                        for owner in owners
                    ],
                    axis=0,
                )
                out[:, spot : spot + size] = jnp.dot(
                    ordered, one, preferred_element_type=jnp.float32
                ).astype(out.dtype)
            spot += size


def last_products(normed, projected, pre_grads, both, cots, first, me, place):
    count = len(cots)
    height = normed.shape[1]
    offsets = chip_offsets(lax.axis_size("blk") // 2)
    width = projected.shape[0] * projected.shape[2] + 2 * pre_grads[0].shape[1]
    return pl.pallas_call(
        functools.partial(last_kernel, count, first, offsets),
        out_shape=[
            jax.ShapeDtypeStruct((height // 2, width), jnp.float32),
            jax.ShapeDtypeStruct((height // 2, width), jnp.bfloat16),
        ],
        in_specs=[pl.BlockSpec(memory_space=pltpu.SMEM)]
        + [pl.BlockSpec(memory_space=pltpu.VMEM)] * (3 + 2 * count),
        out_specs=[pl.BlockSpec(memory_space=pltpu.VMEM)] * 2,
        scratch_shapes=[pltpu.VMEM((3, height, normed.shape[0]), jnp.bfloat16)],
        compiler_params=pltpu.CompilerParams(vmem_limit_bytes=40 * 2**20),
        cost_estimate=COST,
        name="last_products",
    )(jnp.stack([me, place]), normed, projected, both, *pre_grads, *cots)


def half_kernel(kept, other, stay, go):
    height = stay.shape[0]
    stay[...] = kept[:height, :] + other[:height, :].astype(jnp.float32)
    go[...] = (kept[height:, :] + other[height:, :].astype(jnp.float32)).astype(go.dtype)


def merge_half(kept, other):
    height, width = kept.shape
    return pl.pallas_call(
        half_kernel,
        out_shape=[
            jax.ShapeDtypeStruct((height // 2, width), jnp.float32),
            jax.ShapeDtypeStruct((height // 2, width), jnp.bfloat16),
        ],
        in_specs=[pl.BlockSpec(memory_space=pltpu.VMEM)] * 2,
        out_specs=[pl.BlockSpec(memory_space=pltpu.VMEM)] * 2,
        compiler_params=pltpu.CompilerParams(vmem_limit_bytes=40 * 2**20),
        cost_estimate=COST,
        name="merge_half",
    )(kept, other)


def pair_kernel(count, *refs):
    parts, out = refs[:count], refs[-1]
    width = out.shape[2]
    for j in range(out.shape[0] // count):
        for k in range(count):
            out[j * count + k] = parts[k][:, j * width : (j + 1) * width]


def pair_up(parts, pairs):
    count = len(parts)
    cells, width = parts[0].shape
    return pl.pallas_call(
        functools.partial(pair_kernel, count),
        out_shape=jax.ShapeDtypeStruct((pairs * count, cells, width // pairs), parts[0].dtype),
        in_specs=[pl.BlockSpec(memory_space=pltpu.VMEM)] * count,
        out_specs=pl.BlockSpec(memory_space=pltpu.VMEM),
        cost_estimate=COST,
        name="pair_up",
    )(*parts)


def assemble_kernel(count, sizes, me_ref, *refs):
    early, parts = refs[:5], refs[5 : 5 + count]
    down, up, qkv, attn, latent, decode, middle, last, sems = refs[5 + count :]
    blocks, pairs, pair, quarter, half = sizes
    me = me_ref[0]
    rows, width = attn.shape
    cut = rows // 2
    upper, lower = pl.ds(0, cut), pl.ds(cut, cut)
    ours, upper_x, lower_y, uppers, lowers = early
    moves = [
        (ours, middle.at[me]),
        (upper_x, middle.at[jnp.bitwise_xor(me, 1), upper, :]),
        (lower_y, middle.at[jnp.bitwise_xor(me, 2), lower, :]),
        (uppers.at[upper, :], middle.at[jnp.bitwise_xor(me, 2), upper, :]),
        (uppers.at[lower, :], middle.at[jnp.bitwise_xor(me, 3), upper, :]),
        (lowers.at[upper, :], middle.at[jnp.bitwise_xor(me, 1), lower, :]),
        (lowers.at[lower, :], middle.at[jnp.bitwise_xor(me, 3), lower, :]),
    ] + [(parts[k], last.at[jnp.bitwise_xor(me, k)]) for k in range(count)]
    copies = [
        pltpu.make_async_copy(source, target, sems.at[k])
        for k, (source, target) in enumerate(moves)
    ]
    for one in copies:
        one.start()
    for one in copies:
        one.wait()
    part = width // count
    ff = up.shape[1] // (count * blocks)
    latents, genes = decode.shape

    def piece(array, q, spot, size):
        return array[q, :, spot : spot + size].astype(jnp.float32)

    for q in range(count):
        down[q * rows : (q + 1) * rows, :] = piece(middle, q, 0, width)
        spot = width
        for b in range(blocks):
            up[:, (b * count + q) * ff : (b * count + q + 1) * ff] = piece(middle, q, spot, ff)
            spot += ff
        for side in range(2):
            first = q * quarter + side * half
            size = min(half, quarter - side * half, genes - first)
            if size > 0:
                decode[:, first : first + size] = middle[
                    q, side * latents : (side + 1) * latents, spot : spot + size
                ].astype(jnp.float32)
        spot = 0
        for j in range(pairs):
            for t in range(3):
                first = t * width + q * part + j * pair
                qkv[:, first : first + pair] = piece(last, q, spot, pair)
                spot += pair
        for out in (attn, latent):
            out[:, q * part : (q + 1) * part] = piece(last, q, spot, part)
            spot += part


def assemble(early, last, me, genes, quarter, half, latents, blocks, pairs, pair):
    count = len(last)
    rows = last[0].shape[0]
    width = blocks * rows
    shapes = [
        (count * rows, width),
        (rows, count * width),
        (rows, 3 * width),
        (rows, width),
        (rows, width),
        (latents, genes),
    ]
    return pl.pallas_call(
        functools.partial(assemble_kernel, count, (blocks, pairs, pair, quarter, half)),
        out_shape=[jax.ShapeDtypeStruct(shape, jnp.float32) for shape in shapes],
        in_specs=[pl.BlockSpec(memory_space=pltpu.SMEM)]
        + [pl.BlockSpec(memory_space=pl.ANY)] * (5 + count),
        out_specs=[pl.BlockSpec(memory_space=pltpu.VMEM)] * len(shapes),
        scratch_shapes=[
            pltpu.VMEM((count,) + early[0].shape, jnp.bfloat16),
            pltpu.VMEM((count,) + last[0].shape, jnp.bfloat16),
            pltpu.SemaphoreType.DMA((7 + count,)),
        ],
        compiler_params=pltpu.CompilerParams(vmem_limit_bytes=48 * 2**20),
        cost_estimate=COST,
        name="assemble",
    )(me.reshape(1), *early, *last)


def genes_kernel(count, table, *refs):
    rows, outs, stacked = refs[:count], refs[count : 2 * count], refs[-1]
    cells = rows[0].shape[0]

    @pl.when(pl.program_id(0) == 0)
    def _():
        for k in range(count):
            stacked[:, k * cells : (k + 1) * cells] = jnp.transpose(rows[k][...])

    product = jnp.dot(table[...], stacked[...], preferred_element_type=jnp.float32)
    for k in range(count):
        outs[k][...] = product[:, k * cells : (k + 1) * cells].astype(outs[k].dtype)


def cells_to_genes(table, rows, quarter):
    count = len(rows)
    cells, width = rows[0].shape
    return pl.pallas_call(
        functools.partial(genes_kernel, count),
        grid=(quarter // TALL,),
        out_shape=[jax.ShapeDtypeStruct((quarter, cells), jnp.bfloat16)] * count,
        in_specs=[pl.BlockSpec((TALL, width), lambda step: (step, 0))]
        + [pl.BlockSpec((cells, width), lambda step: (0, 0))] * count,
        out_specs=[pl.BlockSpec((TALL, cells), lambda step: (step, 0))] * count,
        scratch_shapes=[pltpu.VMEM((width, count * cells), jnp.bfloat16)],
        compiler_params=pltpu.CompilerParams(vmem_limit_bytes=58 * 2**20),
        cost_estimate=COST,
        name="cells_to_genes",
    )(table, *rows)


def embed_kernel(count, *refs):
    parts, rows = refs[:count], refs[count : 2 * count]
    small, out, stacked, results, sems = refs[2 * count :]
    steps = parts[0].shape[0] // STEP
    height = rows[0].shape[0]
    blocks, _, block = out.shape
    for k in range(count):
        stacked[k * height : (k + 1) * height, :] = rows[k][...]

    def leave(slot, step):
        start = pl.multiple_of(step * STEP, STEP)
        return pltpu.make_async_copy(
            results.at[slot], out.at[:, pl.ds(start, STEP), :], sems.at[slot]
        )

    last = pltpu.make_async_copy(
        small, out.at[:, pl.ds(steps * STEP, small.shape[1]), :], sems.at[2]
    )
    last.start()

    @pl.loop(0, steps)
    def _(step):
        slot = lax.rem(step, 2)

        @pl.when(step >= 2)
        def _():
            leave(slot, step - 2).wait()

        here = pl.ds(pl.multiple_of(step * STEP, STEP), STEP)
        product = jnp.dot(
            jnp.concatenate([part[here, :] for part in parts], axis=1),
            stacked[...],
            preferred_element_type=jnp.float32,
        ).astype(results.dtype)
        for k in range(blocks):
            results[slot, k] = product[:, k * block : (k + 1) * block]
        leave(slot, step).start()

    for step in range(max(steps - 2, 0), steps):
        leave(step % 2, step).wait()
    last.wait()


def embed_products(parts, rows, small):
    count = len(parts)
    quarter, cells = parts[0].shape
    width = rows[0].shape[1]
    blocks, extra, block = small.shape
    return pl.pallas_call(
        functools.partial(embed_kernel, count),
        out_shape=jax.ShapeDtypeStruct((blocks, quarter + extra, block), jnp.bfloat16),
        in_specs=[pl.BlockSpec(memory_space=pltpu.VMEM)] * (2 * count + 1),
        out_specs=pl.BlockSpec(memory_space=pltpu.HBM),
        scratch_shapes=[
            pltpu.VMEM((count * cells, width), jnp.bfloat16),
            pltpu.VMEM((2, blocks, STEP, block), jnp.bfloat16),
            pltpu.SemaphoreType.DMA((3,)),
        ],
        compiler_params=pltpu.CompilerParams(vmem_limit_bytes=58 * 2**20),
        cost_estimate=COST,
        name="embed_products",
    )(*parts, *rows, small)


def products_kernel(count, *refs):
    out = refs[-1]
    spot = 0
    for k in range(count):
        rows = jnp.transpose(refs[2 * k][...])
        columns = refs[2 * k + 1]
        width = columns.shape[1]
        for start in range(0, width, 256):
            out[:, spot + start : spot + start + 256] = jnp.dot(
                rows, columns[:, start : start + 256], preferred_element_type=jnp.float32
            ).astype(out.dtype)
        spot += width


def row_products(pairs):
    operands = [one for pair in pairs for one in pair]
    height = pairs[0][0].shape[1]
    width = sum(b.shape[1] for _, b in pairs)
    return pl.pallas_call(
        functools.partial(products_kernel, len(pairs)),
        out_shape=jax.ShapeDtypeStruct((height, width), jnp.bfloat16),
        in_specs=[pl.BlockSpec(memory_space=pltpu.VMEM)] * len(operands),
        out_specs=pl.BlockSpec(memory_space=pltpu.VMEM),
        compiler_params=pltpu.CompilerParams(vmem_limit_bytes=48 * 2**20),
        cost_estimate=COST,
        name="row_products",
    )(*operands)


def decoder_kernel(count, *refs):
    rows, cots, out, turned = refs[:count], refs[count : 2 * count], refs[-2], refs[-1]
    cells = rows[0].shape[0]

    @pl.when(pl.program_id(0) == 0)
    def _():
        for k in range(count):
            turned[:, k * cells : (k + 1) * cells] = jnp.transpose(rows[k][...])

    out[...] = lax.dot_general(
        turned[...],
        jnp.concatenate([one[...] for one in cots], axis=1),
        (((1,), (1,)), ((), ())),
        preferred_element_type=jnp.float32,
    ).astype(out.dtype)


def decoder_products(latents, cots, width):
    count = len(latents)
    cells = latents[0].shape[0]
    last = latents[0].shape[1] // width - 1
    quarter = cots[0].shape[0]
    step_rows = math.gcd(quarter, 1152)
    return pl.pallas_call(
        functools.partial(decoder_kernel, count),
        grid=(quarter // step_rows,),
        out_shape=jax.ShapeDtypeStruct((width, quarter), jnp.bfloat16),
        in_specs=[pl.BlockSpec((cells, width), lambda step: (0, last))] * count
        + [pl.BlockSpec((step_rows, cells), lambda step: (step, 0))] * count,
        out_specs=pl.BlockSpec((width, step_rows), lambda step: (0, step)),
        scratch_shapes=[pltpu.VMEM((width, count * cells), jnp.bfloat16)],
        compiler_params=pltpu.CompilerParams(vmem_limit_bytes=40 * 2**20),
        cost_estimate=COST,
        name="decoder_products",
    )(*latents, *cots)


def head_probs(keys, queries, scaling):
    scores = (
        lax.dot_general(keys, queries, (((1,), (1,)), ((), ())), preferred_element_type=jnp.float32)
        * scaling
    )
    scores = jnp.exp(scores - jnp.max(scores, axis=0, keepdims=True))
    return scores * (1.0 / jnp.sum(scores, axis=0, keepdims=True))


def attend_kernel(heads, width, rows_ref, out, turned):
    step = pl.program_id(0)
    height = out.shape[0]
    group = heads * width

    @pl.when(step == 0)
    def _():
        turned[...] = jnp.transpose(rows_ref[:, 2 * group : 3 * group])

    block = rows_ref[pl.ds(pl.multiple_of(step * height, height), height), :group]
    results = []
    for h in range(heads):
        probs = head_probs(
            rows_ref[:, group + h * width : group + (h + 1) * width],
            block[:, h * width : (h + 1) * width],
            width ** (-0.5),
        ).astype(jnp.bfloat16)
        results.append(
            jnp.dot(turned[h * width : (h + 1) * width, :], probs, preferred_element_type=jnp.float32)
        )
    out[...] = jnp.transpose(jnp.concatenate(results, axis=0)).astype(out.dtype)


def attend(rows, heads):
    cells, total = rows.shape
    group = total // 3
    height = math.gcd(cells, 1024)
    return pl.pallas_call(
        functools.partial(attend_kernel, heads, group // heads),
        grid=(cells // height,),
        out_shape=jax.ShapeDtypeStruct((cells, group), jnp.bfloat16),
        in_specs=[pl.BlockSpec((cells, total), lambda step: (0, 0))],
        out_specs=pl.BlockSpec((height, group), lambda step: (step, 0)),
        scratch_shapes=[pltpu.VMEM((group, cells), jnp.bfloat16)],
        compiler_params=pltpu.CompilerParams(vmem_limit_bytes=40 * 2**20),
        cost_estimate=COST,
        name="attend",
    )(rows)


def attend_back_kernel(heads, width, rows_ref, cot_ref, out, turned, key_sum, value_sum):
    step = pl.program_id(0)
    group = heads * width
    height = rows_ref.shape[0] // pl.num_programs(0)
    scaling = width ** (-0.5)

    @pl.when(step == 0)
    def _():
        turned[...] = jnp.transpose(rows_ref[:, group : 2 * group])
        key_sum[...] = jnp.zeros_like(key_sum)
        value_sum[...] = jnp.zeros_like(value_sum)

    here = pl.ds(pl.multiple_of(step * height, height), height)
    block = rows_ref[here, :group]
    cots = cot_ref[here, :]
    results = []
    for h in range(heads):
        columns = slice(h * width, (h + 1) * width)
        queries = block[:, columns]
        cot = cots[:, columns]
        probs = head_probs(
            rows_ref[:, group + h * width : group + (h + 1) * width], queries, scaling
        )
        prob_grad = lax.dot_general(
            rows_ref[:, 2 * group + h * width : 2 * group + (h + 1) * width],
            cot,
            (((1,), (1,)), ((), ())),
            preferred_element_type=jnp.float32,
        )
        delta = jnp.sum(probs * prob_grad, axis=0, keepdims=True)
        score_grad = (probs * (prob_grad - delta)).astype(jnp.bfloat16)
        results.append(
            jnp.dot(turned[columns, :], score_grad, preferred_element_type=jnp.float32) * scaling
        )
        key_sum[:, columns] += jnp.dot(score_grad, queries, preferred_element_type=jnp.float32)
        value_sum[:, columns] += jnp.dot(
            probs.astype(jnp.bfloat16), cot, preferred_element_type=jnp.float32
        )
    out[here, :group] = jnp.transpose(jnp.concatenate(results, axis=0)).astype(out.dtype)

    @pl.when(step == pl.num_programs(0) - 1)
    def _():
        out[:, group : 2 * group] = (key_sum[...] * scaling).astype(out.dtype)
        out[:, 2 * group :] = value_sum[...].astype(out.dtype)


def attend_back(rows, cot, heads):
    cells, total = rows.shape
    group = total // 3
    height = math.gcd(cells, 1024)
    return pl.pallas_call(
        functools.partial(attend_back_kernel, heads, group // heads),
        grid=(cells // height,),
        out_shape=jax.ShapeDtypeStruct((cells, total), jnp.bfloat16),
        in_specs=[
            pl.BlockSpec((cells, total), lambda step: (0, 0)),
            pl.BlockSpec((cells, group), lambda step: (0, 0)),
        ],
        out_specs=pl.BlockSpec((cells, total), lambda step: (0, 0)),
        scratch_shapes=[
            pltpu.VMEM((group, cells), jnp.bfloat16),
            pltpu.VMEM((cells, group), jnp.float32),
            pltpu.VMEM((cells, group), jnp.float32),
        ],
        compiler_params=pltpu.CompilerParams(vmem_limit_bytes=40 * 2**20),
        cost_estimate=COST,
        name="attend_back",
    )(rows, cot)


def split_model(
    counts,
    library,
    coords,
    noise,
    decoded_cot,
    prior_cot,
    embed_t,
    w_qkv,
    w_attn_out,
    w_up,
    up_bias,
    w_down,
    w_latent,
    w_decode,
    comp_means,
    norm_params,
):
    slides = lax.axis_size("slide")
    blocks = lax.axis_size("blk")
    me = lax.axis_index("slide")
    genes = embed_t.shape[1]
    cells = counts.shape[1]
    model_width = w_attn_out.shape[1]
    own_rows = w_qkv.shape[0]
    latent_width = w_decode.shape[0] * blocks
    mixture_count = comp_means.shape[1]
    quarter = -(-genes // (slides * ROWS)) * ROWS
    padded = quarter * slides
    head_part = model_width // slides
    pair = model_width // blocks
    pairs = head_part // pair
    ff_part = up_bias.shape[0] // slides
    latent_part = model_width // slides

    def place_of(k):
        return jnp.bitwise_xor(me, k)

    def column_part(rows, width, place):
        return lax.dynamic_slice_in_dim(rows, place * width, width, 1)

    def whole(piece, axis):
        return in_order(share(piece, slides), me, axis)

    def wide(piece):
        return piece.astype(jnp.float32)

    embed_part = lax.dynamic_slice_in_dim(
        jnp.pad(embed_t.T, ((0, padded - genes), (0, 0))), me * quarter, quarter, 0
    )
    bias_part = lax.dynamic_slice_in_dim(up_bias, me * ff_part, ff_part, 0)
    mean_cols = comp_means.size // own_rows
    folds = mixture_count // mean_cols
    own_latents = w_decode.shape[0]
    small = jnp.concatenate(
        [
            norm_params.T,
            jnp.concatenate(
                [comp_means.T[k * mean_cols : (k + 1) * mean_cols] for k in range(folds)], axis=1
            ),
            bias_part.reshape(-1, own_rows),
        ],
        axis=0,
    )
    small_rows = small.shape[0]
    small = jnp.pad(small, ((0, SMALL - small_rows), (0, 0)))
    qkv_width = pairs * 3 * pair
    qkv_part = [
        lax.dynamic_slice_in_dim(w_qkv, k * model_width + me * head_part, head_part, 1)
        for k in range(3)
    ]
    qkv_part = jnp.concatenate(
        [part[:, j * pair : (j + 1) * pair] for j in range(pairs) for part in qkv_part], axis=1
    ).T
    out_latent = jnp.concatenate(
        [
            lax.dynamic_slice_in_dim(weight, me * head_part, head_part, 1)
            for weight in (w_attn_out, w_latent)
        ],
        axis=1,
    ).T
    embedding = gather_blk(
        jnp.concatenate([embed_part, small, qkv_part, out_latent], axis=0), 1
    )
    small_all = embedding[quarter : quarter + SMALL]
    qkv_end = quarter + SMALL + qkv_width
    weight_qkv = embedding[quarter + SMALL : qkv_end].reshape(pairs, 3 * pair, model_width)
    out_latent = embedding[qkv_end:]
    norm_float = small_all[:4].astype(jnp.float32)
    centres = small_all[4 : 4 + mean_cols].reshape(mean_cols, blocks, folds, own_latents)
    centres = jnp.transpose(centres, (1, 3, 2, 0)).reshape(latent_width, mixture_count)
    bias_up = small_all[4 + mean_cols].astype(jnp.float32)
    expr_parts = swap(expression_parts(counts, library, me, slides, quarter))

    cot_all = jnp.pad(decoded_cot[0].T, ((0, padded - genes), (0, 0)))
    cot_first = [
        lax.dynamic_slice_in_dim(cot_all, place_of(k) * quarter, quarter, 0)
        for k in range(slides)
    ]
    cot_parts = swap([after(piece, *expr_parts[1:]) for piece in cot_first])
    up_part = jnp.concatenate(
        [
            lax.dynamic_slice_in_dim(w_up, (k * slides + me) * ff_part, ff_part, 1)
            for k in range(blocks)
        ],
        axis=1,
    )
    down_part = lax.dynamic_slice_in_dim(w_down, me * ff_part, ff_part, 0)
    expr_rows = turn_parts(expr_parts)
    half = -(-quarter // 256) * 128
    decode_part = lax.dynamic_slice_in_dim(
        jnp.pad(w_decode, ((0, 0), (0, padded - genes))), me * quarter, quarter, 1
    )
    decode_part = jnp.concatenate(
        [decode_part[:, :half], jnp.pad(decode_part[:, half:], ((0, 0), (0, 2 * half - quarter)))],
        axis=0,
    )
    middle = gather_blk(
        after(
            jnp.concatenate([up_part, decode_part], axis=1),
            embedding,
            expr_rows,
            *cot_parts[1:],
        )
    )
    halves = middle[:, model_width:].reshape(blocks, 2, own_latents, half)
    weight_decode = jnp.concatenate(
        [
            halves[:, 0].reshape(latent_width, half),
            halves[:, 1].reshape(latent_width, half)[:, : quarter - half],
        ],
        axis=1,
    )

    h_zero = collect(embed_cells(expr_rows, embedding, slides))
    h_zero = h_zero + spatial_code(coords[0], model_width)
    normed_one, norm_one_back = jax.vjp(layer_norm, h_zero, norm_float[0], norm_float[1])
    normed_one_all = jnp.concatenate(share(normed_one.astype(jnp.bfloat16), slides), axis=0)
    projected = jnp.einsum(
        "ck,pfk->pcf", normed_one_all, weight_qkv, preferred_element_type=jnp.float32
    ).astype(jnp.bfloat16)

    def to_heads(rows):
        return lax.all_to_all(
            rows.reshape(blocks, cells, rows.shape[-1]), "blk", 0, 0, tiled=True
        ).reshape(blocks * cells, rows.shape[-1])

    out_shares = share(after(out_latent[:head_part], normed_one_all), slides)
    latent_cots = cots_to_latents(cot_parts, weight_decode)
    centres_float = centres.astype(jnp.float32)
    half_norms = 0.5 * jnp.sum(centres_float * centres_float, axis=0)
    head_rows, half_norms, centres_float = lax.optimization_barrier(
        (after(to_heads(projected), latent_cots[-1], *out_shares[1:]), half_norms, centres_float)
    )
    per_pair = pair // HEAD_DIM
    latent_shares = share(after(out_latent[head_part:], head_rows), slides)
    weight_out = order_rows(out_shares, me)
    weight_latent = order_rows(latent_shares, me)
    head_out = attend(head_rows, per_pair)
    weight_down = gather_blk(after(down_part, middle, weight_out))
    own_heads = to_heads(head_out).reshape(pairs, slides, cells, pair)
    own_heads = after(own_heads, *latent_shares[1:])
    attended_parts = swap(
        [
            jnp.concatenate([own_heads[j, k] for j in range(pairs)], axis=1)
            for k in range(slides)
        ]
    )
    attended_low = in_order(attended_parts, me, 1)
    h_one = h_zero + contract_cols(attended_low, weight_out)
    normed_two, norm_two_back = jax.vjp(layer_norm, h_one, norm_float[2], norm_float[3])
    normed_two_low = normed_two.astype(jnp.bfloat16)
    normed_two_rows = share(normed_two_low, slides)
    normed_two_rows[0] = after(normed_two_rows[0], weight_latent)
    hidden_pre, hidden_low, *h_two_parts = feed_forward(
        normed_two_rows, middle, bias_up[None], weight_down
    )
    normed_two_all = jnp.concatenate(normed_two_rows, axis=0)
    h_two_sum = collect(h_two_parts)
    latent_from_decode = collect(latent_cots)
    h_two = h_one + after(h_two_sum, latent_from_decode)
    h_two_low = h_two.astype(jnp.bfloat16)
    both_rows = lax.all_gather(
        jnp.concatenate([attended_low, h_two_low], axis=1), "slide", axis=0, tiled=True
    )
    latent_pre = contract_cols(h_two_low, weight_latent)
    spread = jnp.exp(0.5 * latent_pre[:, latent_width:])
    latent = latent_pre[:, :latent_width] + spread * noise[0]
    mixing = latent_width ** (-0.5)
    mix = (exact_dot(latent, centres_float, 1, 0) - half_norms) * mixing
    mix_max = jnp.max(mix, axis=-1, keepdims=True)
    mix_exp = jnp.exp(mix - mix_max)
    mix_sum = jnp.sum(mix_exp, axis=-1, keepdims=True)
    prior = -(mix_max + jnp.log(mix_sum))[:, 0]
    shares = prior_cot[0][:, None] * (mix_exp / mix_sum)
    latent_from_prior = exact_dot(shares, centres_float, 1, 1) * -mixing
    centre_grad = (
        centres_float * jnp.sum(shares, axis=0) - exact_dot(latent, shares, 0, 0)
    ) * mixing

    latent_total = latent_from_decode + latent_from_prior
    pre_grad = jnp.concatenate(
        [latent_total, latent_total * noise[0] * spread * 0.5], axis=-1
    ).astype(jnp.bfloat16)
    both_parts = share(
        jnp.concatenate([pre_grad, latent.astype(jnp.bfloat16)], axis=1), slides
    )
    h_two_grad, down_input, pre_hidden_grad, up_bias_grad, *normed_two_parts = feed_back(
        both_parts, weight_latent, weight_down, middle, hidden_pre
    )
    normed_two_grad = collect(normed_two_parts)
    latent_parts = [after(part, normed_two_parts[-1]) for part in both_parts]
    decode_local = decoder_products(latent_parts, cot_parts, latent_width)
    decoded_rows = decode_genes(latent_parts, weight_decode)
    normed_two_grad = after(normed_two_grad, decode_local, decoded_rows[-1])
    decode_own = scatter_blk(after(decode_local, both_rows, normed_two_grad))
    h_one_part, gain_two_grad, shift_two_grad = norm_two_back(normed_two_grad)
    h_one_grad = h_two_grad + h_one_part
    out_input = h_one_grad.astype(jnp.bfloat16)
    attended_grad = jnp.dot(out_input, weight_out, preferred_element_type=jnp.float32).astype(jnp.bfloat16)
    grad_parts = swap([column_part(attended_grad, head_part, place_of(k)) for k in range(slides)])
    out_heads = to_heads(pair_up(grad_parts, pairs))

    middle_local = row_products(
        [
            (hidden_low, after(down_input, *grad_parts[1:])),
            (normed_two_all, pre_hidden_grad),
        ]
    )
    out_heads = after(out_heads, middle_local)
    decoded_parts = swap(
        [after(one, *grad_parts[1:]) for one in decoded_rows[:-1]]
        + [after(decoded_rows[-1], out_heads)]
    )
    out_heads = after(out_heads, *decoded_parts[1:-1])
    head_grads = attend_back(head_rows, out_heads, per_pair)
    middle_grad = scatter_blk(after(middle_local, decode_own, head_grads))
    cot_cols = swap(
        [
            after(column_part(out_input, head_part, place_of(k)), head_grads)
            for k in range(slides)
        ]
    )
    projected_grad = to_heads(head_grads).reshape(pairs, slides * cells, 3 * pair)
    projected_grad = after(projected_grad, decoded_parts[-1], *cot_cols[1:])
    normed_one_parts = lowered(
        split_rows(
            jnp.einsum(
                "pcf,pfk->ck", projected_grad, weight_qkv, preferred_element_type=jnp.float32
            ),
            slides,
        )
    )
    normed_one_grad = collect(normed_one_parts)
    last_kept, last_sent = last_products(
        normed_one_all,
        after(projected_grad, normed_one_parts[-1]),
        [column_part(part, latent_part, me) for part in both_parts],
        both_rows,
        cot_cols,
        0,
        me,
        lax.axis_index("blk"),
    )
    last_kept, last_sent = merge_half(last_kept, to_core(last_sent))
    normed_one_grad = after(normed_one_grad, last_sent)
    h_zero_part, gain_one_grad, shift_one_grad = norm_one_back(normed_one_grad)
    h_zero_low = (h_one_grad + h_zero_part).astype(jnp.bfloat16)
    h_zero_parts = share(h_zero_low, slides)
    bit = 1
    while last_kept.shape[0] > own_rows:
        last_kept, last_sent = merge_half(last_kept, to_chip(last_sent, bit))
        bit *= 2
    h_zero_parts = [after(h_zero_parts[0], last_sent)] + h_zero_parts[1:]
    last_other = to_chip(last_sent, bit)

    small_grad = jnp.concatenate(
        [
            jnp.stack([gain_one_grad, shift_one_grad, gain_two_grad, shift_two_grad], axis=0),
            jnp.transpose(
                centre_grad.reshape(blocks, own_latents, folds, mean_cols), (3, 0, 2, 1)
            ).reshape(mean_cols, model_width),
            up_bias_grad,
        ],
        axis=0,
    )
    small_grad = jnp.pad(small_grad, ((0, SMALL - small_rows), (0, 0))).astype(jnp.bfloat16)
    small_grad = jnp.transpose(small_grad.reshape(SMALL, blocks, own_rows), (1, 0, 2))
    embed_local = embed_products(expr_parts, h_zero_parts, small_grad)
    gene_rows = cells_to_genes(
        embedding, [after(part, embed_local) for part in h_zero_parts], quarter
    )
    embed_own = scatter_blk(after(embed_local, middle_grad))[0]
    decode_half = jnp.concatenate(
        [decode_own[:, :half], jnp.pad(decode_own[:, half:], ((0, 0), (0, 2 * half - quarter)))],
        axis=0,
    )
    early = after(jnp.concatenate([middle_grad, decode_half], axis=1), *h_zero_parts[1:])
    early_parts = share_halves(early)
    gene_parts = swap([after(part, *early_parts[1:3]) for part in gene_rows])
    last_low = (last_kept + after(last_other, *gene_parts[1:3]).astype(jnp.float32)).astype(
        jnp.bfloat16
    )
    last_shares = share(last_low, slides)
    embed_shares = share(
        after(embed_own, *gene_parts[1:], *last_shares[1:], *early_parts[1:]), slides
    )
    expr_grad = spread_parts(gene_parts, me, genes)
    decoded = join_parts(decoded_parts, me, quarter, genes, jnp.bfloat16).T
    down_grad, up_grad, qkv_grad, attn_out_grad, latent_grad, decode_grad = assemble(
        early_parts, last_shares, me, genes, quarter, half, own_latents, blocks, pairs, pair
    )
    embed_grad, norm_grad, means_grad, up_bias_grad = finish(
        embed_shares, me, quarter, genes, mean_cols, folds
    )

    return (
        decoded[None],
        prior[None],
        expr_grad,
        embed_grad.T,
        qkv_grad,
        attn_out_grad,
        up_grad,
        up_bias_grad.reshape(-1),
        down_grad,
        latent_grad,
        decode_grad,
        means_grad.T,
        norm_grad.T,
    )


def fits(mesh):
    slides, blocks = mesh.shape["slide"], mesh.shape["blk"]
    return slides & (slides - 1) == 0 and HEADS % slides == 0 and HEADS % blocks == 0


def solution(mesh):
    placed = (
        P("slide", "blk", None),
        P("slide", "blk"),
        P("slide", "blk", None),
        P("slide", "blk", None),
        P("slide", "blk", None),
        P("slide", "blk"),
        P("blk", None),
        P("blk", None),
        P("blk", None),
        P("blk", None),
        P("blk"),
        P("blk", None),
        P("blk", None),
        P("blk", None),
        P("blk", None),
        P("blk", None),
    )
    return jax.shard_map(
        split_model if fits(mesh) else local,
        mesh=mesh,
        in_specs=placed,
        out_specs=(
            P("slide", "blk", None),
            P("slide", "blk"),
            P("slide", "blk", None),
            P("blk", None),
            P("blk", None),
            P("blk", None),
            P("blk", None),
            P("blk"),
            P("blk", None),
            P("blk", None),
            P("blk", None),
            P("blk", None),
            P("blk", None),
        ),
        check_vma=False,
    )
```

```python
import functools
import math

import jax
import jax.numpy as jnp
from jax import lax
from jax.experimental import pallas as pl
from jax.experimental.pallas import tpu as pltpu
from jax.sharding import PartitionSpec as P

HEADS = 16
HEAD_DIM = 64


eps_norm = 1e-05


def contract_rows(former, latter):
    return lax.dot_general(
        former, latter, (((0,), (0,)), ((), ())), preferred_element_type=jnp.float32
    )


def contract_cols(former, latter):
    return lax.dot_general(
        former, latter, (((1,), (1,)), ((), ())), preferred_element_type=jnp.float32
    )


def layer_norm(tensor, norm_gain, norm_shift):
    center = tensor - jnp.mean(tensor, axis=-1, keepdims=True)
    inverse = lax.rsqrt(jnp.mean(center * center, axis=-1, keepdims=True) + eps_norm)
    return center * inverse * norm_gain + norm_shift


def spatial_code(coords, model_width):
    quarter = model_width // 4
    frequency = jnp.exp(-math.log(10000.0) * jnp.arange(quarter, dtype=jnp.float32) / quarter)
    first_axis = coords[..., 0:1].astype(jnp.float32) * frequency
    second_axis = coords[..., 1:2].astype(jnp.float32) * frequency
    return jnp.concatenate(
        [jnp.sin(first_axis), jnp.cos(first_axis), jnp.sin(second_axis), jnp.cos(second_axis)],
        axis=-1,
    )


def mixture_term(latent, centres):
    scores = (
        jnp.dot(
            latent, centres, precision=lax.Precision.HIGHEST, preferred_element_type=jnp.float32
        )
        - 0.5 * jnp.sum(centres * centres, axis=0)
    ) * latent.shape[-1] ** (-0.5)
    return -jax.nn.logsumexp(scores, axis=-1)


def split_single(rows_in, head_count):
    arrived_rows = rows_in.shape[0]
    block_rows = 512
    return rows_in.reshape(
        (arrived_rows // block_rows, block_rows, head_count, rows_in.shape[1] // head_count)
    )


def split_blocks(key_rows, value_rows, head_count):
    return (split_single(key_rows, head_count), split_single(value_rows, head_count))


def local(
    counts,
    library,
    coords,
    noise,
    decoded_cot,
    prior_cot,
    embed_t,
    w_qkv,
    w_attn_out,
    w_up,
    up_bias,
    w_down,
    w_latent,
    w_decode,
    comp_means,
    norm_params,
):
    gathered = (
        lax.all_gather(embed_t, "blk", axis=0, tiled=True),
        lax.all_gather(w_qkv, "blk", axis=0, tiled=True),
        lax.all_gather(w_attn_out, "blk", axis=0, tiled=True),
        lax.all_gather(w_up, "blk", axis=0, tiled=True),
        lax.all_gather(up_bias, "blk", axis=0, tiled=True),
        lax.all_gather(w_down, "blk", axis=0, tiled=True),
        lax.all_gather(w_latent, "blk", axis=0, tiled=True),
        lax.all_gather(w_decode, "blk", axis=0, tiled=True),
        lax.all_gather(comp_means, "blk", axis=0, tiled=True),
        lax.all_gather(norm_params, "blk", axis=0, tiled=True),
    )
    (
        embedding,
        weight_qkv,
        weight_out,
        weight_up,
        bias_up,
        weight_down,
        weight_latent,
        weight_decode,
        centres,
        norm_table,
    ) = gathered
    head_count = HEADS
    head_width = HEAD_DIM
    scaling = head_width ** (-0.5)
    model_width = embedding.shape[0]
    latent_width = weight_decode.shape[0]
    blk_count = lax.axis_size("blk")
    expression = jnp.log1p(
        counts[0].astype(jnp.float32) * 10000.0 / library[0].astype(jnp.float32)[:, None]
    )
    expression_low = expression.astype(jnp.bfloat16)
    local_cells = expression.shape[0]
    norm_float = norm_table.astype(jnp.float32)
    h_zero = contract_cols(expression_low, embedding) + spatial_code(coords[0], model_width)
    normed_one, norm_one_back = jax.vjp(layer_norm, h_zero, norm_float[:, 0], norm_float[:, 1])
    normed_one_low = normed_one.astype(jnp.bfloat16)
    projected = jnp.dot(normed_one_low, weight_qkv, preferred_element_type=jnp.float32).astype(
        jnp.bfloat16
    )
    queries = projected[:, :model_width].reshape(local_cells, head_count, head_width)
    key_rows = projected[:, model_width : 2 * model_width]
    value_rows = projected[:, 2 * model_width :]
    stat_start = (
        jnp.full((head_count, local_cells), -1e30, jnp.float32),
        jnp.zeros((head_count, local_cells), jnp.float32),
    )
    key_blocks = split_single(lax.all_gather(key_rows, "blk", axis=0, tiled=True), head_count)

    def per_block(status, key_block):
        running_max, running_sum = status
        scores = (
            jnp.einsum("thd,khd->htk", queries, key_block, preferred_element_type=jnp.float32)
            * scaling
        )
        new_max = jnp.maximum(running_max, jnp.max(scores, axis=-1))
        running_sum = running_sum * jnp.exp(running_max - new_max) + jnp.sum(
            jnp.exp(scores - new_max[..., None]), axis=-1
        )
        return ((new_max, running_sum), None)

    result, unused = lax.scan(per_block, stat_start, key_blocks)
    running_max, running_sum = result
    log_total = running_max + jnp.log(running_sum)
    arrived = (
        lax.all_gather(key_rows, "blk", axis=0, tiled=True),
        lax.all_gather(value_rows, "blk", axis=0, tiled=True),
    )
    key_blocks, value_blocks = split_blocks(arrived[0], arrived[1], head_count)

    def per_block(weighted, block_pair):
        scores = (
            jnp.einsum("thd,khd->htk", queries, block_pair[0], preferred_element_type=jnp.float32)
            * scaling
        )
        probs_low = jnp.exp(scores - log_total[..., None]).astype(jnp.bfloat16)
        weighted = weighted + jnp.einsum(
            "htk,khd->htd", probs_low, block_pair[1], preferred_element_type=jnp.float32
        )
        return (weighted, None)

    result, unused = lax.scan(
        per_block,
        jnp.zeros((head_count, local_cells, head_width), jnp.float32),
        (key_blocks, value_blocks),
    )
    attended_cells = jnp.transpose(result, (1, 0, 2))
    attended_low = attended_cells.reshape(local_cells, model_width).astype(jnp.bfloat16)
    h_one = h_zero + jnp.dot(attended_low, weight_out, preferred_element_type=jnp.float32)
    normed_two, norm_two_back = jax.vjp(layer_norm, h_one, norm_float[:, 2], norm_float[:, 3])
    normed_two_low = normed_two.astype(jnp.bfloat16)
    hidden_pre = jnp.dot(
        normed_two_low, weight_up, preferred_element_type=jnp.float32
    ) + bias_up.astype(jnp.float32)
    hidden_act, gelu_back = jax.vjp(jax.nn.gelu, hidden_pre)
    hidden_low = hidden_act.astype(jnp.bfloat16)
    h_two = h_one + jnp.dot(hidden_low, weight_down, preferred_element_type=jnp.float32)
    h_two_low = h_two.astype(jnp.bfloat16)
    latent_pre = jnp.dot(h_two_low, weight_latent, preferred_element_type=jnp.float32)
    spread = jnp.exp(0.5 * latent_pre[:, latent_width:])
    latent = latent_pre[:, :latent_width] + spread * noise[0]
    latent_low = latent.astype(jnp.bfloat16)
    decoded = jnp.dot(latent_low, weight_decode, preferred_element_type=jnp.float32).astype(
        jnp.bfloat16
    )
    prior, prior_back = jax.vjp(mixture_term, latent, centres.astype(jnp.float32))
    out_grad = decoded_cot[0]
    latent_from_decode = contract_cols(out_grad, weight_decode)
    latent_from_prior, centre_grad = prior_back(prior_cot[0])
    latent_total = latent_from_decode + latent_from_prior
    pre_grad = jnp.concatenate(
        [latent_total, latent_total * noise[0] * spread * 0.5], axis=-1
    ).astype(jnp.bfloat16)
    latent_weight_grad = contract_rows(h_two_low, pre_grad)
    h_two_grad = contract_cols(pre_grad, weight_latent)
    down_input = h_two_grad.astype(jnp.bfloat16)
    down_grad = contract_rows(hidden_low, down_input)
    hidden_grad = contract_cols(down_input, weight_down)
    pre_hidden_grad = gelu_back(hidden_grad)[0].astype(jnp.bfloat16)
    up_bias_grad = jnp.sum(pre_hidden_grad.astype(jnp.float32), axis=0)
    up_grad = contract_rows(normed_two_low, pre_hidden_grad)
    normed_two_grad = contract_cols(pre_hidden_grad, weight_up)
    h_one_part, gain_two_grad, shift_two_grad = norm_two_back(normed_two_grad)
    h_one_grad = h_two_grad + h_one_part
    out_input = h_one_grad.astype(jnp.bfloat16)
    attn_out_grad = contract_rows(attended_low, out_input)
    attended_grad = contract_cols(out_input, weight_out).astype(jnp.bfloat16)
    out_heads = attended_grad.reshape(local_cells, head_count, head_width)
    row_delta = jnp.sum(out_heads.astype(jnp.float32) * attended_cells, axis=-1).T
    query_zero = jnp.zeros((head_count, local_cells, head_width), jnp.float32)
    start_back = (query_zero, jnp.zeros((local_cells * blk_count, 2 * model_width), jnp.float32))
    arrived = (
        lax.all_gather(key_rows, "blk", axis=0, tiled=True),
        lax.all_gather(value_rows, "blk", axis=0, tiled=True),
    )
    key_blocks, value_blocks = split_blocks(arrived[0], arrived[1], head_count)
    arrived_rows = arrived[0].shape[0]

    def per_block(query_sum, block_pair):
        scores = (
            jnp.einsum("thd,khd->htk", queries, block_pair[0], preferred_element_type=jnp.float32)
            * scaling
        )
        probs = jnp.exp(scores - log_total[..., None])
        prob_grad = jnp.einsum(
            "thd,khd->htk", out_heads, block_pair[1], preferred_element_type=jnp.float32
        )
        score_grad = (probs * (prob_grad - row_delta[..., None])).astype(jnp.bfloat16)
        query_sum = query_sum + jnp.einsum(
            "htk,khd->htd", score_grad, block_pair[0], preferred_element_type=jnp.float32
        )
        key_part = (
            jnp.einsum("htk,thd->khd", score_grad, queries, preferred_element_type=jnp.float32)
            * scaling
        )
        value_part = jnp.einsum(
            "htk,thd->khd",
            probs.astype(jnp.bfloat16),
            out_heads,
            preferred_element_type=jnp.float32,
        )
        block_rows = key_part.shape[0]
        return (
            query_sum,
            jnp.concatenate(
                [key_part.reshape(block_rows, -1), value_part.reshape(block_rows, -1)], axis=-1
            ),
        )

    query_total, stacked = lax.scan(per_block, start_back[0], (key_blocks, value_blocks))
    stacked = stacked.reshape(arrived_rows, stacked.shape[-1])
    carried_back = (query_total, stacked)
    query_total = carried_back[0]
    own_pairs = lax.psum_scatter(
        carried_back[1].astype(jnp.bfloat16), "blk", scatter_dimension=0, tiled=True
    ).astype(jnp.float32)
    query_rows = jnp.transpose(query_total * scaling, (1, 0, 2)).reshape(local_cells, model_width)
    projected_grad = jnp.concatenate([query_rows, own_pairs], axis=-1).astype(jnp.bfloat16)
    qkv_grad = contract_rows(normed_one_low, projected_grad)
    normed_one_grad = contract_cols(projected_grad, weight_qkv)
    h_zero_part, gain_one_grad, shift_one_grad = norm_one_back(normed_one_grad)
    h_zero_low = (h_one_grad + h_zero_part).astype(jnp.bfloat16)
    expr_grad = jnp.dot(h_zero_low, embedding, preferred_element_type=jnp.float32)
    norm_grad = jnp.stack([gain_one_grad, shift_one_grad, gain_two_grad, shift_two_grad], axis=0).T
    centre_grad = centre_grad.T.T
    embed_slot = contract_rows(h_zero_low, expression_low)
    decode_slot = contract_rows(latent_low, out_grad)
    block_parts = (
        lax.psum_scatter(
            embed_slot.astype(jnp.bfloat16), "blk", scatter_dimension=0, tiled=True
        ).astype(jnp.float32),
        lax.psum_scatter(
            qkv_grad.astype(jnp.bfloat16), "blk", scatter_dimension=0, tiled=True
        ).astype(jnp.float32),
        lax.psum_scatter(
            attn_out_grad.astype(jnp.bfloat16), "blk", scatter_dimension=0, tiled=True
        ).astype(jnp.float32),
        lax.psum_scatter(
            up_grad.astype(jnp.bfloat16), "blk", scatter_dimension=0, tiled=True
        ).astype(jnp.float32),
        lax.psum_scatter(
            up_bias_grad.astype(jnp.bfloat16), "blk", scatter_dimension=0, tiled=True
        ).astype(jnp.float32),
        lax.psum_scatter(
            down_grad.astype(jnp.bfloat16), "blk", scatter_dimension=0, tiled=True
        ).astype(jnp.float32),
        lax.psum_scatter(
            latent_weight_grad.astype(jnp.bfloat16), "blk", scatter_dimension=0, tiled=True
        ).astype(jnp.float32),
        lax.psum_scatter(
            decode_slot.astype(jnp.bfloat16), "blk", scatter_dimension=0, tiled=True
        ).astype(jnp.float32),
        lax.psum_scatter(
            centre_grad.astype(jnp.bfloat16), "blk", scatter_dimension=0, tiled=True
        ).astype(jnp.float32),
        lax.psum_scatter(
            norm_grad.astype(jnp.bfloat16), "blk", scatter_dimension=0, tiled=True
        ).astype(jnp.float32),
    )
    summed = (
        lax.psum(block_parts[0].astype(jnp.bfloat16), "slide").astype(jnp.float32),
        lax.psum(block_parts[1].astype(jnp.bfloat16), "slide").astype(jnp.float32),
        lax.psum(block_parts[2].astype(jnp.bfloat16), "slide").astype(jnp.float32),
        lax.psum(block_parts[3].astype(jnp.bfloat16), "slide").astype(jnp.float32),
        lax.psum(block_parts[4].astype(jnp.bfloat16), "slide").astype(jnp.float32),
        lax.psum(block_parts[5].astype(jnp.bfloat16), "slide").astype(jnp.float32),
        lax.psum(block_parts[6].astype(jnp.bfloat16), "slide").astype(jnp.float32),
        lax.psum(block_parts[7].astype(jnp.bfloat16), "slide").astype(jnp.float32),
        lax.psum(block_parts[8].astype(jnp.bfloat16), "slide").astype(jnp.float32),
        lax.psum(block_parts[9].astype(jnp.bfloat16), "slide").astype(jnp.float32),
    )
    embed_out = summed[0]
    decode_out = summed[7]
    return (
        decoded[None],
        prior[None],
        expr_grad[None],
        embed_out,
        summed[1],
        summed[2],
        summed[3],
        summed[4],
        summed[5],
        summed[6],
        decode_out,
        summed[8],
        summed[9],
    )


def peers(offset, count):
    return [(place, place ^ offset) for place in range(count)]


def swap(pieces):
    count = len(pieces)
    return [pieces[0]] + [
        lax.ppermute(pieces[k], "slide", peers(k, count)) for k in range(1, count)
    ]


def share_halves(rows):
    half = rows.shape[0] // 2
    upper, lower = rows[:half], rows[half:]
    upper_x = lax.ppermute(upper, "slide", peers(1, 4))
    lower_y = lax.ppermute(lower, "slide", peers(2, 4))
    uppers = lax.ppermute(jnp.concatenate([upper, upper_x], axis=0), "slide", peers(2, 4))
    lowers = lax.ppermute(jnp.concatenate([lower, lower_y], axis=0), "slide", peers(1, 4))
    return [rows, upper_x, lower_y, uppers, lowers]


def share(rows, count):
    return swap([rows] * count)


def after(value, *earlier):
    return lax.optimization_barrier((value,) + earlier)[0]


def in_order(pieces, me, axis):
    stacked = jnp.stack(pieces)
    return jnp.concatenate(
        [
            lax.dynamic_index_in_dim(stacked, jnp.bitwise_xor(me, k), 0, keepdims=False)
            for k in range(len(pieces))
        ],
        axis=axis,
    )


def exact_dot(former, latter, left, right):
    return lax.dot_general(
        former,
        latter,
        (((left,), (right,)), ((), ())),
        precision=lax.Precision.HIGHEST,
        preferred_element_type=jnp.float32,
    )


def lowered(partials):
    return [partials[0]] + [piece.astype(jnp.bfloat16) for piece in partials[1:]]


def collect(partials):
    arrived = swap(partials)
    total = arrived[0]
    for piece in arrived[1:]:
        total = total + piece.astype(jnp.float32)
    return total


def gather_blk(piece, axis=0):
    return lax.all_gather(piece, "blk", axis=axis, tiled=True)


def scatter_blk(piece, axis=0):
    return lax.psum_scatter(piece, "blk", scatter_dimension=axis, tiled=True)


def to_core(rows):
    count = lax.axis_size("blk")
    return lax.ppermute(rows, "blk", [(place, place ^ 1) for place in range(count)])


def to_chip(rows, offset):
    count = lax.axis_size("blk")
    return lax.ppermute(rows, "blk", [(place, place ^ (2 * offset)) for place in range(count)])


def split_rows(rows, count):
    height = rows.shape[0] // count
    return [rows[k * height : (k + 1) * height] for k in range(count)]


ROWS = 432
STEP = 864
TALL = 1728
WIDE = 3456
CHUNKS = 2
SMALL = 16
COST = pl.CostEstimate(flops=0, bytes_accessed=0, transcendentals=0)


def expression_kernel(count, quarter, genes, me_ref, library_ref, counts_ref, *rest):
    outs, buffers, sems = rest[:count], rest[count], rest[count + 1]
    me = me_ref[0]
    tail = genes - (count - 1) * quarter
    library = library_ref[...].astype(jnp.float32)

    def copy(k, rows):
        start = pl.multiple_of(jnp.bitwise_xor(me, k) * quarter, 8)
        return pltpu.make_async_copy(
            counts_ref.at[pl.ds(start, rows), 0, :],
            buffers.at[k, pl.ds(0, rows), :],
            sems.at[k],
        )

    def each(k, act):
        last = jnp.bitwise_xor(me, k) == count - 1

        @pl.when(last)
        def _():
            act(copy(k, tail))

        @pl.when(jnp.logical_not(last))
        def _():
            act(copy(k, quarter))

    order = list(range(1, count)) + [0]
    for k in order:
        each(k, lambda one: one.start())
    for k in order:
        each(k, lambda one: one.wait())
        have = genes - jnp.bitwise_xor(me, k) * quarter

        @pl.loop(0, quarter // ROWS)
        def _(step):
            start = pl.multiple_of(step * ROWS, ROWS)
            values = buffers[k, pl.ds(start, ROWS), :].astype(jnp.float32)
            values = jnp.log1p(values * 10000.0 / library)
            row = start + lax.broadcasted_iota(jnp.int32, values.shape, 0)
            outs[k][pl.ds(start, ROWS), :] = jnp.where(row < have, values, 0.0).astype(jnp.bfloat16)


def expression_parts(counts, library, me, count, quarter):
    genes = counts.shape[2]
    cells = counts.shape[1]
    part = jax.ShapeDtypeStruct((quarter, cells), jnp.bfloat16)
    return pl.pallas_call(
        functools.partial(expression_kernel, count, quarter, genes),
        out_shape=[part] * count,
        in_specs=[
            pl.BlockSpec(memory_space=pltpu.SMEM),
            pl.BlockSpec(memory_space=pltpu.VMEM),
            pl.BlockSpec(memory_space=pltpu.HBM),
        ],
        out_specs=[pl.BlockSpec(memory_space=pltpu.VMEM)] * count,
        scratch_shapes=[
            pltpu.VMEM((count, quarter, cells), jnp.int32),
            pltpu.SemaphoreType.DMA((count,)),
        ],
        compiler_params=pltpu.CompilerParams(vmem_limit_bytes=58 * 2**20),
        cost_estimate=COST,
        name="expression",
    )(me.reshape(1), library, jnp.transpose(counts, (2, 0, 1)))


def spread_kernel(count, quarter, genes, me_ref, *rest):
    pieces, out, held, wide, sems_in, sems_out = rest[:count], *rest[count:]
    me = me_ref[0]
    tail = genes - (count - 1) * quarter

    def arrive(k):
        return pltpu.make_async_copy(pieces[k], held.at[k], sems_in.at[k])

    def leave(k):
        rows = tail if k == count - 1 else quarter
        return pltpu.make_async_copy(
            wide.at[k, pl.ds(0, rows), :], out.at[pl.ds(k * quarter, rows), 0, :], sems_out.at[k]
        )

    for k in range(count):
        arrive(k).start()
    for k in range(count):
        arrive(k).wait()
    for k in range(count):
        source = jnp.bitwise_xor(me, k)

        @pl.loop(0, quarter // ROWS)
        def _(step):
            rows = pl.ds(pl.multiple_of(step * ROWS, ROWS), ROWS)
            wide[k, rows, :] = held[source, rows, :].astype(jnp.float32)

        leave(k).start()
    for k in range(count):
        leave(k).wait()


def spread_parts(pieces, me, genes):
    count = len(pieces)
    quarter, cells = pieces[0].shape
    out = pl.pallas_call(
        functools.partial(spread_kernel, count, quarter, genes),
        out_shape=jax.ShapeDtypeStruct((genes, 1, cells), jnp.float32),
        in_specs=[pl.BlockSpec(memory_space=pltpu.SMEM)]
        + [pl.BlockSpec(memory_space=pl.ANY)] * count,
        out_specs=pl.BlockSpec(memory_space=pltpu.HBM),
        scratch_shapes=[
            pltpu.VMEM((count, quarter, cells), jnp.bfloat16),
            pltpu.VMEM((count, quarter, cells), jnp.float32),
            pltpu.SemaphoreType.DMA((count,)),
            pltpu.SemaphoreType.DMA((count,)),
        ],
        compiler_params=pltpu.CompilerParams(vmem_limit_bytes=40 * 2**20),
        cost_estimate=COST,
        name="spread",
    )(me.reshape(1), *pieces)
    return jnp.transpose(out, (1, 2, 0))


def join_kernel(count, me_ref, *rest):
    pieces, out, held, sems = rest[:count], *rest[count:]
    slot = pl.program_id(0)

    def arrive(k):
        rows = pl.ds(0, held.shape[1])
        return pltpu.make_async_copy(pieces[k].at[rows, :], held.at[k], sems.at[k])

    @pl.when(slot == 0)
    def _():
        for k in range(count):
            arrive(k).start()
        for k in range(count):
            arrive(k).wait()

    source = jnp.bitwise_xor(me_ref[0], slot)

    @pl.loop(0, out.shape[0] // ROWS)
    def _(step):
        rows = pl.ds(pl.multiple_of(step * ROWS, ROWS), ROWS)
        out[rows, :] = held[source, rows, :].astype(out.dtype)


def join_parts(pieces, me, quarter, genes, dtype):
    count = len(pieces)
    cells = pieces[0].shape[1]
    return pl.pallas_call(
        functools.partial(join_kernel, count),
        grid=(count,),
        out_shape=jax.ShapeDtypeStruct((genes, cells), dtype),
        in_specs=[pl.BlockSpec(memory_space=pltpu.SMEM)]
        + [pl.BlockSpec(memory_space=pl.ANY)] * count,
        out_specs=pl.BlockSpec((quarter, cells), lambda slot: (slot, 0)),
        scratch_shapes=[
            pltpu.VMEM((count, quarter, cells), jnp.bfloat16),
            pltpu.SemaphoreType.DMA((count,)),
        ],
        compiler_params=pltpu.CompilerParams(vmem_limit_bytes=40 * 2**20),
        cost_estimate=COST,
        name="join",
    )(me.reshape(1), *pieces)


def order_kernel(count, me_ref, *refs):
    pieces, out, sems = refs[:count], refs[-2], refs[-1]
    height = pieces[0].shape[0]

    def move(k):
        first = pl.multiple_of(jnp.bitwise_xor(me_ref[0], k) * height, height)
        return pltpu.make_async_copy(pieces[k], out.at[pl.ds(first, height), :], sems.at[k])

    for k in range(count):
        move(k).start()
    for k in range(count):
        move(k).wait()


def order_rows(pieces, me):
    count = len(pieces)
    height, width = pieces[0].shape
    return pl.pallas_call(
        functools.partial(order_kernel, count),
        out_shape=jax.ShapeDtypeStruct((count * height, width), pieces[0].dtype),
        in_specs=[pl.BlockSpec(memory_space=pltpu.SMEM)]
        + [pl.BlockSpec(memory_space=pl.ANY)] * count,
        out_specs=pl.BlockSpec(memory_space=pltpu.VMEM),
        scratch_shapes=[pltpu.SemaphoreType.DMA((count,))],
        cost_estimate=COST,
        name="order_rows",
    )(me.reshape(1), *pieces)


def turn_kernel(count, *refs):
    out = refs[-1]
    for k in range(count):
        height = refs[k].shape[1]
        out[k * height : (k + 1) * height, :] = jnp.transpose(refs[k][...])


def turn_parts(parts):
    count = len(parts)
    quarter, cells = parts[0].shape
    return pl.pallas_call(
        functools.partial(turn_kernel, count),
        grid=(quarter // WIDE,),
        out_shape=jax.ShapeDtypeStruct((count * cells, quarter), jnp.bfloat16),
        in_specs=[pl.BlockSpec((WIDE, cells), lambda step: (step, 0))] * count,
        out_specs=pl.BlockSpec((count * cells, WIDE), lambda step: (0, step)),
        compiler_params=pltpu.CompilerParams(vmem_limit_bytes=40 * 2**20),
        cost_estimate=COST,
        name="turn_parts",
    )(*parts)


def finish_kernel(count, quarter, mean_cols, folds, me_ref, *refs):
    pieces = refs[:count]
    out, norm, means, bias, held, sems = refs[count:]
    slot = pl.program_id(0)

    def arrive(k):
        place = jnp.bitwise_xor(me_ref[0], k)
        return pltpu.make_async_copy(pieces[k], held.at[place], sems.at[k])

    @pl.when(slot == 0)
    def _():
        for k in range(count):
            arrive(k).start()
        for k in range(count):
            arrive(k).wait()
        small = [held[q, quarter:, :].astype(jnp.float32) for q in range(count)]
        total = sum(small[1:], small[0])
        norm[...] = total[:4, :]
        width = means.shape[1]
        for k in range(folds):
            means[k * mean_cols : (k + 1) * mean_cols, :] = total[
                4 : 4 + mean_cols, k * width : (k + 1) * width
            ]
        bias[...] = jnp.concatenate(
            [one[4 + mean_cols : 5 + mean_cols, :] for one in small], axis=0
        )

    out[...] = held[slot, :quarter, :].astype(out.dtype)


def finish(pieces, me, quarter, genes, mean_cols, folds):
    count = len(pieces)
    height, cells = pieces[0].shape
    return pl.pallas_call(
        functools.partial(finish_kernel, count, quarter, mean_cols, folds),
        grid=(count,),
        out_shape=[
            jax.ShapeDtypeStruct((genes, cells), jnp.float32),
            jax.ShapeDtypeStruct((4, cells), jnp.float32),
            jax.ShapeDtypeStruct((folds * mean_cols, cells // folds), jnp.float32),
            jax.ShapeDtypeStruct((count, cells), jnp.float32),
        ],
        in_specs=[pl.BlockSpec(memory_space=pltpu.SMEM)]
        + [pl.BlockSpec(memory_space=pl.ANY)] * count,
        out_specs=[
            pl.BlockSpec((quarter, cells), lambda slot: (slot, 0)),
            pl.BlockSpec((4, cells), lambda slot: (0, 0)),
            pl.BlockSpec((folds * mean_cols, cells // folds), lambda slot: (0, 0)),
            pl.BlockSpec((count, cells), lambda slot: (0, 0)),
        ],
        scratch_shapes=[
            pltpu.VMEM((count, height, cells), jnp.bfloat16),
            pltpu.SemaphoreType.DMA((count,)),
        ],
        compiler_params=pltpu.CompilerParams(vmem_limit_bytes=40 * 2**20),
        cost_estimate=COST,
        name="finish",
    )(me.reshape(1), *pieces)


def scores_kernel(rows, table, *outs):
    product = jnp.dot(rows[...], table[...], preferred_element_type=jnp.float32)
    height = outs[0].shape[0]
    for k in range(len(outs)):
        outs[k][...] = product[k * height : (k + 1) * height, :].astype(outs[k].dtype)


def embed_cells(rows, table, count):
    height, quarter = rows.shape
    width = table.shape[1]
    block = math.gcd(width, 512)
    return pl.pallas_call(
        scores_kernel,
        grid=(width // block,),
        out_shape=[
            jax.ShapeDtypeStruct((height // count, width), jnp.float32 if k == 0 else jnp.bfloat16)
            for k in range(count)
        ],
        in_specs=[
            pl.BlockSpec((height, quarter), lambda step: (0, 0)),
            pl.BlockSpec((quarter, block), lambda step: (0, step)),
        ],
        out_specs=[pl.BlockSpec((height // count, block), lambda step: (0, step))] * count,
        compiler_params=pltpu.CompilerParams(vmem_limit_bytes=58 * 2**20),
        cost_estimate=COST,
        name="embed_cells",
    )(rows, table)


def latents_kernel(count, table, *refs):
    cots, outs, total = refs[:count], refs[count:-1], refs[-1]
    step = pl.program_id(0)
    product = jnp.dot(
        table[...],
        jnp.concatenate([one[...] for one in cots], axis=1),
        preferred_element_type=jnp.float32,
    )

    @pl.when(step == 0)
    def _():
        total[...] = product

    @pl.when(step > 0)
    def _():
        total[...] += product

    @pl.when(step == pl.num_programs(0) - 1)
    def _():
        cells = outs[0].shape[0]
        for k in range(count):
            outs[k][...] = jnp.transpose(total[:, k * cells : (k + 1) * cells]).astype(
                outs[k].dtype
            )


def cots_to_latents(cots, table):
    count = len(cots)
    width, quarter = table.shape
    cells = cots[0].shape[1]
    return pl.pallas_call(
        functools.partial(latents_kernel, count),
        grid=(quarter // WIDE,),
        out_shape=[
            jax.ShapeDtypeStruct((cells, width), jnp.float32 if k == 0 else jnp.bfloat16)
            for k in range(count)
        ],
        in_specs=[pl.BlockSpec((width, WIDE), lambda step: (0, step))]
        + [pl.BlockSpec((WIDE, cells), lambda step: (step, 0))] * count,
        out_specs=[pl.BlockSpec((cells, width), lambda step: (0, 0))] * count,
        scratch_shapes=[pltpu.VMEM((width, count * cells), jnp.float32)],
        compiler_params=pltpu.CompilerParams(vmem_limit_bytes=40 * 2**20),
        cost_estimate=COST,
        name="cots_to_latents",
    )(table, *cots)


def gelu_slope(rows):
    scale = math.sqrt(2.0 / math.pi)
    squares = rows * rows
    bent = jnp.tanh(scale * (rows + 0.044715 * (squares * rows)))
    inner = scale * (1.0 + (3.0 * 0.044715) * squares)
    return 0.5 * (1.0 + bent) + 0.5 * rows * (1.0 - bent * bent) * inner


UNITS = 1024


def feed_forward_kernel(count, up, bias, down, *refs):
    parts, stacked, total = refs[:count], refs[-2], refs[-1]
    pre, hidden, *outs = refs[count:-2]
    cells = parts[0].shape[0]
    step = pl.program_id(0)

    @pl.when(step == 0)
    def _():
        for k in range(count):
            stacked[k * cells : (k + 1) * cells, :] = parts[k][...]

    rows = jnp.dot(stacked[...], up[...], preferred_element_type=jnp.float32) + bias[...]
    pre[...] = rows
    bent = jnp.tanh(math.sqrt(2.0 / math.pi) * (rows + 0.044715 * (rows * rows * rows)))
    low = (rows * (0.5 * (1.0 + bent))).astype(jnp.bfloat16)
    hidden[...] = low
    product = jnp.dot(low, down[...], preferred_element_type=jnp.float32)

    @pl.when(step == 0)
    def _():
        total[...] = product

    @pl.when(step > 0)
    def _():
        total[...] += product

    @pl.when(step == pl.num_programs(0) - 1)
    def _():
        for k in range(count):
            outs[k][...] = total[k * cells : (k + 1) * cells, :].astype(outs[k].dtype)


def feed_forward(parts, up, bias, down):
    count = len(parts)
    cells, width = parts[0].shape
    units = down.shape[0]
    rows = count * cells
    return pl.pallas_call(
        functools.partial(feed_forward_kernel, count),
        grid=(units // UNITS,),
        out_shape=[
            jax.ShapeDtypeStruct((rows, units), jnp.float32),
            jax.ShapeDtypeStruct((rows, units), jnp.bfloat16),
        ]
        + [
            jax.ShapeDtypeStruct((cells, width), jnp.float32 if k == 0 else jnp.bfloat16)
            for k in range(count)
        ],
        in_specs=[
            pl.BlockSpec((width, UNITS), lambda step: (0, step)),
            pl.BlockSpec((1, UNITS), lambda step: (0, step)),
            pl.BlockSpec((UNITS, width), lambda step: (step, 0)),
        ]
        + [pl.BlockSpec((cells, width), lambda step: (0, 0))] * count,
        out_specs=[pl.BlockSpec((rows, UNITS), lambda step: (0, step))] * 2
        + [pl.BlockSpec((cells, width), lambda step: (0, 0))] * count,
        scratch_shapes=[
            pltpu.VMEM((rows, width), jnp.bfloat16),
            pltpu.VMEM((rows, width), jnp.float32),
        ],
        compiler_params=pltpu.CompilerParams(vmem_limit_bytes=48 * 2**20),
        cost_estimate=COST,
        name="feed_forward",
    )(up, bias, down, *parts)


def feed_back_kernel(count, latent, down, up, pre, *refs):
    parts = refs[:count]
    own, down_input, pre_grad, bias, *outs = refs[count:]
    cells = own.shape[0]
    width = own.shape[1]
    h_grad = jnp.dot(
        jnp.concatenate([part[:, : latent.shape[0]] for part in parts], axis=0),
        latent[...],
        preferred_element_type=jnp.float32,
    )
    own[...] = h_grad[:cells, :]
    down_input[...] = h_grad.astype(jnp.bfloat16)
    step = 256
    for start in range(0, pre.shape[1], step):
        columns = slice(start, start + step)
        hidden_grad = lax.dot_general(
            down_input[...],
            down[columns, :],
            (((1,), (1,)), ((), ())),
            preferred_element_type=jnp.float32,
        )
        low = (hidden_grad * gelu_slope(pre[:, columns])).astype(jnp.bfloat16)
        pre_grad[:, columns] = low
        bias[:, columns] = jnp.sum(low.astype(jnp.float32), axis=0, keepdims=True)
    product = lax.dot_general(
        pre_grad[...], up[...], (((1,), (1,)), ((), ())), preferred_element_type=jnp.float32
    )
    for k in range(count):
        outs[k][...] = product[k * cells : (k + 1) * cells, :].astype(outs[k].dtype)


def feed_back(parts, latent, down, up, pre):
    count = len(parts)
    cells = parts[0].shape[0]
    width = latent.shape[1]
    units = pre.shape[1]

    def whole(array):
        return pl.BlockSpec(array.shape, lambda step: (0,) * len(array.shape))

    shapes = [
        jax.ShapeDtypeStruct((cells, width), jnp.float32),
        jax.ShapeDtypeStruct((count * cells, width), jnp.bfloat16),
        jax.ShapeDtypeStruct((count * cells, units), jnp.bfloat16),
        jax.ShapeDtypeStruct((1, units), jnp.float32),
    ] + [
        jax.ShapeDtypeStruct((cells, width), jnp.float32 if k == 0 else jnp.bfloat16)
        for k in range(count)
    ]
    operands = [latent, down, up, pre, *parts]
    return pl.pallas_call(
        functools.partial(feed_back_kernel, count),
        grid=(1,),
        out_shape=shapes,
        in_specs=[whole(one) for one in operands[:2]]
        + [pl.BlockSpec((width, units), lambda step: (0, 0))]
        + [whole(one) for one in operands[3:]],
        out_specs=[whole(one) for one in shapes],
        compiler_params=pltpu.CompilerParams(vmem_limit_bytes=56 * 2**20),
        cost_estimate=COST,
        name="feed_back",
    )(*operands)


def decode_kernel(count, table, *refs):
    rows, outs = refs[:count], refs[count:]
    cells = rows[0].shape[0]
    product = jnp.dot(
        jnp.concatenate([one[...] for one in rows], axis=0),
        table[...],
        preferred_element_type=jnp.float32,
    ).astype(jnp.bfloat16)
    for k in range(count):
        outs[k][...] = jnp.transpose(product[k * cells : (k + 1) * cells, :])


def decode_genes(latents, table):
    count = len(latents)
    cells = latents[0].shape[0]
    width, quarter = table.shape
    last = latents[0].shape[1] // width - 1
    return pl.pallas_call(
        functools.partial(decode_kernel, count),
        grid=(1,),
        out_shape=[jax.ShapeDtypeStruct((quarter, cells), jnp.bfloat16)] * count,
        in_specs=[pl.BlockSpec((width, quarter), lambda step: (0, 0))]
        + [pl.BlockSpec((cells, width), lambda step: (0, last))] * count,
        out_specs=[pl.BlockSpec((quarter, cells), lambda step: (0, 0))] * count,
        compiler_params=pltpu.CompilerParams(vmem_limit_bytes=40 * 2**20),
        cost_estimate=COST,
        name="decode_genes",
    )(table, *latents)


def chip_offsets(chips):
    order = [0]
    bit = chips // 2
    while bit:
        order = order + [one + bit for one in order]
        bit //= 2
    return order


def last_kernel(count, first, offsets, places, normed, projected, both, *refs):
    pre_grads, cots = refs[:count], refs[count : 2 * count]
    kept, sent, turned = refs[2 * count :]
    me, place = places[0], places[1]
    cells = cots[0].shape[0]
    width = normed.shape[1]
    block = kept.shape[0] // len(offsets)

    def by_offset(first):
        return jnp.concatenate(
            [
                both[
                    pl.ds(pl.multiple_of(jnp.bitwise_xor(me, k) * cells, cells), cells),
                    first : first + width,
                ]
                for k in range(count)
            ],
            axis=0,
        )

    spot = 0
    for group, (rows, columns) in enumerate(
        (
            (normed[...], [projected[k] for k in range(projected.shape[0])]),
            (by_offset(0), [jnp.concatenate([one[:, first:] for one in cots], axis=0)]),
            (by_offset(width), [jnp.concatenate([one[...] for one in pre_grads], axis=0)]),
        )
    ):
        turned[group] = jnp.transpose(rows)
        for one in columns:
            size = one.shape[1]
            for out, core in ((kept, place % 2), (sent, 1 - place % 2)):
                owners = [jnp.bitwise_xor(place // 2, k) * 2 + core for k in offsets]
                ordered = jnp.concatenate(
                    [
                        turned[group, pl.ds(pl.multiple_of(owner * block, block), block), :]
                        for owner in owners
                    ],
                    axis=0,
                )
                out[:, spot : spot + size] = jnp.dot(
                    ordered, one, preferred_element_type=jnp.float32
                ).astype(out.dtype)
            spot += size


def last_products(normed, projected, pre_grads, both, cots, first, me, place):
    count = len(cots)
    height = normed.shape[1]
    offsets = chip_offsets(lax.axis_size("blk") // 2)
    width = projected.shape[0] * projected.shape[2] + 2 * pre_grads[0].shape[1]
    return pl.pallas_call(
        functools.partial(last_kernel, count, first, offsets),
        out_shape=[
            jax.ShapeDtypeStruct((height // 2, width), jnp.float32),
            jax.ShapeDtypeStruct((height // 2, width), jnp.bfloat16),
        ],
        in_specs=[pl.BlockSpec(memory_space=pltpu.SMEM)]
        + [pl.BlockSpec(memory_space=pltpu.VMEM)] * (3 + 2 * count),
        out_specs=[pl.BlockSpec(memory_space=pltpu.VMEM)] * 2,
        scratch_shapes=[pltpu.VMEM((3, height, normed.shape[0]), jnp.bfloat16)],
        compiler_params=pltpu.CompilerParams(vmem_limit_bytes=40 * 2**20),
        cost_estimate=COST,
        name="last_products",
    )(jnp.stack([me, place]), normed, projected, both, *pre_grads, *cots)


def half_kernel(kept, other, stay, go):
    height = stay.shape[0]
    stay[...] = kept[:height, :] + other[:height, :].astype(jnp.float32)
    go[...] = (kept[height:, :] + other[height:, :].astype(jnp.float32)).astype(go.dtype)


def merge_half(kept, other):
    height, width = kept.shape
    return pl.pallas_call(
        half_kernel,
        out_shape=[
            jax.ShapeDtypeStruct((height // 2, width), jnp.float32),
            jax.ShapeDtypeStruct((height // 2, width), jnp.bfloat16),
        ],
        in_specs=[pl.BlockSpec(memory_space=pltpu.VMEM)] * 2,
        out_specs=[pl.BlockSpec(memory_space=pltpu.VMEM)] * 2,
        compiler_params=pltpu.CompilerParams(vmem_limit_bytes=40 * 2**20),
        cost_estimate=COST,
        name="merge_half",
    )(kept, other)


def pair_kernel(count, *refs):
    parts, out = refs[:count], refs[-1]
    width = out.shape[2]
    for j in range(out.shape[0] // count):
        for k in range(count):
            out[j * count + k] = parts[k][:, j * width : (j + 1) * width]


def pair_up(parts, pairs):
    count = len(parts)
    cells, width = parts[0].shape
    return pl.pallas_call(
        functools.partial(pair_kernel, count),
        out_shape=jax.ShapeDtypeStruct((pairs * count, cells, width // pairs), parts[0].dtype),
        in_specs=[pl.BlockSpec(memory_space=pltpu.VMEM)] * count,
        out_specs=pl.BlockSpec(memory_space=pltpu.VMEM),
        cost_estimate=COST,
        name="pair_up",
    )(*parts)


def assemble_kernel(count, sizes, me_ref, *refs):
    early, parts = refs[:5], refs[5 : 5 + count]
    down, up, qkv, attn, latent, decode, middle, last, sems = refs[5 + count :]
    blocks, pairs, pair, quarter, half = sizes
    me = me_ref[0]
    rows, width = attn.shape
    cut = rows // 2
    upper, lower = pl.ds(0, cut), pl.ds(cut, cut)
    ours, upper_x, lower_y, uppers, lowers = early
    moves = [
        (ours, middle.at[me]),
        (upper_x, middle.at[jnp.bitwise_xor(me, 1), upper, :]),
        (lower_y, middle.at[jnp.bitwise_xor(me, 2), lower, :]),
        (uppers.at[upper, :], middle.at[jnp.bitwise_xor(me, 2), upper, :]),
        (uppers.at[lower, :], middle.at[jnp.bitwise_xor(me, 3), upper, :]),
        (lowers.at[upper, :], middle.at[jnp.bitwise_xor(me, 1), lower, :]),
        (lowers.at[lower, :], middle.at[jnp.bitwise_xor(me, 3), lower, :]),
    ] + [(parts[k], last.at[jnp.bitwise_xor(me, k)]) for k in range(count)]
    copies = [
        pltpu.make_async_copy(source, target, sems.at[k])
        for k, (source, target) in enumerate(moves)
    ]
    for one in copies:
        one.start()
    for one in copies:
        one.wait()
    part = width // count
    ff = up.shape[1] // (count * blocks)
    latents, genes = decode.shape

    def piece(array, q, spot, size):
        return array[q, :, spot : spot + size].astype(jnp.float32)

    for q in range(count):
        down[q * rows : (q + 1) * rows, :] = piece(middle, q, 0, width)
        spot = width
        for b in range(blocks):
            up[:, (b * count + q) * ff : (b * count + q + 1) * ff] = piece(middle, q, spot, ff)
            spot += ff
        for side in range(2):
            first = q * quarter + side * half
            size = min(half, quarter - side * half, genes - first)
            if size > 0:
                decode[:, first : first + size] = middle[
                    q, side * latents : (side + 1) * latents, spot : spot + size
                ].astype(jnp.float32)
        spot = 0
        for j in range(pairs):
            for t in range(3):
                first = t * width + q * part + j * pair
                qkv[:, first : first + pair] = piece(last, q, spot, pair)
                spot += pair
        for out in (attn, latent):
            out[:, q * part : (q + 1) * part] = piece(last, q, spot, part)
            spot += part


def assemble(early, last, me, genes, quarter, half, latents, blocks, pairs, pair):
    count = len(last)
    rows = last[0].shape[0]
    width = blocks * rows
    shapes = [
        (count * rows, width),
        (rows, count * width),
        (rows, 3 * width),
        (rows, width),
        (rows, width),
        (latents, genes),
    ]
    return pl.pallas_call(
        functools.partial(assemble_kernel, count, (blocks, pairs, pair, quarter, half)),
        out_shape=[jax.ShapeDtypeStruct(shape, jnp.float32) for shape in shapes],
        in_specs=[pl.BlockSpec(memory_space=pltpu.SMEM)]
        + [pl.BlockSpec(memory_space=pl.ANY)] * (5 + count),
        out_specs=[pl.BlockSpec(memory_space=pltpu.VMEM)] * len(shapes),
        scratch_shapes=[
            pltpu.VMEM((count,) + early[0].shape, jnp.bfloat16),
            pltpu.VMEM((count,) + last[0].shape, jnp.bfloat16),
            pltpu.SemaphoreType.DMA((7 + count,)),
        ],
        compiler_params=pltpu.CompilerParams(vmem_limit_bytes=48 * 2**20),
        cost_estimate=COST,
        name="assemble",
    )(me.reshape(1), *early, *last)


def genes_kernel(count, table, *refs):
    rows, outs, stacked = refs[:count], refs[count : 2 * count], refs[-1]
    cells = rows[0].shape[0]

    @pl.when(pl.program_id(0) == 0)
    def _():
        for k in range(count):
            stacked[:, k * cells : (k + 1) * cells] = jnp.transpose(rows[k][...])

    product = jnp.dot(table[...], stacked[...], preferred_element_type=jnp.float32)
    for k in range(count):
        outs[k][...] = product[:, k * cells : (k + 1) * cells].astype(outs[k].dtype)


def cells_to_genes(table, rows, quarter):
    count = len(rows)
    cells, width = rows[0].shape
    return pl.pallas_call(
        functools.partial(genes_kernel, count),
        grid=(quarter // TALL,),
        out_shape=[jax.ShapeDtypeStruct((quarter, cells), jnp.bfloat16)] * count,
        in_specs=[pl.BlockSpec((TALL, width), lambda step: (step, 0))]
        + [pl.BlockSpec((cells, width), lambda step: (0, 0))] * count,
        out_specs=[pl.BlockSpec((TALL, cells), lambda step: (step, 0))] * count,
        scratch_shapes=[pltpu.VMEM((width, count * cells), jnp.bfloat16)],
        compiler_params=pltpu.CompilerParams(vmem_limit_bytes=58 * 2**20),
        cost_estimate=COST,
        name="cells_to_genes",
    )(table, *rows)


def embed_kernel(count, *refs):
    parts, rows = refs[:count], refs[count : 2 * count]
    small, out, stacked, results, sems = refs[2 * count :]
    steps = parts[0].shape[0] // STEP
    height = rows[0].shape[0]
    blocks, _, block = out.shape
    for k in range(count):
        stacked[k * height : (k + 1) * height, :] = rows[k][...]

    def leave(slot, step):
        start = pl.multiple_of(step * STEP, STEP)
        return pltpu.make_async_copy(
            results.at[slot], out.at[:, pl.ds(start, STEP), :], sems.at[slot]
        )

    last = pltpu.make_async_copy(
        small, out.at[:, pl.ds(steps * STEP, small.shape[1]), :], sems.at[2]
    )
    last.start()

    @pl.loop(0, steps)
    def _(step):
        slot = lax.rem(step, 2)

        @pl.when(step >= 2)
        def _():
            leave(slot, step - 2).wait()

        here = pl.ds(pl.multiple_of(step * STEP, STEP), STEP)
        product = jnp.dot(
            jnp.concatenate([part[here, :] for part in parts], axis=1),
            stacked[...],
            preferred_element_type=jnp.float32,
        ).astype(results.dtype)
        for k in range(blocks):
            results[slot, k] = product[:, k * block : (k + 1) * block]
        leave(slot, step).start()

    for step in range(max(steps - 2, 0), steps):
        leave(step % 2, step).wait()
    last.wait()


def embed_products(parts, rows, small):
    count = len(parts)
    quarter, cells = parts[0].shape
    width = rows[0].shape[1]
    blocks, extra, block = small.shape
    return pl.pallas_call(
        functools.partial(embed_kernel, count),
        out_shape=jax.ShapeDtypeStruct((blocks, quarter + extra, block), jnp.bfloat16),
        in_specs=[pl.BlockSpec(memory_space=pltpu.VMEM)] * (2 * count + 1),
        out_specs=pl.BlockSpec(memory_space=pltpu.HBM),
        scratch_shapes=[
            pltpu.VMEM((count * cells, width), jnp.bfloat16),
            pltpu.VMEM((2, blocks, STEP, block), jnp.bfloat16),
            pltpu.SemaphoreType.DMA((3,)),
        ],
        compiler_params=pltpu.CompilerParams(vmem_limit_bytes=58 * 2**20),
        cost_estimate=COST,
        name="embed_products",
    )(*parts, *rows, small)


def products_kernel(count, *refs):
    out = refs[-1]
    spot = 0
    for k in range(count):
        rows = jnp.transpose(refs[2 * k][...])
        columns = refs[2 * k + 1]
        width = columns.shape[1]
        for start in range(0, width, 256):
            out[:, spot + start : spot + start + 256] = jnp.dot(
                rows, columns[:, start : start + 256], preferred_element_type=jnp.float32
            ).astype(out.dtype)
        spot += width


def row_products(pairs):
    operands = [one for pair in pairs for one in pair]
    height = pairs[0][0].shape[1]
    width = sum(b.shape[1] for _, b in pairs)
    return pl.pallas_call(
        functools.partial(products_kernel, len(pairs)),
        out_shape=jax.ShapeDtypeStruct((height, width), jnp.bfloat16),
        in_specs=[pl.BlockSpec(memory_space=pltpu.VMEM)] * len(operands),
        out_specs=pl.BlockSpec(memory_space=pltpu.VMEM),
        compiler_params=pltpu.CompilerParams(vmem_limit_bytes=48 * 2**20),
        cost_estimate=COST,
        name="row_products",
    )(*operands)


def decoder_kernel(count, *refs):
    rows, cots, out, turned = refs[:count], refs[count : 2 * count], refs[-2], refs[-1]
    cells = rows[0].shape[0]

    @pl.when(pl.program_id(0) == 0)
    def _():
        for k in range(count):
            turned[:, k * cells : (k + 1) * cells] = jnp.transpose(rows[k][...])

    out[...] = lax.dot_general(
        turned[...],
        jnp.concatenate([one[...] for one in cots], axis=1),
        (((1,), (1,)), ((), ())),
        preferred_element_type=jnp.float32,
    ).astype(out.dtype)


def decoder_products(latents, cots, width):
    count = len(latents)
    cells = latents[0].shape[0]
    last = latents[0].shape[1] // width - 1
    quarter = cots[0].shape[0]
    step_rows = math.gcd(quarter, 1152)
    return pl.pallas_call(
        functools.partial(decoder_kernel, count),
        grid=(quarter // step_rows,),
        out_shape=jax.ShapeDtypeStruct((width, quarter), jnp.bfloat16),
        in_specs=[pl.BlockSpec((cells, width), lambda step: (0, last))] * count
        + [pl.BlockSpec((step_rows, cells), lambda step: (step, 0))] * count,
        out_specs=pl.BlockSpec((width, step_rows), lambda step: (0, step)),
        scratch_shapes=[pltpu.VMEM((width, count * cells), jnp.bfloat16)],
        compiler_params=pltpu.CompilerParams(vmem_limit_bytes=40 * 2**20),
        cost_estimate=COST,
        name="decoder_products",
    )(*latents, *cots)


def head_probs(keys, queries, scaling):
    scores = (
        lax.dot_general(keys, queries, (((1,), (1,)), ((), ())), preferred_element_type=jnp.float32)
        * scaling
    )
    scores = jnp.exp(scores - jnp.max(scores, axis=0, keepdims=True))
    return scores * (1.0 / jnp.sum(scores, axis=0, keepdims=True))


def attend_kernel(heads, width, rows_ref, out, turned):
    step = pl.program_id(0)
    height = out.shape[0]
    group = heads * width

    @pl.when(step == 0)
    def _():
        turned[...] = jnp.transpose(rows_ref[:, 2 * group : 3 * group])

    block = rows_ref[pl.ds(pl.multiple_of(step * height, height), height), :group]
    results = []
    for h in range(heads):
        probs = head_probs(
            rows_ref[:, group + h * width : group + (h + 1) * width],
            block[:, h * width : (h + 1) * width],
            width ** (-0.5),
        ).astype(jnp.bfloat16)
        results.append(
            jnp.dot(turned[h * width : (h + 1) * width, :], probs, preferred_element_type=jnp.float32)
        )
    out[...] = jnp.transpose(jnp.concatenate(results, axis=0)).astype(out.dtype)


def attend(rows, heads):
    cells, total = rows.shape
    group = total // 3
    height = math.gcd(cells, 1024)
    return pl.pallas_call(
        functools.partial(attend_kernel, heads, group // heads),
        grid=(cells // height,),
        out_shape=jax.ShapeDtypeStruct((cells, group), jnp.bfloat16),
        in_specs=[pl.BlockSpec((cells, total), lambda step: (0, 0))],
        out_specs=pl.BlockSpec((height, group), lambda step: (step, 0)),
        scratch_shapes=[pltpu.VMEM((group, cells), jnp.bfloat16)],
        compiler_params=pltpu.CompilerParams(vmem_limit_bytes=40 * 2**20),
        cost_estimate=COST,
        name="attend",
    )(rows)


def attend_back_kernel(heads, width, rows_ref, cot_ref, out, turned, key_sum, value_sum):
    step = pl.program_id(0)
    group = heads * width
    height = rows_ref.shape[0] // pl.num_programs(0)
    scaling = width ** (-0.5)

    @pl.when(step == 0)
    def _():
        turned[...] = jnp.transpose(rows_ref[:, group : 2 * group])
        key_sum[...] = jnp.zeros_like(key_sum)
        value_sum[...] = jnp.zeros_like(value_sum)

    here = pl.ds(pl.multiple_of(step * height, height), height)
    block = rows_ref[here, :group]
    cots = cot_ref[here, :]
    results = []
    for h in range(heads):
        columns = slice(h * width, (h + 1) * width)
        queries = block[:, columns]
        cot = cots[:, columns]
        probs = head_probs(
            rows_ref[:, group + h * width : group + (h + 1) * width], queries, scaling
        )
        prob_grad = lax.dot_general(
            rows_ref[:, 2 * group + h * width : 2 * group + (h + 1) * width],
            cot,
            (((1,), (1,)), ((), ())),
            preferred_element_type=jnp.float32,
        )
        delta = jnp.sum(probs * prob_grad, axis=0, keepdims=True)
        score_grad = (probs * (prob_grad - delta)).astype(jnp.bfloat16)
        results.append(
            jnp.dot(turned[columns, :], score_grad, preferred_element_type=jnp.float32) * scaling
        )
        key_sum[:, columns] += jnp.dot(score_grad, queries, preferred_element_type=jnp.float32)
        value_sum[:, columns] += jnp.dot(
            probs.astype(jnp.bfloat16), cot, preferred_element_type=jnp.float32
        )
    out[here, :group] = jnp.transpose(jnp.concatenate(results, axis=0)).astype(out.dtype)

    @pl.when(step == pl.num_programs(0) - 1)
    def _():
        out[:, group : 2 * group] = (key_sum[...] * scaling).astype(out.dtype)
        out[:, 2 * group :] = value_sum[...].astype(out.dtype)


def attend_back(rows, cot, heads):
    cells, total = rows.shape
    group = total // 3
    height = math.gcd(cells, 1024)
    return pl.pallas_call(
        functools.partial(attend_back_kernel, heads, group // heads),
        grid=(cells // height,),
        out_shape=jax.ShapeDtypeStruct((cells, total), jnp.bfloat16),
        in_specs=[
            pl.BlockSpec((cells, total), lambda step: (0, 0)),
            pl.BlockSpec((cells, group), lambda step: (0, 0)),
        ],
        out_specs=pl.BlockSpec((cells, total), lambda step: (0, 0)),
        scratch_shapes=[
            pltpu.VMEM((group, cells), jnp.bfloat16),
            pltpu.VMEM((cells, group), jnp.float32),
            pltpu.VMEM((cells, group), jnp.float32),
        ],
        compiler_params=pltpu.CompilerParams(vmem_limit_bytes=40 * 2**20),
        cost_estimate=COST,
        name="attend_back",
    )(rows, cot)


def split_model(
    counts,
    library,
    coords,
    noise,
    decoded_cot,
    prior_cot,
    embed_t,
    w_qkv,
    w_attn_out,
    w_up,
    up_bias,
    w_down,
    w_latent,
    w_decode,
    comp_means,
    norm_params,
):
    slides = lax.axis_size("slide")
    blocks = lax.axis_size("blk")
    me = lax.axis_index("slide")
    genes = embed_t.shape[1]
    cells = counts.shape[1]
    model_width = w_attn_out.shape[1]
    own_rows = w_qkv.shape[0]
    latent_width = w_decode.shape[0] * blocks
    mixture_count = comp_means.shape[1]
    quarter = -(-genes // (slides * ROWS)) * ROWS
    padded = quarter * slides
    head_part = model_width // slides
    pair = model_width // blocks
    pairs = head_part // pair
    ff_part = up_bias.shape[0] // slides
    latent_part = model_width // slides

    def place_of(k):
        return jnp.bitwise_xor(me, k)

    def column_part(rows, width, place):
        return lax.dynamic_slice_in_dim(rows, place * width, width, 1)

    def whole(piece, axis):
        return in_order(share(piece, slides), me, axis)

    def wide(piece):
        return piece.astype(jnp.float32)

    embed_part = lax.dynamic_slice_in_dim(
        jnp.pad(embed_t.T, ((0, padded - genes), (0, 0))), me * quarter, quarter, 0
    )
    bias_part = lax.dynamic_slice_in_dim(up_bias, me * ff_part, ff_part, 0)
    mean_cols = comp_means.size // own_rows
    folds = mixture_count // mean_cols
    own_latents = w_decode.shape[0]
    small = jnp.concatenate(
        [
            norm_params.T,
            jnp.concatenate(
                [comp_means.T[k * mean_cols : (k + 1) * mean_cols] for k in range(folds)], axis=1
            ),
            bias_part.reshape(-1, own_rows),
        ],
        axis=0,
    )
    small_rows = small.shape[0]
    small = jnp.pad(small, ((0, SMALL - small_rows), (0, 0)))
    qkv_width = pairs * 3 * pair
    qkv_part = [
        lax.dynamic_slice_in_dim(w_qkv, k * model_width + me * head_part, head_part, 1)
        for k in range(3)
    ]
    qkv_part = jnp.concatenate(
        [part[:, j * pair : (j + 1) * pair] for j in range(pairs) for part in qkv_part], axis=1
    ).T
    out_latent = jnp.concatenate(
        [
            lax.dynamic_slice_in_dim(weight, me * head_part, head_part, 1)
            for weight in (w_attn_out, w_latent)
        ],
        axis=1,
    ).T
    embedding = gather_blk(
        jnp.concatenate([embed_part, small, qkv_part, out_latent], axis=0), 1
    )
    small_all = embedding[quarter : quarter + SMALL]
    qkv_end = quarter + SMALL + qkv_width
    weight_qkv = embedding[quarter + SMALL : qkv_end].reshape(pairs, 3 * pair, model_width)
    out_latent = embedding[qkv_end:]
    norm_float = small_all[:4].astype(jnp.float32)
    centres = small_all[4 : 4 + mean_cols].reshape(mean_cols, blocks, folds, own_latents)
    centres = jnp.transpose(centres, (1, 3, 2, 0)).reshape(latent_width, mixture_count)
    bias_up = small_all[4 + mean_cols].astype(jnp.float32)
    expr_parts = swap(expression_parts(counts, library, me, slides, quarter))

    cot_all = jnp.pad(decoded_cot[0].T, ((0, padded - genes), (0, 0)))
    cot_first = [
        lax.dynamic_slice_in_dim(cot_all, place_of(k) * quarter, quarter, 0)
        for k in range(slides)
    ]
    cot_parts = swap([after(piece, *expr_parts[1:]) for piece in cot_first])
    up_part = jnp.concatenate(
        [
            lax.dynamic_slice_in_dim(w_up, (k * slides + me) * ff_part, ff_part, 1)
            for k in range(blocks)
        ],
        axis=1,
    )
    down_part = lax.dynamic_slice_in_dim(w_down, me * ff_part, ff_part, 0)
    expr_rows = turn_parts(expr_parts)
    half = -(-quarter // 256) * 128
    decode_part = lax.dynamic_slice_in_dim(
        jnp.pad(w_decode, ((0, 0), (0, padded - genes))), me * quarter, quarter, 1
    )
    decode_part = jnp.concatenate(
        [decode_part[:, :half], jnp.pad(decode_part[:, half:], ((0, 0), (0, 2 * half - quarter)))],
        axis=0,
    )
    middle = gather_blk(
        after(
            jnp.concatenate([up_part, decode_part], axis=1),
            embedding,
            expr_rows,
            *cot_parts[1:],
        )
    )
    halves = middle[:, model_width:].reshape(blocks, 2, own_latents, half)
    weight_decode = jnp.concatenate(
        [
            halves[:, 0].reshape(latent_width, half),
            halves[:, 1].reshape(latent_width, half)[:, : quarter - half],
        ],
        axis=1,
    )

    h_zero = collect(embed_cells(expr_rows, embedding, slides))
    h_zero = h_zero + spatial_code(coords[0], model_width)
    normed_one, norm_one_back = jax.vjp(layer_norm, h_zero, norm_float[0], norm_float[1])
    normed_one_all = jnp.concatenate(share(normed_one.astype(jnp.bfloat16), slides), axis=0)
    projected = jnp.einsum(
        "ck,pfk->pcf", normed_one_all, weight_qkv, preferred_element_type=jnp.float32
    ).astype(jnp.bfloat16)

    def to_heads(rows):
        return lax.all_to_all(
            rows.reshape(blocks, cells, rows.shape[-1]), "blk", 0, 0, tiled=True
        ).reshape(blocks * cells, rows.shape[-1])

    out_shares = share(after(out_latent[:head_part], normed_one_all), slides)
    latent_cots = cots_to_latents(cot_parts, weight_decode)
    centres_float = centres.astype(jnp.float32)
    half_norms = 0.5 * jnp.sum(centres_float * centres_float, axis=0)
    head_rows, half_norms, centres_float = lax.optimization_barrier(
        (after(to_heads(projected), latent_cots[-1], *out_shares[1:]), half_norms, centres_float)
    )
    per_pair = pair // HEAD_DIM
    latent_shares = share(after(out_latent[head_part:], head_rows), slides)
    weight_out = order_rows(out_shares, me)
    weight_latent = order_rows(latent_shares, me)
    head_out = attend(head_rows, per_pair)
    weight_down = gather_blk(after(down_part, middle, weight_out))
    own_heads = to_heads(head_out).reshape(pairs, slides, cells, pair)
    own_heads = after(own_heads, *latent_shares[1:])
    attended_parts = swap(
        [
            jnp.concatenate([own_heads[j, k] for j in range(pairs)], axis=1)
            for k in range(slides)
        ]
    )
    attended_low = in_order(attended_parts, me, 1)
    h_one = h_zero + contract_cols(attended_low, weight_out)
    normed_two, norm_two_back = jax.vjp(layer_norm, h_one, norm_float[2], norm_float[3])
    normed_two_low = normed_two.astype(jnp.bfloat16)
    normed_two_rows = share(normed_two_low, slides)
    normed_two_rows[0] = after(normed_two_rows[0], weight_latent)
    hidden_pre, hidden_low, *h_two_parts = feed_forward(
        normed_two_rows, middle, bias_up[None], weight_down
    )
    normed_two_all = jnp.concatenate(normed_two_rows, axis=0)
    h_two_sum = collect(h_two_parts)
    latent_from_decode = collect(latent_cots)
    h_two = h_one + after(h_two_sum, latent_from_decode)
    h_two_low = h_two.astype(jnp.bfloat16)
    both_rows = lax.all_gather(
        jnp.concatenate([attended_low, h_two_low], axis=1), "slide", axis=0, tiled=True
    )
    latent_pre = contract_cols(h_two_low, weight_latent)
    spread = jnp.exp(0.5 * latent_pre[:, latent_width:])
    latent = latent_pre[:, :latent_width] + spread * noise[0]
    mixing = latent_width ** (-0.5)
    mix = (exact_dot(latent, centres_float, 1, 0) - half_norms) * mixing
    mix_max = jnp.max(mix, axis=-1, keepdims=True)
    mix_exp = jnp.exp(mix - mix_max)
    mix_sum = jnp.sum(mix_exp, axis=-1, keepdims=True)
    prior = -(mix_max + jnp.log(mix_sum))[:, 0]
    shares = prior_cot[0][:, None] * (mix_exp / mix_sum)
    latent_from_prior = exact_dot(shares, centres_float, 1, 1) * -mixing
    centre_grad = (
        centres_float * jnp.sum(shares, axis=0) - exact_dot(latent, shares, 0, 0)
    ) * mixing

    latent_total = latent_from_decode + latent_from_prior
    pre_grad = jnp.concatenate(
        [latent_total, latent_total * noise[0] * spread * 0.5], axis=-1
    ).astype(jnp.bfloat16)
    both_parts = share(
        jnp.concatenate([pre_grad, latent.astype(jnp.bfloat16)], axis=1), slides
    )
    h_two_grad, down_input, pre_hidden_grad, up_bias_grad, *normed_two_parts = feed_back(
        both_parts, weight_latent, weight_down, middle, hidden_pre
    )
    normed_two_grad = collect(normed_two_parts)
    latent_parts = [after(part, normed_two_parts[-1]) for part in both_parts]
    decode_local = decoder_products(latent_parts, cot_parts, latent_width)
    decoded_rows = decode_genes(latent_parts, weight_decode)
    normed_two_grad = after(normed_two_grad, decode_local, decoded_rows[-1])
    decode_own = scatter_blk(after(decode_local, both_rows, normed_two_grad))
    h_one_part, gain_two_grad, shift_two_grad = norm_two_back(normed_two_grad)
    h_one_grad = h_two_grad + h_one_part
    out_input = h_one_grad.astype(jnp.bfloat16)
    attended_grad = jnp.dot(out_input, weight_out, preferred_element_type=jnp.float32).astype(jnp.bfloat16)
    grad_parts = swap([column_part(attended_grad, head_part, place_of(k)) for k in range(slides)])
    out_heads = to_heads(pair_up(grad_parts, pairs))

    middle_local = row_products(
        [
            (hidden_low, after(down_input, *grad_parts[1:])),
            (normed_two_all, pre_hidden_grad),
        ]
    )
    out_heads = after(out_heads, middle_local)
    decoded_parts = swap(
        [after(one, *grad_parts[1:]) for one in decoded_rows[:-1]]
        + [after(decoded_rows[-1], out_heads)]
    )
    out_heads = after(out_heads, *decoded_parts[1:-1])
    head_grads = attend_back(head_rows, out_heads, per_pair)
    middle_grad = scatter_blk(after(middle_local, decode_own, head_grads))
    cot_cols = swap(
        [
            after(column_part(out_input, head_part, place_of(k)), head_grads)
            for k in range(slides)
        ]
    )
    projected_grad = to_heads(head_grads).reshape(pairs, slides * cells, 3 * pair)
    projected_grad = after(projected_grad, decoded_parts[-1], *cot_cols[1:])
    normed_one_parts = lowered(
        split_rows(
            jnp.einsum(
                "pcf,pfk->ck", projected_grad, weight_qkv, preferred_element_type=jnp.float32
            ),
            slides,
        )
    )
    normed_one_grad = collect(normed_one_parts)
    last_kept, last_sent = last_products(
        normed_one_all,
        after(projected_grad, normed_one_parts[-1]),
        [column_part(part, latent_part, me) for part in both_parts],
        both_rows,
        cot_cols,
        0,
        me,
        lax.axis_index("blk"),
    )
    last_kept, last_sent = merge_half(last_kept, to_core(last_sent))
    normed_one_grad = after(normed_one_grad, last_sent)
    h_zero_part, gain_one_grad, shift_one_grad = norm_one_back(normed_one_grad)
    h_zero_low = (h_one_grad + h_zero_part).astype(jnp.bfloat16)
    h_zero_parts = share(h_zero_low, slides)
    bit = 1
    while last_kept.shape[0] > own_rows:
        last_kept, last_sent = merge_half(last_kept, to_chip(last_sent, bit))
        bit *= 2
    h_zero_parts = [after(h_zero_parts[0], last_sent)] + h_zero_parts[1:]
    last_other = to_chip(last_sent, bit)

    small_grad = jnp.concatenate(
        [
            jnp.stack([gain_one_grad, shift_one_grad, gain_two_grad, shift_two_grad], axis=0),
            jnp.transpose(
                centre_grad.reshape(blocks, own_latents, folds, mean_cols), (3, 0, 2, 1)
            ).reshape(mean_cols, model_width),
            up_bias_grad,
        ],
        axis=0,
    )
    small_grad = jnp.pad(small_grad, ((0, SMALL - small_rows), (0, 0))).astype(jnp.bfloat16)
    small_grad = jnp.transpose(small_grad.reshape(SMALL, blocks, own_rows), (1, 0, 2))
    embed_local = embed_products(expr_parts, h_zero_parts, small_grad)
    gene_rows = cells_to_genes(
        embedding, [after(part, embed_local) for part in h_zero_parts], quarter
    )
    embed_own = scatter_blk(after(embed_local, middle_grad))[0]
    decode_half = jnp.concatenate(
        [decode_own[:, :half], jnp.pad(decode_own[:, half:], ((0, 0), (0, 2 * half - quarter)))],
        axis=0,
    )
    early = after(jnp.concatenate([middle_grad, decode_half], axis=1), *h_zero_parts[1:])
    early_parts = share_halves(early)
    gene_parts = swap([after(part, *early_parts[1:3]) for part in gene_rows])
    last_low = (last_kept + after(last_other, *gene_parts[1:3]).astype(jnp.float32)).astype(
        jnp.bfloat16
    )
    last_shares = share(last_low, slides)
    embed_shares = share(
        after(embed_own, *gene_parts[1:], *last_shares[1:], *early_parts[1:]), slides
    )
    expr_grad = spread_parts(gene_parts, me, genes)
    decoded = join_parts(decoded_parts, me, quarter, genes, jnp.bfloat16).T
    down_grad, up_grad, qkv_grad, attn_out_grad, latent_grad, decode_grad = assemble(
        early_parts, last_shares, me, genes, quarter, half, own_latents, blocks, pairs, pair
    )
    embed_grad, norm_grad, means_grad, up_bias_grad = finish(
        embed_shares, me, quarter, genes, mean_cols, folds
    )

    return (
        decoded[None],
        prior[None],
        expr_grad,
        embed_grad.T,
        qkv_grad,
        attn_out_grad,
        up_grad,
        up_bias_grad.reshape(-1),
        down_grad,
        latent_grad,
        decode_grad,
        means_grad.T,
        norm_grad.T,
    )


def fits(mesh):
    slides, blocks = mesh.shape["slide"], mesh.shape["blk"]
    return slides & (slides - 1) == 0 and HEADS % slides == 0 and HEADS % blocks == 0


def solution(mesh):
    placed = (
        P("slide", "blk", None),
        P("slide", "blk"),
        P("slide", "blk", None),
        P("slide", "blk", None),
        P("slide", "blk", None),
        P("slide", "blk"),
        P("blk", None),
        P("blk", None),
        P("blk", None),
        P("blk", None),
        P("blk"),
        P("blk", None),
        P("blk", None),
        P("blk", None),
        P("blk", None),
        P("blk", None),
    )
    return jax.shard_map(
        split_model if fits(mesh) else local,
        mesh=mesh,
        in_specs=placed,
        out_specs=(
            P("slide", "blk", None),
            P("slide", "blk"),
            P("slide", "blk", None),
            P("blk", None),
            P("blk", None),
            P("blk", None),
            P("blk", None),
            P("blk"),
            P("blk", None),
            P("blk", None),
            P("blk", None),
            P("blk", None),
            P("blk", None),
        ),
        check_vma=False,
    )
```

```python
import functools
import math

import jax
import jax.numpy as jnp
from jax import lax
from jax.experimental import pallas as pl
from jax.experimental.pallas import tpu as pltpu
from jax.sharding import PartitionSpec as P

HEADS = 16
HEAD_DIM = 64


eps_norm = 1e-05


def contract_rows(former, latter):
    return lax.dot_general(
        former, latter, (((0,), (0,)), ((), ())), preferred_element_type=jnp.float32
    )


def contract_cols(former, latter):
    return lax.dot_general(
        former, latter, (((1,), (1,)), ((), ())), preferred_element_type=jnp.float32
    )


def layer_norm(tensor, norm_gain, norm_shift):
    center = tensor - jnp.mean(tensor, axis=-1, keepdims=True)
    inverse = lax.rsqrt(jnp.mean(center * center, axis=-1, keepdims=True) + eps_norm)
    return center * inverse * norm_gain + norm_shift


def spatial_code(coords, model_width):
    quarter = model_width // 4
    frequency = jnp.exp(-math.log(10000.0) * jnp.arange(quarter, dtype=jnp.float32) / quarter)
    first_axis = coords[..., 0:1].astype(jnp.float32) * frequency
    second_axis = coords[..., 1:2].astype(jnp.float32) * frequency
    return jnp.concatenate(
        [jnp.sin(first_axis), jnp.cos(first_axis), jnp.sin(second_axis), jnp.cos(second_axis)],
        axis=-1,
    )


def mixture_term(latent, centres):
    scores = (
        jnp.dot(
            latent, centres, precision=lax.Precision.HIGHEST, preferred_element_type=jnp.float32
        )
        - 0.5 * jnp.sum(centres * centres, axis=0)
    ) * latent.shape[-1] ** (-0.5)
    return -jax.nn.logsumexp(scores, axis=-1)


def split_single(rows_in, head_count):
    arrived_rows = rows_in.shape[0]
    block_rows = 512
    return rows_in.reshape(
        (arrived_rows // block_rows, block_rows, head_count, rows_in.shape[1] // head_count)
    )


def split_blocks(key_rows, value_rows, head_count):
    return (split_single(key_rows, head_count), split_single(value_rows, head_count))


def local(
    counts,
    library,
    coords,
    noise,
    decoded_cot,
    prior_cot,
    embed_t,
    w_qkv,
    w_attn_out,
    w_up,
    up_bias,
    w_down,
    w_latent,
    w_decode,
    comp_means,
    norm_params,
):
    gathered = (
        lax.all_gather(embed_t, "blk", axis=0, tiled=True),
        lax.all_gather(w_qkv, "blk", axis=0, tiled=True),
        lax.all_gather(w_attn_out, "blk", axis=0, tiled=True),
        lax.all_gather(w_up, "blk", axis=0, tiled=True),
        lax.all_gather(up_bias, "blk", axis=0, tiled=True),
        lax.all_gather(w_down, "blk", axis=0, tiled=True),
        lax.all_gather(w_latent, "blk", axis=0, tiled=True),
        lax.all_gather(w_decode, "blk", axis=0, tiled=True),
        lax.all_gather(comp_means, "blk", axis=0, tiled=True),
        lax.all_gather(norm_params, "blk", axis=0, tiled=True),
    )
    (
        embedding,
        weight_qkv,
        weight_out,
        weight_up,
        bias_up,
        weight_down,
        weight_latent,
        weight_decode,
        centres,
        norm_table,
    ) = gathered
    head_count = HEADS
    head_width = HEAD_DIM
    scaling = head_width ** (-0.5)
    model_width = embedding.shape[0]
    latent_width = weight_decode.shape[0]
    blk_count = lax.axis_size("blk")
    expression = jnp.log1p(
        counts[0].astype(jnp.float32) * 10000.0 / library[0].astype(jnp.float32)[:, None]
    )
    expression_low = expression.astype(jnp.bfloat16)
    local_cells = expression.shape[0]
    norm_float = norm_table.astype(jnp.float32)
    h_zero = contract_cols(expression_low, embedding) + spatial_code(coords[0], model_width)
    normed_one, norm_one_back = jax.vjp(layer_norm, h_zero, norm_float[:, 0], norm_float[:, 1])
    normed_one_low = normed_one.astype(jnp.bfloat16)
    projected = jnp.dot(normed_one_low, weight_qkv, preferred_element_type=jnp.float32).astype(
        jnp.bfloat16
    )
    queries = projected[:, :model_width].reshape(local_cells, head_count, head_width)
    key_rows = projected[:, model_width : 2 * model_width]
    value_rows = projected[:, 2 * model_width :]
    stat_start = (
        jnp.full((head_count, local_cells), -1e30, jnp.float32),
        jnp.zeros((head_count, local_cells), jnp.float32),
    )
    key_blocks = split_single(lax.all_gather(key_rows, "blk", axis=0, tiled=True), head_count)

    def per_block(status, key_block):
        running_max, running_sum = status
        scores = (
            jnp.einsum("thd,khd->htk", queries, key_block, preferred_element_type=jnp.float32)
            * scaling
        )
        new_max = jnp.maximum(running_max, jnp.max(scores, axis=-1))
        running_sum = running_sum * jnp.exp(running_max - new_max) + jnp.sum(
            jnp.exp(scores - new_max[..., None]), axis=-1
        )
        return ((new_max, running_sum), None)

    result, unused = lax.scan(per_block, stat_start, key_blocks)
    running_max, running_sum = result
    log_total = running_max + jnp.log(running_sum)
    arrived = (
        lax.all_gather(key_rows, "blk", axis=0, tiled=True),
        lax.all_gather(value_rows, "blk", axis=0, tiled=True),
    )
    key_blocks, value_blocks = split_blocks(arrived[0], arrived[1], head_count)

    def per_block(weighted, block_pair):
        scores = (
            jnp.einsum("thd,khd->htk", queries, block_pair[0], preferred_element_type=jnp.float32)
            * scaling
        )
        probs_low = jnp.exp(scores - log_total[..., None]).astype(jnp.bfloat16)
        weighted = weighted + jnp.einsum(
            "htk,khd->htd", probs_low, block_pair[1], preferred_element_type=jnp.float32
        )
        return (weighted, None)

    result, unused = lax.scan(
        per_block,
        jnp.zeros((head_count, local_cells, head_width), jnp.float32),
        (key_blocks, value_blocks),
    )
    attended_cells = jnp.transpose(result, (1, 0, 2))
    attended_low = attended_cells.reshape(local_cells, model_width).astype(jnp.bfloat16)
    h_one = h_zero + jnp.dot(attended_low, weight_out, preferred_element_type=jnp.float32)
    normed_two, norm_two_back = jax.vjp(layer_norm, h_one, norm_float[:, 2], norm_float[:, 3])
    normed_two_low = normed_two.astype(jnp.bfloat16)
    hidden_pre = jnp.dot(
        normed_two_low, weight_up, preferred_element_type=jnp.float32
    ) + bias_up.astype(jnp.float32)
    hidden_act, gelu_back = jax.vjp(jax.nn.gelu, hidden_pre)
    hidden_low = hidden_act.astype(jnp.bfloat16)
    h_two = h_one + jnp.dot(hidden_low, weight_down, preferred_element_type=jnp.float32)
    h_two_low = h_two.astype(jnp.bfloat16)
    latent_pre = jnp.dot(h_two_low, weight_latent, preferred_element_type=jnp.float32)
    spread = jnp.exp(0.5 * latent_pre[:, latent_width:])
    latent = latent_pre[:, :latent_width] + spread * noise[0]
    latent_low = latent.astype(jnp.bfloat16)
    decoded = jnp.dot(latent_low, weight_decode, preferred_element_type=jnp.float32).astype(
        jnp.bfloat16
    )
    prior, prior_back = jax.vjp(mixture_term, latent, centres.astype(jnp.float32))
    out_grad = decoded_cot[0]
    latent_from_decode = contract_cols(out_grad, weight_decode)
    latent_from_prior, centre_grad = prior_back(prior_cot[0])
    latent_total = latent_from_decode + latent_from_prior
    pre_grad = jnp.concatenate(
        [latent_total, latent_total * noise[0] * spread * 0.5], axis=-1
    ).astype(jnp.bfloat16)
    latent_weight_grad = contract_rows(h_two_low, pre_grad)
    h_two_grad = contract_cols(pre_grad, weight_latent)
    down_input = h_two_grad.astype(jnp.bfloat16)
    down_grad = contract_rows(hidden_low, down_input)
    hidden_grad = contract_cols(down_input, weight_down)
    pre_hidden_grad = gelu_back(hidden_grad)[0].astype(jnp.bfloat16)
    up_bias_grad = jnp.sum(pre_hidden_grad.astype(jnp.float32), axis=0)
    up_grad = contract_rows(normed_two_low, pre_hidden_grad)
    normed_two_grad = contract_cols(pre_hidden_grad, weight_up)
    h_one_part, gain_two_grad, shift_two_grad = norm_two_back(normed_two_grad)
    h_one_grad = h_two_grad + h_one_part
    out_input = h_one_grad.astype(jnp.bfloat16)
    attn_out_grad = contract_rows(attended_low, out_input)
    attended_grad = contract_cols(out_input, weight_out).astype(jnp.bfloat16)
    out_heads = attended_grad.reshape(local_cells, head_count, head_width)
    row_delta = jnp.sum(out_heads.astype(jnp.float32) * attended_cells, axis=-1).T
    query_zero = jnp.zeros((head_count, local_cells, head_width), jnp.float32)
    start_back = (query_zero, jnp.zeros((local_cells * blk_count, 2 * model_width), jnp.float32))
    arrived = (
        lax.all_gather(key_rows, "blk", axis=0, tiled=True),
        lax.all_gather(value_rows, "blk", axis=0, tiled=True),
    )
    key_blocks, value_blocks = split_blocks(arrived[0], arrived[1], head_count)
    arrived_rows = arrived[0].shape[0]

    def per_block(query_sum, block_pair):
        scores = (
            jnp.einsum("thd,khd->htk", queries, block_pair[0], preferred_element_type=jnp.float32)
            * scaling
        )
        probs = jnp.exp(scores - log_total[..., None])
        prob_grad = jnp.einsum(
            "thd,khd->htk", out_heads, block_pair[1], preferred_element_type=jnp.float32
        )
        score_grad = (probs * (prob_grad - row_delta[..., None])).astype(jnp.bfloat16)
        query_sum = query_sum + jnp.einsum(
            "htk,khd->htd", score_grad, block_pair[0], preferred_element_type=jnp.float32
        )
        key_part = (
            jnp.einsum("htk,thd->khd", score_grad, queries, preferred_element_type=jnp.float32)
            * scaling
        )
        value_part = jnp.einsum(
            "htk,thd->khd",
            probs.astype(jnp.bfloat16),
            out_heads,
            preferred_element_type=jnp.float32,
        )
        block_rows = key_part.shape[0]
        return (
            query_sum,
            jnp.concatenate(
                [key_part.reshape(block_rows, -1), value_part.reshape(block_rows, -1)], axis=-1
            ),
        )

    query_total, stacked = lax.scan(per_block, start_back[0], (key_blocks, value_blocks))
    stacked = stacked.reshape(arrived_rows, stacked.shape[-1])
    carried_back = (query_total, stacked)
    query_total = carried_back[0]
    own_pairs = lax.psum_scatter(
        carried_back[1].astype(jnp.bfloat16), "blk", scatter_dimension=0, tiled=True
    ).astype(jnp.float32)
    query_rows = jnp.transpose(query_total * scaling, (1, 0, 2)).reshape(local_cells, model_width)
    projected_grad = jnp.concatenate([query_rows, own_pairs], axis=-1).astype(jnp.bfloat16)
    qkv_grad = contract_rows(normed_one_low, projected_grad)
    normed_one_grad = contract_cols(projected_grad, weight_qkv)
    h_zero_part, gain_one_grad, shift_one_grad = norm_one_back(normed_one_grad)
    h_zero_low = (h_one_grad + h_zero_part).astype(jnp.bfloat16)
    expr_grad = jnp.dot(h_zero_low, embedding, preferred_element_type=jnp.float32)
    norm_grad = jnp.stack([gain_one_grad, shift_one_grad, gain_two_grad, shift_two_grad], axis=0).T
    centre_grad = centre_grad.T.T
    embed_slot = contract_rows(h_zero_low, expression_low)
    decode_slot = contract_rows(latent_low, out_grad)
    block_parts = (
        lax.psum_scatter(
            embed_slot.astype(jnp.bfloat16), "blk", scatter_dimension=0, tiled=True
        ).astype(jnp.float32),
        lax.psum_scatter(
            qkv_grad.astype(jnp.bfloat16), "blk", scatter_dimension=0, tiled=True
        ).astype(jnp.float32),
        lax.psum_scatter(
            attn_out_grad.astype(jnp.bfloat16), "blk", scatter_dimension=0, tiled=True
        ).astype(jnp.float32),
        lax.psum_scatter(
            up_grad.astype(jnp.bfloat16), "blk", scatter_dimension=0, tiled=True
        ).astype(jnp.float32),
        lax.psum_scatter(
            up_bias_grad.astype(jnp.bfloat16), "blk", scatter_dimension=0, tiled=True
        ).astype(jnp.float32),
        lax.psum_scatter(
            down_grad.astype(jnp.bfloat16), "blk", scatter_dimension=0, tiled=True
        ).astype(jnp.float32),
        lax.psum_scatter(
            latent_weight_grad.astype(jnp.bfloat16), "blk", scatter_dimension=0, tiled=True
        ).astype(jnp.float32),
        lax.psum_scatter(
            decode_slot.astype(jnp.bfloat16), "blk", scatter_dimension=0, tiled=True
        ).astype(jnp.float32),
        lax.psum_scatter(
            centre_grad.astype(jnp.bfloat16), "blk", scatter_dimension=0, tiled=True
        ).astype(jnp.float32),
        lax.psum_scatter(
            norm_grad.astype(jnp.bfloat16), "blk", scatter_dimension=0, tiled=True
        ).astype(jnp.float32),
    )
    summed = (
        lax.psum(block_parts[0].astype(jnp.bfloat16), "slide").astype(jnp.float32),
        lax.psum(block_parts[1].astype(jnp.bfloat16), "slide").astype(jnp.float32),
        lax.psum(block_parts[2].astype(jnp.bfloat16), "slide").astype(jnp.float32),
        lax.psum(block_parts[3].astype(jnp.bfloat16), "slide").astype(jnp.float32),
        lax.psum(block_parts[4].astype(jnp.bfloat16), "slide").astype(jnp.float32),
        lax.psum(block_parts[5].astype(jnp.bfloat16), "slide").astype(jnp.float32),
        lax.psum(block_parts[6].astype(jnp.bfloat16), "slide").astype(jnp.float32),
        lax.psum(block_parts[7].astype(jnp.bfloat16), "slide").astype(jnp.float32),
        lax.psum(block_parts[8].astype(jnp.bfloat16), "slide").astype(jnp.float32),
        lax.psum(block_parts[9].astype(jnp.bfloat16), "slide").astype(jnp.float32),
    )
    embed_out = summed[0]
    decode_out = summed[7]
    return (
        decoded[None],
        prior[None],
        expr_grad[None],
        embed_out,
        summed[1],
        summed[2],
        summed[3],
        summed[4],
        summed[5],
        summed[6],
        decode_out,
        summed[8],
        summed[9],
    )


def peers(offset, count):
    return [(place, place ^ offset) for place in range(count)]


def swap(pieces):
    count = len(pieces)
    return [pieces[0]] + [
        lax.ppermute(pieces[k], "slide", peers(k, count)) for k in range(1, count)
    ]


def share_halves(rows):
    half = rows.shape[0] // 2
    upper, lower = rows[:half], rows[half:]
    upper_x = lax.ppermute(upper, "slide", peers(1, 4))
    lower_y = lax.ppermute(lower, "slide", peers(2, 4))
    uppers = lax.ppermute(jnp.concatenate([upper, upper_x], axis=0), "slide", peers(2, 4))
    lowers = lax.ppermute(jnp.concatenate([lower, lower_y], axis=0), "slide", peers(1, 4))
    return [rows, upper_x, lower_y, uppers, lowers]


def share(rows, count):
    return swap([rows] * count)


def after(value, *earlier):
    return lax.optimization_barrier((value,) + earlier)[0]


def in_order(pieces, me, axis):
    stacked = jnp.stack(pieces)
    return jnp.concatenate(
        [
            lax.dynamic_index_in_dim(stacked, jnp.bitwise_xor(me, k), 0, keepdims=False)
            for k in range(len(pieces))
        ],
        axis=axis,
    )


def exact_dot(former, latter, left, right):
    return lax.dot_general(
        former,
        latter,
        (((left,), (right,)), ((), ())),
        precision=lax.Precision.HIGHEST,
        preferred_element_type=jnp.float32,
    )


def lowered(partials):
    return [partials[0]] + [piece.astype(jnp.bfloat16) for piece in partials[1:]]


def collect(partials):
    arrived = swap(partials)
    total = arrived[0]
    for piece in arrived[1:]:
        total = total + piece.astype(jnp.float32)
    return total


def gather_blk(piece, axis=0):
    return lax.all_gather(piece, "blk", axis=axis, tiled=True)


def scatter_blk(piece, axis=0):
    return lax.psum_scatter(piece, "blk", scatter_dimension=axis, tiled=True)


def to_core(rows):
    count = lax.axis_size("blk")
    return lax.ppermute(rows, "blk", [(place, place ^ 1) for place in range(count)])


def to_chip(rows, offset):
    count = lax.axis_size("blk")
    return lax.ppermute(rows, "blk", [(place, place ^ (2 * offset)) for place in range(count)])


def split_rows(rows, count):
    height = rows.shape[0] // count
    return [rows[k * height : (k + 1) * height] for k in range(count)]


ROWS = 432
STEP = 864
TALL = 1728
WIDE = 3456
CHUNKS = 2
SMALL = 16
COST = pl.CostEstimate(flops=0, bytes_accessed=0, transcendentals=0)


def expression_kernel(count, quarter, genes, me_ref, library_ref, counts_ref, *rest):
    outs, buffers, sems = rest[:count], rest[count], rest[count + 1]
    me = me_ref[0]
    tail = genes - (count - 1) * quarter
    library = library_ref[...].astype(jnp.float32)

    def copy(k, rows):
        start = pl.multiple_of(jnp.bitwise_xor(me, k) * quarter, 8)
        return pltpu.make_async_copy(
            counts_ref.at[pl.ds(start, rows), 0, :],
            buffers.at[k, pl.ds(0, rows), :],
            sems.at[k],
        )

    def each(k, act):
        last = jnp.bitwise_xor(me, k) == count - 1

        @pl.when(last)
        def _():
            act(copy(k, tail))

        @pl.when(jnp.logical_not(last))
        def _():
            act(copy(k, quarter))

    order = list(range(1, count)) + [0]
    for k in order:
        each(k, lambda one: one.start())
    for k in order:
        each(k, lambda one: one.wait())
        have = genes - jnp.bitwise_xor(me, k) * quarter

        @pl.loop(0, quarter // ROWS)
        def _(step):
            start = pl.multiple_of(step * ROWS, ROWS)
            values = buffers[k, pl.ds(start, ROWS), :].astype(jnp.float32)
            values = jnp.log1p(values * 10000.0 / library)
            row = start + lax.broadcasted_iota(jnp.int32, values.shape, 0)
            outs[k][pl.ds(start, ROWS), :] = jnp.where(row < have, values, 0.0).astype(jnp.bfloat16)


def expression_parts(counts, library, me, count, quarter):
    genes = counts.shape[2]
    cells = counts.shape[1]
    part = jax.ShapeDtypeStruct((quarter, cells), jnp.bfloat16)
    return pl.pallas_call(
        functools.partial(expression_kernel, count, quarter, genes),
        out_shape=[part] * count,
        in_specs=[
            pl.BlockSpec(memory_space=pltpu.SMEM),
            pl.BlockSpec(memory_space=pltpu.VMEM),
            pl.BlockSpec(memory_space=pltpu.HBM),
        ],
        out_specs=[pl.BlockSpec(memory_space=pltpu.VMEM)] * count,
        scratch_shapes=[
            pltpu.VMEM((count, quarter, cells), jnp.int32),
            pltpu.SemaphoreType.DMA((count,)),
        ],
        compiler_params=pltpu.CompilerParams(vmem_limit_bytes=58 * 2**20),
        cost_estimate=COST,
        name="expression",
    )(me.reshape(1), library, jnp.transpose(counts, (2, 0, 1)))


def spread_kernel(count, quarter, genes, me_ref, *rest):
    pieces, out, held, wide, sems_in, sems_out = rest[:count], *rest[count:]
    me = me_ref[0]
    tail = genes - (count - 1) * quarter

    def arrive(k):
        return pltpu.make_async_copy(pieces[k], held.at[k], sems_in.at[k])

    def leave(k):
        rows = tail if k == count - 1 else quarter
        return pltpu.make_async_copy(
            wide.at[k, pl.ds(0, rows), :], out.at[pl.ds(k * quarter, rows), 0, :], sems_out.at[k]
        )

    for k in range(count):
        arrive(k).start()
    for k in range(count):
        arrive(k).wait()
    for k in range(count):
        source = jnp.bitwise_xor(me, k)

        @pl.loop(0, quarter // ROWS)
        def _(step):
            rows = pl.ds(pl.multiple_of(step * ROWS, ROWS), ROWS)
            wide[k, rows, :] = held[source, rows, :].astype(jnp.float32)

        leave(k).start()
    for k in range(count):
        leave(k).wait()


def spread_parts(pieces, me, genes):
    count = len(pieces)
    quarter, cells = pieces[0].shape
    out = pl.pallas_call(
        functools.partial(spread_kernel, count, quarter, genes),
        out_shape=jax.ShapeDtypeStruct((genes, 1, cells), jnp.float32),
        in_specs=[pl.BlockSpec(memory_space=pltpu.SMEM)]
        + [pl.BlockSpec(memory_space=pl.ANY)] * count,
        out_specs=pl.BlockSpec(memory_space=pltpu.HBM),
        scratch_shapes=[
            pltpu.VMEM((count, quarter, cells), jnp.bfloat16),
            pltpu.VMEM((count, quarter, cells), jnp.float32),
            pltpu.SemaphoreType.DMA((count,)),
            pltpu.SemaphoreType.DMA((count,)),
        ],
        compiler_params=pltpu.CompilerParams(vmem_limit_bytes=40 * 2**20),
        cost_estimate=COST,
        name="spread",
    )(me.reshape(1), *pieces)
    return jnp.transpose(out, (1, 2, 0))


def join_kernel(count, me_ref, *rest):
    pieces, out, held, sems = rest[:count], *rest[count:]
    slot = pl.program_id(0)

    def arrive(k):
        rows = pl.ds(0, held.shape[1])
        return pltpu.make_async_copy(pieces[k].at[rows, :], held.at[k], sems.at[k])

    @pl.when(slot == 0)
    def _():
        for k in range(count):
            arrive(k).start()
        for k in range(count):
            arrive(k).wait()

    source = jnp.bitwise_xor(me_ref[0], slot)

    @pl.loop(0, out.shape[0] // ROWS)
    def _(step):
        rows = pl.ds(pl.multiple_of(step * ROWS, ROWS), ROWS)
        out[rows, :] = held[source, rows, :].astype(out.dtype)


def join_parts(pieces, me, quarter, genes, dtype):
    count = len(pieces)
    cells = pieces[0].shape[1]
    return pl.pallas_call(
        functools.partial(join_kernel, count),
        grid=(count,),
        out_shape=jax.ShapeDtypeStruct((genes, cells), dtype),
        in_specs=[pl.BlockSpec(memory_space=pltpu.SMEM)]
        + [pl.BlockSpec(memory_space=pl.ANY)] * count,
        out_specs=pl.BlockSpec((quarter, cells), lambda slot: (slot, 0)),
        scratch_shapes=[
            pltpu.VMEM((count, quarter, cells), jnp.bfloat16),
            pltpu.SemaphoreType.DMA((count,)),
        ],
        compiler_params=pltpu.CompilerParams(vmem_limit_bytes=40 * 2**20),
        cost_estimate=COST,
        name="join",
    )(me.reshape(1), *pieces)


def order_kernel(count, me_ref, *refs):
    pieces, out, sems = refs[:count], refs[-2], refs[-1]
    height = pieces[0].shape[0]

    def move(k):
        first = pl.multiple_of(jnp.bitwise_xor(me_ref[0], k) * height, height)
        return pltpu.make_async_copy(pieces[k], out.at[pl.ds(first, height), :], sems.at[k])

    for k in range(count):
        move(k).start()
    for k in range(count):
        move(k).wait()


def order_rows(pieces, me):
    count = len(pieces)
    height, width = pieces[0].shape
    return pl.pallas_call(
        functools.partial(order_kernel, count),
        out_shape=jax.ShapeDtypeStruct((count * height, width), pieces[0].dtype),
        in_specs=[pl.BlockSpec(memory_space=pltpu.SMEM)]
        + [pl.BlockSpec(memory_space=pl.ANY)] * count,
        out_specs=pl.BlockSpec(memory_space=pltpu.VMEM),
        scratch_shapes=[pltpu.SemaphoreType.DMA((count,))],
        cost_estimate=COST,
        name="order_rows",
    )(me.reshape(1), *pieces)


def turn_kernel(count, *refs):
    out = refs[-1]
    for k in range(count):
        height = refs[k].shape[1]
        out[k * height : (k + 1) * height, :] = jnp.transpose(refs[k][...])


def turn_parts(parts):
    count = len(parts)
    quarter, cells = parts[0].shape
    return pl.pallas_call(
        functools.partial(turn_kernel, count),
        grid=(quarter // WIDE,),
        out_shape=jax.ShapeDtypeStruct((count * cells, quarter), jnp.bfloat16),
        in_specs=[pl.BlockSpec((WIDE, cells), lambda step: (step, 0))] * count,
        out_specs=pl.BlockSpec((count * cells, WIDE), lambda step: (0, step)),
        compiler_params=pltpu.CompilerParams(vmem_limit_bytes=40 * 2**20),
        cost_estimate=COST,
        name="turn_parts",
    )(*parts)


def finish_kernel(count, quarter, mean_cols, folds, me_ref, *refs):
    pieces = refs[:count]
    out, norm, means, bias, held, sems = refs[count:]
    slot = pl.program_id(0)

    def arrive(k):
        place = jnp.bitwise_xor(me_ref[0], k)
        return pltpu.make_async_copy(pieces[k], held.at[place], sems.at[k])

    @pl.when(slot == 0)
    def _():
        for k in range(count):
            arrive(k).start()
        for k in range(count):
            arrive(k).wait()
        small = [held[q, quarter:, :].astype(jnp.float32) for q in range(count)]
        total = sum(small[1:], small[0])
        norm[...] = total[:4, :]
        width = means.shape[1]
        for k in range(folds):
            means[k * mean_cols : (k + 1) * mean_cols, :] = total[
                4 : 4 + mean_cols, k * width : (k + 1) * width
            ]
        bias[...] = jnp.concatenate(
            [one[4 + mean_cols : 5 + mean_cols, :] for one in small], axis=0
        )

    out[...] = held[slot, :quarter, :].astype(out.dtype)


def finish(pieces, me, quarter, genes, mean_cols, folds):
    count = len(pieces)
    height, cells = pieces[0].shape
    return pl.pallas_call(
        functools.partial(finish_kernel, count, quarter, mean_cols, folds),
        grid=(count,),
        out_shape=[
            jax.ShapeDtypeStruct((genes, cells), jnp.float32),
            jax.ShapeDtypeStruct((4, cells), jnp.float32),
            jax.ShapeDtypeStruct((folds * mean_cols, cells // folds), jnp.float32),
            jax.ShapeDtypeStruct((count, cells), jnp.float32),
        ],
        in_specs=[pl.BlockSpec(memory_space=pltpu.SMEM)]
        + [pl.BlockSpec(memory_space=pl.ANY)] * count,
        out_specs=[
            pl.BlockSpec((quarter, cells), lambda slot: (slot, 0)),
            pl.BlockSpec((4, cells), lambda slot: (0, 0)),
            pl.BlockSpec((folds * mean_cols, cells // folds), lambda slot: (0, 0)),
            pl.BlockSpec((count, cells), lambda slot: (0, 0)),
        ],
        scratch_shapes=[
            pltpu.VMEM((count, height, cells), jnp.bfloat16),
            pltpu.SemaphoreType.DMA((count,)),
        ],
        compiler_params=pltpu.CompilerParams(vmem_limit_bytes=40 * 2**20),
        cost_estimate=COST,
        name="finish",
    )(me.reshape(1), *pieces)


def scores_kernel(rows, table, *outs):
    product = jnp.dot(rows[...], table[...], preferred_element_type=jnp.float32)
    height = outs[0].shape[0]
    for k in range(len(outs)):
        outs[k][...] = product[k * height : (k + 1) * height, :].astype(outs[k].dtype)


def embed_cells(rows, table, count):
    height, quarter = rows.shape
    width = table.shape[1]
    block = math.gcd(width, 512)
    return pl.pallas_call(
        scores_kernel,
        grid=(width // block,),
        out_shape=[
            jax.ShapeDtypeStruct((height // count, width), jnp.float32 if k == 0 else jnp.bfloat16)
            for k in range(count)
        ],
        in_specs=[
            pl.BlockSpec((height, quarter), lambda step: (0, 0)),
            pl.BlockSpec((quarter, block), lambda step: (0, step)),
        ],
        out_specs=[pl.BlockSpec((height // count, block), lambda step: (0, step))] * count,
        compiler_params=pltpu.CompilerParams(vmem_limit_bytes=58 * 2**20),
        cost_estimate=COST,
        name="embed_cells",
    )(rows, table)


def latents_kernel(count, table, *refs):
    cots, outs, total = refs[:count], refs[count:-1], refs[-1]
    step = pl.program_id(0)
    product = jnp.dot(
        table[...],
        jnp.concatenate([one[...] for one in cots], axis=1),
        preferred_element_type=jnp.float32,
    )

    @pl.when(step == 0)
    def _():
        total[...] = product

    @pl.when(step > 0)
    def _():
        total[...] += product

    @pl.when(step == pl.num_programs(0) - 1)
    def _():
        cells = outs[0].shape[0]
        for k in range(count):
            outs[k][...] = jnp.transpose(total[:, k * cells : (k + 1) * cells]).astype(
                outs[k].dtype
            )


def cots_to_latents(cots, table):
    count = len(cots)
    width, quarter = table.shape
    cells = cots[0].shape[1]
    return pl.pallas_call(
        functools.partial(latents_kernel, count),
        grid=(quarter // WIDE,),
        out_shape=[
            jax.ShapeDtypeStruct((cells, width), jnp.float32 if k == 0 else jnp.bfloat16)
            for k in range(count)
        ],
        in_specs=[pl.BlockSpec((width, WIDE), lambda step: (0, step))]
        + [pl.BlockSpec((WIDE, cells), lambda step: (step, 0))] * count,
        out_specs=[pl.BlockSpec((cells, width), lambda step: (0, 0))] * count,
        scratch_shapes=[pltpu.VMEM((width, count * cells), jnp.float32)],
        compiler_params=pltpu.CompilerParams(vmem_limit_bytes=40 * 2**20),
        cost_estimate=COST,
        name="cots_to_latents",
    )(table, *cots)


def gelu_slope(rows):
    scale = math.sqrt(2.0 / math.pi)
    squares = rows * rows
    bent = jnp.tanh(scale * (rows + 0.044715 * (squares * rows)))
    inner = scale * (1.0 + (3.0 * 0.044715) * squares)
    return 0.5 * (1.0 + bent) + 0.5 * rows * (1.0 - bent * bent) * inner


UNITS = 1024


def feed_forward_kernel(count, up, bias, down, *refs):
    parts, stacked, total = refs[:count], refs[-2], refs[-1]
    pre, hidden, *outs = refs[count:-2]
    cells = parts[0].shape[0]
    step = pl.program_id(0)

    @pl.when(step == 0)
    def _():
        for k in range(count):
            stacked[k * cells : (k + 1) * cells, :] = parts[k][...]

    rows = jnp.dot(stacked[...], up[...], preferred_element_type=jnp.float32) + bias[...]
    pre[...] = rows
    bent = jnp.tanh(math.sqrt(2.0 / math.pi) * (rows + 0.044715 * (rows * rows * rows)))
    low = (rows * (0.5 * (1.0 + bent))).astype(jnp.bfloat16)
    hidden[...] = low
    product = jnp.dot(low, down[...], preferred_element_type=jnp.float32)

    @pl.when(step == 0)
    def _():
        total[...] = product

    @pl.when(step > 0)
    def _():
        total[...] += product

    @pl.when(step == pl.num_programs(0) - 1)
    def _():
        for k in range(count):
            outs[k][...] = total[k * cells : (k + 1) * cells, :].astype(outs[k].dtype)


def feed_forward(parts, up, bias, down):
    count = len(parts)
    cells, width = parts[0].shape
    units = down.shape[0]
    rows = count * cells
    return pl.pallas_call(
        functools.partial(feed_forward_kernel, count),
        grid=(units // UNITS,),
        out_shape=[
            jax.ShapeDtypeStruct((rows, units), jnp.float32),
            jax.ShapeDtypeStruct((rows, units), jnp.bfloat16),
        ]
        + [
            jax.ShapeDtypeStruct((cells, width), jnp.float32 if k == 0 else jnp.bfloat16)
            for k in range(count)
        ],
        in_specs=[
            pl.BlockSpec((width, UNITS), lambda step: (0, step)),
            pl.BlockSpec((1, UNITS), lambda step: (0, step)),
            pl.BlockSpec((UNITS, width), lambda step: (step, 0)),
        ]
        + [pl.BlockSpec((cells, width), lambda step: (0, 0))] * count,
        out_specs=[pl.BlockSpec((rows, UNITS), lambda step: (0, step))] * 2
        + [pl.BlockSpec((cells, width), lambda step: (0, 0))] * count,
        scratch_shapes=[
            pltpu.VMEM((rows, width), jnp.bfloat16),
            pltpu.VMEM((rows, width), jnp.float32),
        ],
        compiler_params=pltpu.CompilerParams(vmem_limit_bytes=48 * 2**20),
        cost_estimate=COST,
        name="feed_forward",
    )(up, bias, down, *parts)


def feed_back_kernel(count, latent, down, up, pre, *refs):
    parts = refs[:count]
    own, down_input, pre_grad, bias, *outs = refs[count:]
    cells = own.shape[0]
    width = own.shape[1]
    h_grad = jnp.dot(
        jnp.concatenate([part[:, : latent.shape[0]] for part in parts], axis=0),
        latent[...],
        preferred_element_type=jnp.float32,
    )
    own[...] = h_grad[:cells, :]
    down_input[...] = h_grad.astype(jnp.bfloat16)
    step = 256
    for start in range(0, pre.shape[1], step):
        columns = slice(start, start + step)
        hidden_grad = lax.dot_general(
            down_input[...],
            down[columns, :],
            (((1,), (1,)), ((), ())),
            preferred_element_type=jnp.float32,
        )
        low = (hidden_grad * gelu_slope(pre[:, columns])).astype(jnp.bfloat16)
        pre_grad[:, columns] = low
        bias[:, columns] = jnp.sum(low.astype(jnp.float32), axis=0, keepdims=True)
    product = lax.dot_general(
        pre_grad[...], up[...], (((1,), (1,)), ((), ())), preferred_element_type=jnp.float32
    )
    for k in range(count):
        outs[k][...] = product[k * cells : (k + 1) * cells, :].astype(outs[k].dtype)


def feed_back(parts, latent, down, up, pre):
    count = len(parts)
    cells = parts[0].shape[0]
    width = latent.shape[1]
    units = pre.shape[1]

    def whole(array):
        return pl.BlockSpec(array.shape, lambda step: (0,) * len(array.shape))

    shapes = [
        jax.ShapeDtypeStruct((cells, width), jnp.float32),
        jax.ShapeDtypeStruct((count * cells, width), jnp.bfloat16),
        jax.ShapeDtypeStruct((count * cells, units), jnp.bfloat16),
        jax.ShapeDtypeStruct((1, units), jnp.float32),
    ] + [
        jax.ShapeDtypeStruct((cells, width), jnp.float32 if k == 0 else jnp.bfloat16)
        for k in range(count)
    ]
    operands = [latent, down, up, pre, *parts]
    return pl.pallas_call(
        functools.partial(feed_back_kernel, count),
        grid=(1,),
        out_shape=shapes,
        in_specs=[whole(one) for one in operands[:2]]
        + [pl.BlockSpec((width, units), lambda step: (0, 0))]
        + [whole(one) for one in operands[3:]],
        out_specs=[whole(one) for one in shapes],
        compiler_params=pltpu.CompilerParams(vmem_limit_bytes=56 * 2**20),
        cost_estimate=COST,
        name="feed_back",
    )(*operands)


def decode_kernel(count, table, *refs):
    rows, outs = refs[:count], refs[count:]
    cells = rows[0].shape[0]
    product = jnp.dot(
        jnp.concatenate([one[...] for one in rows], axis=0),
        table[...],
        preferred_element_type=jnp.float32,
    ).astype(jnp.bfloat16)
    for k in range(count):
        outs[k][...] = jnp.transpose(product[k * cells : (k + 1) * cells, :])


def decode_genes(latents, table):
    count = len(latents)
    cells = latents[0].shape[0]
    width, quarter = table.shape
    last = latents[0].shape[1] // width - 1
    return pl.pallas_call(
        functools.partial(decode_kernel, count),
        grid=(1,),
        out_shape=[jax.ShapeDtypeStruct((quarter, cells), jnp.bfloat16)] * count,
        in_specs=[pl.BlockSpec((width, quarter), lambda step: (0, 0))]
        + [pl.BlockSpec((cells, width), lambda step: (0, last))] * count,
        out_specs=[pl.BlockSpec((quarter, cells), lambda step: (0, 0))] * count,
        compiler_params=pltpu.CompilerParams(vmem_limit_bytes=40 * 2**20),
        cost_estimate=COST,
        name="decode_genes",
    )(table, *latents)


def chip_offsets(chips):
    order = [0]
    bit = chips // 2
    while bit:
        order = order + [one + bit for one in order]
        bit //= 2
    return order


def last_kernel(count, first, offsets, places, normed, projected, both, *refs):
    pre_grads, cots = refs[:count], refs[count : 2 * count]
    kept, sent, turned = refs[2 * count :]
    me, place = places[0], places[1]
    cells = cots[0].shape[0]
    width = normed.shape[1]
    block = kept.shape[0] // len(offsets)

    def by_offset(first):
        return jnp.concatenate(
            [
                both[
                    pl.ds(pl.multiple_of(jnp.bitwise_xor(me, k) * cells, cells), cells),
                    first : first + width,
                ]
                for k in range(count)
            ],
            axis=0,
        )

    spot = 0
    for group, (rows, columns) in enumerate(
        (
            (normed[...], [projected[k] for k in range(projected.shape[0])]),
            (by_offset(0), [jnp.concatenate([one[:, first:] for one in cots], axis=0)]),
            (by_offset(width), [jnp.concatenate([one[...] for one in pre_grads], axis=0)]),
        )
    ):
        turned[group] = jnp.transpose(rows)
        for one in columns:
            size = one.shape[1]
            for out, core in ((kept, place % 2), (sent, 1 - place % 2)):
                owners = [jnp.bitwise_xor(place // 2, k) * 2 + core for k in offsets]
                ordered = jnp.concatenate(
                    [
                        turned[group, pl.ds(pl.multiple_of(owner * block, block), block), :]
                        for owner in owners
                    ],
                    axis=0,
                )
                out[:, spot : spot + size] = jnp.dot(
                    ordered, one, preferred_element_type=jnp.float32
                ).astype(out.dtype)
            spot += size


def last_products(normed, projected, pre_grads, both, cots, first, me, place):
    count = len(cots)
    height = normed.shape[1]
    offsets = chip_offsets(lax.axis_size("blk") // 2)
    width = projected.shape[0] * projected.shape[2] + 2 * pre_grads[0].shape[1]
    return pl.pallas_call(
        functools.partial(last_kernel, count, first, offsets),
        out_shape=[
            jax.ShapeDtypeStruct((height // 2, width), jnp.float32),
            jax.ShapeDtypeStruct((height // 2, width), jnp.bfloat16),
        ],
        in_specs=[pl.BlockSpec(memory_space=pltpu.SMEM)]
        + [pl.BlockSpec(memory_space=pltpu.VMEM)] * (3 + 2 * count),
        out_specs=[pl.BlockSpec(memory_space=pltpu.VMEM)] * 2,
        scratch_shapes=[pltpu.VMEM((3, height, normed.shape[0]), jnp.bfloat16)],
        compiler_params=pltpu.CompilerParams(vmem_limit_bytes=40 * 2**20),
        cost_estimate=COST,
        name="last_products",
    )(jnp.stack([me, place]), normed, projected, both, *pre_grads, *cots)


def half_kernel(kept, other, stay, go):
    height = stay.shape[0]
    stay[...] = kept[:height, :] + other[:height, :].astype(jnp.float32)
    go[...] = (kept[height:, :] + other[height:, :].astype(jnp.float32)).astype(go.dtype)


def merge_half(kept, other):
    height, width = kept.shape
    return pl.pallas_call(
        half_kernel,
        out_shape=[
            jax.ShapeDtypeStruct((height // 2, width), jnp.float32),
            jax.ShapeDtypeStruct((height // 2, width), jnp.bfloat16),
        ],
        in_specs=[pl.BlockSpec(memory_space=pltpu.VMEM)] * 2,
        out_specs=[pl.BlockSpec(memory_space=pltpu.VMEM)] * 2,
        compiler_params=pltpu.CompilerParams(vmem_limit_bytes=40 * 2**20),
        cost_estimate=COST,
        name="merge_half",
    )(kept, other)


def pair_kernel(count, *refs):
    parts, out = refs[:count], refs[-1]
    width = out.shape[2]
    for j in range(out.shape[0] // count):
        for k in range(count):
            out[j * count + k] = parts[k][:, j * width : (j + 1) * width]


def pair_up(parts, pairs):
    count = len(parts)
    cells, width = parts[0].shape
    return pl.pallas_call(
        functools.partial(pair_kernel, count),
        out_shape=jax.ShapeDtypeStruct((pairs * count, cells, width // pairs), parts[0].dtype),
        in_specs=[pl.BlockSpec(memory_space=pltpu.VMEM)] * count,
        out_specs=pl.BlockSpec(memory_space=pltpu.VMEM),
        cost_estimate=COST,
        name="pair_up",
    )(*parts)


def assemble_kernel(count, sizes, me_ref, *refs):
    early, parts = refs[:5], refs[5 : 5 + count]
    down, up, qkv, attn, latent, decode, middle, last, sems = refs[5 + count :]
    blocks, pairs, pair, quarter, half = sizes
    me = me_ref[0]
    rows, width = attn.shape
    cut = rows // 2
    upper, lower = pl.ds(0, cut), pl.ds(cut, cut)
    ours, upper_x, lower_y, uppers, lowers = early
    moves = [
        (ours, middle.at[me]),
        (upper_x, middle.at[jnp.bitwise_xor(me, 1), upper, :]),
        (lower_y, middle.at[jnp.bitwise_xor(me, 2), lower, :]),
        (uppers.at[upper, :], middle.at[jnp.bitwise_xor(me, 2), upper, :]),
        (uppers.at[lower, :], middle.at[jnp.bitwise_xor(me, 3), upper, :]),
        (lowers.at[upper, :], middle.at[jnp.bitwise_xor(me, 1), lower, :]),
        (lowers.at[lower, :], middle.at[jnp.bitwise_xor(me, 3), lower, :]),
    ] + [(parts[k], last.at[jnp.bitwise_xor(me, k)]) for k in range(count)]
    copies = [
        pltpu.make_async_copy(source, target, sems.at[k])
        for k, (source, target) in enumerate(moves)
    ]
    for one in copies:
        one.start()
    for one in copies:
        one.wait()
    part = width // count
    ff = up.shape[1] // (count * blocks)
    latents, genes = decode.shape

    def piece(array, q, spot, size):
        return array[q, :, spot : spot + size].astype(jnp.float32)

    for q in range(count):
        down[q * rows : (q + 1) * rows, :] = piece(middle, q, 0, width)
        spot = width
        for b in range(blocks):
            up[:, (b * count + q) * ff : (b * count + q + 1) * ff] = piece(middle, q, spot, ff)
            spot += ff
        for side in range(2):
            first = q * quarter + side * half
            size = min(half, quarter - side * half, genes - first)
            if size > 0:
                decode[:, first : first + size] = middle[
                    q, side * latents : (side + 1) * latents, spot : spot + size
                ].astype(jnp.float32)
        spot = 0
        for j in range(pairs):
            for t in range(3):
                first = t * width + q * part + j * pair
                qkv[:, first : first + pair] = piece(last, q, spot, pair)
                spot += pair
        for out in (attn, latent):
            out[:, q * part : (q + 1) * part] = piece(last, q, spot, part)
            spot += part


def assemble(early, last, me, genes, quarter, half, latents, blocks, pairs, pair):
    count = len(last)
    rows = last[0].shape[0]
    width = blocks * rows
    shapes = [
        (count * rows, width),
        (rows, count * width),
        (rows, 3 * width),
        (rows, width),
        (rows, width),
        (latents, genes),
    ]
    return pl.pallas_call(
        functools.partial(assemble_kernel, count, (blocks, pairs, pair, quarter, half)),
        out_shape=[jax.ShapeDtypeStruct(shape, jnp.float32) for shape in shapes],
        in_specs=[pl.BlockSpec(memory_space=pltpu.SMEM)]
        + [pl.BlockSpec(memory_space=pl.ANY)] * (5 + count),
        out_specs=[pl.BlockSpec(memory_space=pltpu.VMEM)] * len(shapes),
        scratch_shapes=[
            pltpu.VMEM((count,) + early[0].shape, jnp.bfloat16),
            pltpu.VMEM((count,) + last[0].shape, jnp.bfloat16),
            pltpu.SemaphoreType.DMA((7 + count,)),
        ],
        compiler_params=pltpu.CompilerParams(vmem_limit_bytes=48 * 2**20),
        cost_estimate=COST,
        name="assemble",
    )(me.reshape(1), *early, *last)


def genes_kernel(count, table, *refs):
    rows, outs, stacked = refs[:count], refs[count : 2 * count], refs[-1]
    cells = rows[0].shape[0]

    @pl.when(pl.program_id(0) == 0)
    def _():
        for k in range(count):
            stacked[:, k * cells : (k + 1) * cells] = jnp.transpose(rows[k][...])

    product = jnp.dot(table[...], stacked[...], preferred_element_type=jnp.float32)
    for k in range(count):
        outs[k][...] = product[:, k * cells : (k + 1) * cells].astype(outs[k].dtype)


def cells_to_genes(table, rows, quarter):
    count = len(rows)
    cells, width = rows[0].shape
    return pl.pallas_call(
        functools.partial(genes_kernel, count),
        grid=(quarter // TALL,),
        out_shape=[jax.ShapeDtypeStruct((quarter, cells), jnp.bfloat16)] * count,
        in_specs=[pl.BlockSpec((TALL, width), lambda step: (step, 0))]
        + [pl.BlockSpec((cells, width), lambda step: (0, 0))] * count,
        out_specs=[pl.BlockSpec((TALL, cells), lambda step: (step, 0))] * count,
        scratch_shapes=[pltpu.VMEM((width, count * cells), jnp.bfloat16)],
        compiler_params=pltpu.CompilerParams(vmem_limit_bytes=58 * 2**20),
        cost_estimate=COST,
        name="cells_to_genes",
    )(table, *rows)


def embed_kernel(count, *refs):
    parts, rows = refs[:count], refs[count : 2 * count]
    small, out, stacked, results, sems = refs[2 * count :]
    steps = parts[0].shape[0] // STEP
    height = rows[0].shape[0]
    blocks, _, block = out.shape
    for k in range(count):
        stacked[k * height : (k + 1) * height, :] = rows[k][...]

    def leave(slot, step):
        start = pl.multiple_of(step * STEP, STEP)
        return pltpu.make_async_copy(
            results.at[slot], out.at[:, pl.ds(start, STEP), :], sems.at[slot]
        )

    last = pltpu.make_async_copy(
        small, out.at[:, pl.ds(steps * STEP, small.shape[1]), :], sems.at[2]
    )
    last.start()

    @pl.loop(0, steps)
    def _(step):
        slot = lax.rem(step, 2)

        @pl.when(step >= 2)
        def _():
            leave(slot, step - 2).wait()

        here = pl.ds(pl.multiple_of(step * STEP, STEP), STEP)
        product = jnp.dot(
            jnp.concatenate([part[here, :] for part in parts], axis=1),
            stacked[...],
            preferred_element_type=jnp.float32,
        ).astype(results.dtype)
        for k in range(blocks):
            results[slot, k] = product[:, k * block : (k + 1) * block]
        leave(slot, step).start()

    for step in range(max(steps - 2, 0), steps):
        leave(step % 2, step).wait()
    last.wait()


def embed_products(parts, rows, small):
    count = len(parts)
    quarter, cells = parts[0].shape
    width = rows[0].shape[1]
    blocks, extra, block = small.shape
    return pl.pallas_call(
        functools.partial(embed_kernel, count),
        out_shape=jax.ShapeDtypeStruct((blocks, quarter + extra, block), jnp.bfloat16),
        in_specs=[pl.BlockSpec(memory_space=pltpu.VMEM)] * (2 * count + 1),
        out_specs=pl.BlockSpec(memory_space=pltpu.HBM),
        scratch_shapes=[
            pltpu.VMEM((count * cells, width), jnp.bfloat16),
            pltpu.VMEM((2, blocks, STEP, block), jnp.bfloat16),
            pltpu.SemaphoreType.DMA((3,)),
        ],
        compiler_params=pltpu.CompilerParams(vmem_limit_bytes=58 * 2**20),
        cost_estimate=COST,
        name="embed_products",
    )(*parts, *rows, small)


def products_kernel(count, *refs):
    out = refs[-1]
    spot = 0
    for k in range(count):
        rows = jnp.transpose(refs[2 * k][...])
        columns = refs[2 * k + 1]
        width = columns.shape[1]
        for start in range(0, width, 256):
            out[:, spot + start : spot + start + 256] = jnp.dot(
                rows, columns[:, start : start + 256], preferred_element_type=jnp.float32
            ).astype(out.dtype)
        spot += width


def row_products(pairs):
    operands = [one for pair in pairs for one in pair]
    height = pairs[0][0].shape[1]
    width = sum(b.shape[1] for _, b in pairs)
    return pl.pallas_call(
        functools.partial(products_kernel, len(pairs)),
        out_shape=jax.ShapeDtypeStruct((height, width), jnp.bfloat16),
        in_specs=[pl.BlockSpec(memory_space=pltpu.VMEM)] * len(operands),
        out_specs=pl.BlockSpec(memory_space=pltpu.VMEM),
        compiler_params=pltpu.CompilerParams(vmem_limit_bytes=48 * 2**20),
        cost_estimate=COST,
        name="row_products",
    )(*operands)


def decoder_kernel(count, *refs):
    rows, cots, out, turned = refs[:count], refs[count : 2 * count], refs[-2], refs[-1]
    cells = rows[0].shape[0]

    @pl.when(pl.program_id(0) == 0)
    def _():
        for k in range(count):
            turned[:, k * cells : (k + 1) * cells] = jnp.transpose(rows[k][...])

    out[...] = lax.dot_general(
        turned[...],
        jnp.concatenate([one[...] for one in cots], axis=1),
        (((1,), (1,)), ((), ())),
        preferred_element_type=jnp.float32,
    ).astype(out.dtype)


def decoder_products(latents, cots, width):
    count = len(latents)
    cells = latents[0].shape[0]
    last = latents[0].shape[1] // width - 1
    quarter = cots[0].shape[0]
    step_rows = math.gcd(quarter, WIDE)
    return pl.pallas_call(
        functools.partial(decoder_kernel, count),
        grid=(quarter // step_rows,),
        out_shape=jax.ShapeDtypeStruct((width, quarter), jnp.bfloat16),
        in_specs=[pl.BlockSpec((cells, width), lambda step: (0, last))] * count
        + [pl.BlockSpec((step_rows, cells), lambda step: (step, 0))] * count,
        out_specs=pl.BlockSpec((width, step_rows), lambda step: (0, step)),
        scratch_shapes=[pltpu.VMEM((width, count * cells), jnp.bfloat16)],
        compiler_params=pltpu.CompilerParams(vmem_limit_bytes=40 * 2**20),
        cost_estimate=COST,
        name="decoder_products",
    )(*latents, *cots)


def head_probs(keys, queries, scaling):
    scores = (
        lax.dot_general(keys, queries, (((1,), (1,)), ((), ())), preferred_element_type=jnp.float32)
        * scaling
    )
    scores = jnp.exp(scores - jnp.max(scores, axis=0, keepdims=True))
    return scores * (1.0 / jnp.sum(scores, axis=0, keepdims=True))


def attend_kernel(heads, width, rows_ref, out, turned):
    step = pl.program_id(0)
    height = out.shape[0]
    group = heads * width

    @pl.when(step == 0)
    def _():
        turned[...] = jnp.transpose(rows_ref[:, 2 * group : 3 * group])

    block = rows_ref[pl.ds(pl.multiple_of(step * height, height), height), :group]
    results = []
    for h in range(heads):
        probs = head_probs(
            rows_ref[:, group + h * width : group + (h + 1) * width],
            block[:, h * width : (h + 1) * width],
            width ** (-0.5),
        ).astype(jnp.bfloat16)
        results.append(
            jnp.dot(turned[h * width : (h + 1) * width, :], probs, preferred_element_type=jnp.float32)
        )
    out[...] = jnp.transpose(jnp.concatenate(results, axis=0)).astype(out.dtype)


def attend(rows, heads):
    cells, total = rows.shape
    group = total // 3
    height = math.gcd(cells, 1024)
    return pl.pallas_call(
        functools.partial(attend_kernel, heads, group // heads),
        grid=(cells // height,),
        out_shape=jax.ShapeDtypeStruct((cells, group), jnp.bfloat16),
        in_specs=[pl.BlockSpec((cells, total), lambda step: (0, 0))],
        out_specs=pl.BlockSpec((height, group), lambda step: (step, 0)),
        scratch_shapes=[pltpu.VMEM((group, cells), jnp.bfloat16)],
        compiler_params=pltpu.CompilerParams(vmem_limit_bytes=40 * 2**20),
        cost_estimate=COST,
        name="attend",
    )(rows)


def attend_back_kernel(heads, width, rows_ref, cot_ref, out, turned, key_sum, value_sum):
    step = pl.program_id(0)
    group = heads * width
    height = rows_ref.shape[0] // pl.num_programs(0)
    scaling = width ** (-0.5)

    @pl.when(step == 0)
    def _():
        turned[...] = jnp.transpose(rows_ref[:, group : 2 * group])
        key_sum[...] = jnp.zeros_like(key_sum)
        value_sum[...] = jnp.zeros_like(value_sum)

    here = pl.ds(pl.multiple_of(step * height, height), height)
    block = rows_ref[here, :group]
    cots = cot_ref[here, :]
    results = []
    for h in range(heads):
        columns = slice(h * width, (h + 1) * width)
        queries = block[:, columns]
        cot = cots[:, columns]
        probs = head_probs(
            rows_ref[:, group + h * width : group + (h + 1) * width], queries, scaling
        )
        prob_grad = lax.dot_general(
            rows_ref[:, 2 * group + h * width : 2 * group + (h + 1) * width],
            cot,
            (((1,), (1,)), ((), ())),
            preferred_element_type=jnp.float32,
        )
        delta = jnp.sum(probs * prob_grad, axis=0, keepdims=True)
        score_grad = (probs * (prob_grad - delta)).astype(jnp.bfloat16)
        results.append(
            jnp.dot(turned[columns, :], score_grad, preferred_element_type=jnp.float32) * scaling
        )
        key_sum[:, columns] += jnp.dot(score_grad, queries, preferred_element_type=jnp.float32)
        value_sum[:, columns] += jnp.dot(
            probs.astype(jnp.bfloat16), cot, preferred_element_type=jnp.float32
        )
    out[here, :group] = jnp.transpose(jnp.concatenate(results, axis=0)).astype(out.dtype)

    @pl.when(step == pl.num_programs(0) - 1)
    def _():
        out[:, group : 2 * group] = (key_sum[...] * scaling).astype(out.dtype)
        out[:, 2 * group :] = value_sum[...].astype(out.dtype)


def attend_back(rows, cot, heads):
    cells, total = rows.shape
    group = total // 3
    height = math.gcd(cells, 1024)
    return pl.pallas_call(
        functools.partial(attend_back_kernel, heads, group // heads),
        grid=(cells // height,),
        out_shape=jax.ShapeDtypeStruct((cells, total), jnp.bfloat16),
        in_specs=[
            pl.BlockSpec((cells, total), lambda step: (0, 0)),
            pl.BlockSpec((cells, group), lambda step: (0, 0)),
        ],
        out_specs=pl.BlockSpec((cells, total), lambda step: (0, 0)),
        scratch_shapes=[
            pltpu.VMEM((group, cells), jnp.bfloat16),
            pltpu.VMEM((cells, group), jnp.float32),
            pltpu.VMEM((cells, group), jnp.float32),
        ],
        compiler_params=pltpu.CompilerParams(vmem_limit_bytes=40 * 2**20),
        cost_estimate=COST,
        name="attend_back",
    )(rows, cot)


def split_model(
    counts,
    library,
    coords,
    noise,
    decoded_cot,
    prior_cot,
    embed_t,
    w_qkv,
    w_attn_out,
    w_up,
    up_bias,
    w_down,
    w_latent,
    w_decode,
    comp_means,
    norm_params,
):
    slides = lax.axis_size("slide")
    blocks = lax.axis_size("blk")
    me = lax.axis_index("slide")
    genes = embed_t.shape[1]
    cells = counts.shape[1]
    model_width = w_attn_out.shape[1]
    own_rows = w_qkv.shape[0]
    latent_width = w_decode.shape[0] * blocks
    mixture_count = comp_means.shape[1]
    quarter = -(-genes // (slides * ROWS)) * ROWS
    padded = quarter * slides
    head_part = model_width // slides
    pair = model_width // blocks
    pairs = head_part // pair
    ff_part = up_bias.shape[0] // slides
    latent_part = model_width // slides

    def place_of(k):
        return jnp.bitwise_xor(me, k)

    def column_part(rows, width, place):
        return lax.dynamic_slice_in_dim(rows, place * width, width, 1)

    def whole(piece, axis):
        return in_order(share(piece, slides), me, axis)

    def wide(piece):
        return piece.astype(jnp.float32)

    embed_part = lax.dynamic_slice_in_dim(
        jnp.pad(embed_t.T, ((0, padded - genes), (0, 0))), me * quarter, quarter, 0
    )
    bias_part = lax.dynamic_slice_in_dim(up_bias, me * ff_part, ff_part, 0)
    mean_cols = comp_means.size // own_rows
    folds = mixture_count // mean_cols
    own_latents = w_decode.shape[0]
    small = jnp.concatenate(
        [
            norm_params.T,
            jnp.concatenate(
                [comp_means.T[k * mean_cols : (k + 1) * mean_cols] for k in range(folds)], axis=1
            ),
            bias_part.reshape(-1, own_rows),
        ],
        axis=0,
    )
    small_rows = small.shape[0]
    small = jnp.pad(small, ((0, SMALL - small_rows), (0, 0)))
    qkv_width = pairs * 3 * pair
    qkv_part = [
        lax.dynamic_slice_in_dim(w_qkv, k * model_width + me * head_part, head_part, 1)
        for k in range(3)
    ]
    qkv_part = jnp.concatenate(
        [part[:, j * pair : (j + 1) * pair] for j in range(pairs) for part in qkv_part], axis=1
    ).T
    out_latent = jnp.concatenate(
        [
            lax.dynamic_slice_in_dim(weight, me * head_part, head_part, 1)
            for weight in (w_attn_out, w_latent)
        ],
        axis=1,
    ).T
    embedding = gather_blk(
        jnp.concatenate([embed_part, small, qkv_part, out_latent], axis=0), 1
    )
    small_all = embedding[quarter : quarter + SMALL]
    qkv_end = quarter + SMALL + qkv_width
    weight_qkv = embedding[quarter + SMALL : qkv_end].reshape(pairs, 3 * pair, model_width)
    out_latent = embedding[qkv_end:]
    norm_float = small_all[:4].astype(jnp.float32)
    centres = small_all[4 : 4 + mean_cols].reshape(mean_cols, blocks, folds, own_latents)
    centres = jnp.transpose(centres, (1, 3, 2, 0)).reshape(latent_width, mixture_count)
    bias_up = small_all[4 + mean_cols].astype(jnp.float32)
    expr_parts = swap(expression_parts(counts, library, me, slides, quarter))

    cot_all = jnp.pad(decoded_cot[0].T, ((0, padded - genes), (0, 0)))
    cot_first = [
        lax.dynamic_slice_in_dim(cot_all, place_of(k) * quarter, quarter, 0)
        for k in range(slides)
    ]
    cot_parts = swap([after(piece, *expr_parts[1:]) for piece in cot_first])
    up_part = jnp.concatenate(
        [
            lax.dynamic_slice_in_dim(w_up, (k * slides + me) * ff_part, ff_part, 1)
            for k in range(blocks)
        ],
        axis=1,
    )
    down_part = lax.dynamic_slice_in_dim(w_down, me * ff_part, ff_part, 0)
    expr_rows = turn_parts(expr_parts)
    half = -(-quarter // 256) * 128
    decode_part = lax.dynamic_slice_in_dim(
        jnp.pad(w_decode, ((0, 0), (0, padded - genes))), me * quarter, quarter, 1
    )
    decode_part = jnp.concatenate(
        [decode_part[:, :half], jnp.pad(decode_part[:, half:], ((0, 0), (0, 2 * half - quarter)))],
        axis=0,
    )
    middle = gather_blk(
        after(
            jnp.concatenate([up_part, decode_part], axis=1),
            embedding,
            expr_rows,
            *cot_parts[1:],
        )
    )
    halves = middle[:, model_width:].reshape(blocks, 2, own_latents, half)
    weight_decode = jnp.concatenate(
        [
            halves[:, 0].reshape(latent_width, half),
            halves[:, 1].reshape(latent_width, half)[:, : quarter - half],
        ],
        axis=1,
    )

    h_zero = collect(embed_cells(expr_rows, embedding, slides))
    h_zero = h_zero + spatial_code(coords[0], model_width)
    normed_one, norm_one_back = jax.vjp(layer_norm, h_zero, norm_float[0], norm_float[1])
    normed_one_all = jnp.concatenate(share(normed_one.astype(jnp.bfloat16), slides), axis=0)
    projected = jnp.einsum(
        "ck,pfk->pcf", normed_one_all, weight_qkv, preferred_element_type=jnp.float32
    ).astype(jnp.bfloat16)

    def to_heads(rows):
        return lax.all_to_all(
            rows.reshape(blocks, cells, rows.shape[-1]), "blk", 0, 0, tiled=True
        ).reshape(blocks * cells, rows.shape[-1])

    out_shares = share(after(out_latent[:head_part], normed_one_all), slides)
    latent_cots = cots_to_latents(cot_parts, weight_decode)
    centres_float = centres.astype(jnp.float32)
    half_norms = 0.5 * jnp.sum(centres_float * centres_float, axis=0)
    head_rows, half_norms, centres_float = lax.optimization_barrier(
        (after(to_heads(projected), latent_cots[-1], *out_shares[1:]), half_norms, centres_float)
    )
    per_pair = pair // HEAD_DIM
    latent_shares = share(after(out_latent[head_part:], head_rows), slides)
    weight_out = order_rows(out_shares, me)
    weight_latent = order_rows(latent_shares, me)
    head_out = attend(head_rows, per_pair)
    weight_down = gather_blk(after(down_part, middle, weight_out))
    own_heads = to_heads(head_out).reshape(pairs, slides, cells, pair)
    own_heads = after(own_heads, *latent_shares[1:])
    attended_parts = swap(
        [
            jnp.concatenate([own_heads[j, k] for j in range(pairs)], axis=1)
            for k in range(slides)
        ]
    )
    attended_low = in_order(attended_parts, me, 1)
    h_one = h_zero + contract_cols(attended_low, weight_out)
    normed_two, norm_two_back = jax.vjp(layer_norm, h_one, norm_float[2], norm_float[3])
    normed_two_low = normed_two.astype(jnp.bfloat16)
    normed_two_rows = share(normed_two_low, slides)
    normed_two_rows[0] = after(normed_two_rows[0], weight_latent)
    hidden_pre, hidden_low, *h_two_parts = feed_forward(
        normed_two_rows, middle, bias_up[None], weight_down
    )
    normed_two_all = jnp.concatenate(normed_two_rows, axis=0)
    h_two_sum = collect(h_two_parts)
    latent_from_decode = collect(latent_cots)
    h_two = h_one + after(h_two_sum, latent_from_decode)
    h_two_low = h_two.astype(jnp.bfloat16)
    both_rows = lax.all_gather(
        jnp.concatenate([attended_low, h_two_low], axis=1), "slide", axis=0, tiled=True
    )
    latent_pre = contract_cols(h_two_low, weight_latent)
    spread = jnp.exp(0.5 * latent_pre[:, latent_width:])
    latent = latent_pre[:, :latent_width] + spread * noise[0]
    mixing = latent_width ** (-0.5)
    mix = (exact_dot(latent, centres_float, 1, 0) - half_norms) * mixing
    mix_max = jnp.max(mix, axis=-1, keepdims=True)
    mix_exp = jnp.exp(mix - mix_max)
    mix_sum = jnp.sum(mix_exp, axis=-1, keepdims=True)
    prior = -(mix_max + jnp.log(mix_sum))[:, 0]
    shares = prior_cot[0][:, None] * (mix_exp / mix_sum)
    latent_from_prior = exact_dot(shares, centres_float, 1, 1) * -mixing
    centre_grad = (
        centres_float * jnp.sum(shares, axis=0) - exact_dot(latent, shares, 0, 0)
    ) * mixing

    latent_total = latent_from_decode + latent_from_prior
    pre_grad = jnp.concatenate(
        [latent_total, latent_total * noise[0] * spread * 0.5], axis=-1
    ).astype(jnp.bfloat16)
    both_parts = share(
        jnp.concatenate([pre_grad, latent.astype(jnp.bfloat16)], axis=1), slides
    )
    h_two_grad, down_input, pre_hidden_grad, up_bias_grad, *normed_two_parts = feed_back(
        both_parts, weight_latent, weight_down, middle, hidden_pre
    )
    normed_two_grad = collect(normed_two_parts)
    latent_parts = [after(part, normed_two_parts[-1]) for part in both_parts]
    decode_local = decoder_products(latent_parts, cot_parts, latent_width)
    decoded_rows = decode_genes(latent_parts, weight_decode)
    normed_two_grad = after(normed_two_grad, decode_local, decoded_rows[-1])
    decode_own = scatter_blk(after(decode_local, both_rows, normed_two_grad))
    h_one_part, gain_two_grad, shift_two_grad = norm_two_back(normed_two_grad)
    h_one_grad = h_two_grad + h_one_part
    out_input = h_one_grad.astype(jnp.bfloat16)
    attended_grad = jnp.dot(out_input, weight_out, preferred_element_type=jnp.float32).astype(jnp.bfloat16)
    grad_parts = swap([column_part(attended_grad, head_part, place_of(k)) for k in range(slides)])
    out_heads = to_heads(pair_up(grad_parts, pairs))

    middle_local = row_products(
        [
            (hidden_low, after(down_input, *grad_parts[1:])),
            (normed_two_all, pre_hidden_grad),
        ]
    )
    out_heads = after(out_heads, middle_local)
    decoded_parts = swap(
        [after(one, *grad_parts[1:]) for one in decoded_rows[:-1]]
        + [after(decoded_rows[-1], out_heads)]
    )
    out_heads = after(out_heads, *decoded_parts[1:-1])
    head_grads = attend_back(head_rows, out_heads, per_pair)
    middle_grad = scatter_blk(after(middle_local, decode_own, head_grads))
    cot_cols = swap(
        [
            after(column_part(out_input, head_part, place_of(k)), head_grads)
            for k in range(slides)
        ]
    )
    projected_grad = to_heads(head_grads).reshape(pairs, slides * cells, 3 * pair)
    projected_grad = after(projected_grad, decoded_parts[-1], *cot_cols[1:])
    normed_one_parts = lowered(
        split_rows(
            jnp.einsum(
                "pcf,pfk->ck", projected_grad, weight_qkv, preferred_element_type=jnp.float32
            ),
            slides,
        )
    )
    normed_one_grad = collect(normed_one_parts)
    last_kept, last_sent = last_products(
        normed_one_all,
        after(projected_grad, normed_one_parts[-1]),
        [column_part(part, latent_part, me) for part in both_parts],
        both_rows,
        cot_cols,
        0,
        me,
        lax.axis_index("blk"),
    )
    last_kept, last_sent = merge_half(last_kept, to_core(last_sent))
    normed_one_grad = after(normed_one_grad, last_sent)
    h_zero_part, gain_one_grad, shift_one_grad = norm_one_back(normed_one_grad)
    h_zero_low = (h_one_grad + h_zero_part).astype(jnp.bfloat16)
    h_zero_parts = share(h_zero_low, slides)
    bit = 1
    while last_kept.shape[0] > own_rows:
        last_kept, last_sent = merge_half(last_kept, to_chip(last_sent, bit))
        bit *= 2
    h_zero_parts = [after(h_zero_parts[0], last_sent)] + h_zero_parts[1:]
    last_other = to_chip(last_sent, bit)

    small_grad = jnp.concatenate(
        [
            jnp.stack([gain_one_grad, shift_one_grad, gain_two_grad, shift_two_grad], axis=0),
            jnp.transpose(
                centre_grad.reshape(blocks, own_latents, folds, mean_cols), (3, 0, 2, 1)
            ).reshape(mean_cols, model_width),
            up_bias_grad,
        ],
        axis=0,
    )
    small_grad = jnp.pad(small_grad, ((0, SMALL - small_rows), (0, 0))).astype(jnp.bfloat16)
    small_grad = jnp.transpose(small_grad.reshape(SMALL, blocks, own_rows), (1, 0, 2))
    embed_local = embed_products(expr_parts, h_zero_parts, small_grad)
    gene_rows = cells_to_genes(
        embedding, [after(part, embed_local) for part in h_zero_parts], quarter
    )
    embed_own = scatter_blk(after(embed_local, middle_grad))[0]
    decode_half = jnp.concatenate(
        [decode_own[:, :half], jnp.pad(decode_own[:, half:], ((0, 0), (0, 2 * half - quarter)))],
        axis=0,
    )
    early = after(jnp.concatenate([middle_grad, decode_half], axis=1), *h_zero_parts[1:])
    early_parts = share_halves(early)
    gene_parts = swap([after(part, *early_parts[1:3]) for part in gene_rows])
    last_low = (last_kept + after(last_other, *gene_parts[1:3]).astype(jnp.float32)).astype(
        jnp.bfloat16
    )
    last_shares = share(last_low, slides)
    embed_shares = share(
        after(embed_own, *gene_parts[1:], *last_shares[1:], *early_parts[1:]), slides
    )
    expr_grad = spread_parts(gene_parts, me, genes)
    decoded = join_parts(decoded_parts, me, quarter, genes, jnp.bfloat16).T
    down_grad, up_grad, qkv_grad, attn_out_grad, latent_grad, decode_grad = assemble(
        early_parts, last_shares, me, genes, quarter, half, own_latents, blocks, pairs, pair
    )
    embed_grad, norm_grad, means_grad, up_bias_grad = finish(
        embed_shares, me, quarter, genes, mean_cols, folds
    )

    return (
        decoded[None],
        prior[None],
        expr_grad,
        embed_grad.T,
        qkv_grad,
        attn_out_grad,
        up_grad,
        up_bias_grad.reshape(-1),
        down_grad,
        latent_grad,
        decode_grad,
        means_grad.T,
        norm_grad.T,
    )


def fits(mesh):
    slides, blocks = mesh.shape["slide"], mesh.shape["blk"]
    return slides & (slides - 1) == 0 and HEADS % slides == 0 and HEADS % blocks == 0


def solution(mesh):
    placed = (
        P("slide", "blk", None),
        P("slide", "blk"),
        P("slide", "blk", None),
        P("slide", "blk", None),
        P("slide", "blk", None),
        P("slide", "blk"),
        P("blk", None),
        P("blk", None),
        P("blk", None),
        P("blk", None),
        P("blk"),
        P("blk", None),
        P("blk", None),
        P("blk", None),
        P("blk", None),
        P("blk", None),
    )
    return jax.shard_map(
        split_model if fits(mesh) else local,
        mesh=mesh,
        in_specs=placed,
        out_specs=(
            P("slide", "blk", None),
            P("slide", "blk"),
            P("slide", "blk", None),
            P("blk", None),
            P("blk", None),
            P("blk", None),
            P("blk", None),
            P("blk"),
            P("blk", None),
            P("blk", None),
            P("blk", None),
            P("blk", None),
            P("blk", None),
        ),
        check_vma=False,
    )
```
